32 devices in a mesh: dp: 4 (over y, core), group: 8 (over z, x).
Axes of the slice: x: 2, y: 2, z: 4, core: 2. Of those that a mesh axis runs over, the one named last changes fastest.
Arguments:
- tile_maps: bfloat16 [256, 16, 16, 384], P(('dp', 'group')), may hold values from -45 to 45
- positions: int32 [2, 256], P(None, ('dp', 'group')), may hold values from 0 to 511
- counts: int32 [4], P('dp'), may hold values from 1 to 64, as said below
- routing: int32 [4, 8, 8], P(None, 'group'), may hold values from -1 to 15, as said below
- depth_kernel: float32 [49, 384], replicated, may hold values from -0.875 to 0.875
- depth_bias: float32 [384], replicated, may hold values from -3 to 3
- norm_gain: float32 [384], replicated, may hold values from 0.25 to 1.75
- norm_shift: float32 [384], replicated, may hold values from -2 to 2
- expand_weight: bfloat16 [384, 1536], replicated, may hold values from -0.3125 to 0.3125
- expand_bias: float32 [1536], replicated, may hold values from -1.15 to -0.75
- reduce_weight: bfloat16 [1536, 384], replicated, may hold values from -0.15625 to 0.15625
- reduce_bias: float32 [384], replicated, may hold values from -2 to 2
- layer_scale: float32 [384], replicated, may hold values from 0.3 to 1.5
- head_weight: bfloat16 [384, 768], replicated, may hold values from -0.3125 to 0.3125
- slide_taps: float32 [7, 768], replicated, may hold values from -2.5 to 2.5
- slide_weight: bfloat16 [768, 768], replicated, may hold values from -0.21875 to 0.21875
- slide_bias: float32 [768], replicated, may hold values from -2 to 2
- cotangent: float32 [4, 768], P('dp'), may hold values from -180 to 180
Outputs:
- tile_out: bfloat16 [128, 16, 16, 384], P(('dp', 'group'))
- slide_feature: float32 [4, 768], P('dp')
- grad_expand: float32 [589824], P(('dp', 'group'))
- grad_reduce: float32 [589824], P(('dp', 'group'))
- grad_depth: float32 [18816], P(('dp', 'group'))
The draws below stay inside these ranges and needn't reach their ends.
Inputs may be any that keep to these rules, and one draw needn't show every extreme that they name: counts[d] is the number of tiles of slide d. At each group index the present tiles of all slides number at most 16, at group index 0 exactly that. routing[d, g, s] is -1 where the slot holds no tile, else e * 4 + p: the tile is processed at slot p of the device with dp index e and group index g. Each processing slot receives at most one tile; at group index 0 every one receives a tile. A device sends at most 2 tiles to each dp index, and some device sends exactly 2 to each.
All inputs are finite; a program needn't handle non-finite values.
Results may differ from the reference program's by a relative error of at most 0.013.
Values may be sent and summed in bfloat16 or wider, within the bound.
No kernel may reach another device: no remote copies, remote signals or barrier semaphores. Data moves between devices by JAX's collectives and lax.ppermute only.
A program may use at most 128 MiB of HBM per device.

```python
import math
import jax
import jax.numpy as jnp
from jax import lax

C = 384
HID = 1536
E = 768
KS = 7
TH = 16
KERNEL_TAPS = 7
TILE_DILATION = 3
PROC = 4
SLIDES = 4
GSIZE = 8
SLOTS = 8
SEQ = 64
TILES = 256
PTILES = 128


def slide_plan(key):
    base_key = jax.random.fold_in(key, 7001)
    busy = jax.random.randint(jax.random.fold_in(base_key, 1), (), 0, SLIDES)
    slide_ids = jnp.arange(SLIDES, dtype=jnp.int32)
    others = slide_ids != busy
    weights = jnp.where(others, jax.random.randint(jax.random.fold_in(base_key, 2), (SLIDES,), 2, 5), 0)
    avail = SLIDES * PROC - SLOTS - (SLIDES - 1)
    shares = avail * weights // jnp.sum(weights)
    leftover = avail - jnp.sum(shares)
    other_rank = jnp.cumsum(others.astype(jnp.int32)) - 1
    extra = jnp.where(others & (other_rank < leftover), 1, 0)
    per_device = jnp.where(others, 1 + shares + extra, SLOTS)
    tails = jax.random.randint(jax.random.fold_in(base_key, 3), (SLIDES,), 1, GSIZE + 1)
    tails = jnp.where(others, tails, GSIZE)
    return (GSIZE * (per_device - 1) + tails).astype(jnp.int32)


def draw_counts(key, part):
    return slide_plan(key)


def draw_routing(key, part):
    slide_counts = slide_plan(key)
    base_key = jax.random.fold_in(key, 7002)
    slot_ids = jnp.arange(SLOTS, dtype=jnp.int32)
    member_ids = jnp.arange(GSIZE, dtype=jnp.int32)
    present = slot_ids[None, None, :] * GSIZE + member_ids[None, :, None] < slide_counts[:, None, None]
    column = jnp.transpose(present, (1, 0, 2)).reshape(GSIZE, SLIDES * SLOTS).astype(jnp.int32)
    placed = jnp.cumsum(column, axis=1) - column
    dest_keys = jax.random.split(jax.random.fold_in(base_key, 1), GSIZE)
    dest_perm = jax.vmap(lambda one_key: jax.random.permutation(one_key, SLIDES))(dest_keys).astype(jnp.int32)
    slot_key_list = jax.random.split(jax.random.fold_in(base_key, 2), GSIZE * SLIDES)
    slot_perm = jax.vmap(lambda one_key: jax.random.permutation(one_key, PROC))(slot_key_list).astype(jnp.int32).reshape(GSIZE, SLIDES * PROC)
    receiver = jnp.take_along_axis(dest_perm, placed % SLIDES, axis=1)
    depth_rank = jnp.minimum(placed // SLIDES, PROC - 1)
    processor_slot = jnp.take_along_axis(slot_perm, receiver * PROC + depth_rank, axis=1)
    routed = jnp.where(column > 0, receiver * PROC + processor_slot, -1)
    return jnp.transpose(routed.reshape(GSIZE, SLIDES, SLOTS), (1, 0, 2)).astype(jnp.int32)


def draw_tile_maps(key, part):
    base_key = jax.random.fold_in(key, 7003)
    shape_all = (TILES, TH, TH, C)
    channel_scale = jnp.exp(jax.random.uniform(jax.random.fold_in(base_key, 2), (C,), jnp.float32, jnp.log(0.3), jnp.log(3.0)))
    cell_scale = jnp.exp(jax.random.uniform(jax.random.fold_in(base_key, 3), (TILES, TH, TH, 1), jnp.float32, jnp.log(0.4), jnp.log(2.5)))
    values = jnp.clip(jax.random.normal(jax.random.fold_in(base_key, 1), shape_all, jnp.float32), -6.0, 6.0)
    return (values * channel_scale * cell_scale).astype(jnp.bfloat16)


def place_ends(values, rng, low, largest):
    longest = values.shape.index(max(values.shape))
    spots = []
    for shift in (0, 1):
        where = [jax.random.randint(jax.random.fold_in(rng, axis), (), 0, length) for axis, length in enumerate(values.shape)]
        where[longest] = (where[longest] + shift) % values.shape[longest]
        spots.append(tuple(where))
    return values.at[spots[0]].set(low).at[spots[1]].set(largest)


def steps_of(key, shape, cuts, least, top_value):
    level = 1.0
    for dim, shards_of in cuts:
        draws = jax.random.uniform(jax.random.fold_in(jax.random.fold_in(key, 6), dim), (shards_of,), jnp.float32, least / len(cuts), top_value / len(cuts))
        level = level * jnp.repeat(jnp.exp(draws), shape[dim] // shards_of).reshape((-1,) + (1,) * (len(shape) - 1 - dim))
    return level


def bell_draw(rng, shape, spread, reach, cuts=(), kind=jnp.bfloat16):
    array = jax.random.normal(rng, shape, jnp.float32) * spread
    if len(cuts) > 0:
        array = steps_of(rng, shape, cuts, -0.22, 0.18) * array
    return jnp.clip(array, min=-reach, max=reach).astype(kind)


def setup_inputs(seed: int = 0) -> dict:
    seeds = jax.random.split(jax.random.key(seed), 19)
    return {
        "tile_maps": draw_tile_maps(jax.random.fold_in(seeds[18], 71), 0),
        "positions": place_ends(jax.random.randint(seeds[1], (2, TILES), 0, 512), jax.random.fold_in(seeds[1], 1), 0, 511).astype(jnp.int32),
        "counts": draw_counts(jax.random.fold_in(seeds[18], 71), 0),
        "routing": draw_routing(jax.random.fold_in(seeds[18], 71), 0),
        "depth_kernel": bell_draw(seeds[4], (KS * KS, C), (KS * KS) ** -0.5, 0.875, (), jnp.float32),
        "depth_bias": bell_draw(seeds[5], (C,), 0.5, 3.0, (), jnp.float32),
        "norm_gain": jnp.clip(1.0 + 0.15 * jax.random.normal(seeds[6], (C,), jnp.float32), 0.25, 1.75),
        "norm_shift": bell_draw(seeds[7], (C,), 0.3, 2.0, (), jnp.float32),
        "expand_weight": bell_draw(seeds[8], (C, HID), C ** -0.5, 0.3125),
        "expand_bias": jnp.clip(jax.random.uniform(seeds[9], (HID,), jnp.float32, -1.15, -0.75), -1.15, -0.75),
        "reduce_weight": bell_draw(seeds[10], (HID, C), HID ** -0.5, 0.15625),
        "reduce_bias": bell_draw(seeds[11], (C,), 0.3, 2.0, (), jnp.float32),
        "layer_scale": jnp.clip(jnp.exp(jax.random.uniform(seeds[12], (C,), jnp.float32, math.log(0.3), math.log(1.5))), 0.3, 1.5),
        "head_weight": bell_draw(seeds[13], (C, E), C ** -0.5, 0.3125),
        "slide_taps": bell_draw(seeds[14], (KERNEL_TAPS, E), 0.4, 2.5, (), jnp.float32),
        "slide_weight": bell_draw(seeds[15], (E, E), E ** -0.5, 0.21875),
        "slide_bias": bell_draw(seeds[16], (E,), 0.3, 2.0, (), jnp.float32),
        "cotangent": bell_draw(seeds[17], (SLIDES, E), 30.0, 180.0, ((0, 4),), jnp.float32),
    }


EPSILON = 1e-06
HALF_ROOT = 0.7071067811865476
INV_ROOT_TAU = 0.3989422804014327

def gelu_exact(values):
    return 0.5 * values * (1.0 + jax.scipy.special.erf(values * HALF_ROOT))

def gelu_slope(values):
    return 0.5 * (1.0 + jax.scipy.special.erf(values * HALF_ROOT)) + values * INV_ROOT_TAU * jnp.exp(-0.5 * values * values)

def contract_rows(left_side, right_side):
    return lax.dot_general(left_side, right_side, (((0,), (0,)), ((), ())), preferred_element_type=jnp.float32)

def contract_cols(left_side, right_side):
    return lax.dot_general(left_side, right_side, (((1,), (1,)), ((), ())), preferred_element_type=jnp.float32)

def padded_tiles(work_tiles):
    border_width = KS // 2
    return jnp.pad(work_tiles, ((0, 0), (border_width, border_width), (border_width, border_width), (0, 0)))

def block_forward(work_tiles, depth_kernel, depth_bias, norm_gain, norm_shift, expand_weight, expand_bias, reduce_weight, reduce_bias, layer_scale, head_weight):
    tile_count = work_tiles.shape[0]
    tile_side = work_tiles.shape[1]
    channels = work_tiles.shape[3]
    pixels = tile_side * tile_side
    padded = padded_tiles(work_tiles)
    running = jnp.zeros(work_tiles.shape, jnp.float32) + depth_bias
    for tap_row in range(KS):
        for tap_col in range(KS):
            running = running + depth_kernel[tap_row * KS + tap_col] * padded[:, tap_row:tap_row + tile_side, tap_col:tap_col + tile_side]
    depth_out = running.reshape(tile_count * pixels, channels)
    chan_mean = lax.optimization_barrier(jnp.mean(depth_out, axis=1, keepdims=True))
    centred = depth_out - chan_mean
    inv_std = lax.rsqrt(lax.optimization_barrier(jnp.mean(centred * centred, axis=1, keepdims=True)) + EPSILON)
    unit_norm = centred * inv_std
    normed = (unit_norm * norm_gain + norm_shift).astype(jnp.bfloat16)
    pre_act = jnp.dot(normed, expand_weight, preferred_element_type=jnp.float32) + expand_bias
    hidden = gelu_exact(pre_act).astype(jnp.bfloat16)
    mlp_out = jnp.dot(hidden, reduce_weight, preferred_element_type=jnp.float32) + reduce_bias
    section_rows = (work_tiles.reshape(tile_count * pixels, channels) + layer_scale * mlp_out).astype(jnp.bfloat16)
    head_pre = jnp.dot(section_rows, head_weight, preferred_element_type=jnp.float32)
    tile_embed = lax.optimization_barrier(jnp.mean(gelu_exact(head_pre).reshape(tile_count, pixels, -1), axis=1)).astype(jnp.bfloat16)
    return (section_rows.reshape(work_tiles.shape), tile_embed, (unit_norm, inv_std, normed, pre_act, hidden, head_pre))

def block_backward(work_tiles, saved_acts, embed_grad, norm_gain, expand_weight, reduce_weight, layer_scale, head_weight):
    unit_norm, inv_std, normed, pre_act, hidden, head_pre = saved_acts
    tile_count = work_tiles.shape[0]
    tile_side = work_tiles.shape[1]
    channels = work_tiles.shape[3]
    pixels = tile_side * tile_side
    slope_head = gelu_slope(head_pre).reshape(tile_count, pixels, -1)
    grad_head = (embed_grad.astype(jnp.float32)[:, None, :] / float(pixels) * slope_head).astype(jnp.bfloat16)
    grad_head = grad_head.reshape(tile_count * pixels, -1)
    grad_block = contract_cols(grad_head, head_weight)
    grad_mlp = (layer_scale * grad_block).astype(jnp.bfloat16)
    reduce_grad = contract_rows(hidden, grad_mlp)
    grad_hidden = contract_cols(grad_mlp, reduce_weight)
    grad_pre = (grad_hidden * gelu_slope(pre_act)).astype(jnp.bfloat16)
    expand_grad = contract_rows(normed, grad_pre)
    grad_norm = contract_cols(grad_pre, expand_weight)
    scaled_grad = grad_norm * norm_gain
    grad_depthwise = inv_std * (scaled_grad - lax.optimization_barrier(jnp.mean(scaled_grad, axis=1, keepdims=True)) - unit_norm * lax.optimization_barrier(jnp.mean(scaled_grad * unit_norm, axis=1, keepdims=True)))
    grad_depthwise = grad_depthwise.reshape(tile_count, tile_side, tile_side, channels)
    padded = padded_tiles(work_tiles)
    tap_grads = []
    for tap_row in range(KS):
        for tap_col in range(KS):
            tap_grads.append(lax.optimization_barrier(jnp.sum(grad_depthwise * padded[:, tap_row:tap_row + tile_side, tap_col:tap_col + tile_side], axis=(0, 1, 2))))
    return (expand_grad, reduce_grad, jnp.stack(tap_grads))

def position_code(positions):
    half_width = E // 2
    channel_ids = jnp.arange(half_width, dtype=jnp.int32)
    frequency = jnp.exp((2 * (channel_ids // 2)).astype(jnp.float32) * (-math.log(10000.0) / half_width))
    pieces = []
    for coord_axis in range(2):
        angles = positions[coord_axis].astype(jnp.float32)[:, None] * frequency[None, :]
        pieces.append(jnp.where(channel_ids % 2 == 0, jnp.sin(angles), jnp.cos(angles)))
    return jnp.concatenate(pieces, axis=1)

def dilate(seq_float, slide_taps, travel_direction):
    length = seq_float.shape[0]
    border_width = KERNEL_TAPS // 2 * TILE_DILATION
    padded = jnp.pad(seq_float, ((border_width, border_width), (0, 0)))
    running = jnp.zeros(seq_float.shape, jnp.float32)
    for shift_amount in range(KERNEL_TAPS):
        leading_row = border_width + travel_direction * (shift_amount - KERNEL_TAPS // 2) * TILE_DILATION
        running = running + slide_taps[shift_amount] * padded[leading_row:leading_row + length]
    return running

def slide_pass(sequence, seq_present, slide_count, slide_cot, slide_taps, slide_weight, slide_bias):
    seq_float = sequence.astype(jnp.float32)
    mixed = (seq_float + dilate(seq_float, slide_taps, 1)).astype(jnp.bfloat16)
    agg_pre = jnp.dot(mixed, slide_weight, preferred_element_type=jnp.float32) + slide_bias
    weight = seq_present.astype(jnp.float32) / slide_count.astype(jnp.float32)
    feature = lax.optimization_barrier(jnp.sum(gelu_exact(agg_pre) * weight[:, None], axis=0))
    grad_agg = (slide_cot[None, :] * weight[:, None] * gelu_slope(agg_pre)).astype(jnp.bfloat16)
    grad_mixed = contract_cols(grad_agg, slide_weight)
    seq_grad = ((grad_mixed + dilate(grad_mixed, slide_taps, -1)) * seq_present.astype(jnp.float32)[:, None]).astype(jnp.bfloat16)
    return (feature, seq_grad)

def reference(tile_maps, positions, counts, routing, depth_kernel, depth_bias, norm_gain, norm_shift, expand_weight, expand_bias, reduce_weight, reduce_bias, layer_scale, head_weight, slide_taps, slide_weight, slide_bias, cotangent):
    params = (depth_kernel, depth_bias, norm_gain, norm_shift, expand_weight, expand_bias, reduce_weight, reduce_bias, layer_scale, head_weight)
    tile_ids = jnp.arange(TILES, dtype=jnp.int32)
    group_of = tile_ids // SLOTS % GSIZE
    slide_of = tile_ids // (GSIZE * SLOTS)
    seq_index = tile_ids % SLOTS * GSIZE + group_of
    present = seq_index < counts[slide_of]
    route_flat = routing.reshape(-1)
    routed = route_flat >= 0
    target = jnp.where(routed, (route_flat // PROC * GSIZE + group_of) * PROC + route_flat % PROC, PTILES).astype(jnp.int32)
    source = jnp.full((PTILES,), -1, jnp.int32).at[target].set(tile_ids, mode='drop')
    filled = source >= 0
    safe_index = jnp.maximum(source, 0).astype(jnp.int32)

    def forward_one(tile_index):
        work_tiles = lax.dynamic_index_in_dim(tile_maps, tile_index, 0, keepdims=True)
        section_out, tile_embed, _ = block_forward(work_tiles, *params)
        return (section_out[0], tile_embed[0])
    tile_outs, tile_embeds = lax.map(forward_one, safe_index)
    tile_out = jnp.where(filled[:, None, None, None], tile_outs, jnp.zeros((), jnp.bfloat16))
    owner_index = jnp.where(filled, source, TILES).astype(jnp.int32)
    owner_emb = jnp.zeros((TILES, E), jnp.bfloat16).at[owner_index].set(tile_embeds, mode='drop')
    pos_code = position_code(positions)
    slide_rows = jnp.where(present[:, None], (owner_emb.astype(jnp.float32) + pos_code).astype(jnp.bfloat16), jnp.zeros((), jnp.bfloat16))
    seq_all = slide_rows.reshape(SLIDES, GSIZE, SLOTS, E).transpose(0, 2, 1, 3).reshape(SLIDES, SEQ, E)
    present_all = present.reshape(SLIDES, GSIZE, SLOTS).transpose(0, 2, 1).reshape(SLIDES, SEQ)

    def slide_one(slide_item):
        return slide_pass(slide_item[0], slide_item[1], slide_item[2], slide_item[3], slide_taps, slide_weight, slide_bias)
    features, seq_grads = lax.map(slide_one, (seq_all, present_all, counts, cotangent))
    row_grads = seq_grads.reshape(SLIDES, SLOTS, GSIZE, E).transpose(0, 2, 1, 3).reshape(TILES, E)
    embed_grads = jnp.where(filled[:, None], row_grads[safe_index], jnp.zeros((), jnp.bfloat16))

    def back_one(totals, scan_item):
        tile_index, grad_row = scan_item
        work_tiles = lax.dynamic_index_in_dim(tile_maps, tile_index, 0, keepdims=True)
        _, _, saved_acts = block_forward(work_tiles, *params)
        expand_grad, reduce_grad, depth_grad = block_backward(work_tiles, saved_acts, grad_row[None, :], norm_gain, expand_weight, reduce_weight, layer_scale, head_weight)
        return ((totals[0] + expand_grad, totals[1] + reduce_grad, totals[2] + depth_grad), None)
    zero_grads = (jnp.zeros((C, HID), jnp.float32), jnp.zeros((HID, C), jnp.float32), jnp.zeros((KS * KS, C), jnp.float32))
    sums, _ = lax.scan(back_one, zero_grads, (safe_index, embed_grads))
    return (tile_out, features, sums[0].reshape(-1), sums[1].reshape(-1), sums[2].reshape(-1))
```

```python
import math

import jax
import jax.numpy as jnp
from jax import lax
from jax.sharding import Mesh, PartitionSpec as P

E = 768
KS = 7
KERNEL_TAPS = 7
TILE_DILATION = 3
PROC = 4
DP = ("y", "core")
GROUP = ("g1", "g2")
ALL = DP + GROUP


EPSILON = 1e-06
HALF_ROOT = 0.7071067811865476
INV_ROOT_TAU = 0.3989422804014327


def gelu_exact(values):
    return 0.5 * values * (1.0 + jax.scipy.special.erf(values * HALF_ROOT))


def gelu_slope(values):
    return 0.5 * (
        1.0 + jax.scipy.special.erf(values * HALF_ROOT)
    ) + values * INV_ROOT_TAU * jnp.exp(-0.5 * values * values)


def contract_rows(left_side, right_side):
    return lax.dot_general(
        left_side, right_side, (((0,), (0,)), ((), ())), preferred_element_type=jnp.float32
    )


def contract_cols(left_side, right_side):
    return lax.dot_general(
        left_side, right_side, (((1,), (1,)), ((), ())), preferred_element_type=jnp.float32
    )


def padded_tiles(work_tiles):
    border_width = KS // 2
    return jnp.pad(
        work_tiles, ((0, 0), (border_width, border_width), (border_width, border_width), (0, 0))
    )


def block_forward(
    work_tiles,
    depth_kernel,
    depth_bias,
    norm_gain,
    norm_shift,
    expand_weight,
    expand_bias,
    reduce_weight,
    reduce_bias,
    layer_scale,
    head_weight,
):
    tile_count = work_tiles.shape[0]
    tile_side = work_tiles.shape[1]
    channels = work_tiles.shape[3]
    pixels = tile_side * tile_side
    padded = padded_tiles(work_tiles)
    running = jnp.zeros(work_tiles.shape, jnp.float32) + depth_bias
    for tap_row in range(KS):
        for tap_col in range(KS):
            running = (
                running
                + depth_kernel[tap_row * KS + tap_col]
                * padded[:, tap_row : tap_row + tile_side, tap_col : tap_col + tile_side]
            )
    depth_out = running.reshape(tile_count * pixels, channels)
    chan_mean = jnp.mean(depth_out, axis=1, keepdims=True)
    centred = depth_out - chan_mean
    inv_std = lax.rsqrt(jnp.mean(centred * centred, axis=1, keepdims=True) + EPSILON)
    unit_norm = centred * inv_std
    normed = (unit_norm * norm_gain + norm_shift).astype(jnp.bfloat16)
    pre_act = jnp.dot(normed, expand_weight, preferred_element_type=jnp.float32) + expand_bias
    hidden = gelu_exact(pre_act).astype(jnp.bfloat16)
    mlp_out = jnp.dot(hidden, reduce_weight, preferred_element_type=jnp.float32) + reduce_bias
    section_rows = (
        work_tiles.reshape(tile_count * pixels, channels) + layer_scale * mlp_out
    ).astype(jnp.bfloat16)
    head_pre = jnp.dot(section_rows, head_weight, preferred_element_type=jnp.float32)
    tile_embed = jnp.mean(gelu_exact(head_pre).reshape(tile_count, pixels, -1), axis=1).astype(
        jnp.bfloat16
    )
    return (
        section_rows.reshape(work_tiles.shape),
        tile_embed,
        (unit_norm, inv_std, normed, pre_act, hidden, head_pre),
    )


def block_backward(
    work_tiles,
    saved_acts,
    embed_grad,
    norm_gain,
    expand_weight,
    reduce_weight,
    layer_scale,
    head_weight,
):
    unit_norm, inv_std, normed, pre_act, hidden, head_pre = saved_acts
    tile_count = work_tiles.shape[0]
    tile_side = work_tiles.shape[1]
    channels = work_tiles.shape[3]
    pixels = tile_side * tile_side
    slope_head = gelu_slope(head_pre).reshape(tile_count, pixels, -1)
    grad_head = (embed_grad.astype(jnp.float32)[:, None, :] / float(pixels) * slope_head).astype(
        jnp.bfloat16
    )
    grad_head = grad_head.reshape(tile_count * pixels, -1)
    grad_block = contract_cols(grad_head, head_weight)
    grad_mlp = (layer_scale * grad_block).astype(jnp.bfloat16)
    reduce_grad = contract_rows(hidden, grad_mlp)
    grad_hidden = contract_cols(grad_mlp, reduce_weight)
    grad_pre = (grad_hidden * gelu_slope(pre_act)).astype(jnp.bfloat16)
    expand_grad = contract_rows(normed, grad_pre)
    grad_norm = contract_cols(grad_pre, expand_weight)
    scaled_grad = grad_norm * norm_gain
    grad_depthwise = inv_std * (
        scaled_grad
        - jnp.mean(scaled_grad, axis=1, keepdims=True)
        - unit_norm * jnp.mean(scaled_grad * unit_norm, axis=1, keepdims=True)
    )
    grad_depthwise = grad_depthwise.reshape(tile_count, tile_side, tile_side, channels)
    padded = padded_tiles(work_tiles)
    tap_grads = []
    for tap_row in range(KS):
        for tap_col in range(KS):
            tap_grads.append(
                jnp.sum(
                    grad_depthwise
                    * padded[:, tap_row : tap_row + tile_side, tap_col : tap_col + tile_side],
                    axis=(0, 1, 2),
                )
            )
    return (expand_grad, reduce_grad, jnp.stack(tap_grads))


def position_code(positions):
    half_width = E // 2
    channel_ids = jnp.arange(half_width, dtype=jnp.int32)
    frequency = jnp.exp(
        (2 * (channel_ids // 2)).astype(jnp.float32) * (-math.log(10000.0) / half_width)
    )
    pieces = []
    for coord_axis in range(2):
        angles = positions[coord_axis].astype(jnp.float32)[:, None] * frequency[None, :]
        pieces.append(jnp.where(channel_ids % 2 == 0, jnp.sin(angles), jnp.cos(angles)))
    return jnp.concatenate(pieces, axis=1)


def dilate(seq_float, slide_taps, travel_direction):
    length = seq_float.shape[0]
    border_width = KERNEL_TAPS // 2 * TILE_DILATION
    padded = jnp.pad(seq_float, ((border_width, border_width), (0, 0)))
    running = jnp.zeros(seq_float.shape, jnp.float32)
    for shift_amount in range(KERNEL_TAPS):
        leading_row = (
            border_width + travel_direction * (shift_amount - KERNEL_TAPS // 2) * TILE_DILATION
        )
        running = running + slide_taps[shift_amount] * padded[leading_row : leading_row + length]
    return running


def slide_pass(sequence, seq_present, slide_count, slide_cot, slide_taps, slide_weight, slide_bias):
    seq_float = sequence.astype(jnp.float32)
    mixed = (seq_float + dilate(seq_float, slide_taps, 1)).astype(jnp.bfloat16)
    agg_pre = jnp.dot(mixed, slide_weight, preferred_element_type=jnp.float32) + slide_bias
    weight = seq_present.astype(jnp.float32) / slide_count.astype(jnp.float32)
    feature = jnp.sum(gelu_exact(agg_pre) * weight[:, None], axis=0)
    grad_agg = (slide_cot[None, :] * weight[:, None] * gelu_slope(agg_pre)).astype(jnp.bfloat16)
    grad_mixed = contract_cols(grad_agg, slide_weight)
    seq_grad = (
        (grad_mixed + dilate(grad_mixed, slide_taps, -1)) * seq_present.astype(jnp.float32)[:, None]
    ).astype(jnp.bfloat16)
    return (feature, seq_grad)


def sender_table(my_list, slides, places):
    dest_dev = jnp.where(my_list >= 0, my_list // PROC, -1)
    is_hit = dest_dev[None, :] == jnp.arange(slides, dtype=jnp.int32)[:, None]
    order_rank = jnp.cumsum(is_hit.astype(jnp.int32), axis=1) - 1
    chosen = is_hit[:, None, :] & (
        order_rank[:, None, :] == jnp.arange(places, dtype=jnp.int32)[None, :, None]
    )
    return chosen.reshape(slides * places, -1)


def receiver_table(route_rows, my_slide, places):
    dest_dev = jnp.where(route_rows >= 0, route_rows // PROC, -1)
    is_hit = dest_dev == my_slide
    order_rank = jnp.cumsum(is_hit.astype(jnp.int32), axis=1) - 1
    chosen = is_hit[:, None, :] & (
        order_rank[:, None, :] == jnp.arange(places, dtype=jnp.int32)[None, :, None]
    )
    target = jnp.sum(jnp.where(chosen, (route_rows % PROC)[:, None, :], 0), axis=2).reshape(-1)
    is_used = jnp.any(chosen, axis=2).reshape(-1)
    return (target[None, :] == jnp.arange(PROC, dtype=jnp.int32)[:, None]) & is_used[None, :]


def on_device(
    tile_maps,
    positions,
    counts,
    routing,
    depth_kernel,
    depth_bias,
    norm_gain,
    norm_shift,
    expand_weight,
    expand_bias,
    reduce_weight,
    reduce_bias,
    layer_scale,
    head_weight,
    slide_taps,
    slide_weight,
    slide_bias,
    cotangent,
):
    params = (
        depth_kernel,
        depth_bias,
        norm_gain,
        norm_shift,
        expand_weight,
        expand_bias,
        reduce_weight,
        reduce_bias,
        layer_scale,
        head_weight,
    )
    slides = lax.axis_size(DP)
    members = lax.axis_size(GROUP)
    my_slide = lax.axis_index(DP)
    my_member = lax.axis_index(GROUP)
    slot_count = tile_maps.shape[0]
    embed_width = head_weight.shape[1]
    places = slot_count // slides
    route_rows = routing[:, 0, :]
    device_count = slides * members
    extras = jnp.concatenate(
        [
            cotangent[0],
            route_rows.reshape(-1).astype(jnp.float32),
            jnp.zeros((960 - embed_width - slides * slot_count,), jnp.float32),
            positions.reshape(-1).astype(jnp.float32),
            jnp.zeros((1023 - 960 - 2 * slot_count,), jnp.float32),
            counts.astype(jnp.float32),
        ]
    )
    extras = lax.all_to_all(
        jnp.broadcast_to(extras, (device_count, 1024)), ALL, split_axis=0, concat_axis=0, tiled=True
    )
    my_list = lax.dynamic_index_in_dim(route_rows, my_slide, 0, keepdims=False)
    send_pick = sender_table(my_list, slides, places).astype(jnp.bfloat16)
    take_bool = receiver_table(route_rows, my_slide, places)
    take_pick = take_bool.astype(jnp.bfloat16)
    filled = jnp.any(take_bool, axis=1)
    packed = jnp.dot(
        send_pick, tile_maps.reshape(slot_count, -1), preferred_element_type=jnp.float32
    ).astype(jnp.bfloat16)
    packed = packed.reshape((slides * places,) + tile_maps.shape[1:])
    arrived = lax.all_to_all(packed, DP, split_axis=0, concat_axis=0, tiled=True)
    work_tiles = jnp.dot(
        take_pick, arrived.reshape(slides * places, -1), preferred_element_type=jnp.float32
    ).astype(jnp.bfloat16)
    work_tiles = work_tiles.reshape((take_pick.shape[0],) + tile_maps.shape[1:])
    section_out, tile_embed, saved_acts = block_forward(work_tiles, *params)
    tile_out = jnp.where(filled[:, None, None, None], section_out, jnp.zeros((), jnp.bfloat16))
    all_embed = lax.all_to_all(
        jnp.broadcast_to(tile_embed, (device_count,) + tile_embed.shape),
        ALL,
        split_axis=0,
        concat_axis=0,
        tiled=True,
    ).reshape(slides, members, PROC, embed_width)
    route_all = extras[:, embed_width : embed_width + slides * slot_count].astype(jnp.int32)
    route_all = route_all.reshape(slides, members, slides, slot_count)[0]
    pos_all = extras[:, 960:976].astype(jnp.int32).reshape(device_count, 2, slot_count)
    counts_all = extras[:, 1023].astype(jnp.int32).reshape(slides, members)[:, 0]
    cot_all = extras[:, :embed_width].reshape(slides, members, embed_width)[:, 0]
    flat_embed = jnp.transpose(all_embed, (1, 0, 2, 3)).reshape(members, slides * PROC, embed_width)
    pick = (
        route_all.reshape(members, slides * slot_count)[:, :, None]
        == jnp.arange(slides * PROC, dtype=jnp.int32)
    ).astype(jnp.bfloat16)
    own_all = jnp.einsum("gts,gse->gte", pick, flat_embed, preferred_element_type=jnp.float32)
    own_all = own_all.reshape(members, slides, slot_count, embed_width).transpose(1, 2, 0, 3)
    own_all = own_all.reshape(slides, slot_count * members, embed_width)
    codes = position_code(jnp.transpose(pos_all, (1, 0, 2)).reshape(2, -1))
    codes = codes.reshape(slides, members, slot_count, embed_width).transpose(0, 2, 1, 3)
    codes = codes.reshape(slides, slot_count * members, embed_width)
    present_all = jnp.arange(slot_count * members, dtype=jnp.int32)[None, :] < counts_all[:, None]
    seq_all = jnp.where(
        present_all[:, :, None],
        (own_all + codes).astype(jnp.bfloat16),
        jnp.zeros((), jnp.bfloat16),
    )
    feature_all, grad_all = jax.vmap(slide_pass, in_axes=(0, 0, 0, 0, None, None, None))(
        seq_all, present_all, counts_all, cot_all, slide_taps, slide_weight, slide_bias
    )
    feature = lax.dynamic_index_in_dim(feature_all, my_slide, 0, keepdims=False)
    my_rows = lax.dynamic_index_in_dim(
        grad_all.reshape(slides, slot_count, members, embed_width), my_member, 2, keepdims=False
    ).reshape(slides * slot_count, embed_width)
    place = my_slide * PROC + jnp.arange(PROC, dtype=jnp.int32)
    my_pick = (place[:, None] == route_rows.reshape(-1)[None, :]).astype(jnp.bfloat16)
    embed_grad = jnp.dot(my_pick, my_rows, preferred_element_type=jnp.float32).astype(jnp.bfloat16)
    expand_grad, reduce_grad, depth_grad = block_backward(
        work_tiles,
        saved_acts,
        embed_grad,
        norm_gain,
        expand_weight,
        reduce_weight,
        layer_scale,
        head_weight,
    )
    shares = [
        scatter_sum(part.astype(jnp.bfloat16).reshape(-1)) for part in (expand_grad, reduce_grad, depth_grad)
    ]
    return (tile_out, feature[None, :], shares[0], shares[1], shares[2])


def scatter_sum(values):
    sizes = [lax.axis_size(name) for name in ALL]
    grid = values.reshape(sizes + [-1]).transpose(1, 0, 3, 2, 4)
    grid = grid.reshape(sizes[1], sizes[0] * sizes[3], sizes[2], -1)
    for names in (("core",), ("y", "g2"), ("g1",)):
        grid = lax.all_to_all(grid, names, split_axis=0, concat_axis=0, tiled=True)
        grid = jnp.sum(grid.astype(jnp.float32), axis=0)
        if names != ("g1",):
            grid = grid.astype(jnp.bfloat16)
    return grid


def solution(mesh):
    slides, members = mesh.shape["dp"], mesh.shape["group"]
    fine = Mesh(mesh.devices.reshape(slides // 2, 2, 4, members // 4), ALL)
    return jax.shard_map(
        on_device,
        mesh=fine,
        in_specs=(
            P(ALL, None, None, None),
            P(None, ALL),
            P(DP),
            P(None, GROUP, None),
            P(),
            P(),
            P(),
            P(),
            P(),
            P(),
            P(),
            P(),
            P(),
            P(),
            P(),
            P(),
            P(),
            P(DP, None),
        ),
        out_specs=(
            P(ALL, None, None, None),
            P(DP, None),
            P(ALL),
            P(ALL),
            P(ALL),
        ),
        check_vma=False,
    )
```

```python
import functools
import math

import jax
import jax.numpy as jnp
import numpy as np
from jax import lax
from jax.experimental import pallas as pl
from jax.experimental.pallas import tpu as pltpu
from jax.sharding import Mesh, PartitionSpec as P

E = 768
KS = 7
KERNEL_TAPS = 7
TILE_DILATION = 3
PROC = 4
DP = ("y", "core")
GROUP = ("g1", "g2")
ALL = DP + GROUP

EPSILON = 1e-06
HALF_ROOT = 0.7071067811865476
INV_ROOT_TAU = 0.3989422804014327
LANES = 128
ROW_UNIT = 16
DEPTH_ROWS = 4
VMEM_BYTES = 56 * 1024 * 1024
ERFC_P = 0.3275911
ERFC_A = (0.254829592, -0.284496736, 1.421413741, -1.453152027, 1.061405429)

HBM = pl.BlockSpec(memory_space=pl.ANY)


def whole(shape):
    return pl.BlockSpec(shape, lambda *_: (0,) * len(shape))


def gelu_and_slope(values):
    size = jnp.abs(values)
    divisor = 1.0 + (ERFC_P * HALF_ROOT) * size
    guess = pl.reciprocal(divisor, approx=True)
    t = guess * (2.0 - divisor * guess)
    bell = jnp.exp(-0.5 * values * values)
    poly = 0.5 * ERFC_A[4]
    for coefficient in ERFC_A[3::-1]:
        poly = poly * t + 0.5 * coefficient
    tail = poly * t * bell
    phi = jnp.where(values >= 0.0, 1.0 - tail, tail)
    return values * phi, phi + values * (INV_ROOT_TAU * bell)


def mix_cols(left_side, right_side):
    return lax.dot_general(
        left_side, right_side, (((1,), (1,)), ((), ())), preferred_element_type=jnp.float32
    )


def mix(left_side, right_side):
    return jnp.dot(left_side, right_side, preferred_element_type=jnp.float32)


def pack_kernel(slides, slots, places, my_ref, route_ref, tiles_ref, packed_ref, table_ref, count_ref, sems):
    my_slide = my_ref[0]

    def copy_of(slot, target):
        return pltpu.make_async_copy(tiles_ref.at[slot], packed_ref.at[target], sems.at[slot])

    for dest in range(slides):
        count_ref[dest] = 0
    for slot in range(slots):
        entry = route_ref[my_slide * slots + slot]

        @pl.when(entry >= 0)
        def _send():
            dest = lax.div(entry, PROC)
            rank = count_ref[dest]
            count_ref[dest] = rank + 1
            copy_of(slot, dest * places + rank).start()

    for field in range(4 * PROC):
        table_ref[field] = 0
    for source in range(slides):
        count_ref[0] = 0
        for slot in range(slots):
            entry = route_ref[source * slots + slot]
            inside = (entry >= my_slide * PROC) & (entry < my_slide * PROC + PROC)

            @pl.when(inside)
            def _take():
                proc = entry - my_slide * PROC
                rank = count_ref[0]
                count_ref[0] = rank + 1
                table_ref[proc] = source * places + rank
                table_ref[PROC + proc] = 1
                table_ref[2 * PROC + proc] = source
                table_ref[3 * PROC + proc] = slot

    for slot in range(slots):
        entry = route_ref[my_slide * slots + slot]

        @pl.when(entry >= 0)
        def _wait():
            copy_of(slot, 0).wait()


def pack_tiles(my_slide, route, tile_maps, slides, places):
    slots = tile_maps.shape[0]
    smem = pl.BlockSpec(memory_space=pltpu.SMEM)
    return pl.pallas_call(
        functools.partial(pack_kernel, slides, slots, places),
        out_shape=(
            jax.ShapeDtypeStruct((slides * places,) + tile_maps.shape[1:], tile_maps.dtype),
            jax.ShapeDtypeStruct((4 * PROC,), jnp.int32),
        ),
        in_specs=[smem, smem, HBM],
        out_specs=(HBM, smem),
        scratch_shapes=[pltpu.SMEM((slides,), jnp.int32), pltpu.SemaphoreType.DMA((slots,))],
        name="pack_tiles",
    )(my_slide, route, tile_maps)


def forward_kernel(
    table_ref,
    tile_ref,
    taps_ref,
    depth_bias_ref,
    gain_ref,
    shift_ref,
    expand_ref,
    expand_bias_ref,
    reduce_ref,
    reduce_bias_ref,
    scale_ref,
    head_ref,
    out_ref,
    embed_ref,
    unit_ref,
    inv_ref,
    hidden_ref,
    slope_ref,
    head_slope_ref,
    source_ref,
    padded,
    depth_out,
    normed,
):
    filled = table_ref[PROC + pl.program_id(0)]
    side = tile_ref.shape[1]
    channels = tile_ref.shape[3]
    cells = side * side
    bands = channels // LANES
    low = ROW_UNIT // 2
    reach = KS // 2

    @pl.when(filled == 0)
    def _empty():
        for ref in (out_ref, embed_ref, unit_ref, inv_ref, hidden_ref, slope_ref, head_slope_ref, source_ref):
            ref[...] = jnp.zeros(ref.shape, ref.dtype)

    @pl.when(filled != 0)
    def _work():
        source_ref[...] = tile_ref[...]
        edge = jnp.zeros((side, low, LANES), jnp.float32)
        for band in range(bands):
            padded[band, :, 0:low, :] = edge
            padded[band, :, low + side :, :] = edge
            padded[band, :, low : low + side, :] = tile_ref[
                0, :, :, band * LANES : (band + 1) * LANES
            ].astype(jnp.float32)

        def convolve(band, carry):
            totals = [
                jnp.broadcast_to(depth_bias_ref[band], (side, LANES)) for _ in range(side)
            ]
            for col in range(KS):
                start = low - reach + col
                weights = [taps_ref[band, pl.ds(row * KS + col, 1), :] for row in range(KS)]
                for at in range(side):
                    line = padded[band, at, start : start + side, :]
                    for row in range(KS):
                        place = at - row + reach
                        if 0 <= place < side:
                            totals[place] = totals[place] + weights[row] * line
            for place in range(side):
                depth_out[band, place * side : (place + 1) * side, :] = totals[place]
            return carry

        lax.fori_loop(0, bands, convolve, 0)

        part = 64
        for start in range(0, cells, part):
            rows = slice(start, start + part)
            pieces = [depth_out[band, rows, :] for band in range(bands)]
            mean = jnp.sum(sum(pieces), axis=1, keepdims=True) * (1.0 / channels)
            pieces = [piece - mean for piece in pieces]
            var = jnp.sum(sum(p * p for p in pieces), axis=1, keepdims=True) * (1.0 / channels)
            inv = lax.rsqrt(var + EPSILON)
            inv_ref[0, rows, :] = jnp.broadcast_to(inv, (part, LANES))
            for band in range(bands):
                lanes = slice(band * LANES, (band + 1) * LANES)
                unit = pieces[band] * inv
                unit_ref[0, rows, lanes] = unit
                normed[rows, lanes] = (unit * gain_ref[:, lanes] + shift_ref[:, lanes]).astype(
                    jnp.bfloat16
                )

        width = 256
        for start in range(0, expand_ref.shape[1], width):
            cols = slice(start, start + width)
            pre = mix(normed[...], expand_ref[:, cols]) + expand_bias_ref[:, cols]
            act, slope = gelu_and_slope(pre)
            hidden_ref[0, :, cols] = act.astype(jnp.bfloat16)
            slope_ref[0, :, cols] = slope.astype(jnp.bfloat16)
        branch = scale_ref[...] * (mix(hidden_ref[0], reduce_ref[...]) + reduce_bias_ref[...])
        section = (tile_ref[0].reshape(cells, channels).astype(jnp.float32) + branch).astype(
            jnp.bfloat16
        )
        out_ref[0] = section.reshape(side, side, channels)
        for start in range(0, head_ref.shape[1], width):
            cols = slice(start, start + width)
            act, slope = gelu_and_slope(mix(section, head_ref[:, cols]))
            head_slope_ref[0, :, cols] = slope.astype(jnp.bfloat16)
            embed_ref[0, :, cols] = jnp.sum(act, axis=0, keepdims=True) * (1.0 / cells)


def forward_block(table, arrived, taps, depth_bias, gain, shift, expand, expand_bias, reduce, reduce_bias, scale, head):
    side, channels = arrived.shape[1], arrived.shape[3]
    cells, hid, embed = side * side, expand.shape[1], head.shape[1]
    bands = channels // LANES

    def per_slot(*shape):
        return pl.BlockSpec((1,) + shape, lambda i, table: (i,) + (0,) * len(shape))

    outs = (
        ((side, side, channels), jnp.bfloat16),
        ((1, embed), jnp.float32),
        ((cells, channels), jnp.float32),
        ((cells, LANES), jnp.float32),
        ((cells, hid), jnp.bfloat16),
        ((cells, hid), jnp.bfloat16),
        ((cells, embed), jnp.bfloat16),
        ((side, side, channels), jnp.bfloat16),
    )
    consts = (taps, depth_bias, gain, shift, expand, expand_bias, reduce, reduce_bias, scale, head)
    return pl.pallas_call(
        forward_kernel,
        out_shape=tuple(jax.ShapeDtypeStruct((PROC,) + shape, kind) for shape, kind in outs),
        grid_spec=pltpu.PrefetchScalarGridSpec(
            num_scalar_prefetch=1,
            grid=(PROC,),
            in_specs=[
                pl.BlockSpec((1, side, side, channels), lambda i, table: (table[i], 0, 0, 0))
            ]
            + [whole(const.shape) for const in consts],
            out_specs=[per_slot(*shape) for shape, _ in outs],
            scratch_shapes=[
                pltpu.VMEM((bands, side, side + ROW_UNIT, LANES), jnp.float32),
                pltpu.VMEM((bands, cells, LANES), jnp.float32),
                pltpu.VMEM((cells, channels), jnp.bfloat16),
            ],
        ),
        compiler_params=pltpu.CompilerParams(vmem_limit_bytes=VMEM_BYTES),
        cost_estimate=pl.CostEstimate(
            flops=2 * PROC * cells * channels * (2 * hid + embed + KS * KS),
            bytes_accessed=24 * 1024 * 1024,
            transcendentals=2 * PROC * cells * (hid + embed),
        ),
        name="forward_block",
    )(table, arrived, *consts)


def slide_kernel(
    length,
    slides,
    info_ref,
    embeds_ref,
    pick_ref,
    codes_ref,
    weight_ref,
    cot_ref,
    taps_ref,
    matrix_ref,
    bias_ref,
    feature_ref,
    grad_ref,
    rows,
    back,
    features,
):
    border = ROW_UNIT
    edge = jnp.zeros((border, rows.shape[2]), jnp.float32)
    reach = KERNEL_TAPS // 2

    def dilate(ref, slide, direction):
        total = ref[slide, border : border + length, :]
        for tap in range(KERNEL_TAPS):
            start = border + direction * (tap - reach) * TILE_DILATION
            total = total + taps_ref[tap : tap + 1, :] * ref[slide, start : start + length, :]
        return total

    def one_slide(slide, carry):
        share = weight_ref[slide]
        here = share > 0.0
        own = mix(pick_ref[slide], embeds_ref[...]) + codes_ref[slide]
        for ref in (rows, back):
            ref[slide, 0:border, :] = edge
            ref[slide, border + length :, :] = edge
        rows[slide, border : border + length, :] = (
            jnp.where(here, own, 0.0).astype(jnp.bfloat16).astype(jnp.float32)
        )
        mixed = dilate(rows, slide, 1).astype(jnp.bfloat16)
        act, slope = gelu_and_slope(mix(mixed, matrix_ref[...]) + bias_ref[...])
        features[pl.ds(slide, 1), :] = jnp.sum(act * share, axis=0, keepdims=True)
        grad_agg = (cot_ref[slide] * share * slope).astype(jnp.bfloat16)
        back[slide, border : border + length, :] = mix_cols(grad_agg, matrix_ref[...])
        total = jnp.where(here, dilate(back, slide, -1), 0.0)
        rows[slide, border : border + length, :] = total.astype(jnp.bfloat16).astype(jnp.float32)
        return carry

    lax.fori_loop(0, slides, one_slide, 0)
    feature_ref[...] = features[pl.ds(info_ref[4 * PROC], 1), :]
    for proc in range(PROC):
        filled = info_ref[PROC + proc]
        at = border + info_ref[3 * PROC + proc]
        row = rows[info_ref[2 * PROC + proc], pl.ds(at, 1), :]
        grad_ref[proc] = jnp.where(filled != 0, row, 0.0)


def slide_grads(info, embeds, pick, codes, weight, cot, taps, matrix, bias):
    slides, length, embed = codes.shape
    smem = pl.BlockSpec(memory_space=pltpu.SMEM)
    vmem = pl.BlockSpec(memory_space=pltpu.VMEM)
    padded = (slides, length + 2 * ROW_UNIT, embed)
    return pl.pallas_call(
        functools.partial(slide_kernel, length, slides),
        out_shape=(
            jax.ShapeDtypeStruct((1, embed), jnp.float32),
            jax.ShapeDtypeStruct((PROC, 1, embed), jnp.float32),
        ),
        in_specs=[smem] + [vmem] * 8,
        out_specs=(vmem, vmem),
        scratch_shapes=[
            pltpu.VMEM(padded, jnp.float32),
            pltpu.VMEM(padded, jnp.float32),
            pltpu.VMEM((max(slides, 8), embed), jnp.float32),
        ],
        compiler_params=pltpu.CompilerParams(vmem_limit_bytes=VMEM_BYTES),
        name="slide_grads",
    )(info, embeds, pick, codes, weight, cot, taps, matrix, bias)


def backward_kernel(
    plan,
    table_ref,
    grad_ref,
    source_ref,
    unit_ref,
    inv_ref,
    hidden_ref,
    slope_ref,
    head_slope_ref,
    gain_ref,
    shift_ref,
    scale_ref,
    expand_ref,
    reduce_ref,
    head_ref,
    expand_order_ref,
    reduce_order_ref,
    eye_ref,
    out_ref,
    grad_pre_all,
    hidden_all,
    normed_all,
    grad_mlp_all,
    padded,
    depth_back,
    tap_sums,
    tap_rows,
):
    step = pl.program_id(0)
    filled = table_ref[PROC + step]
    side = source_ref.shape[1]
    channels = source_ref.shape[3]
    cells = side * side
    bands = channels // LANES
    low = ROW_UNIT // 2
    reach = KS // 2
    rows = pl.ds(pl.multiple_of(step * cells, cells), cells)

    @pl.when(step == 0)
    def _start():
        tap_sums[...] = jnp.zeros(tap_sums.shape, jnp.float32)

    @pl.when(filled == 0)
    def _empty():
        grad_pre_all[rows, :] = jnp.zeros((cells, grad_pre_all.shape[1]), jnp.bfloat16)
        hidden_all[rows, :] = jnp.zeros((cells, hidden_all.shape[1]), jnp.bfloat16)
        normed_all[step] = jnp.zeros(normed_all.shape[1:], jnp.bfloat16)
        grad_mlp_all[step] = jnp.zeros(grad_mlp_all.shape[1:], jnp.bfloat16)

    @pl.when(filled != 0)
    def _work():
        grad_head = (grad_ref[0] * (1.0 / cells) * head_slope_ref[0].astype(jnp.float32)).astype(
            jnp.bfloat16
        )
        grad_mlp = (scale_ref[...] * mix_cols(grad_head, head_ref[...])).astype(jnp.bfloat16)
        grad_mlp_all[step] = mix_cols(eye_ref[...], grad_mlp).astype(jnp.bfloat16)
        hidden_all[rows, :] = hidden_ref[0]
        width = 256
        for start in range(0, expand_ref.shape[1], width):
            cols = slice(start, start + width)
            grad_hidden = mix_cols(grad_mlp, reduce_ref[cols, :])
            grad_pre_all[rows, cols] = (
                grad_hidden * slope_ref[0, :, cols].astype(jnp.float32)
            ).astype(jnp.bfloat16)
        grad_norm = mix_cols(grad_pre_all[rows, :], expand_ref[...])
        normed = (unit_ref[0] * gain_ref[...] + shift_ref[...]).astype(jnp.bfloat16)
        normed_all[step] = mix_cols(expand_order_ref[...], normed).astype(jnp.bfloat16)

        scaled = grad_norm * gain_ref[...]
        unit = unit_ref[0]
        mean = jnp.sum(scaled, axis=1, keepdims=True) * (1.0 / channels)
        mean_unit = jnp.sum(scaled * unit, axis=1, keepdims=True) * (1.0 / channels)
        depth_grad = inv_ref[0, :, 0:1] * (scaled - mean - unit * mean_unit)
        edge = jnp.zeros((side, low, LANES), jnp.float32)
        for band in range(bands):
            lanes = slice(band * LANES, (band + 1) * LANES)
            depth_back[band] = depth_grad[:, lanes]
            padded[band, :, 0:low, :] = edge
            padded[band, :, low + side :, :] = edge
            padded[band, :, low : low + side, :] = source_ref[0, :, :, lanes].astype(jnp.float32)

        def taps_of(band, carry):
            for col in range(KS):
                start = low - reach + col
                sums = [None] * KS
                for at in range(side):
                    line = padded[band, at, start : start + side, :]
                    for row in range(KS):
                        place = at - row + reach
                        if 0 <= place < side:
                            term = line * depth_back[band, place * side : (place + 1) * side, :]
                            sums[row] = term if sums[row] is None else sums[row] + term
                for row in range(KS):
                    total = sums[row]
                    folded = total[0:8, :]
                    for piece in range(8, side, 8):
                        folded = folded + total[piece : piece + 8, :]
                    tap_sums[band, row * KS + col] = tap_sums[band, row * KS + col] + folded
            return carry

        lax.fori_loop(0, bands, taps_of, 0)

    @pl.when(step == pl.num_programs(0) - 1)
    def _finish():
        for band in range(bands):
            lanes = slice(band * LANES, (band + 1) * LANES)
            tap_rows[0 : KS * KS, lanes] = jnp.sum(tap_sums[band], axis=1)
            tap_rows[KS * KS :, lanes] = jnp.zeros((tap_rows.shape[0] - KS * KS, LANES), jnp.float32)
        pieces = expand_ref.shape[1] // channels
        parts = 2 * plan.cross
        for quarter in range(pieces):
            cols = slice(quarter * channels, (quarter + 1) * channels)
            total = mix(normed_all[0], grad_pre_all[0:cells, cols])
            for slot in range(1, PROC):
                total = total + mix(
                    normed_all[slot], grad_pre_all[slot * cells : (slot + 1) * cells, cols]
                )
            out_ref[:, quarter * plan.expand_pad : (quarter + 1) * plan.expand_pad, :] = (
                total.astype(jnp.bfloat16).reshape(parts, plan.expand_pad, channels)
            )
        base = pieces * plan.expand_pad
        block = plan.reduce_block
        span = plan.depth_span * plan.reduce_rows
        for index in range(expand_ref.shape[1] // block):
            cols = slice(index * block, (index + 1) * block)
            total = mix(grad_mlp_all[0], hidden_all[0:cells, cols])
            for slot in range(1, PROC):
                total = total + mix(
                    grad_mlp_all[slot], hidden_all[slot * cells : (slot + 1) * cells, cols]
                )
            turned = mix_cols(reduce_order_ref[...], total.astype(jnp.bfloat16)).astype(jnp.bfloat16)
            y, core = divmod(index, 2)
            for x in range(plan.g2):
                out_ref[core * plan.cross + y * plan.g2 + x, base : base + span, :] = turned[
                    x * span : (x + 1) * span, :
                ]
        base = base + span
        for part in range(parts):
            starts = [plan.tap_start(part, z) for z in range(plan.g1)]
            out_ref[part, base : base + plan.g1 * DEPTH_ROWS, :] = jnp.concatenate(
                [tap_rows[start : start + DEPTH_ROWS, :] for start in starts], axis=0
            ).astype(jnp.bfloat16)


class Plan:

    def __init__(self, slides, members, channels, hid):
        self.devices = slides * members
        self.ys, self.g1, self.g2 = slides // 2, 4, members // 4
        self.cross = self.ys * self.g2
        self.depth_span = self.g1
        self.expand_rows = channels // self.devices
        self.expand_pad = -(-self.g1 * self.expand_rows // ROW_UNIT) * ROW_UNIT
        self.reduce_rows = hid // self.devices
        self.reduce_block = hid // slides
        self.share = KS * KS * channels // self.devices
        self.channels = channels
        self.pieces = hid // channels
        self.rows = self.pieces * self.expand_pad + self.g1 * (self.reduce_rows + DEPTH_ROWS)

    def device(self, part, z):
        core, cross = divmod(part, self.cross)
        y, x = divmod(cross, self.g2)
        return ((y * 2 + core) * self.g1 + z) * self.g2 + x

    def tap_start(self, part, z):
        return self.device(part, z) * self.share // self.channels

    def expand_order(self):
        order = np.zeros((2 * self.cross * self.expand_pad, self.channels), np.float32)
        for part in range(2 * self.cross):
            for z in range(self.g1):
                for row in range(self.expand_rows):
                    target = part * self.expand_pad + z * self.expand_rows + row
                    order[target, self.device(part, z) * self.expand_rows + row] = 1.0
        return order

    def reduce_order(self):
        order = np.zeros((self.reduce_block, self.reduce_block), np.float32)
        for x in range(self.g2):
            for z in range(self.g1):
                for row in range(self.reduce_rows):
                    target = (x * self.g1 + z) * self.reduce_rows + row
                    order[target, (z * self.g2 + x) * self.reduce_rows + row] = 1.0
        return order


def backward_block(plan, table, embed_grad, saved, gain, shift, scale, expand, reduce, head):
    source, unit, inv, hidden, slope, head_slope = saved
    side, channels = source.shape[1], source.shape[3]
    cells, hid = side * side, expand.shape[1]
    bands = channels // LANES
    orders = tuple(
        jnp.asarray(order, jnp.bfloat16)
        for order in (plan.expand_order(), plan.reduce_order(), np.eye(channels, dtype=np.float32))
    )

    def per_slot(array):
        shape = array.shape[1:]
        return pl.BlockSpec((1,) + shape, lambda i, table: (i,) + (0,) * len(shape))

    streams = (embed_grad, source, unit, inv, hidden, slope, head_slope)
    consts = (gain, shift, scale, expand, reduce, head) + orders
    out = (2 * plan.cross, plan.rows, channels)
    return pl.pallas_call(
        functools.partial(backward_kernel, plan),
        out_shape=jax.ShapeDtypeStruct(out, jnp.bfloat16),
        grid_spec=pltpu.PrefetchScalarGridSpec(
            num_scalar_prefetch=1,
            grid=(PROC,),
            in_specs=[per_slot(stream) for stream in streams]
            + [whole(const.shape) for const in consts],
            out_specs=whole(out),
            scratch_shapes=[
                pltpu.VMEM((PROC * cells, hid), jnp.bfloat16),
                pltpu.VMEM((PROC * cells, hid), jnp.bfloat16),
                pltpu.VMEM((PROC, orders[0].shape[0], cells), jnp.bfloat16),
                pltpu.VMEM((PROC, channels, cells), jnp.bfloat16),
                pltpu.VMEM((bands, side, side + ROW_UNIT, LANES), jnp.float32),
                pltpu.VMEM((bands, cells, LANES), jnp.float32),
                pltpu.VMEM((bands, KS * KS, 8, LANES), jnp.float32),
                pltpu.VMEM((KS * KS + 7, channels), jnp.float32),
            ],
        ),
        compiler_params=pltpu.CompilerParams(vmem_limit_bytes=VMEM_BYTES),
        name="backward_block",
    )(table, *streams, *consts)


def exchange(values, names):
    return lax.all_to_all(values, names, split_axis=0, concat_axis=0, tiled=True)


def scatter_sum(plan, payload, my_device):
    channels = plan.channels
    grid = payload.reshape(2, plan.cross, plan.rows, channels)
    grid = jnp.sum(exchange(grid, ("core",)).astype(jnp.float32), axis=0).astype(jnp.bfloat16)
    total = jnp.sum(exchange(grid, ("y", "g2")).astype(jnp.float32), axis=0).astype(jnp.bfloat16)
    cut = plan.pieces * plan.expand_pad
    later = cut + plan.g1 * plan.reduce_rows
    expand = total[:cut].reshape(plan.pieces, plan.expand_pad, channels)
    expand = expand[:, : plan.g1 * plan.expand_rows].reshape(
        plan.pieces, plan.g1, plan.expand_rows, channels
    )
    expand = expand.transpose(1, 0, 2, 3).reshape(plan.g1, -1, channels)
    reduce = total[cut:later].reshape(plan.g1, plan.reduce_rows, channels)
    depth = total[later:].reshape(plan.g1, DEPTH_ROWS, channels)
    last = jnp.concatenate([expand, reduce, depth], axis=1)
    last = jnp.sum(exchange(last, ("g1",)).astype(jnp.float32), axis=0)
    cut = plan.pieces * plan.expand_rows
    later = cut + plan.reduce_rows
    expand = last[:cut].reshape(plan.pieces, plan.expand_rows, channels).transpose(1, 0, 2)
    first = my_device * plan.share
    depth = lax.dynamic_slice(
        last[later:].reshape(-1), (first - first // channels * channels,), (plan.share,)
    )
    return expand.reshape(-1), last[cut:later].reshape(-1), depth


def position_code(positions):
    half_width = E // 2
    channel_ids = jnp.arange(E, dtype=jnp.int32) % half_width
    frequency = jnp.exp(
        (2 * (channel_ids // 2)).astype(jnp.float32) * (-math.log(10000.0) / half_width)
    )
    phase = jnp.where(channel_ids % 2 == 0, 0.0, 0.5 * math.pi)
    rows = jnp.where(
        jnp.arange(E, dtype=jnp.int32) < half_width, positions[0][..., None], positions[1][..., None]
    )
    return jnp.sin(rows.astype(jnp.float32) * frequency + phase)


def on_device(
    tile_maps,
    positions,
    counts,
    routing,
    depth_kernel,
    depth_bias,
    norm_gain,
    norm_shift,
    expand_weight,
    expand_bias,
    reduce_weight,
    reduce_bias,
    layer_scale,
    head_weight,
    slide_taps,
    slide_weight,
    slide_bias,
    cotangent,
):
    slides = lax.axis_size(DP)
    members = lax.axis_size(GROUP)
    my_slide = lax.axis_index(DP)
    my_member = lax.axis_index(GROUP)
    my_device = my_slide * members + my_member
    slots, channels = tile_maps.shape[0], tile_maps.shape[3]
    devices, length, places = slides * members, slots * members, slots // slides
    plan = Plan(slides, members, channels, expand_weight.shape[1])
    route = routing.reshape(-1)
    bands = channels // LANES

    packed, table = pack_tiles(my_slide.reshape(1), route, tile_maps, slides, places)
    arrived = exchange(packed, DP)

    extras = jnp.concatenate(
        [
            cotangent[0],
            route.astype(jnp.float32),
            jnp.zeros((960 - E - slides * slots,), jnp.float32),
            positions.reshape(-1).astype(jnp.float32),
            jnp.zeros((1023 - 960 - 2 * slots,), jnp.float32),
            counts.astype(jnp.float32),
        ]
    )
    extras = exchange(jnp.broadcast_to(extras, (devices, 1024)), ALL)
    route_all = extras[:, E : E + slides * slots].astype(jnp.int32)
    route_all = route_all.reshape(slides, members, slides, slots)[0]
    pos_all = extras[:, 960 : 960 + 2 * slots].reshape(slides, members, 2, slots)
    pos_all = pos_all.transpose(2, 0, 3, 1).reshape(2, slides, length)
    counts_all = extras[:, 1023].reshape(slides, members)[:, 0]
    cot_all = extras[:, :E].reshape(slides, members, 1, E)[:, 0]
    codes = position_code(pos_all)
    member_ids = jnp.arange(members, dtype=jnp.int32)[:, None, None]
    target = jnp.where(
        route_all >= 0, (route_all // PROC * members + member_ids) * PROC + route_all % PROC, -1
    )
    target = target.transpose(1, 2, 0).reshape(slides, length, 1)
    pick = (target == jnp.arange(devices * PROC, dtype=jnp.int32)).astype(jnp.bfloat16)
    steps = jnp.arange(length, dtype=jnp.int32)[None, :, None].astype(jnp.float32)
    weight = jnp.where(steps < counts_all[:, None, None], 1.0 / counts_all[:, None, None], 0.0)

    def row(vector):
        return vector.reshape(1, -1)

    outs = forward_block(
        table,
        arrived,
        depth_kernel.reshape(KS * KS, bands, LANES).transpose(1, 0, 2),
        depth_bias.reshape(bands, 1, LANES),
        row(norm_gain),
        row(norm_shift),
        expand_weight,
        row(expand_bias),
        reduce_weight,
        row(reduce_bias),
        row(layer_scale),
        head_weight,
    )
    tile_out, tile_embed, unit, inv, hidden, slope, head_slope, source = outs
    embeds = exchange(
        jnp.broadcast_to(tile_embed.reshape(PROC, E).astype(jnp.bfloat16), (devices, PROC, E)), ALL
    )
    info = jnp.concatenate(
        [
            table[: 3 * PROC],
            table[3 * PROC :] * members + my_member,
            my_slide.reshape(1),
            jnp.zeros((3,), jnp.int32),
        ]
    )
    feature, embed_grad = slide_grads(
        info,
        embeds.reshape(devices * PROC, E),
        pick,
        codes,
        weight,
        cot_all,
        slide_taps,
        slide_weight,
        row(slide_bias),
    )
    payload = backward_block(
        plan,
        table,
        embed_grad,
        (source, unit, inv, hidden, slope, head_slope),
        row(norm_gain),
        row(norm_shift),
        row(layer_scale),
        expand_weight,
        reduce_weight,
        head_weight,
    )
    shares = scatter_sum(plan, payload, my_device)
    return (tile_out, feature, shares[0], shares[1], shares[2])


def solution(mesh):
    slides, members = mesh.shape["dp"], mesh.shape["group"]
    fine = Mesh(mesh.devices.reshape(slides // 2, 2, 4, members // 4), ALL)
    return jax.shard_map(
        on_device,
        mesh=fine,
        in_specs=(
            P(ALL, None, None, None),
            P(None, ALL),
            P(DP),
            P(None, GROUP, None),
        )
        + (P(),) * 13
        + (P(DP, None),),
        out_specs=(
            P(ALL, None, None, None),
            P(DP, None),
            P(ALL),
            P(ALL),
            P(ALL),
        ),
        check_vma=False,
    )
```

```python
import functools
import math

import jax
import jax.numpy as jnp
import numpy as np
from jax import lax
from jax.experimental import pallas as pl
from jax.experimental.pallas import tpu as pltpu
from jax.sharding import Mesh, PartitionSpec as P

E = 768
KS = 7
KERNEL_TAPS = 7
TILE_DILATION = 3
PROC = 4
DP = ("y", "core")
GROUP = ("g1", "g2")
ALL = DP + GROUP

EPSILON = 1e-06
HALF_ROOT = 0.7071067811865476
INV_ROOT_TAU = 0.3989422804014327
LANES = 128
ROW_UNIT = 16
DEPTH_ROWS = 4
VMEM_BYTES = 56 * 1024 * 1024
PART = 32
WIDTH = 256
GAIN, SHIFT, SCALE, REDUCE_BIAS, DEPTH_BIAS, EXPAND_BIAS, SLIDE_BIAS = range(7)
ERFC_P = 0.3275911
ERFC_A = (0.254829592, -0.284496736, 1.421413741, -1.453152027, 1.061405429)

HBM = pl.BlockSpec(memory_space=pl.ANY)


def whole(shape):
    return pl.BlockSpec(shape, lambda *_: (0,) * len(shape))


def gelu_and_slope(values):
    size = jnp.abs(values)
    divisor = 1.0 + (ERFC_P * HALF_ROOT) * size
    guess = pl.reciprocal(divisor, approx=True)
    t = guess * (2.0 - divisor * guess)
    bell = jnp.exp(-0.5 * values * values)
    poly = 0.5 * ERFC_A[4]
    for coefficient in ERFC_A[3::-1]:
        poly = poly * t + 0.5 * coefficient
    tail = poly * t * bell
    phi = jnp.where(values >= 0.0, 1.0 - tail, tail)
    return values * phi, phi + values * (INV_ROOT_TAU * bell)


def mix_cols(left_side, right_side):
    return lax.dot_general(
        left_side, right_side, (((1,), (1,)), ((), ())), preferred_element_type=jnp.float32
    )


def mix(left_side, right_side):
    return jnp.dot(left_side, right_side, preferred_element_type=jnp.float32)


def pack_kernel(slides, slots, places, my_ref, route_ref, tiles_ref, packed_ref, table_ref, count_ref, sems):
    my_slide = my_ref[0]

    def copy_of(slot, target):
        return pltpu.make_async_copy(tiles_ref.at[slot], packed_ref.at[target], sems.at[slot])

    for dest in range(slides):
        count_ref[dest] = 0
    for slot in range(slots):
        entry = route_ref[my_slide * slots + slot]

        @pl.when(entry >= 0)
        def _send():
            dest = lax.div(entry, PROC)
            rank = count_ref[dest]
            count_ref[dest] = rank + 1
            copy_of(slot, dest * places + rank).start()

    for field in range(4 * PROC):
        table_ref[field] = 0
    for source in range(slides):
        count_ref[0] = 0
        for slot in range(slots):
            entry = route_ref[source * slots + slot]
            inside = (entry >= my_slide * PROC) & (entry < my_slide * PROC + PROC)

            @pl.when(inside)
            def _take():
                proc = entry - my_slide * PROC
                rank = count_ref[0]
                count_ref[0] = rank + 1
                table_ref[proc] = source * places + rank
                table_ref[PROC + proc] = 1
                table_ref[2 * PROC + proc] = source
                table_ref[3 * PROC + proc] = slot

    for slot in range(slots):
        entry = route_ref[my_slide * slots + slot]

        @pl.when(entry >= 0)
        def _wait():
            copy_of(slot, 0).wait()


def pack_tiles(my_slide, route, tile_maps, slides, places):
    slots = tile_maps.shape[0]
    smem = pl.BlockSpec(memory_space=pltpu.SMEM)
    return pl.pallas_call(
        functools.partial(pack_kernel, slides, slots, places),
        out_shape=(
            jax.ShapeDtypeStruct((slides * places,) + tile_maps.shape[1:], tile_maps.dtype),
            jax.ShapeDtypeStruct((4 * PROC,), jnp.int32),
        ),
        in_specs=[smem, smem, HBM],
        out_specs=(pl.BlockSpec(memory_space=pltpu.VMEM), smem),
        scratch_shapes=[pltpu.SMEM((slides,), jnp.int32), pltpu.SemaphoreType.DMA((slots,))],
        name="pack_tiles",
    )(my_slide, route, tile_maps)


def forward_kernel(
    table_ref,
    tile_ref,
    taps_ref,
    vectors_ref,
    expand_ref,
    reduce_ref,
    head_ref,
    out_ref,
    embed_ref,
    unit_ref,
    inv_ref,
    hidden_ref,
    slope_ref,
    head_slope_ref,
    source_ref,
    padded,
    depth_out,
    normed,
    pre,
    section,
):
    filled = table_ref[PROC + pl.program_id(0)]
    side = tile_ref.shape[1]
    channels = tile_ref.shape[3]
    cells = side * side
    bands = channels // LANES
    low = ROW_UNIT // 2
    reach = KS // 2

    @pl.when(filled == 0)
    def _empty():
        for ref in (out_ref, embed_ref, unit_ref, inv_ref, hidden_ref, slope_ref, head_slope_ref, source_ref):
            ref[...] = jnp.zeros(ref.shape, ref.dtype)

    @pl.when(filled != 0)
    def _work():
        source_ref[...] = tile_ref[...]
        edge = jnp.zeros((side, low, LANES), jnp.float32)
        for band in range(bands):
            padded[band, :, 0:low, :] = edge
            padded[band, :, low + side :, :] = edge
            for at in range(side):
                padded[band, at, low : low + side, :] = tile_ref[
                    0, at, :, band * LANES : (band + 1) * LANES
                ].astype(jnp.float32)

        def convolve(band, carry):
            lanes = pl.ds(pl.multiple_of(band * LANES, LANES), LANES)
            bias = jnp.broadcast_to(vectors_ref[DEPTH_BIAS : DEPTH_BIAS + 1, lanes], (side, LANES))
            totals = [bias for _ in range(side)]
            for col in range(KS):
                start = low - reach + col
                weights = [
                    taps_ref[row * KS + col : row * KS + col + 1, lanes] for row in range(KS)
                ]
                for at in range(side):
                    line = padded[band, at, start : start + side, :]
                    for row in range(KS):
                        place = at - row + reach
                        if 0 <= place < side:
                            totals[place] = totals[place] + weights[row] * line
            for place in range(side):
                depth_out[band, place * side : (place + 1) * side, :] = totals[place]
            return carry

        lax.fori_loop(0, bands, convolve, 0)

        def vector(index, lanes):
            return vectors_ref[index : index + 1, lanes]

        for start in range(0, cells, PART):
            rows = slice(start, start + PART)
            pieces = [depth_out[band, rows, :] for band in range(bands)]
            mean = jnp.sum(sum(pieces), axis=1, keepdims=True) * (1.0 / channels)
            pieces = [piece - mean for piece in pieces]
            var = jnp.sum(sum(p * p for p in pieces), axis=1, keepdims=True) * (1.0 / channels)
            inv = lax.rsqrt(var + EPSILON)
            inv_ref[0, rows, :] = jnp.broadcast_to(inv, (PART, LANES))
            for band in range(bands):
                lanes = slice(band * LANES, (band + 1) * LANES)
                unit = pieces[band] * inv
                unit_ref[0, rows, lanes] = unit
                normed[rows, lanes] = (unit * vector(GAIN, lanes) + vector(SHIFT, lanes)).astype(
                    jnp.bfloat16
                )

        for index, begin in enumerate(range(0, expand_ref.shape[1], WIDTH)):
            cols = slice(begin, begin + WIDTH)
            buffer = index % pre.shape[0]
            pre[buffer] = mix(normed[...], expand_ref[:, cols])
            for start in range(0, cells, PART):
                rows = slice(start, start + PART)
                act, slope = gelu_and_slope(pre[buffer, rows, :] + vector(EXPAND_BIAS, cols))
                hidden_ref[0, rows, cols] = act.astype(jnp.bfloat16)
                slope_ref[0, rows, cols] = slope.astype(jnp.bfloat16)
        lanes = slice(0, channels)
        depth_rows = mix(hidden_ref[0], reduce_ref[...])
        for at in range(side):
            rows = slice(at * side, (at + 1) * side)
            branch = vector(SCALE, lanes) * (depth_rows[rows] + vector(REDUCE_BIAS, lanes))
            line = (tile_ref[0, at].astype(jnp.float32) + branch).astype(jnp.bfloat16)
            section[rows, :] = line
            out_ref[0, at] = line
        for index, begin in enumerate(range(0, head_ref.shape[1], WIDTH)):
            cols = slice(begin, begin + WIDTH)
            buffer = index % pre.shape[0]
            pre[buffer] = mix(section[...], head_ref[:, cols])
            total = None
            for start in range(0, cells, PART):
                rows = slice(start, start + PART)
                act, slope = gelu_and_slope(pre[buffer, rows, :])
                head_slope_ref[0, rows, cols] = slope.astype(jnp.bfloat16)
                folded = act[0:8]
                for piece in range(8, PART, 8):
                    folded = folded + act[piece : piece + 8]
                total = folded if total is None else total + folded
            embed_ref[0, :, cols] = jnp.sum(total, axis=0, keepdims=True) * (1.0 / cells)


def forward_block(table, arrived, taps, vectors, expand, reduce, head):
    side, channels = arrived.shape[1], arrived.shape[3]
    cells, hid, embed = side * side, expand.shape[1], head.shape[1]
    bands = channels // LANES

    def per_slot(*shape):
        return pl.BlockSpec((1,) + shape, lambda i, table: (i,) + (0,) * len(shape))

    outs = (
        ((side, side, channels), jnp.bfloat16),
        ((1, embed), jnp.float32),
        ((cells, channels), jnp.float32),
        ((cells, LANES), jnp.float32),
        ((cells, hid), jnp.bfloat16),
        ((cells, hid), jnp.bfloat16),
        ((cells, embed), jnp.bfloat16),
        ((side, side, channels), jnp.bfloat16),
    )
    consts = (taps, vectors, expand, reduce, head)
    return pl.pallas_call(
        forward_kernel,
        out_shape=tuple(jax.ShapeDtypeStruct((PROC,) + shape, kind) for shape, kind in outs),
        grid_spec=pltpu.PrefetchScalarGridSpec(
            num_scalar_prefetch=1,
            grid=(PROC,),
            in_specs=[
                pl.BlockSpec((1, side, side, channels), lambda i, table: (table[i], 0, 0, 0))
            ]
            + [whole(const.shape) for const in consts],
            out_specs=[per_slot(*shape) for shape, _ in outs],
            scratch_shapes=[
                pltpu.VMEM((bands, side, side + ROW_UNIT, LANES), jnp.float32),
                pltpu.VMEM((bands, cells, LANES), jnp.float32),
                pltpu.VMEM((cells, channels), jnp.bfloat16),
                pltpu.VMEM((3, cells, WIDTH), jnp.float32),
                pltpu.VMEM((cells, channels), jnp.bfloat16),
            ],
        ),
        compiler_params=pltpu.CompilerParams(vmem_limit_bytes=VMEM_BYTES),
        cost_estimate=pl.CostEstimate(
            flops=2 * PROC * cells * channels * (2 * hid + embed + KS * KS),
            bytes_accessed=24 * 1024 * 1024,
            transcendentals=2 * PROC * cells * (hid + embed),
        ),
        name="forward_block",
    )(table, arrived, *consts)


def slide_kernel(
    length,
    slides,
    info_ref,
    embeds_ref,
    pick_ref,
    codes_ref,
    weight_ref,
    cot_ref,
    taps_ref,
    matrix_ref,
    vectors_ref,
    feature_ref,
    grad_ref,
    rows,
    back,
    features,
    mixed,
    pre,
    grad_agg,
):
    border = ROW_UNIT
    edge = jnp.zeros((border, rows.shape[2]), jnp.float32)
    reach = KERNEL_TAPS // 2
    blocks = [slice(start, start + WIDTH) for start in range(0, rows.shape[2], WIDTH)]

    def dilate(ref, slide, direction, cols):
        total = ref[slide, border : border + length, cols]
        for tap in range(KERNEL_TAPS):
            start = border + direction * (tap - reach) * TILE_DILATION
            total = total + taps_ref[tap : tap + 1, cols] * ref[slide, start : start + length, cols]
        return total

    def one_slide(slide, carry):
        here = weight_ref[slide] > 0.0
        for ref in (rows, back):
            ref[slide, 0:border, :] = edge
            ref[slide, border + length :, :] = edge
        for cols in blocks:
            own = mix(pick_ref[slide], embeds_ref[:, cols]) + codes_ref[slide, :, cols]
            rows[slide, border : border + length, cols] = (
                jnp.where(here, own, 0.0).astype(jnp.bfloat16).astype(jnp.float32)
            )
            mixed[:, cols] = dilate(rows, slide, 1, cols).astype(jnp.bfloat16)
        for cols in blocks:
            pre[:, cols] = mix(mixed[...], matrix_ref[:, cols])
            total = None
            for start in range(0, length, PART):
                part = slice(start, start + PART)
                share = weight_ref[slide, part, :]
                act, slope = gelu_and_slope(
                    pre[part, cols] + vectors_ref[SLIDE_BIAS : SLIDE_BIAS + 1, cols]
                )
                grad_agg[part, cols] = (cot_ref[slide, :, cols] * share * slope).astype(jnp.bfloat16)
                piece = jnp.sum(act * share, axis=0, keepdims=True)
                total = piece if total is None else total + piece
            features[pl.ds(slide, 1), cols] = total
        for cols in blocks:
            back[slide, border : border + length, cols] = mix_cols(
                grad_agg[...], matrix_ref[cols, :]
            )
            total = jnp.where(here, dilate(back, slide, -1, cols), 0.0)
            rows[slide, border : border + length, cols] = total.astype(jnp.bfloat16).astype(
                jnp.float32
            )
        return carry

    lax.fori_loop(0, slides, one_slide, 0)
    feature_ref[...] = features[pl.ds(info_ref[4 * PROC], 1), :]
    for proc in range(PROC):
        filled = info_ref[PROC + proc]
        at = border + info_ref[3 * PROC + proc]
        row = rows[info_ref[2 * PROC + proc], pl.ds(at, 1), :]
        grad_ref[proc] = jnp.where(filled != 0, row, 0.0)


def slide_grads(info, embeds, pick, codes, weight, cot, taps, matrix, vectors):
    slides, length, embed = codes.shape
    smem = pl.BlockSpec(memory_space=pltpu.SMEM)
    vmem = pl.BlockSpec(memory_space=pltpu.VMEM)
    padded = (slides, length + 2 * ROW_UNIT, embed)
    return pl.pallas_call(
        functools.partial(slide_kernel, length, slides),
        out_shape=(
            jax.ShapeDtypeStruct((1, embed), jnp.float32),
            jax.ShapeDtypeStruct((PROC, 1, embed), jnp.float32),
        ),
        in_specs=[smem] + [vmem] * 8,
        out_specs=(vmem, vmem),
        scratch_shapes=[
            pltpu.VMEM(padded, jnp.float32),
            pltpu.VMEM(padded, jnp.float32),
            pltpu.VMEM((max(slides, 8), embed), jnp.float32),
            pltpu.VMEM((length, embed), jnp.bfloat16),
            pltpu.VMEM((length, embed), jnp.float32),
            pltpu.VMEM((length, embed), jnp.bfloat16),
        ],
        compiler_params=pltpu.CompilerParams(vmem_limit_bytes=VMEM_BYTES),
        name="slide_grads",
    )(info, embeds, pick, codes, weight, cot, taps, matrix, vectors)


def backward_kernel(
    plan,
    table_ref,
    grad_ref,
    source_ref,
    unit_ref,
    inv_ref,
    hidden_ref,
    slope_ref,
    head_slope_ref,
    vectors_ref,
    expand_ref,
    reduce_ref,
    head_ref,
    expand_order_ref,
    reduce_order_ref,
    eye_ref,
    keep_ref,
    send_ref,
    grad_pre_all,
    hidden_all,
    normed_all,
    grad_mlp_all,
    grad_head,
    grad_norm,
    padded,
    depth_back,
    tap_sums,
    tap_rows,
    staged,
    sems,
):
    step = pl.program_id(0)
    filled = table_ref[PROC + step]
    side = source_ref.shape[1]
    channels = source_ref.shape[3]
    cells = side * side
    bands = channels // LANES
    low = ROW_UNIT // 2
    reach = KS // 2
    rows_all = pl.ds(pl.multiple_of(step * cells, cells), cells)

    def vector(index, lanes):
        return vectors_ref[index : index + 1, lanes]

    @pl.when(step == 0)
    def _start():
        tap_sums[...] = jnp.zeros(tap_sums.shape, jnp.float32)

    @pl.when(filled == 0)
    def _empty():
        for ref in (grad_pre_all, hidden_all):
            ref[rows_all, :] = jnp.zeros((cells, ref.shape[1]), jnp.bfloat16)
        for ref in (normed_all, grad_mlp_all):
            ref[:, rows_all] = jnp.zeros((ref.shape[0], cells), jnp.bfloat16)

    @pl.when(filled != 0)
    def _work():
        every = slice(0, channels)
        for start in range(0, cells, PART):
            rows = slice(start, start + PART)
            grad_head[rows, :] = (
                (grad_ref[0] * (1.0 / cells)) * head_slope_ref[0, rows, :].astype(jnp.float32)
            ).astype(jnp.bfloat16)
        grad_mlp = (vector(SCALE, every) * mix_cols(grad_head[...], head_ref[...])).astype(
            jnp.bfloat16
        )
        grad_mlp_all[:, rows_all] = mix_cols(eye_ref[...], grad_mlp).astype(jnp.bfloat16)
        hidden_all[rows_all, :] = hidden_ref[0]
        for begin in range(0, expand_ref.shape[1], WIDTH):
            cols = slice(begin, begin + WIDTH)
            grad_hidden = mix_cols(grad_mlp, reduce_ref[cols, :])
            grad_pre_all[rows_all, cols] = (
                grad_hidden * slope_ref[0, :, cols].astype(jnp.float32)
            ).astype(jnp.bfloat16)
        grad_norm[...] = mix_cols(grad_pre_all[rows_all, :], expand_ref[...])
        normed = (unit_ref[0] * vector(GAIN, every) + vector(SHIFT, every)).astype(jnp.bfloat16)
        normed_all[:, rows_all] = mix_cols(expand_order_ref[...], normed).astype(jnp.bfloat16)

        for start in range(0, cells, PART):
            rows = slice(start, start + PART)
            scaled = grad_norm[rows, :] * vector(GAIN, every)
            unit = unit_ref[0, rows, :]
            mean = jnp.sum(scaled, axis=1, keepdims=True) * (1.0 / channels)
            mean_unit = jnp.sum(scaled * unit, axis=1, keepdims=True) * (1.0 / channels)
            inv = inv_ref[0, rows, 0:1]
            for band in range(bands):
                lanes = slice(band * LANES, (band + 1) * LANES)
                depth_back[band, rows, :] = inv * (
                    scaled[:, lanes] - mean - unit[:, lanes] * mean_unit
                )
        edge = jnp.zeros((side, low, LANES), jnp.float32)
        for band in range(bands):
            lanes = slice(band * LANES, (band + 1) * LANES)
            padded[band, :, 0:low, :] = edge
            padded[band, :, low + side :, :] = edge
            for at in range(side):
                padded[band, at, low : low + side, :] = source_ref[0, at, :, lanes].astype(
                    jnp.float32
                )

        def taps_of(band, carry):
            for col in range(KS):
                start = low - reach + col
                sums = [None] * KS
                grads = {}
                for at in range(side):
                    line = padded[band, at, start : start + side, :]
                    for row in range(KS):
                        place = at - row + reach
                        if 0 <= place < side:
                            if place not in grads:
                                grads[place] = depth_back[
                                    band, place * side : (place + 1) * side, :
                                ]
                            term = line * grads[place]
                            sums[row] = term if sums[row] is None else sums[row] + term
                for row in range(KS):
                    total = sums[row]
                    folded = total[0:8, :]
                    for piece in range(8, side, 8):
                        folded = folded + total[piece : piece + 8, :]
                    tap_sums[band, row * KS + col] = tap_sums[band, row * KS + col] + folded
            return carry

        lax.fori_loop(0, bands, taps_of, 0)

    @pl.when(step == pl.num_programs(0) - 1)
    def _finish():
        my_core = table_ref[4 * PROC]
        for band in range(bands):
            lanes = slice(band * LANES, (band + 1) * LANES)
            tap_rows[0 : KS * KS, lanes] = jnp.sum(tap_sums[band], axis=1)
            tap_rows[KS * KS :, lanes] = jnp.zeros((tap_rows.shape[0] - KS * KS, LANES), jnp.float32)
        pieces = expand_ref.shape[1] // channels
        pad = plan.expand_pad
        for quarter in range(pieces):
            cols = slice(quarter * channels, (quarter + 1) * channels)
            total = mix(normed_all[...], grad_pre_all[:, cols]).astype(jnp.bfloat16)
            for core in range(2):
                for cross in range(plan.cross):
                    part = core * plan.cross + cross
                    staged[core ^ my_core, cross, quarter * pad : (quarter + 1) * pad, :] = total[
                        part * pad : (part + 1) * pad, :
                    ]
        base = pieces * pad
        block = plan.reduce_block
        span = plan.g1 * plan.reduce_rows
        for index in range(expand_ref.shape[1] // block):
            cols = slice(index * block, (index + 1) * block)
            total = mix(grad_mlp_all[...], hidden_all[:, cols]).astype(jnp.bfloat16)
            turned = mix_cols(reduce_order_ref[...], total).astype(jnp.bfloat16)
            y, core = divmod(index, 2)
            for x in range(plan.g2):
                staged[core ^ my_core, y * plan.g2 + x, base : base + span, :] = turned[
                    x * span : (x + 1) * span, :
                ]
        base = base + span
        for core in range(2):
            for cross in range(plan.cross):
                starts = [plan.tap_start(core * plan.cross + cross, z) for z in range(plan.g1)]
                staged[core ^ my_core, cross, base : base + plan.g1 * DEPTH_ROWS, :] = (
                    jnp.concatenate(
                        [tap_rows[start : start + DEPTH_ROWS, :] for start in starts], axis=0
                    ).astype(jnp.bfloat16)
                )
        copies = [
            pltpu.make_async_copy(staged.at[index], ref, sems.at[index])
            for index, ref in enumerate((keep_ref, send_ref))
        ]
        for copy in copies:
            copy.start()
        for copy in copies:
            copy.wait()


class Plan:

    def __init__(self, slides, members, channels, hid):
        self.devices = slides * members
        self.ys, self.g1, self.g2 = slides // 2, 4, members // 4
        self.cross = self.ys * self.g2
        self.expand_rows = channels // self.devices
        self.expand_pad = -(-self.g1 * self.expand_rows // ROW_UNIT) * ROW_UNIT
        self.reduce_rows = hid // self.devices
        self.reduce_block = hid // slides
        self.share = KS * KS * channels // self.devices
        self.channels = channels
        self.pieces = hid // channels
        self.rows = self.pieces * self.expand_pad + self.g1 * (self.reduce_rows + DEPTH_ROWS)

    def device(self, part, z):
        core, cross = divmod(part, self.cross)
        y, x = divmod(cross, self.g2)
        return ((y * 2 + core) * self.g1 + z) * self.g2 + x

    def tap_start(self, part, z):
        return self.device(part, z) * self.share // self.channels

    def expand_order(self):
        order = np.zeros((2 * self.cross * self.expand_pad, self.channels), np.float32)
        for part in range(2 * self.cross):
            for z in range(self.g1):
                for row in range(self.expand_rows):
                    target = part * self.expand_pad + z * self.expand_rows + row
                    order[target, self.device(part, z) * self.expand_rows + row] = 1.0
        return order

    def reduce_order(self):
        order = np.zeros((self.reduce_block, self.reduce_block), np.float32)
        for x in range(self.g2):
            for z in range(self.g1):
                for row in range(self.reduce_rows):
                    target = (x * self.g1 + z) * self.reduce_rows + row
                    order[target, (z * self.g2 + x) * self.reduce_rows + row] = 1.0
        return order


def backward_block(plan, table, embed_grad, saved, vectors, expand, reduce, head):
    source, unit, inv, hidden, slope, head_slope = saved
    side, channels = source.shape[1], source.shape[3]
    cells, hid = side * side, expand.shape[1]
    bands = channels // LANES
    orders = tuple(
        jnp.asarray(order, jnp.bfloat16)
        for order in (plan.expand_order(), plan.reduce_order(), np.eye(channels, dtype=np.float32))
    )

    def per_slot(array):
        shape = array.shape[1:]
        return pl.BlockSpec((1,) + shape, lambda i, table: (i,) + (0,) * len(shape))

    streams = (embed_grad, source, unit, inv, hidden, slope, head_slope)
    consts = (vectors, expand, reduce, head) + orders
    out = (plan.cross, plan.rows, channels)
    return pl.pallas_call(
        functools.partial(backward_kernel, plan),
        out_shape=(jax.ShapeDtypeStruct(out, jnp.bfloat16),) * 2,
        grid_spec=pltpu.PrefetchScalarGridSpec(
            num_scalar_prefetch=1,
            grid=(PROC,),
            in_specs=[per_slot(stream) for stream in streams]
            + [whole(const.shape) for const in consts],
            out_specs=(HBM, HBM),
            scratch_shapes=[
                pltpu.VMEM((PROC * cells, hid), jnp.bfloat16),
                pltpu.VMEM((PROC * cells, hid), jnp.bfloat16),
                pltpu.VMEM((orders[0].shape[0], PROC * cells), jnp.bfloat16),
                pltpu.VMEM((channels, PROC * cells), jnp.bfloat16),
                pltpu.VMEM((cells, head.shape[1]), jnp.bfloat16),
                pltpu.VMEM((cells, channels), jnp.float32),
                pltpu.VMEM((bands, side, side + ROW_UNIT, LANES), jnp.float32),
                pltpu.VMEM((bands, cells, LANES), jnp.float32),
                pltpu.VMEM((bands, KS * KS, 8, LANES), jnp.float32),
                pltpu.VMEM((KS * KS + 7, channels), jnp.float32),
                pltpu.VMEM((2,) + out, jnp.bfloat16),
                pltpu.SemaphoreType.DMA((2,)),
            ],
        ),
        compiler_params=pltpu.CompilerParams(vmem_limit_bytes=VMEM_BYTES),
        name="backward_block",
    )(table, *streams, *consts)


def exchange(values, names):
    return lax.all_to_all(values, names, split_axis=0, concat_axis=0, tiled=True)


def scatter_sum(plan, kept, sent, my_device):
    channels = plan.channels
    other = lax.ppermute(sent, "core", [(0, 1), (1, 0)])
    grid = (kept.astype(jnp.float32) + other.astype(jnp.float32)).astype(jnp.bfloat16)
    total = jnp.sum(exchange(grid, ("y", "g2")).astype(jnp.float32), axis=0).astype(jnp.bfloat16)
    cut = plan.pieces * plan.expand_pad
    later = cut + plan.g1 * plan.reduce_rows
    expand = total[:cut].reshape(plan.pieces, plan.expand_pad, channels)
    expand = expand[:, : plan.g1 * plan.expand_rows].reshape(
        plan.pieces, plan.g1, plan.expand_rows, channels
    )
    expand = expand.transpose(1, 0, 2, 3).reshape(plan.g1, -1, channels)
    reduce = total[cut:later].reshape(plan.g1, plan.reduce_rows, channels)
    depth = total[later:].reshape(plan.g1, DEPTH_ROWS, channels)
    last = jnp.concatenate([expand, reduce, depth], axis=1)
    last = jnp.sum(exchange(last, ("g1",)).astype(jnp.float32), axis=0)
    cut = plan.pieces * plan.expand_rows
    later = cut + plan.reduce_rows
    expand = last[:cut].reshape(plan.pieces, plan.expand_rows, channels).transpose(1, 0, 2)
    first = my_device * plan.share
    depth = lax.dynamic_slice(
        last[later:].reshape(-1), (first - first // channels * channels,), (plan.share,)
    )
    return expand.reshape(-1), last[cut:later].reshape(-1), depth


def position_code(positions):
    half_width = E // 2
    channel_ids = jnp.arange(E, dtype=jnp.int32) % half_width
    frequency = jnp.exp(
        (2 * (channel_ids // 2)).astype(jnp.float32) * (-math.log(10000.0) / half_width)
    )
    phase = jnp.where(channel_ids % 2 == 0, 0.0, 0.5 * math.pi)
    rows = jnp.where(
        jnp.arange(E, dtype=jnp.int32) < half_width, positions[0][..., None], positions[1][..., None]
    )
    return jnp.sin(rows.astype(jnp.float32) * frequency + phase)


def on_device(
    tile_maps,
    positions,
    counts,
    routing,
    depth_kernel,
    depth_bias,
    norm_gain,
    norm_shift,
    expand_weight,
    expand_bias,
    reduce_weight,
    reduce_bias,
    layer_scale,
    head_weight,
    slide_taps,
    slide_weight,
    slide_bias,
    cotangent,
):
    slides = lax.axis_size(DP)
    members = lax.axis_size(GROUP)
    my_slide = lax.axis_index(DP)
    my_member = lax.axis_index(GROUP)
    my_device = my_slide * members + my_member
    slots, channels = tile_maps.shape[0], tile_maps.shape[3]
    devices, length, places = slides * members, slots * members, slots // slides
    plan = Plan(slides, members, channels, expand_weight.shape[1])
    route = routing.reshape(-1)

    packed, table = pack_tiles(my_slide.reshape(1), route, tile_maps, slides, places)
    vectors = jnp.stack(
        [
            jnp.pad(vector, (0, expand_bias.shape[0] - vector.shape[0]))
            for vector in (
                norm_gain,
                norm_shift,
                layer_scale,
                reduce_bias,
                depth_bias,
                expand_bias,
                slide_bias,
                slide_bias,
            )
        ]
    )
    packed, route, cotangent, positions, counts = lax.optimization_barrier(
        (packed, route, cotangent, positions, counts)
    )
    arrived = exchange(packed, DP)

    extras = jnp.concatenate(
        [
            cotangent[0],
            route.astype(jnp.float32),
            jnp.zeros((960 - E - slides * slots,), jnp.float32),
            positions.reshape(-1).astype(jnp.float32),
            jnp.zeros((1023 - 960 - 2 * slots,), jnp.float32),
            counts.astype(jnp.float32),
        ]
    )
    extras = exchange(jnp.broadcast_to(extras, (devices, 1024)), ALL)
    route_all = extras[:, E : E + slides * slots].astype(jnp.int32)
    route_all = route_all.reshape(slides, members, slides, slots)[0]
    pos_all = extras[:, 960 : 960 + 2 * slots].reshape(slides, members, 2, slots)
    pos_all = pos_all.transpose(2, 0, 3, 1).reshape(2, slides, length)
    counts_all = extras[:, 1023].reshape(slides, members)[:, 0]
    cot_all = extras[:, :E].reshape(slides, members, 1, E)[:, 0]
    codes = position_code(pos_all)
    member_ids = jnp.arange(members, dtype=jnp.int32)[:, None, None]
    target = jnp.where(
        route_all >= 0, (route_all // PROC * members + member_ids) * PROC + route_all % PROC, -1
    )
    target = target.transpose(1, 2, 0).reshape(slides, length, 1)
    pick = (target == jnp.arange(devices * PROC, dtype=jnp.int32)).astype(jnp.bfloat16)
    steps = jnp.arange(length, dtype=jnp.int32)[None, :, None].astype(jnp.float32)
    weight = jnp.where(steps < counts_all[:, None, None], 1.0 / counts_all[:, None, None], 0.0)

    outs = forward_block(
        table, arrived, depth_kernel, vectors, expand_weight, reduce_weight, head_weight
    )
    tile_out, tile_embed, unit, inv, hidden, slope, head_slope, source = outs
    embeds = exchange(
        jnp.broadcast_to(tile_embed.reshape(PROC, E).astype(jnp.bfloat16), (devices, PROC, E)), ALL
    )
    info = jnp.concatenate(
        [
            table[: 3 * PROC],
            table[3 * PROC :] * members + my_member,
            my_slide.reshape(1),
        ]
    )
    feature, embed_grad = slide_grads(
        info,
        embeds.reshape(devices * PROC, E),
        pick,
        codes,
        weight,
        cot_all,
        slide_taps,
        slide_weight,
        vectors,
    )
    kept, sent = backward_block(
        plan,
        jnp.concatenate([table, lax.axis_index("core").reshape(1)]),
        embed_grad,
        (source, unit, inv, hidden, slope, head_slope),
        vectors,
        expand_weight,
        reduce_weight,
        head_weight,
    )
    shares = scatter_sum(plan, kept, sent, my_device)
    return (tile_out, feature, shares[0], shares[1], shares[2])


def solution(mesh):
    slides, members = mesh.shape["dp"], mesh.shape["group"]
    fine = Mesh(mesh.devices.reshape(slides // 2, 2, 4, members // 4), ALL)
    return jax.shard_map(
        on_device,
        mesh=fine,
        in_specs=(
            P(ALL, None, None, None),
            P(None, ALL),
            P(DP),
            P(None, GROUP, None),
        )
        + (P(),) * 13
        + (P(DP, None),),
        out_specs=(
            P(ALL, None, None, None),
            P(DP, None),
            P(ALL),
            P(ALL),
            P(ALL),
        ),
        check_vma=False,
    )
```

```python
import functools
import math

import jax
import jax.numpy as jnp
import numpy as np
from jax import lax
from jax.experimental import pallas as pl
from jax.experimental.pallas import tpu as pltpu
from jax.sharding import Mesh, PartitionSpec as P

E = 768
KS = 7
KERNEL_TAPS = 7
TILE_DILATION = 3
PROC = 4
DP = ("y", "core")
GROUP = ("g1", "g2")
ALL = DP + GROUP

EPSILON = 1e-06
HALF_ROOT = 0.7071067811865476
INV_ROOT_TAU = 0.3989422804014327
LANES = 128
ROW_UNIT = 16
DEPTH_ROWS = 4
VMEM_BYTES = 56 * 1024 * 1024
PART = 32
WIDTH = 256
GAIN, SHIFT, SCALE, REDUCE_BIAS, DEPTH_BIAS, EXPAND_BIAS, SLIDE_BIAS = range(7)
ERFC_P = 0.3275911
ERFC_A = (0.254829592, -0.284496736, 1.421413741, -1.453152027, 1.061405429)

HBM = pl.BlockSpec(memory_space=pl.ANY)


def whole(shape):
    return pl.BlockSpec(shape, lambda *_: (0,) * len(shape))


def gelu_and_slope(values):
    size = jnp.abs(values)
    divisor = 1.0 + (ERFC_P * HALF_ROOT) * size
    guess = pl.reciprocal(divisor, approx=True)
    t = guess * (2.0 - divisor * guess)
    bell = jnp.exp(-0.5 * values * values)
    poly = 0.5 * ERFC_A[4]
    for coefficient in ERFC_A[3::-1]:
        poly = poly * t + 0.5 * coefficient
    tail = poly * t * bell
    phi = jnp.where(values >= 0.0, 1.0 - tail, tail)
    return values * phi, phi + values * (INV_ROOT_TAU * bell)


def mix_cols(left_side, right_side):
    return lax.dot_general(
        left_side, right_side, (((1,), (1,)), ((), ())), preferred_element_type=jnp.float32
    )


def mix(left_side, right_side):
    return jnp.dot(left_side, right_side, preferred_element_type=jnp.float32)


FILLED, SLIDE, PLACE, CLASSES = 0, PROC, 2 * PROC, 3 * PROC
CLASS_SIZE = 1 + 3 * PROC


def class_field(kind, field, item=0):
    return CLASSES + kind * CLASS_SIZE + (1 + field * PROC + item if field >= 0 else 0)


SLOT, FROM, OWN = range(3)


def pack_kernel(slides, slots, places, route_ref, tiles_ref, *refs):
    send_refs, (table_ref, count_ref, slot_ref, sems) = refs[:-4], refs[-4:]
    my_slide = lax.axis_index(DP)
    members = lax.axis_size(GROUP)
    my_member = lax.axis_index(GROUP)

    targets = [(0, rank, rank) for rank in range(places)]
    for rank in range(places):
        for other in range(2, slides):
            targets.append((1 + rank * (slides - 2) + other - 2, 0, other * places + rank))
    targets[:places] = [(0, rank, places + rank) for rank in range(places)]

    def copy_of(index, slot):
        buffer, row, _ = targets[index]
        return pltpu.make_async_copy(tiles_ref.at[slot], send_refs[buffer].at[row], sems.at[index])

    for index in range(slides):
        count_ref[index] = 0
    for index in range(slides * places):
        slot_ref[index] = -1

    def place_slot(slot, carry):
        entry = route_ref[my_slide, 0, slot]

        @pl.when(entry >= 0)
        def _send():
            other = lax.div(entry, PROC) ^ my_slide
            rank = count_ref[other]
            count_ref[other] = rank + 1
            slot_ref[other * places + rank] = slot

        return carry

    lax.fori_loop(0, slots, place_slot, 0)
    for index, (_, _, key) in enumerate(targets):
        slot = slot_ref[key]

        @pl.when(slot >= 0)
        def _start():
            copy_of(index, slot).start()

    kinds = 1 + places
    for field in range(CLASSES + kinds * CLASS_SIZE):
        table_ref[field] = 0
    for kind in range(kinds):
        for item in range(PROC):
            table_ref[class_field(kind, SLOT, item)] = PROC
    for other in range(slides):
        source = my_slide ^ other
        count_ref[0] = 0

        def take(slot, carry):
            entry = route_ref[source, 0, slot]
            proc = entry - my_slide * PROC

            @pl.when((proc >= 0) & (proc < PROC))
            def _take():
                rank = count_ref[0]
                count_ref[0] = rank + 1
                table_ref[FILLED + proc] = 1
                table_ref[SLIDE + proc] = source
                table_ref[PLACE + proc] = slot * members + my_member
                kind = 0 if other < 2 else 1 + rank
                base = CLASSES + kind * CLASS_SIZE
                item = table_ref[base]
                table_ref[base] = item + 1
                table_ref[base + 1 + SLOT * PROC + item] = proc
                if other == 0:
                    table_ref[base + 1 + FROM * PROC + item] = 0
                    table_ref[base + 1 + OWN * PROC + item] = slot
                else:
                    table_ref[base + 1 + FROM * PROC + item] = 1 + rank if other == 1 else other - 2

            return carry

        lax.fori_loop(0, slots, take, 0)
        if other == 0:
            own = table_ref[class_field(0, -1)]
            for item in range(1, PROC):

                @pl.when(item >= own)
                def _hold():
                    table_ref[class_field(0, OWN, item)] = table_ref[class_field(0, OWN, item - 1)]

    for kind in range(kinds):
        items = table_ref[class_field(kind, -1)]
        for item in range(1, PROC):

            @pl.when(item >= items)
            def _hold_slot():
                table_ref[class_field(kind, SLOT, item)] = table_ref[class_field(kind, SLOT, item - 1)]

    for index, (_, _, key) in enumerate(targets):

        @pl.when(slot_ref[key] >= 0)
        def _wait():
            copy_of(index, 0).wait()


def pack_tiles(routing, tile_maps, slides, places):
    slots = tile_maps.shape[0]
    smem = pl.BlockSpec(memory_space=pltpu.SMEM)
    vmem = pl.BlockSpec(memory_space=pltpu.VMEM)
    buffers = 1 + places * (slides - 2)
    shapes = [places] + [1] * (buffers - 1)
    outs = pl.pallas_call(
        functools.partial(pack_kernel, slides, slots, places),
        out_shape=tuple(
            jax.ShapeDtypeStruct((size,) + tile_maps.shape[1:], tile_maps.dtype) for size in shapes
        )
        + (jax.ShapeDtypeStruct((CLASSES + (1 + places) * CLASS_SIZE,), jnp.int32),),
        in_specs=[smem, HBM],
        out_specs=(vmem,) * buffers + (smem,),
        scratch_shapes=[
            pltpu.SMEM((slides,), jnp.int32),
            pltpu.SMEM((slides * places,), jnp.int32),
            pltpu.SemaphoreType.DMA((slides * places,)),
        ],
        compiler_params=pltpu.CompilerParams(vmem_limit_bytes=16 * 1024 * 1024),
        name="pack_tiles",
    )(routing, tile_maps)
    return outs[:-1], outs[-1]


def forward_kernel(kind, inputs, aliased, table_ref, *refs):
    forward_items(kind, table_ref, refs[:inputs], *refs[inputs : inputs + 5], *refs[inputs + 5 + aliased :])


def forward_items(
    kind,
    table_ref,
    tile_refs,
    taps_ref,
    vectors_ref,
    expand_ref,
    reduce_ref,
    head_ref,
    out_ref,
    embed_ref,
    unit_ref,
    inv_ref,
    hidden_ref,
    slope_ref,
    head_slope_ref,
    source_ref,
    padded,
    depth_out,
    normed,
    pre,
    section,
):
    item = pl.program_id(0)
    side = out_ref.shape[1]
    channels = out_ref.shape[3]
    cells = side * side
    bands = channels // LANES
    low = ROW_UNIT // 2
    reach = KS // 2

    @pl.when(item < table_ref[class_field(kind, -1)])
    def _work():
        origin = table_ref[class_field(kind, FROM) + item]
        edge = jnp.zeros((side, low, LANES), jnp.float32)
        for band in range(bands):
            padded[band, :, 0:low, :] = edge
            padded[band, :, low + side :, :] = edge
        place = 0
        for ref in tile_refs:
            for row in range(ref.shape[0]):

                @pl.when(origin == place)
                def _load():
                    source_ref[0] = ref[row]

                place += 1
        for band in range(bands):
            for at in range(side):
                padded[band, at, low : low + side, :] = source_ref[
                    0, at, :, band * LANES : (band + 1) * LANES
                ].astype(jnp.float32)

        def convolve(band, carry):
            lanes = pl.ds(pl.multiple_of(band * LANES, LANES), LANES)
            bias = jnp.broadcast_to(vectors_ref[DEPTH_BIAS : DEPTH_BIAS + 1, lanes], (side, LANES))
            totals = [bias for _ in range(side)]
            for col in range(KS):
                start = low - reach + col
                weights = [
                    taps_ref[row * KS + col : row * KS + col + 1, lanes] for row in range(KS)
                ]
                for at in range(side):
                    line = padded[band, at, start : start + side, :]
                    for row in range(KS):
                        place = at - row + reach
                        if 0 <= place < side:
                            totals[place] = totals[place] + weights[row] * line
            for place in range(side):
                depth_out[band, place * side : (place + 1) * side, :] = totals[place]
            return carry

        lax.fori_loop(0, bands, convolve, 0)

        def vector(index, lanes):
            return vectors_ref[index : index + 1, lanes]

        for start in range(0, cells, PART):
            rows = slice(start, start + PART)
            pieces = [depth_out[band, rows, :] for band in range(bands)]
            mean = jnp.sum(sum(pieces), axis=1, keepdims=True) * (1.0 / channels)
            pieces = [piece - mean for piece in pieces]
            var = jnp.sum(sum(p * p for p in pieces), axis=1, keepdims=True) * (1.0 / channels)
            inv = lax.rsqrt(var + EPSILON)
            inv_ref[0, rows, :] = jnp.broadcast_to(inv, (PART, LANES))
            for band in range(bands):
                lanes = slice(band * LANES, (band + 1) * LANES)
                unit = pieces[band] * inv
                unit_ref[0, rows, lanes] = unit
                normed[rows, lanes] = (unit * vector(GAIN, lanes) + vector(SHIFT, lanes)).astype(
                    jnp.bfloat16
                )

        for index, begin in enumerate(range(0, expand_ref.shape[1], WIDTH)):
            cols = slice(begin, begin + WIDTH)
            buffer = index % pre.shape[0]
            pre[buffer] = mix(normed[...], expand_ref[:, cols])
            for start in range(0, cells, PART):
                rows = slice(start, start + PART)
                act, slope = gelu_and_slope(pre[buffer, rows, :] + vector(EXPAND_BIAS, cols))
                hidden_ref[0, rows, cols] = act.astype(jnp.bfloat16)
                slope_ref[0, rows, cols] = slope.astype(jnp.bfloat16)
        lanes = slice(0, channels)
        depth_rows = mix(hidden_ref[0], reduce_ref[...])
        for at in range(side):
            rows = slice(at * side, (at + 1) * side)
            branch = vector(SCALE, lanes) * (depth_rows[rows] + vector(REDUCE_BIAS, lanes))
            line = (source_ref[0, at].astype(jnp.float32) + branch).astype(jnp.bfloat16)
            section[rows, :] = line
            out_ref[0, at] = line
        for index, begin in enumerate(range(0, head_ref.shape[1], WIDTH)):
            cols = slice(begin, begin + WIDTH)
            buffer = index % pre.shape[0]
            pre[buffer] = mix(section[...], head_ref[:, cols])
            total = None
            for start in range(0, cells, PART):
                rows = slice(start, start + PART)
                act, slope = gelu_and_slope(pre[buffer, rows, :])
                head_slope_ref[0, rows, cols] = slope.astype(jnp.bfloat16)
                folded = act[0:8]
                for piece in range(8, PART, 8):
                    folded = folded + act[piece : piece + 8]
                total = folded if total is None else total + folded
            embed_ref[0, :, cols] = jnp.sum(total, axis=0, keepdims=True) * (1.0 / cells)


def forward_block(kind, items, table, tiles, consts, before):
    side, channels = tiles[0].shape[1], tiles[0].shape[3]
    taps, vectors, expand, reduce, head = consts
    cells, hid, embed = side * side, expand.shape[1], head.shape[1]
    bands = channels // LANES

    def per_slot(*shape):
        return pl.BlockSpec(
            (1,) + shape,
            lambda i, table: (table[class_field(kind, SLOT) + i],) + (0,) * len(shape),
        )

    outs = (
        ((side, side, channels), jnp.bfloat16),
        ((1, embed), jnp.float32),
        ((cells, channels), jnp.float32),
        ((cells, LANES), jnp.float32),
        ((cells, hid), jnp.bfloat16),
        ((cells, hid), jnp.bfloat16),
        ((cells, embed), jnp.bfloat16),
        ((side, side, channels), jnp.bfloat16),
    )
    tile_specs = [whole(tile.shape) for tile in tiles]
    if kind == 0:
        tile_specs[0] = pl.BlockSpec(
            (1, side, side, channels),
            lambda i, table: (table[class_field(kind, OWN) + i], 0, 0, 0),
        )
    first = 1 + len(tiles) + len(consts)
    return pl.pallas_call(
        functools.partial(forward_kernel, kind, len(tiles), len(before)),
        out_shape=tuple(jax.ShapeDtypeStruct((PROC + 1,) + shape, dtype) for shape, dtype in outs),
        grid_spec=pltpu.PrefetchScalarGridSpec(
            num_scalar_prefetch=1,
            grid=(items,),
            in_specs=tile_specs + [whole(const.shape) for const in consts] + [HBM] * len(before),
            out_specs=[per_slot(*shape) for shape, _ in outs],
            scratch_shapes=[
                pltpu.VMEM((bands, side, side + ROW_UNIT, LANES), jnp.float32),
                pltpu.VMEM((bands, cells, LANES), jnp.float32),
                pltpu.VMEM((cells, channels), jnp.bfloat16),
                pltpu.VMEM((3, cells, WIDTH), jnp.float32),
                pltpu.VMEM((cells, channels), jnp.bfloat16),
            ],
        ),
        input_output_aliases={first + index: index for index in range(len(before))},
        compiler_params=pltpu.CompilerParams(vmem_limit_bytes=VMEM_BYTES),
        cost_estimate=cost(6.0 * min(items, 2)),
        name="forward_block_" + str(kind),
    )(table, *tiles, *consts, *before)


def cost(micros):
    return pl.CostEstimate(flops=int(micros * 1e9), bytes_accessed=1024, transcendentals=0)


def slide_kernel(
    length,
    slides,
    pieces,
    table_ref,
    *refs,
):
    slide_items(length, slides, table_ref, refs[:pieces], *refs[pieces:])


def slide_items(
    length,
    slides,
    table_ref,
    piece_refs,
    pick_ref,
    codes_ref,
    weight_ref,
    cot_ref,
    taps_ref,
    matrix_ref,
    vectors_ref,
    feature_ref,
    grad_ref,
    rows,
    back,
    features,
    mixed,
    pre,
    grad_agg,
    embeds_ref,
):
    for index, ref in enumerate(piece_refs):
        size = ref.shape[0]
        embeds_ref[index * size : (index + 1) * size, :] = ref[...]
    border = ROW_UNIT
    edge = jnp.zeros((border, rows.shape[2]), jnp.float32)
    reach = KERNEL_TAPS // 2
    blocks = [slice(start, start + WIDTH) for start in range(0, rows.shape[2], WIDTH)]

    def dilate(ref, slide, direction, cols):
        total = ref[slide, border : border + length, cols]
        for tap in range(KERNEL_TAPS):
            start = border + direction * (tap - reach) * TILE_DILATION
            total = total + taps_ref[tap : tap + 1, cols] * ref[slide, start : start + length, cols]
        return total

    def one_slide(slide, carry):
        here = weight_ref[slide] > 0.0
        for ref in (rows, back):
            ref[slide, 0:border, :] = edge
            ref[slide, border + length :, :] = edge
        for cols in blocks:
            own = mix(pick_ref[slide], embeds_ref[:, cols]) + codes_ref[slide, :, cols]
            rows[slide, border : border + length, cols] = (
                jnp.where(here, own, 0.0).astype(jnp.bfloat16).astype(jnp.float32)
            )
            mixed[:, cols] = dilate(rows, slide, 1, cols).astype(jnp.bfloat16)
        for cols in blocks:
            pre[:, cols] = mix(mixed[...], matrix_ref[:, cols])
            total = None
            for start in range(0, length, PART):
                part = slice(start, start + PART)
                share = weight_ref[slide, part, :]
                act, slope = gelu_and_slope(
                    pre[part, cols] + vectors_ref[SLIDE_BIAS : SLIDE_BIAS + 1, cols]
                )
                grad_agg[part, cols] = (cot_ref[slide, :, cols] * share * slope).astype(jnp.bfloat16)
                piece = jnp.sum(act * share, axis=0, keepdims=True)
                total = piece if total is None else total + piece
            features[pl.ds(slide, 1), cols] = total
        for cols in blocks:
            back[slide, border : border + length, cols] = mix_cols(
                grad_agg[...], matrix_ref[cols, :]
            )
            total = jnp.where(here, dilate(back, slide, -1, cols), 0.0)
            rows[slide, border : border + length, cols] = total.astype(jnp.bfloat16).astype(
                jnp.float32
            )
        return carry

    lax.fori_loop(0, slides, one_slide, 0)
    feature_ref[...] = features[pl.ds(lax.axis_index(DP), 1), :]
    for proc in range(PROC):
        filled = table_ref[FILLED + proc]
        at = border + table_ref[PLACE + proc]
        row = rows[table_ref[SLIDE + proc], pl.ds(at, 1), :]
        grad_ref[proc] = jnp.where(filled != 0, row, 0.0)


def slide_grads(table, pieces, pick, codes, weight, cot, taps, matrix, vectors):
    slides, length, embed = codes.shape
    smem = pl.BlockSpec(memory_space=pltpu.SMEM)
    vmem = pl.BlockSpec(memory_space=pltpu.VMEM)
    padded = (slides, length + 2 * ROW_UNIT, embed)
    return pl.pallas_call(
        functools.partial(slide_kernel, length, slides, len(pieces)),
        out_shape=(
            jax.ShapeDtypeStruct((1, embed), jnp.float32),
            jax.ShapeDtypeStruct((PROC, 1, embed), jnp.float32),
        ),
        in_specs=[smem] + [vmem] * (7 + len(pieces)),
        out_specs=(vmem, vmem),
        scratch_shapes=[
            pltpu.VMEM(padded, jnp.float32),
            pltpu.VMEM(padded, jnp.float32),
            pltpu.VMEM((max(slides, 8), embed), jnp.float32),
            pltpu.VMEM((length, embed), jnp.bfloat16),
            pltpu.VMEM((length, embed), jnp.float32),
            pltpu.VMEM((length, embed), jnp.bfloat16),
            pltpu.VMEM((sum(piece.shape[0] for piece in pieces), embed), jnp.bfloat16),
        ],
        compiler_params=pltpu.CompilerParams(vmem_limit_bytes=VMEM_BYTES),
        cost_estimate=cost(6.0),
        name="slide_grads",
    )(table, *pieces, pick, codes, weight, cot, taps, matrix, vectors)


class Plan:
    def __init__(self, slides, members, channels, hid):
        self.devices = slides * members
        self.ys, self.g1, self.g2 = slides // 2, 4, members // 4
        self.cross = self.ys * self.g2
        self.channels = channels
        self.pieces = hid // channels
        self.expand_rows = channels // self.devices
        self.reduce_rows = hid // self.devices
        self.block_rows = -(-self.reduce_rows // ROW_UNIT) * ROW_UNIT
        self.share = KS * KS * channels // self.devices

    def blocks(self, rows):
        return (self.cross, self.g1, rows, self.channels)

    def spots(self):
        my_core, my_y = lax.axis_index("core"), lax.axis_index("y")
        my_z, my_x = lax.axis_index("g1"), lax.axis_index("g2")
        for device in range(self.devices):
            slide, member = divmod(device, self.g1 * self.g2)
            (y, core), (z, x) = divmod(slide, 2), divmod(member, self.g2)
            cross = lax.rem(y - my_y + self.ys, self.ys) * self.g2
            cross = cross + lax.rem(x - my_x + self.g2, self.g2)
            yield device, (my_core ^ core, cross, lax.rem(z - my_z + self.g1, self.g1))


def send_out(staged, sems, refs):
    copies = [
        pltpu.make_async_copy(staged.at[index], ref, sems.at[index]) for index, ref in enumerate(refs)
    ]
    for copy in copies:
        copy.start()
    for copy in copies:
        copy.wait()


def padded_block(block, rows):
    extra = rows - block.shape[0]
    if extra:
        block = jnp.concatenate([block, jnp.zeros((extra, block.shape[1]), block.dtype)], axis=0)
    return block.astype(jnp.bfloat16)


def reduce_kernel(
    plan,
    table_ref,
    grad_ref,
    hidden_ref,
    head_slope_ref,
    vectors_ref,
    head_ref,
    eye_ref,
    grad_mlp_ref,
    keep_ref,
    send_ref,
    hidden_all,
    grad_mlp_all,
    grad_head,
    staged,
    sems,
):
    step = pl.program_id(0)
    filled = table_ref[FILLED + step]
    cells, channels = grad_mlp_ref.shape[1:]
    rows_all = pl.ds(pl.multiple_of(step * cells, cells), cells)

    @pl.when(filled == 0)
    def _empty():
        hidden_all[rows_all, :] = jnp.zeros((cells, hidden_all.shape[1]), jnp.bfloat16)
        grad_mlp_all[:, rows_all] = jnp.zeros((channels, cells), jnp.bfloat16)
        grad_mlp_ref[...] = jnp.zeros(grad_mlp_ref.shape, jnp.bfloat16)

    @pl.when(filled != 0)
    def _work():
        for start in range(0, cells, PART):
            rows = slice(start, start + PART)
            grad_head[rows, :] = (
                (grad_ref[0] * (1.0 / cells)) * head_slope_ref[0, rows, :].astype(jnp.float32)
            ).astype(jnp.bfloat16)
        scale = vectors_ref[SCALE : SCALE + 1, 0:channels]
        grad_mlp = (scale * mix_cols(grad_head[...], head_ref[...])).astype(jnp.bfloat16)
        grad_mlp_ref[0] = grad_mlp
        grad_mlp_all[:, rows_all] = mix_cols(eye_ref[...], grad_mlp).astype(jnp.bfloat16)
        hidden_all[rows_all, :] = hidden_ref[0]

    @pl.when(step == pl.num_programs(0) - 1)
    def _finish():
        spots = dict(plan.spots())
        per_block = channels // plan.reduce_rows
        for index in range(plan.pieces):
            cols = slice(index * channels, (index + 1) * channels)
            total = mix(grad_mlp_all[...], hidden_all[:, cols]).astype(jnp.bfloat16)
            turned = mix_cols(eye_ref[...], total)
            for part in range(per_block):
                block = turned[part * plan.reduce_rows : (part + 1) * plan.reduce_rows]
                staged[spots[index * per_block + part]] = padded_block(block, plan.block_rows)
        send_out(staged, sems, (keep_ref, send_ref))


def expand_kernel(
    plan,
    table_ref,
    grad_mlp_ref,
    slope_ref,
    unit_ref,
    inv_ref,
    vectors_ref,
    expand_ref,
    reduce_ref,
    eye_ref,
    depth_back_ref,
    keep_ref,
    send_ref,
    grad_pre_all,
    normed_all,
    grad_norm,
    staged,
    sems,
):
    step = pl.program_id(0)
    filled = table_ref[FILLED + step]
    cells, channels = unit_ref.shape[1:]
    bands = channels // LANES
    rows_all = pl.ds(pl.multiple_of(step * cells, cells), cells)
    every = slice(0, channels)

    def vector(index, lanes):
        return vectors_ref[index : index + 1, lanes]

    @pl.when(filled == 0)
    def _empty():
        grad_pre_all[rows_all, :] = jnp.zeros((cells, grad_pre_all.shape[1]), jnp.bfloat16)
        normed_all[:, rows_all] = jnp.zeros((channels, cells), jnp.bfloat16)

    @pl.when(filled != 0)
    def _work():
        for begin in range(0, expand_ref.shape[1], WIDTH):
            cols = slice(begin, begin + WIDTH)
            grad_hidden = mix_cols(grad_mlp_ref[0], reduce_ref[cols, :])
            grad_pre_all[rows_all, cols] = (
                grad_hidden * slope_ref[0, :, cols].astype(jnp.float32)
            ).astype(jnp.bfloat16)
        grad_norm[...] = mix_cols(grad_pre_all[rows_all, :], expand_ref[...])
        normed = (unit_ref[0] * vector(GAIN, every) + vector(SHIFT, every)).astype(jnp.bfloat16)
        normed_all[:, rows_all] = mix_cols(eye_ref[...], normed).astype(jnp.bfloat16)
        for start in range(0, cells, PART):
            rows = slice(start, start + PART)
            scaled = grad_norm[rows, :] * vector(GAIN, every)
            unit = unit_ref[0, rows, :]
            mean = jnp.sum(scaled, axis=1, keepdims=True) * (1.0 / channels)
            mean_unit = jnp.sum(scaled * unit, axis=1, keepdims=True) * (1.0 / channels)
            inv = inv_ref[0, rows, 0:1]
            for band in range(bands):
                lanes = slice(band * LANES, (band + 1) * LANES)
                depth_back_ref[0, band, rows, :] = inv * (
                    scaled[:, lanes] - mean - unit[:, lanes] * mean_unit
                )

    @pl.when(step == pl.num_programs(0) - 1)
    def _finish():
        spots = dict(plan.spots())
        totals = []
        for quarter in range(plan.pieces):
            cols = slice(quarter * channels, (quarter + 1) * channels)
            totals.append(mix(normed_all[...], grad_pre_all[:, cols]))
        size = plan.expand_rows
        for device in range(plan.devices):
            rows = slice(device * size, (device + 1) * size)
            block = jnp.concatenate([total[rows] for total in totals], axis=0)
            staged[spots[device]] = padded_block(block, plan.block_rows)
        send_out(staged, sems, (keep_ref, send_ref))


def taps_kernel(
    plan,
    table_ref,
    source_ref,
    depth_back,
    keep_ref,
    send_ref,
    padded,
    tap_sums,
    tap_rows,
    staged,
    sems,
):
    step = pl.program_id(0)
    filled = table_ref[FILLED + step]
    side, channels = source_ref.shape[1], source_ref.shape[3]
    bands = channels // LANES
    low = ROW_UNIT // 2
    reach = KS // 2

    @pl.when(step == 0)
    def _start():
        tap_sums[...] = jnp.zeros(tap_sums.shape, jnp.float32)

    @pl.when(filled != 0)
    def _work():
        edge = jnp.zeros((side, low, LANES), jnp.float32)
        for band in range(bands):
            lanes = slice(band * LANES, (band + 1) * LANES)
            padded[band, :, 0:low, :] = edge
            padded[band, :, low + side :, :] = edge
            for at in range(side):
                padded[band, at, low : low + side, :] = source_ref[0, at, :, lanes].astype(
                    jnp.float32
                )

        def taps_of(band, carry):
            for col in range(KS):
                start = low - reach + col
                sums = [None] * KS
                grads = {}
                for at in range(side):
                    line = padded[band, at, start : start + side, :]
                    for row in range(KS):
                        place = at - row + reach
                        if 0 <= place < side:
                            if place not in grads:
                                grads[place] = depth_back[
                                    0, band, place * side : (place + 1) * side, :
                                ]
                            term = line * grads[place]
                            sums[row] = term if sums[row] is None else sums[row] + term
                for row in range(KS):
                    total = sums[row]
                    folded = total[0:8, :]
                    for piece in range(8, side, 8):
                        folded = folded + total[piece : piece + 8, :]
                    tap_sums[band, row * KS + col] = tap_sums[band, row * KS + col] + folded
            return carry

        lax.fori_loop(0, bands, taps_of, 0)

    @pl.when(step == pl.num_programs(0) - 1)
    def _finish():
        for band in range(bands):
            lanes = slice(band * LANES, (band + 1) * LANES)
            tap_rows[0 : KS * KS, lanes] = jnp.sum(tap_sums[band], axis=1)
            tap_rows[KS * KS :, lanes] = jnp.zeros((tap_rows.shape[0] - KS * KS, LANES), jnp.float32)
        for device, spot in plan.spots():
            start = device * plan.share // channels
            staged[spot] = padded_block(tap_rows[start : start + DEPTH_ROWS, :], ROW_UNIT)
        send_out(staged, sems, (keep_ref, send_ref))


def backward_call(plan, kernel, name, micros, rows, table, streams, consts, outs, scratch):
    def per_slot(shape):
        return pl.BlockSpec((1,) + tuple(shape), lambda i, table: (i,) + (0,) * len(shape))

    blocks = jax.ShapeDtypeStruct(plan.blocks(rows), jnp.bfloat16)
    return pl.pallas_call(
        functools.partial(kernel, plan),
        out_shape=tuple(jax.ShapeDtypeStruct((PROC,) + shape, kind) for shape, kind in outs)
        + (blocks, blocks),
        grid_spec=pltpu.PrefetchScalarGridSpec(
            num_scalar_prefetch=1,
            grid=(PROC,),
            in_specs=[per_slot(stream.shape[1:]) for stream in streams]
            + [whole(const.shape) for const in consts],
            out_specs=[per_slot(shape) for shape, _ in outs] + [HBM, HBM],
            scratch_shapes=scratch
            + [pltpu.VMEM((2,) + blocks.shape, jnp.bfloat16), pltpu.SemaphoreType.DMA((2,))],
        ),
        compiler_params=pltpu.CompilerParams(vmem_limit_bytes=VMEM_BYTES),
        cost_estimate=cost(micros),
        name=name,
    )(table, *streams, *consts)


def shifted(values, names, sizes, shift):
    count = math.prod(sizes)
    pairs = []
    for index in range(count):
        spot = []
        rest = index
        for size in reversed(sizes):
            spot.append(rest % size)
            rest //= size
        spot = spot[::-1]
        target = 0
        for at, step, size in zip(spot, shift, sizes):
            target = target * size + (at + step) % size
        pairs.append((index, target))
    return lax.ppermute(values, names, pairs)


def shifts(sizes):
    steps = [()]
    for size in sizes:
        steps = [step + (more,) for step in steps for more in range(size)]
    return steps


def gather_all(plan, values):
    pair = jnp.concatenate([values, shifted(values, ("core",), (2,), (1,))], axis=0)
    sizes = (plan.ys, plan.g2)
    column = jnp.concatenate(
        [pair] + [shifted(pair, ("y", "g2"), sizes, step) for step in shifts(sizes)[1:]], axis=0
    )
    return [column] + [shifted(column, ("g1",), (plan.g1,), (step,)) for step in range(1, plan.g1)]


def distance(plan, slide, member):
    my_core, my_y = lax.axis_index("core"), lax.axis_index("y")
    my_z, my_x = lax.axis_index("g1"), lax.axis_index("g2")
    y, core, z, x = slide // 2, slide % 2, member // plan.g2, member % plan.g2
    cross = (my_y - y) % plan.ys * plan.g2 + (my_x - x) % plan.g2
    return ((my_z - z) % plan.g1 * plan.cross + cross) * 2 + (core ^ my_core)


def add_all(parts, kind=jnp.bfloat16):
    total = parts[0].astype(jnp.float32)
    for part in parts[1:]:
        total = total + part.astype(jnp.float32)
    return total.astype(kind)


def other_core(values):
    return shifted(values, ("core",), (2,), (1,))


def sum_axis(kept, sent, name, size, kind=jnp.bfloat16):
    return [kept] + [shifted(part, (name,), (size,), (step + 1,)) for step, part in enumerate(sent)]


def position_code(positions):
    half_width = E // 2
    channel_ids = jnp.arange(E, dtype=jnp.int32) % half_width
    frequency = jnp.exp(
        (2 * (channel_ids // 2)).astype(jnp.float32) * (-math.log(10000.0) / half_width)
    )
    phase = jnp.where(channel_ids % 2 == 0, 0.0, 0.5 * math.pi)
    rows = jnp.where(
        jnp.arange(E, dtype=jnp.int32) < half_width, positions[0][..., None], positions[1][..., None]
    )
    return jnp.sin(rows.astype(jnp.float32) * frequency + phase)


def on_device(
    tile_maps,
    positions,
    counts,
    routing,
    depth_kernel,
    depth_bias,
    norm_gain,
    norm_shift,
    expand_weight,
    expand_bias,
    reduce_weight,
    reduce_bias,
    layer_scale,
    head_weight,
    slide_taps,
    slide_weight,
    slide_bias,
    cotangent,
):
    slides = lax.axis_size(DP)
    members = lax.axis_size(GROUP)
    my_device = lax.axis_index(ALL)
    slots, channels = tile_maps.shape[0], tile_maps.shape[3]
    devices, length, places = slides * members, slots * members, slots // slides
    plan = Plan(slides, members, channels, expand_weight.shape[1])

    packed, table = pack_tiles(routing, tile_maps, slides, places)
    from_core = other_core(packed[0])

    def from_other(buffers):
        return [
            lax.ppermute(buffer, DP, [(index, index ^ (other + 2)) for index in range(slides)])
            for other, buffer in enumerate(buffers)
        ]

    arrived = []
    for rank in range(places):
        buffers = packed[1 + rank * (slides - 2) : 1 + (rank + 1) * (slides - 2)]
        if arrived:
            held = lax.optimization_barrier((tuple(buffers), tuple(arrived[-1])))
            buffers, arrived[-1] = held[0], list(held[1])
        arrived.append(from_other(buffers))

    vectors = jnp.stack(
        [
            jnp.pad(vector, (0, expand_bias.shape[0] - vector.shape[0]))
            for vector in (
                norm_gain,
                norm_shift,
                layer_scale,
                reduce_bias,
                depth_bias,
                expand_bias,
                slide_bias,
                slide_bias,
            )
        ]
    )
    consts = (depth_kernel, vectors, expand_weight, reduce_weight, head_weight)
    saved = forward_block(0, PROC, table, (tile_maps, from_core), consts, ())
    for rank in range(places):
        items = min(PROC, slides - 2)
        saved = forward_block(1 + rank, items, table, arrived[rank], consts, saved)
    section, tile_embed, unit, inv, hidden, slope, head_slope, source = saved
    filled = table[FILLED : FILLED + PROC] != 0
    tile_embed = jnp.where(filled[:, None], tile_embed[:PROC, 0], 0.0).astype(jnp.bfloat16)
    embeds = gather_all(plan, tile_embed)
    tile_out = jnp.where(filled[:, None, None, None], section[:PROC], jnp.zeros((), jnp.bfloat16))

    packed_last, routing, cotangent, positions, counts = lax.optimization_barrier(
        (table, routing, cotangent, positions, counts)
    )
    extras = jnp.concatenate(
        [
            cotangent[0],
            routing.reshape(-1).astype(jnp.float32),
            jnp.zeros((960 - E - slides * slots,), jnp.float32),
            positions.reshape(-1).astype(jnp.float32),
            jnp.zeros((1023 - 960 - 2 * slots,), jnp.float32),
            counts.astype(jnp.float32),
        ]
    )
    extras = jnp.concatenate(gather_all(plan, extras[None, :]), axis=0)
    ids = jnp.arange(devices, dtype=jnp.int32)
    spots = distance(plan, ids // members, ids % members)
    extras = jnp.take(extras, spots, axis=0)
    route_all = extras[:, E : E + slides * slots].astype(jnp.int32)
    route_all = route_all.reshape(slides, members, slides, slots)[0]
    pos_all = extras[:, 960 : 960 + 2 * slots].reshape(slides, members, 2, slots)
    pos_all = pos_all.transpose(2, 0, 3, 1).reshape(2, slides, length)
    counts_all = extras[:, 1023].reshape(slides, members)[:, 0]
    cot_all = extras[:, :E].reshape(slides, members, 1, E)[:, 0]
    codes = position_code(pos_all)
    member_ids = jnp.arange(members, dtype=jnp.int32)[:, None, None]
    target = jnp.where(
        route_all >= 0,
        distance(plan, route_all // PROC, member_ids) * PROC + route_all % PROC,
        -1,
    )
    target = target.transpose(1, 2, 0).reshape(slides, length, 1)
    pick = (target == jnp.arange(devices * PROC, dtype=jnp.int32)).astype(jnp.bfloat16)
    steps = jnp.arange(length, dtype=jnp.int32)[None, :, None].astype(jnp.float32)
    weight = jnp.where(steps < counts_all[:, None, None], 1.0 / counts_all[:, None, None], 0.0)

    feature, embed_grad = slide_grads(
        table, embeds, pick, codes, weight, cot_all, slide_taps, slide_weight, vectors
    )

    side, hid = tile_maps.shape[1], expand_weight.shape[1]
    cells, bands = side * side, channels // LANES
    eye = jnp.asarray(np.eye(channels, dtype=np.float32), jnp.bfloat16)
    grad_mlp, reduce_kept, reduce_sent = backward_call(
        plan,
        reduce_kernel,
        "reduce_grads",
        5.0,
        plan.block_rows,
        table,
        (embed_grad, hidden, head_slope),
        (vectors, head_weight, eye),
        (((cells, channels), jnp.bfloat16),),
        [
            pltpu.VMEM((PROC * cells, hid), jnp.bfloat16),
            pltpu.VMEM((channels, PROC * cells), jnp.bfloat16),
            pltpu.VMEM((cells, E), jnp.bfloat16),
        ],
    )
    reduce_came = other_core(reduce_sent)
    depth_back, expand_kept, expand_sent = backward_call(
        plan,
        expand_kernel,
        "expand_grads",
        8.0,
        plan.block_rows,
        table,
        (grad_mlp, slope, unit, inv),
        (vectors, expand_weight, reduce_weight, eye),
        (((bands, cells, LANES), jnp.float32),),
        [
            pltpu.VMEM((PROC * cells, hid), jnp.bfloat16),
            pltpu.VMEM((channels, PROC * cells), jnp.bfloat16),
            pltpu.VMEM((cells, channels), jnp.float32),
        ],
    )
    expand_came = other_core(expand_sent)

    def column(kept, came, wanted):
        grid = [
            part.reshape((plan.ys, plan.g2) + part.shape[1:]) for part in (kept, came)
        ]
        return add_all([wanted(part) for part in grid])

    reduce_out = [
        column(reduce_kept, reduce_came, lambda part: part[:, step]) for step in range(1, plan.g2)
    ]
    reduce_stay = column(reduce_kept, reduce_came, lambda part: part[:, 0])
    depth_back, reduce_out = lax.optimization_barrier((depth_back, reduce_out))
    reduce_parts = sum_axis(reduce_stay, reduce_out, "g2", plan.g2)
    depth_kept, depth_sent = backward_call(
        plan,
        taps_kernel,
        "tap_grads",
        8.0,
        ROW_UNIT,
        table,
        (source, depth_back),
        (),
        (),
        [
            pltpu.VMEM((bands, side, side + ROW_UNIT, LANES), jnp.float32),
            pltpu.VMEM((bands, KS * KS, 8, LANES), jnp.float32),
            pltpu.VMEM((KS * KS + 7, channels), jnp.float32),
        ],
    )
    depth_came = other_core(depth_sent)
    expand_out = [
        column(expand_kept, expand_came, lambda part: part[step]) for step in range(1, plan.ys)
    ]
    expand_stay = column(expand_kept, expand_came, lambda part: part[0])
    expand_parts = sum_axis(expand_stay, expand_out, "y", plan.ys)

    def finish(parts, name, size):
        out = [add_all([part[step] for part in parts]) for step in range(1, size)]
        stay = add_all([part[0] for part in parts])
        parts = sum_axis(stay, out, name, size)
        out = [add_all([part[step] for part in parts]) for step in range(1, plan.g1)]
        stay = add_all([part[0] for part in parts])
        return add_all(sum_axis(stay, out, "g1", plan.g1), jnp.float32)

    reduce_total = finish(reduce_parts, "y", plan.ys)
    expand_total = finish(expand_parts, "g2", plan.g2)
    sizes = (plan.ys, plan.g2)
    depth_all = add_all([depth_kept, depth_came])
    depth_parts = [depth_all[0]] + [
        shifted(depth_all[index], ("y", "g2"), sizes, step)
        for index, step in enumerate(shifts(sizes))
        if index
    ]
    depth_all = add_all(depth_parts)
    depth_total = add_all(
        sum_axis(depth_all[0], [depth_all[step] for step in range(1, plan.g1)], "g1", plan.g1),
        jnp.float32,
    )

    expand_share = expand_total[: plan.pieces * plan.expand_rows]
    expand_share = expand_share.reshape(plan.pieces, plan.expand_rows, channels).transpose(1, 0, 2)
    reduce_share = reduce_total[: plan.reduce_rows]
    depth_share = lax.dynamic_slice(
        depth_total[:DEPTH_ROWS].reshape(-1), (my_device * plan.share % channels,), (plan.share,)
    )
    return (tile_out, feature, expand_share.reshape(-1), reduce_share.reshape(-1), depth_share)


def solution(mesh):
    slides, members = mesh.shape["dp"], mesh.shape["group"]
    fine = Mesh(mesh.devices.reshape(slides // 2, 2, 4, members // 4), ALL)
    return jax.shard_map(
        on_device,
        mesh=fine,
        in_specs=(
            P(ALL, None, None, None),
            P(None, ALL),
            P(DP),
            P(None, GROUP, None),
        )
        + (P(),) * 13
        + (P(DP, None),),
        out_specs=(
            P(ALL, None, None, None),
            P(DP, None),
            P(ALL),
            P(ALL),
            P(ALL),
        ),
        check_vma=False,
    )
```

```python
import functools
import math

import jax
import jax.numpy as jnp
import numpy as np
from jax import lax
from jax.experimental import pallas as pl
from jax.experimental.pallas import tpu as pltpu
from jax.sharding import Mesh, PartitionSpec as P

E = 768
KS = 7
KERNEL_TAPS = 7
TILE_DILATION = 3
PROC = 4
DP = ("y", "core")
GROUP = ("g1", "g2")
ALL = DP + GROUP

EPSILON = 1e-06
HALF_ROOT = 0.7071067811865476
INV_ROOT_TAU = 0.3989422804014327
LANES = 128
ROW_UNIT = 16
DEPTH_ROWS = 4
MIB = 1024 * 1024
PART = 32
WIDTH = 256
GAIN, SHIFT, SCALE, REDUCE_BIAS, DEPTH_BIAS, EXPAND_BIAS, SLIDE_BIAS = range(7)
ERFC_P = 0.3275911
ERFC_A = (0.254829592, -0.284496736, 1.421413741, -1.453152027, 1.061405429)

HBM = pl.BlockSpec(memory_space=pl.ANY)


def whole(shape):
    return pl.BlockSpec(shape, lambda *_: (0,) * len(shape), pipeline_mode=pl.Buffered(1))


def gelu_and_slope(values):
    size = jnp.abs(values)
    divisor = 1.0 + (ERFC_P * HALF_ROOT) * size
    guess = pl.reciprocal(divisor, approx=True)
    t = guess * (2.0 - divisor * guess)
    bell = jnp.exp(-0.5 * values * values)
    poly = 0.5 * ERFC_A[4]
    for coefficient in ERFC_A[3::-1]:
        poly = poly * t + 0.5 * coefficient
    tail = poly * t * bell
    phi = jnp.where(values >= 0.0, 1.0 - tail, tail)
    return values * phi, phi + values * (INV_ROOT_TAU * bell)


def mix_cols(left_side, right_side):
    return lax.dot_general(
        left_side, right_side, (((1,), (1,)), ((), ())), preferred_element_type=jnp.float32
    )


def mix(left_side, right_side):
    return jnp.dot(left_side, right_side, preferred_element_type=jnp.float32)


FILLED, SLIDE, PLACE, CLASSES = 0, PROC, 2 * PROC, 3 * PROC
CLASS_SIZE = 1 + 3 * PROC


def class_field(kind, field, item=0):
    return CLASSES + kind * CLASS_SIZE + (1 + field * PROC + item if field >= 0 else 0)


SLOT, FROM, OWN = range(3)


def pack_kernel(slides, slots, places, route_ref, tiles_ref, *refs):
    send_refs, (table_ref, count_ref, slot_ref, sems) = refs[:-4], refs[-4:]
    my_slide = lax.axis_index(DP)
    members = lax.axis_size(GROUP)
    my_member = lax.axis_index(GROUP)

    targets = [(0, rank, rank) for rank in range(places)]
    for rank in range(places):
        for other in range(2, slides):
            targets.append((1 + rank * (slides - 2) + other - 2, 0, other * places + rank))
    targets[:places] = [(0, rank, places + rank) for rank in range(places)]

    def copy_of(index, slot):
        buffer, row, _ = targets[index]
        return pltpu.make_async_copy(tiles_ref.at[slot], send_refs[buffer].at[row], sems.at[index])

    for index in range(slides):
        count_ref[index] = 0
    for index in range(slides * places):
        slot_ref[index] = -1

    def place_slot(slot, carry):
        entry = route_ref[my_slide, 0, slot]

        @pl.when(entry >= 0)
        def _send():
            other = lax.div(entry, PROC) ^ my_slide
            rank = count_ref[other]
            count_ref[other] = rank + 1
            slot_ref[other * places + rank] = slot

        return carry

    lax.fori_loop(0, slots, place_slot, 0)
    for index, (_, _, key) in enumerate(targets):
        slot = slot_ref[key]

        @pl.when(slot >= 0)
        def _start():
            copy_of(index, slot).start()

    kinds = 1 + places
    for field in range(CLASSES + kinds * CLASS_SIZE):
        table_ref[field] = 0
    for kind in range(kinds):
        for item in range(PROC):
            table_ref[class_field(kind, SLOT, item)] = PROC
    for other in range(slides):
        source = my_slide ^ other
        count_ref[0] = 0

        def take(slot, carry):
            entry = route_ref[source, 0, slot]
            proc = entry - my_slide * PROC

            @pl.when((proc >= 0) & (proc < PROC))
            def _take():
                rank = count_ref[0]
                count_ref[0] = rank + 1
                table_ref[FILLED + proc] = 1
                table_ref[SLIDE + proc] = source
                table_ref[PLACE + proc] = slot * members + my_member
                kind = 0 if other < 2 else 1 + rank
                base = CLASSES + kind * CLASS_SIZE
                item = table_ref[base]
                table_ref[base] = item + 1
                table_ref[base + 1 + SLOT * PROC + item] = proc
                if other == 0:
                    table_ref[base + 1 + FROM * PROC + item] = 0
                    table_ref[base + 1 + OWN * PROC + item] = slot
                else:
                    table_ref[base + 1 + FROM * PROC + item] = 1 + rank if other == 1 else other - 2

            return carry

        lax.fori_loop(0, slots, take, 0)
        if other == 0:
            own = table_ref[class_field(0, -1)]
            for item in range(1, PROC):

                @pl.when(item >= own)
                def _hold():
                    table_ref[class_field(0, OWN, item)] = table_ref[class_field(0, OWN, item - 1)]

    for kind in range(kinds):
        items = table_ref[class_field(kind, -1)]
        for item in range(1, PROC):

            @pl.when(item >= items)
            def _hold_slot():
                table_ref[class_field(kind, SLOT, item)] = table_ref[class_field(kind, SLOT, item - 1)]

    for index, (_, _, key) in enumerate(targets):

        @pl.when(slot_ref[key] >= 0)
        def _wait():
            copy_of(index, 0).wait()


def pack_tiles(routing, tile_maps, slides, places):
    slots = tile_maps.shape[0]
    smem = pl.BlockSpec(memory_space=pltpu.SMEM)
    vmem = pl.BlockSpec(memory_space=pltpu.VMEM)
    buffers = 1 + places * (slides - 2)
    shapes = [places] + [1] * (buffers - 1)
    outs = pl.pallas_call(
        functools.partial(pack_kernel, slides, slots, places),
        out_shape=tuple(
            jax.ShapeDtypeStruct((size,) + tile_maps.shape[1:], tile_maps.dtype) for size in shapes
        )
        + (jax.ShapeDtypeStruct((CLASSES + (1 + places) * CLASS_SIZE,), jnp.int32),),
        in_specs=[smem, HBM],
        out_specs=(vmem,) * buffers + (smem,),
        scratch_shapes=[
            pltpu.SMEM((slides,), jnp.int32),
            pltpu.SMEM((slides * places,), jnp.int32),
            pltpu.SemaphoreType.DMA((slides * places,)),
        ],
        compiler_params=pltpu.CompilerParams(vmem_limit_bytes=8 * MIB),
        name="pack_tiles",
    )(routing, tile_maps)
    return outs[:-1], outs[-1]


def forward_kernel(kind, inputs, aliased, table_ref, *refs):
    forward_items(kind, table_ref, refs[:inputs], *refs[inputs : inputs + 5], *refs[inputs + 5 + aliased :])


def forward_items(
    kind,
    table_ref,
    tile_refs,
    taps_ref,
    vectors_ref,
    expand_ref,
    reduce_ref,
    head_ref,
    out_ref,
    embed_ref,
    unit_ref,
    inv_ref,
    hidden_ref,
    slope_ref,
    head_slope_ref,
    source_ref,
    padded,
    depth_out,
    normed,
    pre,
    section,
):
    item = pl.program_id(0)
    side = out_ref.shape[1]
    channels = out_ref.shape[3]
    cells = side * side
    bands = channels // LANES
    low = ROW_UNIT // 2
    reach = KS // 2

    @pl.when(item < table_ref[class_field(kind, -1)])
    def _work():
        origin = table_ref[class_field(kind, FROM) + item]
        edge = jnp.zeros((side, low, LANES), jnp.float32)
        for band in range(bands):
            padded[band, :, 0:low, :] = edge
            padded[band, :, low + side :, :] = edge
        place = 0
        for ref in tile_refs:
            for row in range(ref.shape[0]):

                @pl.when(origin == place)
                def _load():
                    source_ref[0] = ref[row]

                place += 1
        for band in range(bands):
            for at in range(side):
                padded[band, at, low : low + side, :] = source_ref[
                    0, at, :, band * LANES : (band + 1) * LANES
                ].astype(jnp.float32)

        def convolve(band, carry):
            lanes = pl.ds(pl.multiple_of(band * LANES, LANES), LANES)
            bias = jnp.broadcast_to(vectors_ref[DEPTH_BIAS : DEPTH_BIAS + 1, lanes], (side, LANES))
            totals = [bias for _ in range(side)]
            for col in range(KS):
                start = low - reach + col
                weights = [
                    taps_ref[row * KS + col : row * KS + col + 1, lanes] for row in range(KS)
                ]
                for at in range(side):
                    line = padded[band, at, start : start + side, :]
                    for row in range(KS):
                        place = at - row + reach
                        if 0 <= place < side:
                            totals[place] = totals[place] + weights[row] * line
            for place in range(side):
                depth_out[band, place * side : (place + 1) * side, :] = totals[place]
            return carry

        lax.fori_loop(0, bands, convolve, 0)

        def vector(index, lanes):
            return vectors_ref[index : index + 1, lanes]

        for start in range(0, cells, PART):
            rows = slice(start, start + PART)
            pieces = [depth_out[band, rows, :] for band in range(bands)]
            mean = jnp.sum(sum(pieces), axis=1, keepdims=True) * (1.0 / channels)
            pieces = [piece - mean for piece in pieces]
            var = jnp.sum(sum(p * p for p in pieces), axis=1, keepdims=True) * (1.0 / channels)
            inv = lax.rsqrt(var + EPSILON)
            inv_ref[0, rows, :] = jnp.broadcast_to(inv, (PART, LANES))
            for band in range(bands):
                lanes = slice(band * LANES, (band + 1) * LANES)
                unit = pieces[band] * inv
                unit_ref[0, rows, lanes] = unit
                normed[rows, lanes] = (unit * vector(GAIN, lanes) + vector(SHIFT, lanes)).astype(
                    jnp.bfloat16
                )

        for index, begin in enumerate(range(0, expand_ref.shape[1], WIDTH)):
            cols = slice(begin, begin + WIDTH)
            buffer = index % pre.shape[0]
            pre[buffer] = mix(normed[...], expand_ref[:, cols])
            for start in range(0, cells, PART):
                rows = slice(start, start + PART)
                act, slope = gelu_and_slope(pre[buffer, rows, :] + vector(EXPAND_BIAS, cols))
                hidden_ref[0, rows, cols] = act.astype(jnp.bfloat16)
                slope_ref[0, rows, cols] = slope.astype(jnp.bfloat16)
        lanes = slice(0, channels)
        depth_rows = mix(hidden_ref[0], reduce_ref[...])
        for at in range(side):
            rows = slice(at * side, (at + 1) * side)
            branch = vector(SCALE, lanes) * (depth_rows[rows] + vector(REDUCE_BIAS, lanes))
            line = (source_ref[0, at].astype(jnp.float32) + branch).astype(jnp.bfloat16)
            section[rows, :] = line
            out_ref[0, at] = line
        for index, begin in enumerate(range(0, head_ref.shape[1], WIDTH)):
            cols = slice(begin, begin + WIDTH)
            buffer = index % pre.shape[0]
            pre[buffer] = mix(section[...], head_ref[:, cols])
            total = None
            for start in range(0, cells, PART):
                rows = slice(start, start + PART)
                act, slope = gelu_and_slope(pre[buffer, rows, :])
                head_slope_ref[0, rows, cols] = slope.astype(jnp.bfloat16)
                folded = act[0:8]
                for piece in range(8, PART, 8):
                    folded = folded + act[piece : piece + 8]
                total = folded if total is None else total + folded
            embed_ref[0, :, cols] = jnp.sum(total, axis=0, keepdims=True) * (1.0 / cells)


def forward_block(kind, items, table, tiles, consts, before):
    side, channels = tiles[0].shape[1], tiles[0].shape[3]
    taps, vectors, expand, reduce, head = consts
    cells, hid, embed = side * side, expand.shape[1], head.shape[1]
    bands = channels // LANES

    def per_slot(*shape):
        return pl.BlockSpec(
            (1,) + shape,
            lambda i, table: (table[class_field(kind, SLOT) + i],) + (0,) * len(shape),
        )

    outs = (
        ((side, side, channels), jnp.bfloat16),
        ((1, embed), jnp.float32),
        ((cells, channels), jnp.float32),
        ((cells, LANES), jnp.float32),
        ((cells, hid), jnp.bfloat16),
        ((cells, hid), jnp.bfloat16),
        ((cells, embed), jnp.bfloat16),
        ((side, side, channels), jnp.bfloat16),
    )
    tile_specs = [whole(tile.shape) for tile in tiles]
    if kind == 0:
        tile_specs[0] = pl.BlockSpec(
            (1, side, side, channels),
            lambda i, table: (table[class_field(kind, OWN) + i], 0, 0, 0),
        )
    first = 1 + len(tiles) + len(consts)
    return pl.pallas_call(
        functools.partial(forward_kernel, kind, len(tiles), len(before)),
        out_shape=tuple(jax.ShapeDtypeStruct((PROC + 1,) + shape, dtype) for shape, dtype in outs),
        grid_spec=pltpu.PrefetchScalarGridSpec(
            num_scalar_prefetch=1,
            grid=(items,),
            in_specs=tile_specs + [whole(const.shape) for const in consts] + [HBM] * len(before),
            out_specs=[per_slot(*shape) for shape, _ in outs],
            scratch_shapes=[
                pltpu.VMEM((bands, side, side + ROW_UNIT, LANES), jnp.float32),
                pltpu.VMEM((bands, cells, LANES), jnp.float32),
                pltpu.VMEM((cells, channels), jnp.bfloat16),
                pltpu.VMEM((3, cells, WIDTH), jnp.float32),
                pltpu.VMEM((cells, channels), jnp.bfloat16),
            ],
        ),
        input_output_aliases={first + index: index for index in range(len(before))},
        compiler_params=pltpu.CompilerParams(vmem_limit_bytes=20 * MIB),
        cost_estimate=cost(6.0 * min(items, 2)),
        name="forward_block_" + str(kind),
    )(table, *tiles, *consts, *before)


def cost(micros):
    return pl.CostEstimate(flops=int(micros * 1e9), bytes_accessed=1024, transcendentals=0)


def slide_kernel(
    length,
    slides,
    pieces,
    table_ref,
    *refs,
):
    slide_items(length, slides, table_ref, refs[:pieces], *refs[pieces:])


def slide_items(
    length,
    slides,
    table_ref,
    piece_refs,
    pick_ref,
    codes_ref,
    weight_ref,
    cot_ref,
    taps_ref,
    matrix_ref,
    vectors_ref,
    feature_ref,
    grad_ref,
    rows,
    back,
    features,
    mixed,
    pre,
    grad_agg,
    embeds_ref,
):
    for index, ref in enumerate(piece_refs):
        size = ref.shape[0]
        embeds_ref[index * size : (index + 1) * size, :] = ref[...]
    border = ROW_UNIT
    edge = jnp.zeros((border, rows.shape[2]), jnp.float32)
    reach = KERNEL_TAPS // 2
    blocks = [slice(start, start + WIDTH) for start in range(0, rows.shape[2], WIDTH)]

    def dilate(ref, slide, direction, cols):
        total = ref[slide, border : border + length, cols]
        for tap in range(KERNEL_TAPS):
            start = border + direction * (tap - reach) * TILE_DILATION
            total = total + taps_ref[tap : tap + 1, cols] * ref[slide, start : start + length, cols]
        return total

    def one_slide(slide, carry):
        here = weight_ref[slide] > 0.0
        for ref in (rows, back):
            ref[slide, 0:border, :] = edge
            ref[slide, border + length :, :] = edge
        for cols in blocks:
            own = mix(pick_ref[slide], embeds_ref[:, cols]) + codes_ref[slide, :, cols]
            rows[slide, border : border + length, cols] = (
                jnp.where(here, own, 0.0).astype(jnp.bfloat16).astype(jnp.float32)
            )
            mixed[:, cols] = dilate(rows, slide, 1, cols).astype(jnp.bfloat16)
        for cols in blocks:
            pre[:, cols] = mix(mixed[...], matrix_ref[:, cols])
            total = None
            for start in range(0, length, PART):
                part = slice(start, start + PART)
                share = weight_ref[slide, part, :]
                act, slope = gelu_and_slope(
                    pre[part, cols] + vectors_ref[SLIDE_BIAS : SLIDE_BIAS + 1, cols]
                )
                grad_agg[part, cols] = (cot_ref[slide, :, cols] * share * slope).astype(jnp.bfloat16)
                piece = jnp.sum(act * share, axis=0, keepdims=True)
                total = piece if total is None else total + piece
            features[pl.ds(slide, 1), cols] = total
        for cols in blocks:
            back[slide, border : border + length, cols] = mix_cols(
                grad_agg[...], matrix_ref[cols, :]
            )
            total = jnp.where(here, dilate(back, slide, -1, cols), 0.0)
            rows[slide, border : border + length, cols] = total.astype(jnp.bfloat16).astype(
                jnp.float32
            )
        return carry

    lax.fori_loop(0, slides, one_slide, 0)
    feature_ref[...] = features[pl.ds(lax.axis_index(DP), 1), :]
    for proc in range(PROC):
        filled = table_ref[FILLED + proc]
        at = border + table_ref[PLACE + proc]
        row = rows[table_ref[SLIDE + proc], pl.ds(at, 1), :]
        grad_ref[proc] = jnp.where(filled != 0, row, 0.0)


def slide_grads(table, pieces, pick, codes, weight, cot, taps, matrix, vectors):
    slides, length, embed = codes.shape
    smem = pl.BlockSpec(memory_space=pltpu.SMEM)
    vmem = pl.BlockSpec(memory_space=pltpu.VMEM)
    padded = (slides, length + 2 * ROW_UNIT, embed)
    return pl.pallas_call(
        functools.partial(slide_kernel, length, slides, len(pieces)),
        out_shape=(
            jax.ShapeDtypeStruct((1, embed), jnp.float32),
            jax.ShapeDtypeStruct((PROC, 1, embed), jnp.float32),
        ),
        in_specs=[smem] + [vmem] * (7 + len(pieces)),
        out_specs=(vmem, vmem),
        scratch_shapes=[
            pltpu.VMEM(padded, jnp.float32),
            pltpu.VMEM(padded, jnp.float32),
            pltpu.VMEM((max(slides, 8), embed), jnp.float32),
            pltpu.VMEM((length, embed), jnp.bfloat16),
            pltpu.VMEM((length, embed), jnp.float32),
            pltpu.VMEM((length, embed), jnp.bfloat16),
            pltpu.VMEM((sum(piece.shape[0] for piece in pieces), embed), jnp.bfloat16),
        ],
        compiler_params=pltpu.CompilerParams(vmem_limit_bytes=16 * MIB),
        cost_estimate=cost(6.0),
        name="slide_grads",
    )(table, *pieces, pick, codes, weight, cot, taps, matrix, vectors)


class Plan:
    def __init__(self, slides, members, channels, hid):
        self.devices = slides * members
        self.ys, self.g1, self.g2 = slides // 2, 4, members // 4
        self.cross = self.ys * self.g2
        self.channels = channels
        self.pieces = hid // channels
        self.expand_rows = channels // self.devices
        self.reduce_rows = hid // self.devices
        self.block_rows = -(-self.reduce_rows // ROW_UNIT) * ROW_UNIT
        self.share = KS * KS * channels // self.devices

    def blocks(self, rows):
        return (self.cross, self.g1, rows, self.channels)

    def spots(self):
        my_core, my_y = lax.axis_index("core"), lax.axis_index("y")
        my_z, my_x = lax.axis_index("g1"), lax.axis_index("g2")
        for device in range(self.devices):
            slide, member = divmod(device, self.g1 * self.g2)
            (y, core), (z, x) = divmod(slide, 2), divmod(member, self.g2)
            cross = lax.rem(y - my_y + self.ys, self.ys) * self.g2
            cross = cross + lax.rem(x - my_x + self.g2, self.g2)
            yield device, (my_core ^ core, cross, lax.rem(z - my_z + self.g1, self.g1))


def send_out(staged, sems, refs):
    copies = [
        pltpu.make_async_copy(staged.at[index], ref, sems.at[index]) for index, ref in enumerate(refs)
    ]
    for copy in copies:
        copy.start()
    for copy in copies:
        copy.wait()


def padded_block(block, rows):
    extra = rows - block.shape[0]
    if extra:
        block = jnp.concatenate([block, jnp.zeros((extra, block.shape[1]), block.dtype)], axis=0)
    return block.astype(jnp.bfloat16)


def weights_kernel(
    plan,
    table_ref,
    grad_ref,
    hidden_ref,
    head_slope_ref,
    slope_ref,
    unit_ref,
    inv_ref,
    vectors_ref,
    head_ref,
    expand_ref,
    reduce_ref,
    eye_ref,
    depth_back_ref,
    keep_ref,
    send_ref,
    hidden_all,
    grad_mlp_all,
    grad_pre_all,
    normed_all,
    grad_head,
    grad_norm,
    staged,
    sems,
):
    step = pl.program_id(0)
    filled = table_ref[FILLED + step]
    cells, channels = unit_ref.shape[1:]
    bands = channels // LANES
    rows_all = pl.ds(pl.multiple_of(step * cells, cells), cells)
    every = slice(0, channels)

    def vector(index, lanes):
        return vectors_ref[index : index + 1, lanes]

    @pl.when(filled == 0)
    def _empty():
        for ref in (hidden_all, grad_pre_all):
            ref[rows_all, :] = jnp.zeros((cells, ref.shape[1]), jnp.bfloat16)
        for ref in (grad_mlp_all, normed_all):
            ref[:, rows_all] = jnp.zeros((channels, cells), jnp.bfloat16)

    @pl.when(filled != 0)
    def _work():
        for start in range(0, cells, PART):
            rows = slice(start, start + PART)
            grad_head[rows, :] = (
                (grad_ref[0] * (1.0 / cells)) * head_slope_ref[0, rows, :].astype(jnp.float32)
            ).astype(jnp.bfloat16)
        grad_mlp = (vector(SCALE, every) * mix_cols(grad_head[...], head_ref[...])).astype(
            jnp.bfloat16
        )
        grad_mlp_all[:, rows_all] = mix_cols(eye_ref[...], grad_mlp).astype(jnp.bfloat16)
        hidden_all[rows_all, :] = hidden_ref[0]
        for begin in range(0, expand_ref.shape[1], WIDTH):
            cols = slice(begin, begin + WIDTH)
            grad_hidden = mix_cols(grad_mlp, reduce_ref[cols, :])
            grad_pre_all[rows_all, cols] = (
                grad_hidden * slope_ref[0, :, cols].astype(jnp.float32)
            ).astype(jnp.bfloat16)
        grad_norm[...] = mix_cols(grad_pre_all[rows_all, :], expand_ref[...])
        normed = (unit_ref[0] * vector(GAIN, every) + vector(SHIFT, every)).astype(jnp.bfloat16)
        normed_all[:, rows_all] = mix_cols(eye_ref[...], normed).astype(jnp.bfloat16)
        for start in range(0, cells, PART):
            rows = slice(start, start + PART)
            scaled = grad_norm[rows, :] * vector(GAIN, every)
            unit = unit_ref[0, rows, :]
            mean = jnp.sum(scaled, axis=1, keepdims=True) * (1.0 / channels)
            mean_unit = jnp.sum(scaled * unit, axis=1, keepdims=True) * (1.0 / channels)
            inv = inv_ref[0, rows, 0:1]
            for band in range(bands):
                lanes = slice(band * LANES, (band + 1) * LANES)
                depth_back_ref[0, band, rows, :] = inv * (
                    scaled[:, lanes] - mean - unit[:, lanes] * mean_unit
                )

    @pl.when(step == pl.num_programs(0) - 1)
    def _finish():
        spots = dict(plan.spots())
        per_block = channels // plan.reduce_rows
        tall = plan.block_rows
        for index in range(plan.pieces):
            cols = slice(index * channels, (index + 1) * channels)
            total = mix(grad_mlp_all[...], hidden_all[:, cols]).astype(jnp.bfloat16)
            turned = mix_cols(eye_ref[...], total)
            for part in range(per_block):
                block = turned[part * plan.reduce_rows : (part + 1) * plan.reduce_rows]
                core, cross, z = spots[index * per_block + part]
                staged[core, 0, cross, z] = padded_block(block, tall)
        totals = []
        for quarter in range(plan.pieces):
            cols = slice(quarter * channels, (quarter + 1) * channels)
            totals.append(mix(normed_all[...], grad_pre_all[:, cols]))
        size = plan.expand_rows
        for device in range(plan.devices):
            rows = slice(device * size, (device + 1) * size)
            block = jnp.concatenate([total[rows] for total in totals], axis=0)
            core, cross, z = spots[device]
            staged[core, 1, cross, z] = padded_block(block, tall)
        send_out(staged, sems, (keep_ref, send_ref))


def taps_kernel(
    plan,
    table_ref,
    source_ref,
    depth_back,
    out_ref,
    padded,
    tap_sums,
    tap_rows,
):
    step = pl.program_id(0)
    filled = table_ref[FILLED + step]
    side, channels = source_ref.shape[1], source_ref.shape[3]
    bands = channels // LANES
    low = ROW_UNIT // 2
    reach = KS // 2

    @pl.when(step == 0)
    def _start():
        tap_sums[...] = jnp.zeros(tap_sums.shape, jnp.float32)

    @pl.when(filled != 0)
    def _work():
        edge = jnp.zeros((side, low, LANES), jnp.float32)
        for band in range(bands):
            lanes = slice(band * LANES, (band + 1) * LANES)
            padded[band, :, 0:low, :] = edge
            padded[band, :, low + side :, :] = edge
            for at in range(side):
                padded[band, at, low : low + side, :] = source_ref[0, at, :, lanes].astype(
                    jnp.float32
                )

        def taps_of(band, carry):
            for col in range(KS):
                start = low - reach + col
                sums = [None] * KS
                grads = {}
                for at in range(side):
                    line = padded[band, at, start : start + side, :]
                    for row in range(KS):
                        place = at - row + reach
                        if 0 <= place < side:
                            if place not in grads:
                                grads[place] = depth_back[
                                    0, band, place * side : (place + 1) * side, :
                                ]
                            term = line * grads[place]
                            sums[row] = term if sums[row] is None else sums[row] + term
                for row in range(KS):
                    total = sums[row]
                    folded = total[0:8, :]
                    for piece in range(8, side, 8):
                        folded = folded + total[piece : piece + 8, :]
                    tap_sums[band, row * KS + col] = tap_sums[band, row * KS + col] + folded
            return carry

        lax.fori_loop(0, bands, taps_of, 0)

    @pl.when(step == pl.num_programs(0) - 1)
    def _finish():
        for band in range(bands):
            lanes = slice(band * LANES, (band + 1) * LANES)
            tap_rows[0 : KS * KS, lanes] = jnp.sum(tap_sums[band], axis=1)
            tap_rows[KS * KS :, lanes] = jnp.zeros((tap_rows.shape[0] - KS * KS, LANES), jnp.float32)
        for device in range(plan.devices):
            start = device * plan.share // channels
            out_ref[device] = tap_rows[start : start + DEPTH_ROWS, :].astype(jnp.bfloat16)


def per_slot(array):
    shape = array.shape[1:]
    return pl.BlockSpec((1,) + shape, lambda i, table: (i,) + (0,) * len(shape))


def weight_grads(plan, table, embed_grad, saved, vectors, head, expand, reduce):
    unit, inv, hidden, slope, head_slope = saved
    cells, channels = unit.shape[1:]
    hid, bands = expand.shape[1], channels // LANES
    eye = jnp.asarray(np.eye(channels, dtype=np.float32), jnp.bfloat16)
    streams = (embed_grad, hidden, head_slope, slope, unit, inv)
    consts = (vectors, head, expand, reduce, eye)
    back = jax.ShapeDtypeStruct((PROC, bands, cells, LANES), jnp.float32)
    blocks = jax.ShapeDtypeStruct(
        (2, plan.cross, plan.g1, plan.block_rows, channels), jnp.bfloat16
    )
    return pl.pallas_call(
        functools.partial(weights_kernel, plan),
        out_shape=(back, blocks, blocks),
        grid_spec=pltpu.PrefetchScalarGridSpec(
            num_scalar_prefetch=1,
            grid=(PROC,),
            in_specs=[per_slot(stream) for stream in streams]
            + [whole(const.shape) for const in consts],
            out_specs=[per_slot(back), HBM, HBM],
            scratch_shapes=[
                pltpu.VMEM((PROC * cells, hid), jnp.bfloat16),
                pltpu.VMEM((channels, PROC * cells), jnp.bfloat16),
                pltpu.VMEM((PROC * cells, hid), jnp.bfloat16),
                pltpu.VMEM((channels, PROC * cells), jnp.bfloat16),
                pltpu.VMEM((cells, head.shape[1]), jnp.bfloat16),
                pltpu.VMEM((cells, channels), jnp.float32),
                pltpu.VMEM((2,) + blocks.shape, jnp.bfloat16),
                pltpu.SemaphoreType.DMA((2,)),
            ],
        ),
        compiler_params=pltpu.CompilerParams(vmem_limit_bytes=32 * MIB),
        cost_estimate=cost(16.0),
        name="weight_grads",
    )(table, *streams, *consts)


def tap_grads(plan, table, source, depth_back):
    side, channels = source.shape[1], source.shape[3]
    bands = channels // LANES
    out = (plan.devices, DEPTH_ROWS, channels)
    return pl.pallas_call(
        functools.partial(taps_kernel, plan),
        out_shape=jax.ShapeDtypeStruct(out, jnp.bfloat16),
        grid_spec=pltpu.PrefetchScalarGridSpec(
            num_scalar_prefetch=1,
            grid=(PROC,),
            in_specs=[per_slot(source), per_slot(depth_back)],
            out_specs=pl.BlockSpec(out, lambda i, table: (0, 0, 0)),
            scratch_shapes=[
                pltpu.VMEM((bands, side, side + ROW_UNIT, LANES), jnp.float32),
                pltpu.VMEM((bands, KS * KS, 8, LANES), jnp.float32),
                pltpu.VMEM((KS * KS + 7, channels), jnp.float32),
            ],
        ),
        compiler_params=pltpu.CompilerParams(vmem_limit_bytes=10 * MIB),
        cost_estimate=cost(8.0),
        name="tap_grads",
    )(table, source, depth_back)


def shifted(values, names, sizes, shift):
    count = math.prod(sizes)
    pairs = []
    for index in range(count):
        spot = []
        rest = index
        for size in reversed(sizes):
            spot.append(rest % size)
            rest //= size
        spot = spot[::-1]
        target = 0
        for at, step, size in zip(spot, shift, sizes):
            target = target * size + (at + step) % size
        pairs.append((index, target))
    return lax.ppermute(values, names, pairs)


def shifts(sizes):
    steps = [()]
    for size in sizes:
        steps = [step + (more,) for step in steps for more in range(size)]
    return steps


def exchange(values, names):
    return lax.all_to_all(values, names, split_axis=0, concat_axis=0, tiled=True)


def add_all(parts, kind=jnp.bfloat16):
    total = parts[0].astype(jnp.float32)
    for part in parts[1:]:
        total = total + part.astype(jnp.float32)
    return total.astype(kind)


def other_core(values):
    return shifted(values, ("core",), (2,), (1,))


def sum_axis(kept, sent, name, size, kind=jnp.bfloat16):
    return [kept] + [shifted(part, (name,), (size,), (step + 1,)) for step, part in enumerate(sent)]


def position_code(positions):
    half_width = E // 2
    channel_ids = jnp.arange(E, dtype=jnp.int32) % half_width
    frequency = jnp.exp(
        (2 * (channel_ids // 2)).astype(jnp.float32) * (-math.log(10000.0) / half_width)
    )
    phase = jnp.where(channel_ids % 2 == 0, 0.0, 0.5 * math.pi)
    rows = jnp.where(
        jnp.arange(E, dtype=jnp.int32) < half_width, positions[0][..., None], positions[1][..., None]
    )
    return jnp.sin(rows.astype(jnp.float32) * frequency + phase)


def on_device(
    tile_maps,
    positions,
    counts,
    routing,
    depth_kernel,
    depth_bias,
    norm_gain,
    norm_shift,
    expand_weight,
    expand_bias,
    reduce_weight,
    reduce_bias,
    layer_scale,
    head_weight,
    slide_taps,
    slide_weight,
    slide_bias,
    cotangent,
):
    slides = lax.axis_size(DP)
    members = lax.axis_size(GROUP)
    my_device = lax.axis_index(ALL)
    slots, channels = tile_maps.shape[0], tile_maps.shape[3]
    devices, length, places = slides * members, slots * members, slots // slides
    plan = Plan(slides, members, channels, expand_weight.shape[1])

    packed, table = pack_tiles(routing, tile_maps, slides, places)
    from_core = other_core(packed[0])

    def from_other(buffers):
        return [
            lax.ppermute(buffer, DP, [(index, index ^ (other + 2)) for index in range(slides)])
            for other, buffer in enumerate(buffers)
        ]

    arrived = []
    for rank in range(places):
        buffers = packed[1 + rank * (slides - 2) : 1 + (rank + 1) * (slides - 2)]
        if rank:
            buffers, from_core = lax.optimization_barrier((buffers, from_core))
        arrived.append(from_other(buffers))
    held = lax.optimization_barrier((table, routing, cotangent, positions, counts))
    _, routing, cotangent, positions, counts = held
    extras = jnp.concatenate(
        [
            cotangent[0],
            routing.reshape(-1).astype(jnp.float32),
            jnp.zeros((960 - E - slides * slots,), jnp.float32),
            positions.reshape(-1).astype(jnp.float32),
            jnp.zeros((1023 - 960 - 2 * slots,), jnp.float32),
            counts.astype(jnp.float32),
        ]
    )
    extras = exchange(jnp.broadcast_to(extras, (devices, 1024)), ALL)

    vectors = jnp.stack(
        [
            jnp.pad(vector, (0, expand_bias.shape[0] - vector.shape[0]))
            for vector in (
                norm_gain,
                norm_shift,
                layer_scale,
                reduce_bias,
                depth_bias,
                expand_bias,
                slide_bias,
                slide_bias,
            )
        ]
    )
    consts = (depth_kernel, vectors, expand_weight, reduce_weight, head_weight)
    saved = forward_block(0, PROC, table, (tile_maps, from_core), consts, ())
    for rank in range(places):
        items = min(PROC, slides - 2)
        saved = forward_block(1 + rank, items, table, arrived[rank], consts, saved)
    section, tile_embed, unit, inv, hidden, slope, head_slope, source = saved
    filled = table[FILLED : FILLED + PROC] != 0
    tile_embed = jnp.where(filled[:, None], tile_embed[:PROC, 0], 0.0).astype(jnp.bfloat16)
    tile_embed = jnp.broadcast_to(tile_embed, (devices, PROC, E))
    tile_embed, extras = lax.optimization_barrier((tile_embed, extras))
    embeds = exchange(tile_embed, ALL).reshape(devices * PROC, E)
    tile_out = jnp.where(filled[:, None, None, None], section[:PROC], jnp.zeros((), jnp.bfloat16))

    route_all = extras[:, E : E + slides * slots].astype(jnp.int32)
    route_all = route_all.reshape(slides, members, slides, slots)[0]
    pos_all = extras[:, 960 : 960 + 2 * slots].reshape(slides, members, 2, slots)
    pos_all = pos_all.transpose(2, 0, 3, 1).reshape(2, slides, length)
    counts_all = extras[:, 1023].reshape(slides, members)[:, 0]
    cot_all = extras[:, :E].reshape(slides, members, 1, E)[:, 0]
    codes = position_code(pos_all)
    member_ids = jnp.arange(members, dtype=jnp.int32)[:, None, None]
    target = jnp.where(
        route_all >= 0, (route_all // PROC * members + member_ids) * PROC + route_all % PROC, -1
    )
    target = target.transpose(1, 2, 0).reshape(slides, length, 1)
    pick = (target == jnp.arange(devices * PROC, dtype=jnp.int32)).astype(jnp.bfloat16)
    steps = jnp.arange(length, dtype=jnp.int32)[None, :, None].astype(jnp.float32)
    weight = jnp.where(steps < counts_all[:, None, None], 1.0 / counts_all[:, None, None], 0.0)

    feature, embed_grad = slide_grads(
        table, [embeds], pick, codes, weight, cot_all, slide_taps, slide_weight, vectors
    )
    depth_back, kept, sent = weight_grads(
        plan,
        table,
        embed_grad,
        (unit, inv, hidden, slope, head_slope),
        vectors,
        head_weight,
        expand_weight,
        reduce_weight,
    )

    came = other_core(sent)
    grid = [
        part.reshape((2, plan.ys, plan.g2) + part.shape[2:]) for part in (kept, came)
    ]

    def sums(parts, wanted, count):
        return add_all([wanted(part)(0) for part in parts]), [
            add_all([wanted(part)(step) for part in parts]) for step in range(1, count)
        ]

    reduce_stay, reduce_out = sums(grid, lambda part: lambda step: part[0][:, step], plan.g2)
    expand_stay, expand_out = sums(grid, lambda part: lambda step: part[1][step], plan.ys)
    held = lax.optimization_barrier((depth_back, reduce_out, expand_out))
    depth_back, reduce_out, expand_out = held
    reduce_parts = sum_axis(reduce_stay, reduce_out, "g2", plan.g2)
    expand_parts = sum_axis(expand_stay, expand_out, "y", plan.ys)
    taps = exchange(tap_grads(plan, table, source, depth_back), ALL)

    def along(part):
        return lambda step: part[step]

    reduce_stay, reduce_out = sums(reduce_parts, along, plan.ys)
    expand_stay, expand_out = sums(expand_parts, along, plan.g2)
    reduce_parts = sum_axis(reduce_stay, reduce_out, "y", plan.ys)
    expand_parts = sum_axis(expand_stay, expand_out, "g2", plan.g2)
    both = jnp.concatenate([add_all(reduce_parts), add_all(expand_parts)], axis=1)
    total = add_all(
        sum_axis(both[0], [both[step] for step in range(1, plan.g1)], "g1", plan.g1), jnp.float32
    )
    reduce_share = total[: plan.reduce_rows]
    expand_share = total[plan.block_rows : plan.block_rows + plan.pieces * plan.expand_rows]
    expand_share = expand_share.reshape(plan.pieces, plan.expand_rows, channels).transpose(1, 0, 2)
    depth_share = lax.dynamic_slice(
        jnp.sum(taps.astype(jnp.float32), axis=0).reshape(-1),
        (my_device * plan.share % channels,),
        (plan.share,),
    )
    return (tile_out, feature, expand_share.reshape(-1), reduce_share.reshape(-1), depth_share)


def solution(mesh):
    slides, members = mesh.shape["dp"], mesh.shape["group"]
    fine = Mesh(mesh.devices.reshape(slides // 2, 2, 4, members // 4), ALL)
    return jax.shard_map(
        on_device,
        mesh=fine,
        in_specs=(
            P(ALL, None, None, None),
            P(None, ALL),
            P(DP),
            P(None, GROUP, None),
        )
        + (P(),) * 13
        + (P(DP, None),),
        out_specs=(
            P(ALL, None, None, None),
            P(DP, None),
            P(ALL),
            P(ALL),
            P(ALL),
        ),
        check_vma=False,
    )
```

```python
import functools
import math

import jax
import jax.numpy as jnp
import numpy as np
from jax import lax
from jax.experimental import pallas as pl
from jax.experimental.pallas import tpu as pltpu
from jax.sharding import Mesh, PartitionSpec as P

E = 768
KS = 7
KERNEL_TAPS = 7
TILE_DILATION = 3
PROC = 4
DP = ("y", "core")
GROUP = ("g1", "g2")
ALL = DP + GROUP

EPSILON = 1e-06
HALF_ROOT = 0.7071067811865476
INV_ROOT_TAU = 0.3989422804014327
LANES = 128
ROW_UNIT = 16
DEPTH_ROWS = 4
MIB = 1024 * 1024
PART = 32
WIDTH = 256
GAIN, SHIFT, SCALE, REDUCE_BIAS, DEPTH_BIAS, EXPAND_BIAS, SLIDE_BIAS = range(7)
VECTORS = 7
ERFC_P = 0.3275911
ERFC_A = (0.254829592, -0.284496736, 1.421413741, -1.453152027, 1.061405429)

HBM = pl.BlockSpec(memory_space=pl.ANY)
IN_HBM = pl.BlockSpec(memory_space=pltpu.HBM)
ROWS_AT, COLS_AT, COUNT_AT, SMALL = E, E + LANES, E + 2 * LANES, E + 3 * LANES


def whole(shape):
    return pl.BlockSpec(shape, lambda *_: (0,) * len(shape), pipeline_mode=pl.Buffered(1))


def gelu_and_slope(values):
    size = jnp.abs(values)
    divisor = 1.0 + (ERFC_P * HALF_ROOT) * size
    guess = pl.reciprocal(divisor, approx=True)
    t = guess * (2.0 - divisor * guess)
    bell = jnp.exp(-0.5 * values * values)
    poly = 0.5 * ERFC_A[4]
    for coefficient in ERFC_A[3::-1]:
        poly = poly * t + 0.5 * coefficient
    tail = poly * t * bell
    phi = jnp.where(values >= 0.0, 1.0 - tail, tail)
    return values * phi, phi + values * (INV_ROOT_TAU * bell)


def mix_cols(left_side, right_side):
    return lax.dot_general(
        left_side, right_side, (((1,), (1,)), ((), ())), preferred_element_type=jnp.float32
    )


def mix(left_side, right_side):
    return jnp.dot(left_side, right_side, preferred_element_type=jnp.float32)


FILLED, SLIDE, PLACE, CLASSES = 0, PROC, 2 * PROC, 3 * PROC
CLASS_SIZE = 1 + 3 * PROC


def class_field(kind, field, item=0):
    return CLASSES + kind * CLASS_SIZE + (1 + field * PROC + item if field >= 0 else 0)


SLOT, FROM, OWN = range(3)


def pack_kernel(slides, slots, places, counts_ref, route_ref, tiles_ref, pos_ref, cot_ref, *refs):
    inputs = (pos_ref, cot_ref) + refs[:VECTORS]
    refs = refs[VECTORS:]
    held_refs, refs = refs[-len(inputs) - 1 : -1], refs[: -len(inputs) - 1] + refs[-1:]
    send_refs, refs = refs[:-7], refs[-7:]
    table_ref, small_ref, vectors_ref, count_ref, slot_ref, sems, input_sems = refs
    loads = [
        pltpu.make_async_copy(ref, held, input_sems.at[index])
        for index, (ref, held) in enumerate(zip(inputs, held_refs))
    ]
    for load in loads:
        load.start()
    pos_ref, cot_ref = held_refs[:2]
    vector_refs = held_refs[2:]
    my_slide = lax.axis_index(DP)

    targets = [(0, rank, rank) for rank in range(places)]
    for rank in range(places):
        for other in range(2, slides):
            targets.append((1 + rank * (slides - 2) + other - 2, 0, other * places + rank))
    targets[:places] = [(0, rank, places + rank) for rank in range(places)]

    def copy_of(index, slot):
        buffer, row, _ = targets[index]
        return pltpu.make_async_copy(tiles_ref.at[slot], send_refs[buffer].at[row], sems.at[index])

    for index in range(slides):
        count_ref[index] = 0
    for index in range(slides * places):
        slot_ref[index] = -1

    def place_slot(slot, carry):
        entry = route_ref[my_slide, 0, slot]

        @pl.when(entry >= 0)
        def _send():
            other = lax.div(entry, PROC) ^ my_slide
            rank = count_ref[other]
            count_ref[other] = rank + 1
            slot_ref[other * places + rank] = slot

        return carry

    lax.fori_loop(0, slots, place_slot, 0)
    for index, (_, _, key) in enumerate(targets):
        slot = slot_ref[key]

        @pl.when(slot >= 0)
        def _start():
            copy_of(index, slot).start()

    for load in loads:
        load.wait()
    small_ref[:, 0:E] = cot_ref[...]
    for row, start in enumerate((ROWS_AT, COLS_AT)):
        small_ref[:, start : start + LANES] = jnp.zeros((1, LANES), jnp.float32)
        small_ref[:, start : start + slots] = pos_ref[row : row + 1, :].astype(jnp.float32)
    small_ref[:, COUNT_AT:SMALL] = jnp.full((1, LANES), counts_ref[0], jnp.int32).astype(jnp.float32)
    vectors_ref[...] = jnp.zeros(vectors_ref.shape, jnp.float32)
    for index, ref in enumerate(vector_refs):
        size = ref.shape[0]
        vectors_ref[index : index + 1, 0:size] = ref[...].reshape(1, size)

    kinds = 1 + places
    for field in range(CLASSES + kinds * CLASS_SIZE):
        table_ref[field] = 0
    for kind in range(kinds):
        for item in range(PROC):
            table_ref[class_field(kind, SLOT, item)] = PROC
    for other in range(slides):
        source = my_slide ^ other
        count_ref[0] = 0

        def take(slot, carry):
            entry = route_ref[source, 0, slot]
            proc = entry - my_slide * PROC

            @pl.when((proc >= 0) & (proc < PROC))
            def _take():
                rank = count_ref[0]
                count_ref[0] = rank + 1
                table_ref[FILLED + proc] = 1
                table_ref[SLIDE + proc] = source
                table_ref[PLACE + proc] = slot
                kind = 0 if other < 2 else 1 + rank
                base = CLASSES + kind * CLASS_SIZE
                item = table_ref[base]
                table_ref[base] = item + 1
                table_ref[base + 1 + SLOT * PROC + item] = proc
                if other == 0:
                    table_ref[base + 1 + FROM * PROC + item] = 0
                    table_ref[base + 1 + OWN * PROC + item] = slot
                else:
                    table_ref[base + 1 + FROM * PROC + item] = 1 + rank if other == 1 else other - 2

            return carry

        lax.fori_loop(0, slots, take, 0)
        if other == 0:
            own = table_ref[class_field(0, -1)]
            for item in range(1, PROC):

                @pl.when(item >= own)
                def _hold():
                    table_ref[class_field(0, OWN, item)] = table_ref[class_field(0, OWN, item - 1)]

    for kind in range(kinds):
        items = table_ref[class_field(kind, -1)]
        for item in range(1, PROC):

            @pl.when(item >= items)
            def _hold_slot():
                table_ref[class_field(kind, SLOT, item)] = table_ref[class_field(kind, SLOT, item - 1)]

    for index, (_, _, key) in enumerate(targets):

        @pl.when(slot_ref[key] >= 0)
        def _wait():
            copy_of(index, 0).wait()


def pack_tiles(counts, routing, tile_maps, positions, cotangent, vectors, slides, places):
    slots = tile_maps.shape[0]
    smem = pl.BlockSpec(memory_space=pltpu.SMEM)
    vmem = pl.BlockSpec(memory_space=pltpu.VMEM)
    buffers = 1 + places * (slides - 2)
    shapes = [places] + [1] * (buffers - 1)
    widest = max(vector.shape[0] for vector in vectors)
    inputs = (positions, cotangent) + vectors
    pinned = [pltpu.with_memory_space_constraint(x, pltpu.HBM) for x in (tile_maps,) + inputs]
    outs = pl.pallas_call(
        functools.partial(pack_kernel, slides, slots, places),
        out_shape=tuple(
            jax.ShapeDtypeStruct((size,) + tile_maps.shape[1:], tile_maps.dtype) for size in shapes
        )
        + (
            jax.ShapeDtypeStruct((CLASSES + (1 + places) * CLASS_SIZE,), jnp.int32),
            jax.ShapeDtypeStruct((1, SMALL), jnp.float32),
            jax.ShapeDtypeStruct((8, widest), jnp.float32),
        ),
        in_specs=[smem, smem] + [IN_HBM] * len(pinned),
        out_specs=(vmem,) * buffers + (smem, vmem, vmem),
        scratch_shapes=[
            pltpu.SMEM((slides,), jnp.int32),
            pltpu.SMEM((slides * places,), jnp.int32),
            pltpu.SemaphoreType.DMA((slides * places,)),
        ]
        + [pltpu.VMEM(x.shape, x.dtype) for x in inputs]
        + [pltpu.SemaphoreType.DMA((len(inputs),))],
        compiler_params=pltpu.CompilerParams(vmem_limit_bytes=8 * MIB),
        name="pack_tiles",
    )(counts, routing, *pinned)
    return outs[:-3], outs[-3:]


def forward_kernel(kind, inputs, aliased, table_ref, *refs):
    forward_items(kind, table_ref, refs[:inputs], *refs[inputs : inputs + 5], *refs[inputs + 5 + aliased :])


def forward_items(
    kind,
    table_ref,
    tile_refs,
    taps_ref,
    vectors_ref,
    expand_ref,
    reduce_ref,
    head_ref,
    out_ref,
    embed_ref,
    unit_ref,
    inv_ref,
    hidden_ref,
    slope_ref,
    head_slope_ref,
    source_ref,
    padded,
    depth_out,
    normed,
    pre,
    section,
):
    item = pl.program_id(0)
    side = out_ref.shape[1]
    channels = out_ref.shape[3]
    cells = side * side
    bands = channels // LANES
    low = ROW_UNIT // 2
    reach = KS // 2

    @pl.when(item < table_ref[class_field(kind, -1)])
    def _work():
        origin = table_ref[class_field(kind, FROM) + item]
        edge = jnp.zeros((side, low, LANES), jnp.float32)
        for band in range(bands):
            padded[band, :, 0:low, :] = edge
            padded[band, :, low + side :, :] = edge
        place = 0
        for ref in tile_refs:
            for row in range(ref.shape[0]):

                @pl.when(origin == place)
                def _load():
                    source_ref[0] = ref[row]

                place += 1
        for band in range(bands):
            for at in range(side):
                padded[band, at, low : low + side, :] = source_ref[
                    0, at, :, band * LANES : (band + 1) * LANES
                ].astype(jnp.float32)

        def convolve(band, carry):
            lanes = pl.ds(pl.multiple_of(band * LANES, LANES), LANES)
            bias = jnp.broadcast_to(vectors_ref[DEPTH_BIAS : DEPTH_BIAS + 1, lanes], (side, LANES))
            totals = [bias for _ in range(side)]
            for col in range(KS):
                start = low - reach + col
                weights = [
                    taps_ref[row * KS + col : row * KS + col + 1, lanes] for row in range(KS)
                ]
                for at in range(side):
                    line = padded[band, at, start : start + side, :]
                    for row in range(KS):
                        place = at - row + reach
                        if 0 <= place < side:
                            totals[place] = totals[place] + weights[row] * line
            for place in range(side):
                depth_out[band, place * side : (place + 1) * side, :] = totals[place]
            return carry

        lax.fori_loop(0, bands, convolve, 0)

        def vector(index, lanes):
            return vectors_ref[index : index + 1, lanes]

        for start in range(0, cells, PART):
            rows = slice(start, start + PART)
            pieces = [depth_out[band, rows, :] for band in range(bands)]
            mean = jnp.sum(sum(pieces), axis=1, keepdims=True) * (1.0 / channels)
            pieces = [piece - mean for piece in pieces]
            var = jnp.sum(sum(p * p for p in pieces), axis=1, keepdims=True) * (1.0 / channels)
            inv = lax.rsqrt(var + EPSILON)
            inv_ref[0, rows, :] = jnp.broadcast_to(inv, (PART, LANES))
            for band in range(bands):
                lanes = slice(band * LANES, (band + 1) * LANES)
                unit = pieces[band] * inv
                unit_ref[0, rows, lanes] = unit
                normed[rows, lanes] = (unit * vector(GAIN, lanes) + vector(SHIFT, lanes)).astype(
                    jnp.bfloat16
                )

        for index, begin in enumerate(range(0, expand_ref.shape[1], WIDTH)):
            cols = slice(begin, begin + WIDTH)
            buffer = index % pre.shape[0]
            pre[buffer] = mix(normed[...], expand_ref[:, cols])
            for start in range(0, cells, PART):
                rows = slice(start, start + PART)
                act, slope = gelu_and_slope(pre[buffer, rows, :] + vector(EXPAND_BIAS, cols))
                hidden_ref[0, rows, cols] = act.astype(jnp.bfloat16)
                slope_ref[0, rows, cols] = slope.astype(jnp.bfloat16)
        lanes = slice(0, channels)
        depth_rows = mix(hidden_ref[0], reduce_ref[...])
        for at in range(side):
            rows = slice(at * side, (at + 1) * side)
            branch = vector(SCALE, lanes) * (depth_rows[rows] + vector(REDUCE_BIAS, lanes))
            line = (source_ref[0, at].astype(jnp.float32) + branch).astype(jnp.bfloat16)
            section[rows, :] = line
            out_ref[0, at] = line
        for index, begin in enumerate(range(0, head_ref.shape[1], WIDTH)):
            cols = slice(begin, begin + WIDTH)
            buffer = index % pre.shape[0]
            pre[buffer] = mix(section[...], head_ref[:, cols])
            total = None
            for start in range(0, cells, PART):
                rows = slice(start, start + PART)
                act, slope = gelu_and_slope(pre[buffer, rows, :])
                head_slope_ref[0, rows, cols] = slope.astype(jnp.bfloat16)
                folded = act[0:8]
                for piece in range(8, PART, 8):
                    folded = folded + act[piece : piece + 8]
                total = folded if total is None else total + folded
            embed_ref[0, :, cols] = jnp.sum(total, axis=0, keepdims=True) * (1.0 / cells)


def forward_block(kind, items, table, tiles, consts, before):
    side, channels = tiles[0].shape[1], tiles[0].shape[3]
    taps, vectors, expand, reduce, head = consts
    cells, hid, embed = side * side, expand.shape[1], head.shape[1]
    bands = channels // LANES

    def per_slot(*shape):
        return pl.BlockSpec(
            (1,) + shape,
            lambda i, table: (table[class_field(kind, SLOT) + i],) + (0,) * len(shape),
        )

    outs = (
        ((side, side, channels), jnp.bfloat16),
        ((1, embed), jnp.float32),
        ((cells, channels), jnp.float32),
        ((cells, LANES), jnp.float32),
        ((cells, hid), jnp.bfloat16),
        ((cells, hid), jnp.bfloat16),
        ((cells, embed), jnp.bfloat16),
        ((side, side, channels), jnp.bfloat16),
    )
    tile_specs = [whole(tile.shape) for tile in tiles]
    if kind == 0:
        tile_specs[0] = pl.BlockSpec(
            (1, side, side, channels),
            lambda i, table: (table[class_field(kind, OWN) + i], 0, 0, 0),
        )
    first = 1 + len(tiles) + len(consts)
    return pl.pallas_call(
        functools.partial(forward_kernel, kind, len(tiles), len(before)),
        out_shape=tuple(pltpu.HBM((PROC + 1,) + shape, dtype) for shape, dtype in outs),
        grid_spec=pltpu.PrefetchScalarGridSpec(
            num_scalar_prefetch=1,
            grid=(items,),
            in_specs=tile_specs + [whole(const.shape) for const in consts] + [IN_HBM] * len(before),
            out_specs=[per_slot(*shape) for shape, _ in outs],
            scratch_shapes=[
                pltpu.VMEM((bands, side, side + ROW_UNIT, LANES), jnp.float32),
                pltpu.VMEM((bands, cells, LANES), jnp.float32),
                pltpu.VMEM((cells, channels), jnp.bfloat16),
                pltpu.VMEM((3, cells, WIDTH), jnp.float32),
                pltpu.VMEM((cells, channels), jnp.bfloat16),
            ],
        ),
        input_output_aliases={first + index: index for index in range(len(before))},
        compiler_params=pltpu.CompilerParams(vmem_limit_bytes=20 * MIB),
        cost_estimate=cost(6.0 * min(items, 2)),
        name="forward_block_" + str(kind),
    )(table, *tiles, *consts, *before)


def cost(micros):
    return pl.CostEstimate(flops=int(micros * 1e9), bytes_accessed=1024, transcendentals=0)


def rows_kernel(slides, table_ref, embed_ref, *refs):
    small_refs, out_ref = refs[:slides], refs[slides]
    my_slide, my_member = lax.axis_index(DP), lax.axis_index(GROUP)
    devices = out_ref.shape[0]
    half = E // 2
    channel = lax.broadcasted_iota(jnp.int32, (1, E), 1)
    inner = jnp.where(channel < half, channel, channel - half)
    odd = lax.rem(inner, 2)
    frequency = jnp.exp((inner - odd).astype(jnp.float32) * (-math.log(10000.0) / half))
    phase = odd.astype(jnp.float32) * (0.5 * math.pi)
    lane = lax.broadcasted_iota(jnp.int32, (1, LANES), 1)
    for proc in range(PROC):
        filled = table_ref[FILLED + proc]
        slide = table_ref[SLIDE + proc]
        slot = table_ref[PLACE + proc]
        spots = []
        for start in (ROWS_AT, COLS_AT):
            held = small_refs[0][:, start : start + LANES]
            for other in range(1, slides):
                held = jnp.where(
                    (slide ^ my_slide) == other, small_refs[other][:, start : start + LANES], held
                )
            spots.append(jnp.sum(jnp.where(lane == slot, held, 0.0), axis=1, keepdims=True))
        spot = jnp.where(channel < half, spots[0], spots[1])
        embed = embed_ref[proc].astype(jnp.bfloat16).astype(jnp.float32)
        row = jnp.where(filled != 0, embed + jnp.sin(spot * frequency + phase), 0.0)
        target = jnp.where(lane == 0, slide, jnp.where(lane == 1, slot, my_member))
        target = jnp.where(filled != 0, target, jnp.where(lane == 2, -1, 0))
        target = jnp.where(lane < 3, target, 0)
        out_ref[0, proc : proc + 1, 0:E] = row.astype(jnp.bfloat16).astype(jnp.float32)
        out_ref[0, proc : proc + 1, E:] = target.astype(jnp.float32)


def tile_rows(table, embeds, smalls, devices):
    smem = pl.BlockSpec(memory_space=pltpu.SMEM)
    vmem = pl.BlockSpec(memory_space=pltpu.VMEM)
    return pl.pallas_call(
        functools.partial(rows_kernel, len(smalls)),
        out_shape=jax.ShapeDtypeStruct((1, PROC, E + LANES), jnp.float32),
        in_specs=[smem] + [vmem] * (1 + len(smalls)),
        out_specs=vmem,
        cost_estimate=cost(1.0),
        name="tile_rows",
    )(table, embeds, *smalls)


def slide_kernel(
    length,
    members,
    slides,
    table_ref,
    came_ref,
    taps_ref,
    matrix_ref,
    vectors_ref,
    *refs,
):
    small_refs = refs[:slides]
    feature_ref, grad_ref, rows, back, mixed, pre, grad_agg = refs[slides:]
    my_slide = lax.axis_index(DP)
    border = ROW_UNIT
    edge = jnp.zeros((border, rows.shape[2]), jnp.float32)
    reach = KERNEL_TAPS // 2
    blocks = [slice(start, start + WIDTH) for start in range(0, E, WIDTH)]
    lane = lax.broadcasted_iota(jnp.int32, (8, LANES), 1)
    scales = jnp.where(lane == 0, length, jnp.where(lane == 1, members, jnp.where(lane == 2, 1, 0)))
    target = mix_cols(scales.astype(jnp.float32).astype(jnp.bfloat16), came_ref[:, E:])[0:1, :]
    step = lax.broadcasted_iota(jnp.int32, (length, 1), 0).astype(jnp.float32)

    def dilate(ref, slide, direction, cols):
        total = ref[slide, border : border + length, cols]
        for tap in range(KERNEL_TAPS):
            start = border + direction * (tap - reach) * TILE_DILATION
            total = total + taps_ref[tap : tap + 1, cols] * ref[slide, start : start + length, cols]
        return total

    for other in range(slides):
        slide = my_slide ^ other
        small = small_refs[other]
        count = small[:, COUNT_AT : COUNT_AT + 1]
        here = step < count
        share = jnp.where(here, 1.0 / count, 0.0)
        first = lax.convert_element_type(slide * length, jnp.float32)
        pick = ((target - first) == step).astype(jnp.float32).astype(jnp.bfloat16)
        for ref in (rows, back):
            ref[slide, 0:border, :] = edge
            ref[slide, border + length :, :] = edge
        for cols in blocks:
            rows[slide, border : border + length, cols] = jnp.where(
                here, mix(pick, came_ref[:, cols]), 0.0
            )
            mixed[:, cols] = dilate(rows, slide, 1, cols).astype(jnp.bfloat16)
        for cols in blocks:
            pre[:, cols] = mix(mixed[...], matrix_ref[:, cols])
            total = None
            for start in range(0, length, PART):
                part = slice(start, start + PART)
                act, slope = gelu_and_slope(
                    pre[part, cols] + vectors_ref[SLIDE_BIAS : SLIDE_BIAS + 1, cols]
                )
                grad_agg[part, cols] = (small[:, cols] * share[part] * slope).astype(jnp.bfloat16)
                if other == 0:
                    piece = jnp.sum(act * share[part], axis=0, keepdims=True)
                    total = piece if total is None else total + piece
            if other == 0:
                feature_ref[:, cols] = total
        for cols in blocks:
            back[slide, border : border + length, cols] = mix_cols(
                grad_agg[...], matrix_ref[cols, :]
            )
            total = jnp.where(here, dilate(back, slide, -1, cols), 0.0)
            rows[slide, border : border + length, cols] = total.astype(jnp.bfloat16).astype(
                jnp.float32
            )
    my_member = lax.axis_index(GROUP)
    for proc in range(PROC):
        at = border + table_ref[PLACE + proc] * members + my_member
        row = rows[table_ref[SLIDE + proc], pl.ds(at, 1), :]
        grad_ref[proc] = jnp.where(table_ref[FILLED + proc] != 0, row, 0.0)


def slide_grads(length, members, table, came, taps, matrix, vectors, smalls):
    slides = len(smalls)
    smem = pl.BlockSpec(memory_space=pltpu.SMEM)
    vmem = pl.BlockSpec(memory_space=pltpu.VMEM)
    padded = (slides, length + 2 * ROW_UNIT, E)
    return pl.pallas_call(
        functools.partial(slide_kernel, length, members, slides),
        out_shape=(
            jax.ShapeDtypeStruct((1, E), jnp.float32),
            jax.ShapeDtypeStruct((PROC, 1, E), jnp.float32),
        ),
        in_specs=[smem] + [vmem] * (4 + slides),
        out_specs=(vmem, vmem),
        scratch_shapes=[
            pltpu.VMEM(padded, jnp.float32),
            pltpu.VMEM(padded, jnp.float32),
            pltpu.VMEM((length, E), jnp.bfloat16),
            pltpu.VMEM((length, E), jnp.float32),
            pltpu.VMEM((length, E), jnp.bfloat16),
        ],
        compiler_params=pltpu.CompilerParams(vmem_limit_bytes=24 * MIB),
        cost_estimate=cost(6.0),
        name="slide_grads",
    )(table, came, taps, matrix, vectors, *smalls)


class Plan:
    def __init__(self, slides, members, channels, hid):
        self.devices = slides * members
        self.ys, self.g1, self.g2 = slides // 2, 4, members // 4
        assert self.ys == self.g2
        self.channels = channels
        self.pieces = hid // channels
        self.expand_rows = channels // self.devices
        self.reduce_rows = hid // self.devices
        self.block_rows = -(-self.reduce_rows // ROW_UNIT) * ROW_UNIT
        self.share = KS * KS * channels // self.devices

    def spots(self):
        my_core, my_y = lax.axis_index("core"), lax.axis_index("y")
        my_z, my_x = lax.axis_index("g1"), lax.axis_index("g2")
        for device in range(self.devices):
            slide, member = divmod(device, self.g1 * self.g2)
            (y, core), (z, x) = divmod(slide, 2), divmod(member, self.g2)
            yield (
                my_core ^ core,
                lax.rem(y - my_y + self.ys, self.ys),
                lax.rem(x - my_x + self.g2, self.g2),
                lax.rem(z - my_z + self.g1, self.g1),
            )


def send_out(staged, sems, refs):
    copies = [
        pltpu.make_async_copy(staged.at[index], ref, sems.at[index]) for index, ref in enumerate(refs)
    ]
    for copy in copies:
        copy.start()
    for copy in copies:
        copy.wait()


def padded_block(block, rows):
    extra = rows - block.shape[0]
    if extra:
        block = jnp.concatenate([block, jnp.zeros((extra, block.shape[1]), block.dtype)], axis=0)
    return block.astype(jnp.bfloat16)


def weights_kernel(
    plan,
    table_ref,
    grad_ref,
    hidden_ref,
    head_slope_ref,
    slope_ref,
    unit_ref,
    inv_ref,
    vectors_ref,
    head_ref,
    expand_ref,
    reduce_ref,
    eye_ref,
    depth_back_ref,
    keep_ref,
    send_ref,
    hidden_all,
    grad_mlp_all,
    grad_pre_all,
    normed_all,
    grad_head,
    grad_norm,
    staged,
    sems,
):
    step = pl.program_id(0)
    filled = table_ref[FILLED + step]
    cells, channels = unit_ref.shape[1:]
    bands = channels // LANES
    rows_all = pl.ds(pl.multiple_of(step * cells, cells), cells)
    every = slice(0, channels)

    def vector(index, lanes):
        return vectors_ref[index : index + 1, lanes]

    @pl.when(filled == 0)
    def _empty():
        for ref in (hidden_all, grad_pre_all):
            ref[rows_all, :] = jnp.zeros((cells, ref.shape[1]), jnp.bfloat16)
        for ref in (grad_mlp_all, normed_all):
            ref[:, rows_all] = jnp.zeros((channels, cells), jnp.bfloat16)

    @pl.when(filled != 0)
    def _work():
        for start in range(0, cells, PART):
            rows = slice(start, start + PART)
            grad_head[rows, :] = (
                (grad_ref[0] * (1.0 / cells)) * head_slope_ref[0, rows, :].astype(jnp.float32)
            ).astype(jnp.bfloat16)
        grad_mlp = (vector(SCALE, every) * mix_cols(grad_head[...], head_ref[...])).astype(
            jnp.bfloat16
        )
        grad_mlp_all[:, rows_all] = mix_cols(eye_ref[...], grad_mlp).astype(jnp.bfloat16)
        hidden_all[rows_all, :] = hidden_ref[0]
        for begin in range(0, expand_ref.shape[1], WIDTH):
            cols = slice(begin, begin + WIDTH)
            grad_hidden = mix_cols(grad_mlp, reduce_ref[cols, :])
            grad_pre_all[rows_all, cols] = (
                grad_hidden * slope_ref[0, :, cols].astype(jnp.float32)
            ).astype(jnp.bfloat16)
        grad_norm[...] = mix_cols(grad_pre_all[rows_all, :], expand_ref[...])
        normed = (unit_ref[0] * vector(GAIN, every) + vector(SHIFT, every)).astype(jnp.bfloat16)
        normed_all[:, rows_all] = mix_cols(eye_ref[...], normed).astype(jnp.bfloat16)
        for start in range(0, cells, PART):
            rows = slice(start, start + PART)
            scaled = grad_norm[rows, :] * vector(GAIN, every)
            unit = unit_ref[0, rows, :]
            mean = jnp.sum(scaled, axis=1, keepdims=True) * (1.0 / channels)
            mean_unit = jnp.sum(scaled * unit, axis=1, keepdims=True) * (1.0 / channels)
            inv = inv_ref[0, rows, 0:1]
            for band in range(bands):
                lanes = slice(band * LANES, (band + 1) * LANES)
                depth_back_ref[0, band, rows, :] = inv * (
                    scaled[:, lanes] - mean - unit[:, lanes] * mean_unit
                )

    @pl.when(step == pl.num_programs(0) - 1)
    def _finish():
        spots = list(plan.spots())
        per_block = channels // plan.reduce_rows
        tall = plan.block_rows
        for index in range(plan.pieces):
            cols = slice(index * channels, (index + 1) * channels)
            total = mix(grad_mlp_all[...], hidden_all[:, cols]).astype(jnp.bfloat16)
            turned = mix_cols(eye_ref[...], total)
            for part in range(per_block):
                block = turned[part * plan.reduce_rows : (part + 1) * plan.reduce_rows]
                core, y, x, z = spots[index * per_block + part]
                staged[core, 0, x, y, z] = padded_block(block, tall)
        totals = []
        for quarter in range(plan.pieces):
            cols = slice(quarter * channels, (quarter + 1) * channels)
            totals.append(mix(normed_all[...], grad_pre_all[:, cols]))
        size = plan.expand_rows
        for device in range(plan.devices):
            rows = slice(device * size, (device + 1) * size)
            block = jnp.concatenate([total[rows] for total in totals], axis=0)
            core, y, x, z = spots[device]
            staged[core, 1, y, x, z] = padded_block(block, tall)
        send_out(staged, sems, (keep_ref, send_ref))


def taps_kernel(
    plan,
    first,
    last,
    table_ref,
    source_ref,
    depth_back,
    before_ref,
    out_ref,
    padded,
    tap_sums,
    tap_rows,
):
    step = pl.program_id(0)
    filled = table_ref[FILLED + first + step]
    side, channels = source_ref.shape[1], source_ref.shape[3]
    bands = channels // LANES
    low = ROW_UNIT // 2
    reach = KS // 2

    @pl.when(step == 0)
    def _start():
        if first:
            tap_sums[...] = before_ref[...]
        else:
            tap_sums[...] = jnp.zeros(tap_sums.shape, jnp.float32)

    @pl.when(filled != 0)
    def _work():
        edge = jnp.zeros((side, low, LANES), jnp.float32)
        for band in range(bands):
            lanes = slice(band * LANES, (band + 1) * LANES)
            padded[band, :, 0:low, :] = edge
            padded[band, :, low + side :, :] = edge
            for at in range(side):
                padded[band, at, low : low + side, :] = source_ref[0, at, :, lanes].astype(
                    jnp.float32
                )

        def taps_of(band, carry):
            for col in range(KS):
                start = low - reach + col
                sums = [None] * KS
                grads = {}
                for at in range(side):
                    line = padded[band, at, start : start + side, :]
                    for row in range(KS):
                        place = at - row + reach
                        if 0 <= place < side:
                            if place not in grads:
                                grads[place] = depth_back[
                                    0, band, place * side : (place + 1) * side, :
                                ]
                            term = line * grads[place]
                            sums[row] = term if sums[row] is None else sums[row] + term
                for row in range(KS):
                    total = sums[row]
                    folded = total[0:8, :]
                    for piece in range(8, side, 8):
                        folded = folded + total[piece : piece + 8, :]
                    tap_sums[band, row * KS + col] = tap_sums[band, row * KS + col] + folded
            return carry

        lax.fori_loop(0, bands, taps_of, 0)

    @pl.when(step == pl.num_programs(0) - 1)
    def _finish():
        if not last:
            out_ref[...] = tap_sums[...]
            return
        for band in range(bands):
            lanes = slice(band * LANES, (band + 1) * LANES)
            tap_rows[0 : KS * KS, lanes] = jnp.sum(tap_sums[band], axis=1)
            tap_rows[KS * KS :, lanes] = jnp.zeros((tap_rows.shape[0] - KS * KS, LANES), jnp.float32)
        for device in range(plan.devices):
            start = device * plan.share // channels
            out_ref[device] = tap_rows[start : start + DEPTH_ROWS, :].astype(jnp.bfloat16)


def per_slot(array):
    shape = array.shape[1:]
    return pl.BlockSpec((1,) + shape, lambda i, table: (i,) + (0,) * len(shape))


def weight_grads(plan, table, embed_grad, saved, vectors, head, expand, reduce):
    unit, inv, hidden, slope, head_slope = saved
    cells, channels = unit.shape[1:]
    hid, bands = expand.shape[1], channels // LANES
    eye = jnp.asarray(np.eye(channels, dtype=np.float32), jnp.bfloat16)
    streams = (embed_grad, hidden, head_slope, slope, unit, inv)
    consts = (vectors, head, expand, reduce, eye)
    back = pltpu.HBM((PROC, bands, cells, LANES), jnp.float32)
    blocks = jax.ShapeDtypeStruct(
        (2, plan.ys, plan.g2, plan.g1, plan.block_rows, channels), jnp.bfloat16
    )
    return pl.pallas_call(
        functools.partial(weights_kernel, plan),
        out_shape=(back, blocks, blocks),
        grid_spec=pltpu.PrefetchScalarGridSpec(
            num_scalar_prefetch=1,
            grid=(PROC,),
            in_specs=[per_slot(stream) for stream in streams]
            + [whole(const.shape) for const in consts],
            out_specs=[
                pl.BlockSpec((1, bands, cells, LANES), lambda i, table: (i, 0, 0, 0)),
                HBM,
                HBM,
            ],
            scratch_shapes=[
                pltpu.VMEM((PROC * cells, hid), jnp.bfloat16),
                pltpu.VMEM((channels, PROC * cells), jnp.bfloat16),
                pltpu.VMEM((PROC * cells, hid), jnp.bfloat16),
                pltpu.VMEM((channels, PROC * cells), jnp.bfloat16),
                pltpu.VMEM((cells, head.shape[1]), jnp.bfloat16),
                pltpu.VMEM((cells, channels), jnp.float32),
                pltpu.VMEM((2,) + blocks.shape, jnp.bfloat16),
                pltpu.SemaphoreType.DMA((2,)),
            ],
        ),
        compiler_params=pltpu.CompilerParams(vmem_limit_bytes=32 * MIB),
        cost_estimate=cost(16.0),
        name="weight_grads",
    )(table, *streams, *consts)


def tap_grads(plan, first, last, table, source, depth_back, before):
    side, channels = source.shape[1], source.shape[3]
    bands = channels // LANES
    sums = (bands, KS * KS, 8, LANES)
    out = (plan.devices, DEPTH_ROWS, channels) if last else sums

    def items(array):
        shape = array.shape[1:]
        return pl.BlockSpec((1,) + shape, lambda i, table: (first + i,) + (0,) * len(shape))

    return pl.pallas_call(
        functools.partial(taps_kernel, plan, first, last),
        out_shape=jax.ShapeDtypeStruct(out, jnp.bfloat16 if last else jnp.float32),
        grid_spec=pltpu.PrefetchScalarGridSpec(
            num_scalar_prefetch=1,
            grid=(PROC // 2,),
            in_specs=[items(source), items(depth_back), whole(before.shape)],
            out_specs=pl.BlockSpec(out, lambda i, table: (0,) * len(out)),
            scratch_shapes=[
                pltpu.VMEM((bands, side, side + ROW_UNIT, LANES), jnp.float32),
                pltpu.VMEM(sums, jnp.float32),
                pltpu.VMEM((KS * KS + 7, channels), jnp.float32),
            ],
        ),
        compiler_params=pltpu.CompilerParams(vmem_limit_bytes=12 * MIB),
        cost_estimate=cost(4.0),
        name="tap_grads_" + str(first),
    )(table, source, depth_back, before)


def shifted(values, names, sizes, shift):
    count = math.prod(sizes)
    pairs = []
    for index in range(count):
        spot = []
        rest = index
        for size in reversed(sizes):
            spot.append(rest % size)
            rest //= size
        spot = spot[::-1]
        target = 0
        for at, step, size in zip(spot, shift, sizes):
            target = target * size + (at + step) % size
        pairs.append((index, target))
    return lax.ppermute(values, names, pairs)


def shifts(sizes):
    steps = [()]
    for size in sizes:
        steps = [step + (more,) for step in steps for more in range(size)]
    return steps


def exchange(values, names):
    return lax.all_to_all(values, names, split_axis=0, concat_axis=0, tiled=True)


def add_all(parts, kind=jnp.bfloat16):
    total = parts[0].astype(jnp.float32)
    for part in parts[1:]:
        total = total + part.astype(jnp.float32)
    return total.astype(kind)


def other_core(values):
    return shifted(values, ("core",), (2,), (1,))


def sum_axis(kept, sent, name, size, kind=jnp.bfloat16):
    return [kept] + [shifted(part, (name,), (size,), (step + 1,)) for step, part in enumerate(sent)]


def on_device(
    tile_maps,
    positions,
    counts,
    routing,
    depth_kernel,
    depth_bias,
    norm_gain,
    norm_shift,
    expand_weight,
    expand_bias,
    reduce_weight,
    reduce_bias,
    layer_scale,
    head_weight,
    slide_taps,
    slide_weight,
    slide_bias,
    cotangent,
):
    slides = lax.axis_size(DP)
    members = lax.axis_size(GROUP)
    my_device = lax.axis_index(ALL)
    slots, channels = tile_maps.shape[0], tile_maps.shape[3]
    devices, length, places = slides * members, slots * members, slots // slides
    plan = Plan(slides, members, channels, expand_weight.shape[1])

    raw = (
        norm_gain,
        norm_shift,
        layer_scale,
        reduce_bias,
        depth_bias,
        expand_bias,
        slide_bias,
    )
    packed, (table, small, vectors) = pack_tiles(
        counts, routing, tile_maps, positions, cotangent, raw, slides, places
    )

    def from_other(buffer, other):
        return lax.ppermute(buffer, DP, [(index, index ^ other) for index in range(slides)])

    from_core = from_other(packed[0], 1)
    arrived = []
    for rank in range(places):
        buffers = packed[1 + rank * (slides - 2) : 1 + (rank + 1) * (slides - 2)]
        if rank:
            buffers, from_core = lax.optimization_barrier((buffers, from_core))
        arrived.append([from_other(buffer, other + 2) for other, buffer in enumerate(buffers)])
    small, from_core = lax.optimization_barrier((small, from_core))
    smalls = [small] + [from_other(small, other) for other in range(1, slides)]

    consts = (depth_kernel, vectors, expand_weight, reduce_weight, head_weight)
    saved = forward_block(0, PROC, table, (tile_maps, from_core), consts, ())
    for rank in range(places):
        items = min(PROC, slides - 2)
        saved = forward_block(1 + rank, items, table, arrived[rank], consts, saved)
    section, tile_embed, unit, inv, hidden, slope, head_slope, source = saved
    rows = tile_rows(table, tile_embed, smalls, devices).astype(jnp.bfloat16)
    came = exchange(jnp.broadcast_to(rows, (devices,) + rows.shape[1:]), ALL)
    came = came.reshape(devices * PROC, rows.shape[2])
    filled = table[FILLED : FILLED + PROC] != 0
    tile_out = jnp.where(filled[:, None, None, None], section[:PROC], jnp.zeros((), jnp.bfloat16))
    came, tile_out = lax.optimization_barrier((came, tile_out))

    feature, embed_grad = slide_grads(
        length, members, table, came, slide_taps, slide_weight, vectors, smalls
    )
    depth_back, kept, sent = weight_grads(
        plan,
        table,
        embed_grad,
        (unit, inv, hidden, slope, head_slope),
        vectors,
        head_weight,
        expand_weight,
        reduce_weight,
    )

    names = ("g2", "y")
    size = plan.ys
    came = other_core(sent)
    none = jnp.zeros((channels // LANES, KS * KS, 8, LANES), jnp.float32)
    tap_sums = tap_grads(plan, 0, False, table, source, depth_back, none)
    came, tap_sums = lax.optimization_barrier((came, tap_sums))
    out = [
        [add_all([kept[kind, step], came[kind, step]]) for step in range(1, size)]
        for kind in range(2)
    ]
    stay = [add_all([kept[kind, 0], came[kind, 0]]) for kind in range(2)]
    out, tap_sums = lax.optimization_barrier((out, tap_sums))
    parts = [sum_axis(stay[kind], out[kind], names[kind], size) for kind in range(2)]
    taps = tap_grads(plan, PROC // 2, True, table, source, depth_back, tap_sums)
    out = [
        [add_all([part[step] for part in parts[kind]]) for step in range(1, size)]
        for kind in range(2)
    ]
    stay = [add_all([part[0] for part in parts[kind]]) for kind in range(2)]
    out, taps = lax.optimization_barrier((out, taps))
    taps = exchange(taps, ALL)
    parts = [sum_axis(stay[kind], out[kind], names[1 - kind], size) for kind in range(2)]
    both = jnp.concatenate([add_all(parts[0]), add_all(parts[1])], axis=1)
    total = add_all(
        sum_axis(both[0], [both[step] for step in range(1, plan.g1)], "g1", plan.g1), jnp.float32
    )
    reduce_share = total[: plan.reduce_rows]
    expand_share = total[plan.block_rows : plan.block_rows + plan.pieces * plan.expand_rows]
    expand_share = expand_share.reshape(plan.pieces, plan.expand_rows, channels).transpose(1, 0, 2)
    depth_share = lax.dynamic_slice(
        jnp.sum(taps.astype(jnp.float32), axis=0).reshape(-1),
        (my_device * plan.share % channels,),
        (plan.share,),
    )
    return (tile_out, feature, expand_share.reshape(-1), reduce_share.reshape(-1), depth_share)


def solution(mesh):
    slides, members = mesh.shape["dp"], mesh.shape["group"]
    fine = Mesh(mesh.devices.reshape(slides // 2, 2, 4, members // 4), ALL)
    return jax.shard_map(
        on_device,
        mesh=fine,
        in_specs=(
            P(ALL, None, None, None),
            P(None, ALL),
            P(DP),
            P(None, GROUP, None),
        )
        + (P(),) * 13
        + (P(DP, None),),
        out_specs=(
            P(ALL, None, None, None),
            P(DP, None),
            P(ALL),
            P(ALL),
            P(ALL),
        ),
        check_vma=False,
    )
```

```python
import functools
import math

import jax
import jax.numpy as jnp
from jax import lax
from jax.experimental import pallas as pl
from jax.experimental.pallas import tpu as pltpu
from jax.sharding import Mesh, PartitionSpec as P

E = 768
KS = 7
KERNEL_TAPS = 7
TILE_DILATION = 3
PROC = 4
DP = ("y", "core")
GROUP = ("g1", "g2")
ALL = DP + GROUP

EPSILON = 1e-06
HALF_ROOT = 0.7071067811865476
INV_ROOT_TAU = 0.3989422804014327
BELL_SCALE = -0.7213475204444817
LANES = 128
ROW_UNIT = 16
DEPTH_ROWS = 4
MIB = 1024 * 1024
PART = 32
WIDTH = 256
GAIN, SHIFT, SCALE, REDUCE_BIAS, DEPTH_BIAS, EXPAND_BIAS, SLIDE_BIAS = range(7)
VECTORS = 7
ERFC_P = 0.3275911
ERFC_A = (0.254829592, -0.284496736, 1.421413741, -1.453152027, 1.061405429)

HBM = pl.BlockSpec(memory_space=pl.ANY)
IN_HBM = pl.BlockSpec(memory_space=pltpu.HBM)
ROWS_AT, COLS_AT, COUNT_AT, SMALL = E, E + LANES, E + 2 * LANES, E + 3 * LANES


def whole(shape):
    return pl.BlockSpec(shape, lambda *_: (0,) * len(shape), pipeline_mode=pl.Buffered(1))


def gelu_and_slope(values):
    size = jnp.abs(values)
    divisor = 1.0 + (ERFC_P * HALF_ROOT) * size
    t = pl.reciprocal(divisor, approx=True)
    bell = jnp.exp2(values * (values * BELL_SCALE))
    poly = 0.5 * ERFC_A[4]
    for coefficient in ERFC_A[3::-1]:
        poly = poly * t + 0.5 * coefficient
    tail = poly * t * bell
    phi = jnp.where(values >= 0.0, 1.0 - tail, tail)
    return values * phi, phi + values * (INV_ROOT_TAU * bell)


def mix_cols(left_side, right_side):
    return lax.dot_general(
        left_side, right_side, (((1,), (1,)), ((), ())), preferred_element_type=jnp.float32
    )


def mix(left_side, right_side):
    return jnp.dot(left_side, right_side, preferred_element_type=jnp.float32)


FILLED, SLIDE, PLACE, CLASSES = 0, PROC, 2 * PROC, 3 * PROC
CLASS_SIZE = 1 + 3 * PROC


def class_field(kind, field, item=0):
    return CLASSES + kind * CLASS_SIZE + (1 + field * PROC + item if field >= 0 else 0)


SLOT, FROM, OWN = range(3)


def pack_kernel(slides, slots, places, counts_ref, route_ref, tiles_ref, pos_ref, cot_ref, *refs):
    inputs = (pos_ref, cot_ref) + refs[:VECTORS]
    refs = refs[VECTORS:]
    held_refs, refs = refs[-len(inputs) - 1 : -1], refs[: -len(inputs) - 1] + refs[-1:]
    send_refs, refs = refs[:-7], refs[-7:]
    table_ref, small_ref, vectors_ref, count_ref, slot_ref, sems, input_sems = refs
    loads = [
        pltpu.make_async_copy(ref, held, input_sems.at[index])
        for index, (ref, held) in enumerate(zip(inputs, held_refs))
    ]
    for load in loads:
        load.start()
    pos_ref, cot_ref = held_refs[:2]
    vector_refs = held_refs[2:]
    my_slide = lax.axis_index(DP)

    targets = [(0, rank, rank) for rank in range(places)]
    for rank in range(places):
        for other in range(2, slides):
            targets.append((1 + rank * (slides - 2) + other - 2, 0, other * places + rank))
    targets[:places] = [(0, rank, places + rank) for rank in range(places)]

    def copy_of(index, slot):
        buffer, row, _ = targets[index]
        return pltpu.make_async_copy(tiles_ref.at[slot], send_refs[buffer].at[row], sems.at[index])

    for index in range(slides):
        count_ref[index] = 0
    for index in range(slides * places):
        slot_ref[index] = -1

    def place_slot(slot, carry):
        entry = route_ref[my_slide, 0, slot]

        @pl.when(entry >= 0)
        def _send():
            other = lax.div(entry, PROC) ^ my_slide
            rank = count_ref[other]
            count_ref[other] = rank + 1
            slot_ref[other * places + rank] = slot

        return carry

    lax.fori_loop(0, slots, place_slot, 0)
    for index, (_, _, key) in enumerate(targets):
        slot = slot_ref[key]

        @pl.when(slot >= 0)
        def _start():
            copy_of(index, slot).start()

    for load in loads:
        load.wait()
    small_ref[:, 0:E] = cot_ref[...]
    for row, start in enumerate((ROWS_AT, COLS_AT)):
        small_ref[:, start : start + LANES] = jnp.zeros((1, LANES), jnp.float32)
        small_ref[:, start : start + slots] = pos_ref[row : row + 1, :].astype(jnp.float32)
    small_ref[:, COUNT_AT:SMALL] = jnp.full((1, LANES), counts_ref[0], jnp.int32).astype(jnp.float32)
    vectors_ref[...] = jnp.zeros(vectors_ref.shape, jnp.float32)
    for index, ref in enumerate(vector_refs):
        size = ref.shape[0]
        vectors_ref[index : index + 1, 0:size] = ref[...].reshape(1, size)

    kinds = 1 + places
    for field in range(CLASSES + kinds * CLASS_SIZE):
        table_ref[field] = 0
    for kind in range(kinds):
        for item in range(PROC):
            table_ref[class_field(kind, SLOT, item)] = PROC
    for other in range(slides):
        source = my_slide ^ other
        count_ref[0] = 0

        def take(slot, carry):
            entry = route_ref[source, 0, slot]
            proc = entry - my_slide * PROC

            @pl.when((proc >= 0) & (proc < PROC))
            def _take():
                rank = count_ref[0]
                count_ref[0] = rank + 1
                table_ref[FILLED + proc] = 1
                table_ref[SLIDE + proc] = source
                table_ref[PLACE + proc] = slot
                kind = 0 if other < 2 else 1 + rank
                base = CLASSES + kind * CLASS_SIZE
                item = table_ref[base]
                table_ref[base] = item + 1
                table_ref[base + 1 + SLOT * PROC + item] = proc
                if other == 0:
                    table_ref[base + 1 + FROM * PROC + item] = 0
                    table_ref[base + 1 + OWN * PROC + item] = slot
                else:
                    table_ref[base + 1 + FROM * PROC + item] = 1 + rank if other == 1 else other - 2

            return carry

        lax.fori_loop(0, slots, take, 0)
        if other == 0:
            own = table_ref[class_field(0, -1)]
            for item in range(1, PROC):

                @pl.when(item >= own)
                def _hold():
                    table_ref[class_field(0, OWN, item)] = table_ref[class_field(0, OWN, item - 1)]

    for kind in range(kinds):
        items = table_ref[class_field(kind, -1)]
        for item in range(1, PROC):

            @pl.when(item >= items)
            def _hold_slot():
                table_ref[class_field(kind, SLOT, item)] = table_ref[class_field(kind, SLOT, item - 1)]

    for index, (_, _, key) in enumerate(targets):

        @pl.when(slot_ref[key] >= 0)
        def _wait():
            copy_of(index, 0).wait()


def pack_tiles(counts, routing, tile_maps, positions, cotangent, vectors, slides, places):
    slots = tile_maps.shape[0]
    smem = pl.BlockSpec(memory_space=pltpu.SMEM)
    vmem = pl.BlockSpec(memory_space=pltpu.VMEM)
    buffers = 1 + places * (slides - 2)
    shapes = [places] + [1] * (buffers - 1)
    widest = max(vector.shape[0] for vector in vectors)
    inputs = (positions, cotangent) + vectors
    fixed = [pinned(x) for x in (tile_maps,) + inputs]
    outs = pl.pallas_call(
        functools.partial(pack_kernel, slides, slots, places),
        out_shape=tuple(
            jax.ShapeDtypeStruct((size,) + tile_maps.shape[1:], tile_maps.dtype) for size in shapes
        )
        + (
            jax.ShapeDtypeStruct((CLASSES + (1 + places) * CLASS_SIZE,), jnp.int32),
            jax.ShapeDtypeStruct((1, SMALL), jnp.float32),
            jax.ShapeDtypeStruct((8, widest), jnp.float32),
        ),
        in_specs=[smem, smem] + [IN_HBM] * len(fixed),
        out_specs=(vmem,) * buffers + (smem, vmem, vmem),
        scratch_shapes=[
            pltpu.SMEM((slides,), jnp.int32),
            pltpu.SMEM((slides * places,), jnp.int32),
            pltpu.SemaphoreType.DMA((slides * places,)),
        ]
        + [pltpu.VMEM(x.shape, x.dtype) for x in inputs]
        + [pltpu.SemaphoreType.DMA((len(inputs),))],
        compiler_params=pltpu.CompilerParams(vmem_limit_bytes=8 * MIB),
        name="pack_tiles",
    )(counts, routing, *fixed)
    return outs[:-3], outs[-3:]


def forward_kernel(kind, last, inputs, kept, table_ref, *refs):
    tile_refs, refs = refs[:inputs], refs[inputs:]
    taps_hbm, vectors_ref, expand_hbm, reduce_hbm, head_hbm = refs[:5]
    refs = refs[5 + (0 if kind == 0 else kept) :]
    out_hbms, refs = refs[:kept], refs[kept:]
    held, refs = refs[:kept], refs[kept:]
    taps_ref, expand_ref, reduce_ref, head_ref, padded, depth_out, normed, pre, load_sems = refs[:9]
    tile_sems, out_sems = refs[9:]
    out_s, embed_s, unit_s, inv_s, hidden_s, slope_s, head_slope_s, source_s = held
    items = table_ref[class_field(kind, -1)]
    side, channels = out_s.shape[1], out_s.shape[3]
    cells = side * side
    bands = channels // LANES
    low = ROW_UNIT // 2
    reach = KS // 2
    constants = [
        pltpu.make_async_copy(source, target, load_sems.at[index])
        for index, (source, target) in enumerate(
            (
                (taps_hbm, taps_ref),
                (expand_hbm, expand_ref),
                (reduce_hbm, reduce_ref),
                (head_hbm, head_ref),
            )
        )
    ]

    def tile_copy(ref, row, buffer):
        return pltpu.make_async_copy(ref.at[row], source_s.at[buffer], tile_sems.at[buffer])

    def load(item, buffer):
        origin = table_ref[class_field(kind, FROM) + item]
        place = 0
        for index, ref in enumerate(tile_refs):
            own = kind == 0 and index == 0
            for row in range(1 if own else ref.shape[0]):

                @pl.when(origin == place)
                def _load():
                    at = table_ref[class_field(kind, OWN) + item] if own else row
                    tile_copy(ref, at, buffer).start()

                place += 1

    def keep(part, slot, buffer):
        return pltpu.make_async_copy(
            held[part].at[buffer], out_hbms[part].at[slot], out_sems.at[part, buffer]
        )

    def wait_kept(buffer):
        for part in range(kept - 1):
            keep(part, 0, buffer).wait()

    def vector(index, lanes):
        return vectors_ref[index : index + 1, lanes]

    @pl.when(items > 0)
    def _first():
        load(0, 0)
        for copy in constants:
            copy.start()
        edge = jnp.zeros((side, low, LANES), jnp.float32)
        for band in range(bands):
            padded[band, :, 0:low, :] = edge
            padded[band, :, low + side :, :] = edge

    def one_item(item, carry):
        buffer = lax.rem(item, 2)
        slot = table_ref[class_field(kind, SLOT) + item]

        @pl.when(item >= 2)
        def _free():
            wait_kept(buffer)

        tile_copy(tile_refs[0], 0, buffer).wait()

        @pl.when(item == 0)
        def _taps():
            constants[0].wait()

        for band in range(bands):
            for at in range(side):
                padded[band, at, low : low + side, :] = source_s[
                    buffer, at, :, band * LANES : (band + 1) * LANES
                ].astype(jnp.float32)

        def convolve(band, carry):
            lanes = pl.ds(pl.multiple_of(band * LANES, LANES), LANES)
            bias = jnp.broadcast_to(vectors_ref[DEPTH_BIAS : DEPTH_BIAS + 1, lanes], (side, LANES))
            totals = [bias for _ in range(side)]
            for col in range(KS):
                start = low - reach + col
                weights = [
                    taps_ref[row * KS + col : row * KS + col + 1, lanes] for row in range(KS)
                ]
                for at in range(side):
                    line = padded[band, at, start : start + side, :]
                    for row in range(KS):
                        place = at - row + reach
                        if 0 <= place < side:
                            totals[place] = totals[place] + weights[row] * line
            for place in range(side):
                depth_out[band, place * side : (place + 1) * side, :] = totals[place]
            return carry

        lax.fori_loop(0, bands, convolve, 0)
        for start in range(0, cells, PART):
            rows = slice(start, start + PART)
            pieces = [depth_out[band, rows, :] for band in range(bands)]
            mean = jnp.sum(sum(pieces), axis=1, keepdims=True) * (1.0 / channels)
            pieces = [piece - mean for piece in pieces]
            var = jnp.sum(sum(p * p for p in pieces), axis=1, keepdims=True) * (1.0 / channels)
            inv = lax.rsqrt(var + EPSILON)
            inv_s[buffer, rows, :] = jnp.broadcast_to(inv, (PART, LANES))
            for band in range(bands):
                lanes = slice(band * LANES, (band + 1) * LANES)
                unit = pieces[band] * inv
                unit_s[buffer, rows, lanes] = unit
                normed[rows, lanes] = (unit * vector(GAIN, lanes) + vector(SHIFT, lanes)).astype(
                    jnp.bfloat16
                )

        @pl.when(item == 0)
        def _weights():
            for copy in constants[1:]:
                copy.wait()

        @pl.when(item + 1 < items)
        def _next():
            @pl.when(item >= 1)
            def _source_free():
                keep(kept - 1, 0, 1 - buffer).wait()

            load(item + 1, 1 - buffer)

        for part in (2, 3):
            keep(part, slot, buffer).start()
        for index, begin in enumerate(range(0, expand_ref.shape[1], WIDTH)):
            cols = slice(begin, begin + WIDTH)
            at = index % pre.shape[0]
            pre[at] = mix(normed[...], expand_ref[:, cols])
            for start in range(0, cells, PART):
                rows = slice(start, start + PART)
                act, slope = gelu_and_slope(pre[at, rows, :] + vector(EXPAND_BIAS, cols))
                hidden_s[buffer, rows, cols] = act.astype(jnp.bfloat16)
                slope_s[buffer, rows, cols] = slope.astype(jnp.bfloat16)
        for part in (4, 5):
            keep(part, slot, buffer).start()
        lanes = slice(0, channels)
        depth_rows = mix(hidden_s[buffer], reduce_ref[...])
        for at in range(side):
            rows = slice(at * side, (at + 1) * side)
            branch = vector(SCALE, lanes) * (depth_rows[rows] + vector(REDUCE_BIAS, lanes))
            line = (source_s[buffer, at].astype(jnp.float32) + branch).astype(jnp.bfloat16)
            normed[rows, :] = line
            out_s[buffer, at] = line
        for part in (0, 7):
            keep(part, slot, buffer).start()
        for index, begin in enumerate(range(0, head_ref.shape[1], WIDTH)):
            cols = slice(begin, begin + WIDTH)
            at = index % pre.shape[0]
            pre[at] = mix(normed[...], head_ref[:, cols])
            total = None
            for start in range(0, cells, PART):
                rows = slice(start, start + PART)
                act, slope = gelu_and_slope(pre[at, rows, :])
                head_slope_s[buffer, rows, cols] = slope.astype(jnp.bfloat16)
                folded = act[0:8]
                for piece in range(8, PART, 8):
                    folded = folded + act[piece : piece + 8]
                total = folded if total is None else total + folded
            mean = jnp.sum(total, axis=0, keepdims=True) * (1.0 / cells)
            embed_s[buffer, :, cols] = jnp.broadcast_to(mean, (8, WIDTH))
        for part in (1, 6):
            keep(part, slot, buffer).start()
        return carry

    lax.fori_loop(0, items, one_item, 0)
    for back in (1, 2):

        @pl.when(items >= back)
        def _drain():
            buffer = lax.rem(items - back, 2)
            for part in range(kept):
                keep(part, 0, buffer).wait()

    if last:
        out_s[0] = jnp.zeros(out_s.shape[1:], out_s.dtype)
        for proc in range(PROC):

            @pl.when(table_ref[FILLED + proc] == 0)
            def _empty():
                copy = keep(0, proc, 0)
                copy.start()
                copy.wait()


def pinned(array):
    return pltpu.with_memory_space_constraint(array, pltpu.HBM)


def forward_block(kind, last, table, tiles, taps, vectors, expand, reduce, head, before):
    side, channels = tiles[0].shape[1], tiles[0].shape[3]
    cells, hid, embed = side * side, expand.shape[1], head.shape[1]
    bands = channels // LANES
    outs = (
        ((side, side, channels), jnp.bfloat16),
        ((8, embed), jnp.float32),
        ((cells, channels), jnp.float32),
        ((cells, LANES), jnp.float32),
        ((cells, hid), jnp.bfloat16),
        ((cells, hid), jnp.bfloat16),
        ((cells, embed), jnp.bfloat16),
        ((side, side, channels), jnp.bfloat16),
    )
    smem = pl.BlockSpec(memory_space=pltpu.SMEM)
    vmem = pl.BlockSpec(memory_space=pltpu.VMEM)
    if kind == 0:
        tiles = (pinned(tiles[0]),) + tuple(tiles[1:])
    first = 1 + len(tiles) + 5
    return pl.pallas_call(
        functools.partial(forward_kernel, kind, last, len(tiles), len(outs)),
        out_shape=tuple(pltpu.HBM((PROC,) + shape, dtype) for shape, dtype in outs),
        in_specs=[smem]
        + [HBM] * len(tiles)
        + [IN_HBM, vmem, IN_HBM, IN_HBM, IN_HBM]
        + [IN_HBM] * len(before),
        out_specs=(IN_HBM,) * len(outs),
        scratch_shapes=[pltpu.VMEM((2,) + shape, dtype) for shape, dtype in outs]
        + [
            pltpu.VMEM(taps.shape, jnp.float32),
            pltpu.VMEM(expand.shape, jnp.bfloat16),
            pltpu.VMEM(reduce.shape, jnp.bfloat16),
            pltpu.VMEM(head.shape, jnp.bfloat16),
            pltpu.VMEM((bands, side, side + ROW_UNIT, LANES), jnp.float32),
            pltpu.VMEM((bands, cells, LANES), jnp.float32),
            pltpu.VMEM((cells, channels), jnp.bfloat16),
            pltpu.VMEM((3, cells, WIDTH), jnp.float32),
            pltpu.SemaphoreType.DMA((4,)),
            pltpu.SemaphoreType.DMA((2,)),
            pltpu.SemaphoreType.DMA((len(outs), 2)),
        ],
        input_output_aliases={first + index: index for index in range(len(before))},
        compiler_params=pltpu.CompilerParams(vmem_limit_bytes=24 * MIB),
        cost_estimate=cost(1.0),
        name="forward_block_" + str(kind),
    )(table, *tiles, pinned(taps), vectors, pinned(expand), pinned(reduce), pinned(head), *before)


def cost(micros):
    return pl.CostEstimate(flops=int(micros * 1e9), bytes_accessed=1024, transcendentals=0)


def rows_kernel(slides, table_ref, embed_ref, *refs):
    small_refs, (out_ref, rows_ref) = refs[:slides], refs[slides:]
    my_slide, my_member = lax.axis_index(DP), lax.axis_index(GROUP)
    devices = out_ref.shape[0]
    half = E // 2
    channel = lax.broadcasted_iota(jnp.int32, (1, E), 1)
    inner = jnp.where(channel < half, channel, channel - half)
    odd = lax.rem(inner, 2)
    frequency = jnp.exp((inner - odd).astype(jnp.float32) * (-math.log(10000.0) / half))
    phase = odd.astype(jnp.float32) * (0.5 * math.pi)
    lane = lax.broadcasted_iota(jnp.int32, (1, LANES), 1)
    for proc in range(PROC):
        filled = table_ref[FILLED + proc]
        slide = table_ref[SLIDE + proc]
        slot = table_ref[PLACE + proc]
        spots = []
        for start in (ROWS_AT, COLS_AT):
            held = small_refs[0][:, start : start + LANES]
            for other in range(1, slides):
                held = jnp.where(
                    (slide ^ my_slide) == other, small_refs[other][:, start : start + LANES], held
                )
            spots.append(jnp.sum(jnp.where(lane == slot, held, 0.0), axis=1, keepdims=True))
        spot = jnp.where(channel < half, spots[0], spots[1])
        embed = embed_ref[proc, 0:1, :].astype(jnp.bfloat16).astype(jnp.float32)
        row = jnp.where(filled != 0, embed + jnp.sin(spot * frequency + phase), 0.0)
        target = jnp.where(lane == 0, slide, jnp.where(lane == 1, slot, my_member))
        target = jnp.where(filled != 0, target, jnp.where(lane == 2, -1, 0))
        target = jnp.where(lane < 3, target, 0)
        rows_ref[proc : proc + 1, 0:E] = row
        rows_ref[proc : proc + 1, E:] = target.astype(jnp.float32)
    sent = rows_ref[...].astype(jnp.bfloat16)
    for device in range(devices):
        out_ref[device] = sent


def tile_rows(table, embeds, smalls, devices):
    smem = pl.BlockSpec(memory_space=pltpu.SMEM)
    vmem = pl.BlockSpec(memory_space=pltpu.VMEM)
    return pl.pallas_call(
        functools.partial(rows_kernel, len(smalls)),
        out_shape=jax.ShapeDtypeStruct((devices, PROC, E + LANES), jnp.bfloat16),
        in_specs=[smem] + [vmem] * (1 + len(smalls)),
        out_specs=vmem,
        scratch_shapes=[pltpu.VMEM((PROC, E + LANES), jnp.float32)],
        cost_estimate=cost(1.0),
        name="tile_rows",
    )(table, embeds, *smalls)


def slide_kernel(
    length,
    members,
    slides,
    table_ref,
    came_ref,
    taps_ref,
    matrix_ref,
    vectors_ref,
    *refs,
):
    small_refs = refs[:slides]
    feature_ref, grad_ref, rows, back, mixed, pre, grad_agg = refs[slides:]
    my_slide = lax.axis_index(DP)
    border = ROW_UNIT
    edge = jnp.zeros((border, rows.shape[2]), jnp.float32)
    reach = KERNEL_TAPS // 2
    blocks = [slice(start, start + WIDTH) for start in range(0, E, WIDTH)]
    lane = lax.broadcasted_iota(jnp.int32, (8, LANES), 1)
    scales = jnp.where(lane == 0, length, jnp.where(lane == 1, members, jnp.where(lane == 2, 1, 0)))
    target = mix_cols(scales.astype(jnp.float32).astype(jnp.bfloat16), came_ref[:, E:])[0:1, :]
    step = lax.broadcasted_iota(jnp.int32, (length, 1), 0).astype(jnp.float32)

    def dilate(ref, slide, direction, cols):
        total = ref[slide, border : border + length, cols]
        for tap in range(KERNEL_TAPS):
            start = border + direction * (tap - reach) * TILE_DILATION
            total = total + taps_ref[tap : tap + 1, cols] * ref[slide, start : start + length, cols]
        return total

    for other in range(slides):
        slide = my_slide ^ other
        small = small_refs[other]
        count = small[:, COUNT_AT : COUNT_AT + 1]
        here = step < count
        share = jnp.where(here, 1.0 / count, 0.0)
        first = lax.convert_element_type(slide * length, jnp.float32)
        pick = ((target - first) == step).astype(jnp.float32).astype(jnp.bfloat16)
        for ref in (rows, back):
            ref[slide, 0:border, :] = edge
            ref[slide, border + length :, :] = edge
        for cols in blocks:
            rows[slide, border : border + length, cols] = jnp.where(
                here, mix(pick, came_ref[:, cols]), 0.0
            )
            mixed[:, cols] = dilate(rows, slide, 1, cols).astype(jnp.bfloat16)
        for cols in blocks:
            pre[:, cols] = mix(mixed[...], matrix_ref[:, cols])
            total = None
            for start in range(0, length, PART):
                part = slice(start, start + PART)
                act, slope = gelu_and_slope(
                    pre[part, cols] + vectors_ref[SLIDE_BIAS : SLIDE_BIAS + 1, cols]
                )
                grad_agg[part, cols] = (small[:, cols] * share[part] * slope).astype(jnp.bfloat16)
                if other == 0:
                    piece = jnp.sum(act * share[part], axis=0, keepdims=True)
                    total = piece if total is None else total + piece
            if other == 0:
                feature_ref[:, cols] = total
        for cols in blocks:
            back[slide, border : border + length, cols] = mix_cols(
                grad_agg[...], matrix_ref[cols, :]
            )
            total = jnp.where(here, dilate(back, slide, -1, cols), 0.0)
            rows[slide, border : border + length, cols] = total.astype(jnp.bfloat16).astype(
                jnp.float32
            )
    my_member = lax.axis_index(GROUP)
    for proc in range(PROC):
        at = border + table_ref[PLACE + proc] * members + my_member
        row = rows[table_ref[SLIDE + proc], pl.ds(at, 1), :]
        grad_ref[proc] = jnp.where(table_ref[FILLED + proc] != 0, row, 0.0)


def slide_grads(length, members, table, came, taps, matrix, vectors, smalls):
    slides = len(smalls)
    smem = pl.BlockSpec(memory_space=pltpu.SMEM)
    vmem = pl.BlockSpec(memory_space=pltpu.VMEM)
    padded = (slides, length + 2 * ROW_UNIT, E)
    return pl.pallas_call(
        functools.partial(slide_kernel, length, members, slides),
        out_shape=(
            jax.ShapeDtypeStruct((1, E), jnp.float32),
            jax.ShapeDtypeStruct((PROC, 1, E), jnp.float32),
        ),
        in_specs=[smem] + [vmem] * (4 + slides),
        out_specs=(vmem, vmem),
        scratch_shapes=[
            pltpu.VMEM(padded, jnp.float32),
            pltpu.VMEM(padded, jnp.float32),
            pltpu.VMEM((length, E), jnp.bfloat16),
            pltpu.VMEM((length, E), jnp.float32),
            pltpu.VMEM((length, E), jnp.bfloat16),
        ],
        compiler_params=pltpu.CompilerParams(vmem_limit_bytes=24 * MIB),
        cost_estimate=cost(6.0),
        name="slide_grads",
    )(table, came, taps, matrix, vectors, *smalls)


class Plan:
    def __init__(self, slides, members, channels, hid):
        self.devices = slides * members
        self.ys, self.g1, self.g2 = slides // 2, 4, members // 4
        assert self.ys == self.g2
        self.channels = channels
        self.pieces = hid // channels
        self.expand_rows = channels // self.devices
        self.reduce_rows = hid // self.devices
        self.block_rows = -(-self.reduce_rows // ROW_UNIT) * ROW_UNIT
        self.share = KS * KS * channels // self.devices

    def spots(self):
        my_core, my_y = lax.axis_index("core"), lax.axis_index("y")
        my_z, my_x = lax.axis_index("g1"), lax.axis_index("g2")
        for device in range(self.devices):
            slide, member = divmod(device, self.g1 * self.g2)
            (y, core), (z, x) = divmod(slide, 2), divmod(member, self.g2)
            yield (
                my_core ^ core,
                lax.rem(y - my_y + self.ys, self.ys),
                lax.rem(x - my_x + self.g2, self.g2),
                lax.rem(z - my_z + self.g1, self.g1),
            )


def send_out(staged, sems, refs):
    copies = [
        pltpu.make_async_copy(staged.at[index], ref, sems.at[index]) for index, ref in enumerate(refs)
    ]
    for copy in copies:
        copy.start()
    for copy in copies:
        copy.wait()


def padded_block(block, rows):
    extra = rows - block.shape[0]
    if extra:
        block = jnp.concatenate([block, jnp.zeros((extra, block.shape[1]), block.dtype)], axis=0)
    return block.astype(jnp.bfloat16)


def weights_kernel(
    plan,
    table_ref,
    grad_ref,
    hidden_ref,
    head_slope_ref,
    slope_ref,
    unit_ref,
    vectors_ref,
    head_ref,
    reduce_ref,
    grad_pre_ref,
    keep_ref,
    send_ref,
    hidden_all,
    grad_mlp_all,
    grad_pre_all,
    normed_all,
    grad_head,
    eye_ref,
    staged,
    sems,
):
    step = pl.program_id(0)
    filled = table_ref[FILLED + step]
    cells, channels = unit_ref.shape[1:]
    rows_all = pl.ds(pl.multiple_of(step * cells, cells), cells)
    every = slice(0, channels)

    def vector(index, lanes):
        return vectors_ref[index : index + 1, lanes]

    @pl.when(step == 0)
    def _start():
        spot = lax.broadcasted_iota(jnp.int32, eye_ref.shape, 0)
        same = spot == lax.broadcasted_iota(jnp.int32, eye_ref.shape, 1)
        eye_ref[...] = same.astype(jnp.float32).astype(jnp.bfloat16)

    @pl.when(filled == 0)
    def _empty():
        for ref in (hidden_all, grad_pre_all):
            ref[rows_all, :] = jnp.zeros((cells, ref.shape[1]), jnp.bfloat16)
        for ref in (grad_mlp_all, normed_all):
            ref[:, rows_all] = jnp.zeros((channels, cells), jnp.bfloat16)

    @pl.when(filled != 0)
    def _work():
        for start in range(0, cells, PART):
            rows = slice(start, start + PART)
            grad_head[rows, :] = (
                (grad_ref[0] * (1.0 / cells)) * head_slope_ref[0, rows, :].astype(jnp.float32)
            ).astype(jnp.bfloat16)
        grad_mlp = (vector(SCALE, every) * mix_cols(grad_head[...], head_ref[...])).astype(
            jnp.bfloat16
        )
        grad_mlp_all[:, rows_all] = mix_cols(eye_ref[...], grad_mlp).astype(jnp.bfloat16)
        hidden_all[rows_all, :] = hidden_ref[0]
        for begin in range(0, reduce_ref.shape[0], WIDTH):
            cols = slice(begin, begin + WIDTH)
            grad_hidden = mix_cols(grad_mlp, reduce_ref[cols, :])
            grad_pre = (grad_hidden * slope_ref[0, :, cols].astype(jnp.float32)).astype(
                jnp.bfloat16
            )
            grad_pre_all[rows_all, cols] = grad_pre
            grad_pre_ref[0, :, cols] = grad_pre
        normed = (unit_ref[0] * vector(GAIN, every) + vector(SHIFT, every)).astype(jnp.bfloat16)
        normed_all[:, rows_all] = mix_cols(eye_ref[...], normed).astype(jnp.bfloat16)

    @pl.when(step == pl.num_programs(0) - 1)
    def _finish():
        spots = list(plan.spots())
        per_block = channels // plan.reduce_rows
        tall = plan.block_rows
        for index in range(plan.pieces):
            cols = slice(index * channels, (index + 1) * channels)
            total = mix(grad_mlp_all[...], hidden_all[:, cols]).astype(jnp.bfloat16)
            turned = mix_cols(eye_ref[...], total)
            for part in range(per_block):
                block = turned[part * plan.reduce_rows : (part + 1) * plan.reduce_rows]
                core, y, x, z = spots[index * per_block + part]
                staged[core, 0, x, y, z] = padded_block(block, tall)
        totals = []
        for quarter in range(plan.pieces):
            cols = slice(quarter * channels, (quarter + 1) * channels)
            totals.append(mix(normed_all[...], grad_pre_all[:, cols]))
        size = plan.expand_rows
        for device in range(plan.devices):
            rows = slice(device * size, (device + 1) * size)
            block = jnp.concatenate([total[rows] for total in totals], axis=0)
            core, y, x, z = spots[device]
            staged[core, 1, y, x, z] = padded_block(block, tall)
        send_out(staged, sems, (keep_ref, send_ref))


def taps_kernel(
    plan,
    first,
    last,
    table_ref,
    source_ref,
    grad_pre_ref,
    unit_ref,
    inv_ref,
    before_ref,
    vectors_ref,
    expand_ref,
    out_ref,
    padded,
    tap_sums,
    tap_rows,
    grad_norm,
    depth_back,
):
    step = pl.program_id(0)
    filled = table_ref[FILLED + first + step]
    side, channels = source_ref.shape[1], source_ref.shape[3]
    bands = channels // LANES
    low = ROW_UNIT // 2
    reach = KS // 2

    @pl.when(step == 0)
    def _start():
        if first:
            tap_sums[...] = before_ref[...]
        else:
            tap_sums[...] = jnp.zeros(tap_sums.shape, jnp.float32)

    @pl.when(filled != 0)
    def _work():
        cells = side * side
        gain = vectors_ref[GAIN : GAIN + 1, 0:channels]
        grad_norm[...] = mix_cols(grad_pre_ref[0], expand_ref[...])
        for start in range(0, cells, PART):
            rows = slice(start, start + PART)
            scaled = grad_norm[rows, :] * gain
            unit = unit_ref[0, rows, :]
            mean = jnp.sum(scaled, axis=1, keepdims=True) * (1.0 / channels)
            mean_unit = jnp.sum(scaled * unit, axis=1, keepdims=True) * (1.0 / channels)
            inv = inv_ref[0, rows, 0:1]
            for band in range(bands):
                lanes = slice(band * LANES, (band + 1) * LANES)
                depth_back[band, rows, :] = inv * (
                    scaled[:, lanes] - mean - unit[:, lanes] * mean_unit
                )
        edge = jnp.zeros((side, low, LANES), jnp.float32)
        for band in range(bands):
            lanes = slice(band * LANES, (band + 1) * LANES)
            padded[band, :, 0:low, :] = edge
            padded[band, :, low + side :, :] = edge
            for at in range(side):
                padded[band, at, low : low + side, :] = source_ref[0, at, :, lanes].astype(
                    jnp.float32
                )

        def taps_of(band, carry):
            for col in range(KS):
                start = low - reach + col
                sums = [None] * KS
                grads = {}
                for at in range(side):
                    line = padded[band, at, start : start + side, :]
                    for row in range(KS):
                        place = at - row + reach
                        if 0 <= place < side:
                            if place not in grads:
                                grads[place] = depth_back[
                                    band, place * side : (place + 1) * side, :
                                ]
                            term = line * grads[place]
                            sums[row] = term if sums[row] is None else sums[row] + term
                for row in range(KS):
                    total = sums[row]
                    folded = total[0:8, :]
                    for piece in range(8, side, 8):
                        folded = folded + total[piece : piece + 8, :]
                    tap_sums[band, row * KS + col] = tap_sums[band, row * KS + col] + folded
            return carry

        lax.fori_loop(0, bands, taps_of, 0)

    @pl.when(step == pl.num_programs(0) - 1)
    def _finish():
        if not last:
            out_ref[...] = tap_sums[...]
            return
        for band in range(bands):
            lanes = slice(band * LANES, (band + 1) * LANES)
            tap_rows[0 : KS * KS, lanes] = jnp.sum(tap_sums[band], axis=1)
            tap_rows[KS * KS :, lanes] = jnp.zeros((tap_rows.shape[0] - KS * KS, LANES), jnp.float32)
        for device in range(plan.devices):
            start = device * plan.share // channels
            out_ref[device] = tap_rows[start : start + DEPTH_ROWS, :].astype(jnp.bfloat16)


def per_slot(array):
    shape = array.shape[1:]
    return pl.BlockSpec((1,) + shape, lambda i, table: (i,) + (0,) * len(shape))


def weight_grads(plan, table, embed_grad, saved, vectors, head, reduce):
    unit, hidden, slope, head_slope = saved
    cells, channels = unit.shape[1:]
    hid = reduce.shape[0]
    streams = (embed_grad, hidden, head_slope, slope, unit)
    consts = (vectors, head, reduce)
    back = pltpu.HBM((PROC, cells, hid), jnp.bfloat16)
    blocks = jax.ShapeDtypeStruct(
        (2, plan.ys, plan.g2, plan.g1, plan.block_rows, channels), jnp.bfloat16
    )
    return pl.pallas_call(
        functools.partial(weights_kernel, plan),
        out_shape=(back, blocks, blocks),
        grid_spec=pltpu.PrefetchScalarGridSpec(
            num_scalar_prefetch=1,
            grid=(PROC,),
            in_specs=[per_slot(stream) for stream in streams]
            + [whole(const.shape) for const in consts],
            out_specs=[
                pl.BlockSpec((1, cells, hid), lambda i, table: (i, 0, 0)),
                HBM,
                HBM,
            ],
            scratch_shapes=[
                pltpu.VMEM((PROC * cells, hid), jnp.bfloat16),
                pltpu.VMEM((channels, PROC * cells), jnp.bfloat16),
                pltpu.VMEM((PROC * cells, hid), jnp.bfloat16),
                pltpu.VMEM((channels, PROC * cells), jnp.bfloat16),
                pltpu.VMEM((cells, head.shape[1]), jnp.bfloat16),
                pltpu.VMEM((channels, channels), jnp.bfloat16),
                pltpu.VMEM((2,) + blocks.shape, jnp.bfloat16),
                pltpu.SemaphoreType.DMA((2,)),
            ],
        ),
        compiler_params=pltpu.CompilerParams(vmem_limit_bytes=32 * MIB),
        cost_estimate=cost(16.0),
        name="weight_grads",
    )(table, *streams, *consts)


def tap_grads(plan, first, last, table, streams, before, vectors, expand):
    side, channels = streams[0].shape[1], streams[0].shape[3]
    bands = channels // LANES
    sums = (bands, KS * KS, 8, LANES)
    out = (plan.devices, DEPTH_ROWS, channels) if last else sums

    def items(array):
        shape = array.shape[1:]
        return pl.BlockSpec((1,) + shape, lambda i, table: (first + i,) + (0,) * len(shape))

    return pl.pallas_call(
        functools.partial(taps_kernel, plan, first, last),
        out_shape=jax.ShapeDtypeStruct(out, jnp.bfloat16 if last else jnp.float32),
        grid_spec=pltpu.PrefetchScalarGridSpec(
            num_scalar_prefetch=1,
            grid=(PROC // 2,),
            in_specs=[items(stream) for stream in streams]
            + [whole(before.shape), whole(vectors.shape), whole(expand.shape)],
            out_specs=pl.BlockSpec(out, lambda i, table: (0,) * len(out)),
            scratch_shapes=[
                pltpu.VMEM((bands, side, side + ROW_UNIT, LANES), jnp.float32),
                pltpu.VMEM(sums, jnp.float32),
                pltpu.VMEM((KS * KS + 7, channels), jnp.float32),
                pltpu.VMEM((side * side, channels), jnp.float32),
                pltpu.VMEM((bands, side * side, LANES), jnp.float32),
            ],
        ),
        compiler_params=pltpu.CompilerParams(vmem_limit_bytes=16 * MIB),
        cost_estimate=cost(4.0),
        name="tap_grads_" + str(first),
    )(table, *streams, before, vectors, expand)


def shifted(values, names, sizes, shift):
    count = math.prod(sizes)
    pairs = []
    for index in range(count):
        spot = []
        rest = index
        for size in reversed(sizes):
            spot.append(rest % size)
            rest //= size
        spot = spot[::-1]
        target = 0
        for at, step, size in zip(spot, shift, sizes):
            target = target * size + (at + step) % size
        pairs.append((index, target))
    return lax.ppermute(values, names, pairs)


def shifts(sizes):
    steps = [()]
    for size in sizes:
        steps = [step + (more,) for step in steps for more in range(size)]
    return steps


def exchange(values, names):
    return lax.all_to_all(values, names, split_axis=0, concat_axis=0, tiled=True)


def add_all(parts, kind=jnp.bfloat16):
    total = parts[0].astype(jnp.float32)
    for part in parts[1:]:
        total = total + part.astype(jnp.float32)
    return total.astype(kind)


def other_core(values):
    return shifted(values, ("core",), (2,), (1,))


def sum_axis(kept, sent, name, size, kind=jnp.bfloat16):
    return [kept] + [shifted(part, (name,), (size,), (step + 1,)) for step, part in enumerate(sent)]


def on_device(
    tile_maps,
    positions,
    counts,
    routing,
    depth_kernel,
    depth_bias,
    norm_gain,
    norm_shift,
    expand_weight,
    expand_bias,
    reduce_weight,
    reduce_bias,
    layer_scale,
    head_weight,
    slide_taps,
    slide_weight,
    slide_bias,
    cotangent,
):
    slides = lax.axis_size(DP)
    members = lax.axis_size(GROUP)
    my_device = lax.axis_index(ALL)
    slots, channels = tile_maps.shape[0], tile_maps.shape[3]
    devices, length, places = slides * members, slots * members, slots // slides
    plan = Plan(slides, members, channels, expand_weight.shape[1])

    raw = (
        norm_gain,
        norm_shift,
        layer_scale,
        reduce_bias,
        depth_bias,
        expand_bias,
        slide_bias,
    )
    packed, (table, small, vectors) = pack_tiles(
        counts, routing, tile_maps, positions, cotangent, raw, slides, places
    )

    def from_other(buffer, other):
        return lax.ppermute(buffer, DP, [(index, index ^ other) for index in range(slides)])

    from_core = from_other(packed[0], 1)
    arrived = []
    for rank in range(places):
        buffers = packed[1 + rank * (slides - 2) : 1 + (rank + 1) * (slides - 2)]
        if rank:
            buffers, from_core = lax.optimization_barrier((buffers, from_core))
        arrived.append([from_other(buffer, other + 2) for other, buffer in enumerate(buffers)])
    small, from_core = lax.optimization_barrier((small, from_core))
    smalls = [small] + [from_other(small, other) for other in range(1, slides)]

    consts = (depth_kernel, vectors, expand_weight, reduce_weight, head_weight)
    saved = forward_block(0, False, table, (tile_maps, from_core), *consts, ())
    for rank in range(places):
        saved = forward_block(1 + rank, rank + 1 == places, table, arrived[rank], *consts, saved)
    tile_out, tile_embed, unit, inv, hidden, slope, head_slope, source = saved
    came = exchange(tile_rows(table, tile_embed, smalls, devices), ALL)
    came = came.reshape(devices * PROC, came.shape[2])

    feature, embed_grad = slide_grads(
        length, members, table, came, slide_taps, slide_weight, vectors, smalls
    )
    grad_pre, kept, sent = weight_grads(
        plan,
        table,
        embed_grad,
        (unit, hidden, slope, head_slope),
        vectors,
        head_weight,
        reduce_weight,
    )
    streams = (source, pinned(grad_pre), unit, inv)

    names = ("g2", "y")
    size = plan.ys
    came = other_core(sent)
    none = jnp.zeros((channels // LANES, KS * KS, 8, LANES), jnp.float32)
    tap_sums = tap_grads(plan, 0, False, table, streams, none, vectors, expand_weight)
    came, tap_sums = lax.optimization_barrier((came, tap_sums))
    out = [
        [add_all([kept[kind, step], came[kind, step]]) for step in range(1, size)]
        for kind in range(2)
    ]
    stay = [add_all([kept[kind, 0], came[kind, 0]]) for kind in range(2)]
    out, tap_sums = lax.optimization_barrier((out, tap_sums))
    parts = [sum_axis(stay[kind], out[kind], names[kind], size) for kind in range(2)]
    taps = tap_grads(plan, PROC // 2, True, table, streams, tap_sums, vectors, expand_weight)
    out = [
        [add_all([part[step] for part in parts[kind]]) for step in range(1, size)]
        for kind in range(2)
    ]
    stay = [add_all([part[0] for part in parts[kind]]) for kind in range(2)]
    out, taps = lax.optimization_barrier((out, taps))
    taps = exchange(taps, ALL)
    parts = [sum_axis(stay[kind], out[kind], names[1 - kind], size) for kind in range(2)]
    both = jnp.concatenate([add_all(parts[0]), add_all(parts[1])], axis=1)
    total = add_all(
        sum_axis(both[0], [both[step] for step in range(1, plan.g1)], "g1", plan.g1), jnp.float32
    )
    reduce_share = total[: plan.reduce_rows]
    expand_share = total[plan.block_rows : plan.block_rows + plan.pieces * plan.expand_rows]
    expand_share = expand_share.reshape(plan.pieces, plan.expand_rows, channels).transpose(1, 0, 2)
    depth_share = lax.dynamic_slice(
        jnp.sum(taps.astype(jnp.float32), axis=0).reshape(-1),
        (my_device * plan.share % channels,),
        (plan.share,),
    )
    return (tile_out, feature, expand_share.reshape(-1), reduce_share.reshape(-1), depth_share)


def solution(mesh):
    slides, members = mesh.shape["dp"], mesh.shape["group"]
    fine = Mesh(mesh.devices.reshape(slides // 2, 2, 4, members // 4), ALL)
    return jax.shard_map(
        on_device,
        mesh=fine,
        in_specs=(
            P(ALL, None, None, None),
            P(None, ALL),
            P(DP),
            P(None, GROUP, None),
        )
        + (P(),) * 13
        + (P(DP, None),),
        out_specs=(
            P(ALL, None, None, None),
            P(DP, None),
            P(ALL),
            P(ALL),
            P(ALL),
        ),
        check_vma=False,
    )
```

```python
import functools
import math

import jax
import jax.numpy as jnp
from jax import lax
from jax.experimental import pallas as pl
from jax.experimental.pallas import tpu as pltpu
from jax.sharding import Mesh, PartitionSpec as P

E = 768
KS = 7
KERNEL_TAPS = 7
TILE_DILATION = 3
PROC = 4
DP = ("y", "core")
GROUP = ("g1", "g2")
ALL = DP + GROUP

EPSILON = 1e-06
HALF_ROOT = 0.7071067811865476
INV_ROOT_TAU = 0.3989422804014327
BELL_SCALE = -0.7213475204444817
LANES = 128
ROW_UNIT = 16
DEPTH_ROWS = 4
TAP_ROWS = 8
MIB = 1024 * 1024
PART = 32
WIDTH = 256
GAIN, SHIFT, SCALE, REDUCE_BIAS, DEPTH_BIAS, EXPAND_BIAS, SLIDE_BIAS = range(7)
VECTORS = 7
ERFC_P = 0.3275911
ERFC_A = (0.254829592, -0.284496736, 1.421413741, -1.453152027, 1.061405429)

HBM = pl.BlockSpec(memory_space=pl.ANY)
IN_HBM = pl.BlockSpec(memory_space=pltpu.HBM)
ROWS_AT, COLS_AT, COUNT_AT, SMALL = E, E + LANES, E + 2 * LANES, E + 3 * LANES
PIECES = 3


def whole(shape):
    return pl.BlockSpec(shape, lambda *_: (0,) * len(shape), pipeline_mode=pl.Buffered(1))


def gelu_and_slope(values):
    size = jnp.abs(values)
    divisor = 1.0 + (ERFC_P * HALF_ROOT) * size
    t = pl.reciprocal(divisor, approx=True)
    bell = jnp.exp2(values * (values * BELL_SCALE))
    poly = 0.5 * ERFC_A[4]
    for coefficient in ERFC_A[3::-1]:
        poly = poly * t + 0.5 * coefficient
    tail = poly * t * bell
    phi = jnp.where(values >= 0.0, 1.0 - tail, tail)
    return values * phi, phi + values * (INV_ROOT_TAU * bell)


def mix_cols(left_side, right_side):
    return lax.dot_general(
        left_side, right_side, (((1,), (1,)), ((), ())), preferred_element_type=jnp.float32
    )


def mix(left_side, right_side):
    return jnp.dot(left_side, right_side, preferred_element_type=jnp.float32)


FILLED, SLIDE, PLACE, CLASSES = 0, PROC, 2 * PROC, 3 * PROC
CLASS_SIZE = 1 + 3 * PROC


def class_field(kind, field, item=0):
    return CLASSES + kind * CLASS_SIZE + (1 + field * PROC + item if field >= 0 else 0)


SLOT, FROM, OWN = range(3)


def pack_kernel(slides, slots, places, counts_ref, route_ref, tiles_ref, pos_ref, cot_ref, *refs):
    inputs = (pos_ref, cot_ref) + refs[:VECTORS]
    refs = refs[VECTORS:]
    held_refs, refs = refs[-len(inputs) - 1 : -1], refs[: -len(inputs) - 1] + refs[-1:]
    send_refs, refs = refs[:-7], refs[-7:]
    table_ref, small_ref, vectors_ref, count_ref, slot_ref, sems, input_sems = refs
    loads = [
        pltpu.make_async_copy(ref, held, input_sems.at[index])
        for index, (ref, held) in enumerate(zip(inputs, held_refs))
    ]
    for load in loads:
        load.start()
    pos_ref, cot_ref = held_refs[:2]
    vector_refs = held_refs[2:]
    my_slide = lax.axis_index(DP)

    targets = [(0, rank, rank) for rank in range(places)]
    for rank in range(places):
        for other in range(2, slides):
            targets.append((1 + rank * (slides - 2) + other - 2, 0, other * places + rank))
    targets[:places] = [(0, rank, places + rank) for rank in range(places)]

    def copy_of(index, slot):
        buffer, row, _ = targets[index]
        side = tiles_ref.shape[1]
        lines = send_refs[buffer].at[pl.ds(row * side, side)]
        return pltpu.make_async_copy(tiles_ref.at[slot], lines, sems.at[index])

    for index in range(slides):
        count_ref[index] = 0
    for index in range(slides * places):
        slot_ref[index] = -1

    def place_slot(slot, carry):
        entry = route_ref[my_slide, 0, slot]

        @pl.when(entry >= 0)
        def _send():
            other = lax.div(entry, PROC) ^ my_slide
            rank = count_ref[other]
            count_ref[other] = rank + 1
            slot_ref[other * places + rank] = slot

        return carry

    lax.fori_loop(0, slots, place_slot, 0)
    for index, (_, _, key) in enumerate(targets):
        slot = slot_ref[key]

        @pl.when(slot >= 0)
        def _start():
            copy_of(index, slot).start()

    for load in loads:
        load.wait()
    small_ref[:, 0:E] = cot_ref[...]
    for row, start in enumerate((ROWS_AT, COLS_AT)):
        small_ref[:, start : start + LANES] = jnp.zeros((1, LANES), jnp.float32)
        small_ref[:, start : start + slots] = pos_ref[row : row + 1, :].astype(jnp.float32)
    small_ref[:, COUNT_AT:SMALL] = jnp.full((1, LANES), counts_ref[0], jnp.int32).astype(jnp.float32)
    channels = tiles_ref.shape[3]
    extra = []
    rest = small_ref[...]
    for piece in range(PIECES):
        part = rest.astype(jnp.bfloat16).astype(jnp.float32)
        rest = rest - part
        extra += [part[:, at : at + channels] for at in range(0, SMALL, channels)]
    extra.append(jnp.zeros((ROW_UNIT - len(extra), channels), jnp.float32))
    extra = jnp.concatenate(extra, axis=0).astype(jnp.bfloat16)
    for ref in send_refs[: slides - 1]:
        ref[ref.shape[0] - 1] = extra
    vectors_ref[...] = jnp.zeros(vectors_ref.shape, jnp.float32)
    for index, ref in enumerate(vector_refs):
        size = ref.shape[0]
        vectors_ref[index : index + 1, 0:size] = ref[...].reshape(1, size)

    kinds = 1 + places
    for field in range(CLASSES + kinds * CLASS_SIZE):
        table_ref[field] = 0
    for kind in range(kinds):
        for item in range(PROC):
            table_ref[class_field(kind, SLOT, item)] = PROC
    for other in range(slides):
        source = my_slide ^ other
        count_ref[0] = 0

        def take(slot, carry):
            entry = route_ref[source, 0, slot]
            proc = entry - my_slide * PROC

            @pl.when((proc >= 0) & (proc < PROC))
            def _take():
                rank = count_ref[0]
                count_ref[0] = rank + 1
                table_ref[FILLED + proc] = 1
                table_ref[SLIDE + proc] = source
                table_ref[PLACE + proc] = slot
                kind = 0 if other < 2 else 1 + rank
                base = CLASSES + kind * CLASS_SIZE
                item = table_ref[base]
                table_ref[base] = item + 1
                table_ref[base + 1 + SLOT * PROC + item] = proc
                if other == 0:
                    table_ref[base + 1 + FROM * PROC + item] = 0
                    table_ref[base + 1 + OWN * PROC + item] = slot
                else:
                    table_ref[base + 1 + FROM * PROC + item] = 1 + rank if other == 1 else other - 2

            return carry

        lax.fori_loop(0, slots, take, 0)
        if other == 0:
            own = table_ref[class_field(0, -1)]
            for item in range(1, PROC):

                @pl.when(item >= own)
                def _hold():
                    table_ref[class_field(0, OWN, item)] = table_ref[class_field(0, OWN, item - 1)]

    for kind in range(kinds):
        items = table_ref[class_field(kind, -1)]
        for item in range(1, PROC):

            @pl.when(item >= items)
            def _hold_slot():
                table_ref[class_field(kind, SLOT, item)] = table_ref[class_field(kind, SLOT, item - 1)]

    for index, (_, _, key) in enumerate(targets):

        @pl.when(slot_ref[key] >= 0)
        def _wait():
            copy_of(index, 0).wait()


def pack_tiles(counts, routing, tile_maps, positions, cotangent, vectors, slides, places):
    slots = tile_maps.shape[0]
    smem = pl.BlockSpec(memory_space=pltpu.SMEM)
    vmem = pl.BlockSpec(memory_space=pltpu.VMEM)
    buffers = 1 + places * (slides - 2)
    side = tile_maps.shape[1]
    shapes = [places * side + 1] + [side + 1] * (slides - 2) + [side] * (buffers - slides + 1)
    widest = max(vector.shape[0] for vector in vectors)
    inputs = (positions, cotangent) + vectors
    fixed = [pinned(x) for x in (tile_maps,) + inputs]
    outs = pl.pallas_call(
        functools.partial(pack_kernel, slides, slots, places),
        out_shape=tuple(
            jax.ShapeDtypeStruct((size,) + tile_maps.shape[2:], tile_maps.dtype) for size in shapes
        )
        + (
            jax.ShapeDtypeStruct((CLASSES + (1 + places) * CLASS_SIZE,), jnp.int32),
            jax.ShapeDtypeStruct((1, SMALL), jnp.float32),
            jax.ShapeDtypeStruct((8, widest), jnp.float32),
        ),
        in_specs=[smem, smem] + [IN_HBM] * len(fixed),
        out_specs=(vmem,) * buffers + (smem, vmem, vmem),
        scratch_shapes=[
            pltpu.SMEM((slides,), jnp.int32),
            pltpu.SMEM((slides * places,), jnp.int32),
            pltpu.SemaphoreType.DMA((slides * places,)),
        ]
        + [pltpu.VMEM(x.shape, x.dtype) for x in inputs]
        + [pltpu.SemaphoreType.DMA((len(inputs),))],
        compiler_params=pltpu.CompilerParams(vmem_limit_bytes=8 * MIB),
        name="pack_tiles",
    )(counts, routing, *fixed)
    return outs[:-3], outs[-3:]


def forward_kernel(kind, last, inputs, kept, table_ref, *refs):
    tile_refs, refs = refs[:inputs], refs[inputs:]
    taps_hbm, vectors_ref, expand_hbm, reduce_hbm, head_hbm = refs[:5]
    refs = refs[5 + (0 if kind == 0 else kept) :]
    out_hbms, refs = refs[:kept], refs[kept:]
    held, refs = refs[:kept], refs[kept:]
    taps_ref, expand_ref, reduce_ref, head_ref, padded, depth_out, normed, pre, load_sems = refs[:9]
    tile_sems, out_sems = refs[9:]
    out_s, embed_s, unit_s, inv_s, hidden_s, slope_s, head_slope_s, source_s = held
    items = table_ref[class_field(kind, -1)]
    side, channels = out_s.shape[1], out_s.shape[3]
    cells = side * side
    bands = channels // LANES
    low = ROW_UNIT // 2
    reach = KS // 2
    constants = [
        pltpu.make_async_copy(source, target, load_sems.at[index])
        for index, (source, target) in enumerate(
            (
                (taps_hbm, taps_ref),
                (expand_hbm, expand_ref),
                (reduce_hbm, reduce_ref),
                (head_hbm, head_ref),
            )
        )
    ]

    def tile_copy(ref, row, buffer):
        lines = ref.at[row] if len(ref.shape) == 4 else ref.at[pl.ds(row * side, side)]
        return pltpu.make_async_copy(lines, source_s.at[buffer], tile_sems.at[buffer])

    def load(item, buffer):
        origin = table_ref[class_field(kind, FROM) + item]
        place = 0
        for index, ref in enumerate(tile_refs):
            own = kind == 0 and index == 0
            for row in range(1 if own else ref.shape[0] // side):

                @pl.when(origin == place)
                def _load():
                    at = table_ref[class_field(kind, OWN) + item] if own else row
                    tile_copy(ref, at, buffer).start()

                place += 1

    def keep(part, slot, buffer):
        return pltpu.make_async_copy(
            held[part].at[buffer], out_hbms[part].at[slot], out_sems.at[part, buffer]
        )

    def wait_kept(buffer):
        for part in range(kept - 1):
            keep(part, 0, buffer).wait()

    def vector(index, lanes):
        return vectors_ref[index : index + 1, lanes]

    @pl.when(items > 0)
    def _first():
        load(0, 0)
        for copy in constants:
            copy.start()
        edge = jnp.zeros((side, low, LANES), jnp.float32)
        for band in range(bands):
            padded[band, :, 0:low, :] = edge
            padded[band, :, low + side :, :] = edge

    def one_item(item, carry):
        buffer = lax.rem(item, 2)
        slot = table_ref[class_field(kind, SLOT) + item]

        @pl.when(item >= 2)
        def _free():
            wait_kept(buffer)

        tile_copy(tile_refs[0], 0, buffer).wait()

        @pl.when(item == 0)
        def _taps():
            constants[0].wait()

        for band in range(bands):
            for at in range(side):
                padded[band, at, low : low + side, :] = source_s[
                    buffer, at, :, band * LANES : (band + 1) * LANES
                ].astype(jnp.float32)

        def convolve(band, carry):
            lanes = pl.ds(pl.multiple_of(band * LANES, LANES), LANES)
            bias = jnp.broadcast_to(vectors_ref[DEPTH_BIAS : DEPTH_BIAS + 1, lanes], (side, LANES))
            totals = [bias for _ in range(side)]
            for col in range(KS):
                start = low - reach + col
                weights = [
                    taps_ref[row * KS + col : row * KS + col + 1, lanes] for row in range(KS)
                ]
                for at in range(side):
                    line = padded[band, at, start : start + side, :]
                    for row in range(KS):
                        place = at - row + reach
                        if 0 <= place < side:
                            totals[place] = totals[place] + weights[row] * line
            for place in range(side):
                depth_out[band, place * side : (place + 1) * side, :] = totals[place]
            return carry

        lax.fori_loop(0, bands, convolve, 0)
        for start in range(0, cells, PART):
            rows = slice(start, start + PART)
            pieces = [depth_out[band, rows, :] for band in range(bands)]
            mean = jnp.sum(sum(pieces), axis=1, keepdims=True) * (1.0 / channels)
            pieces = [piece - mean for piece in pieces]
            var = jnp.sum(sum(p * p for p in pieces), axis=1, keepdims=True) * (1.0 / channels)
            inv = lax.rsqrt(var + EPSILON)
            inv_s[buffer, rows, :] = jnp.broadcast_to(inv, (PART, LANES))
            for band in range(bands):
                lanes = slice(band * LANES, (band + 1) * LANES)
                unit = pieces[band] * inv
                unit_s[buffer, rows, lanes] = unit
                normed[rows, lanes] = (unit * vector(GAIN, lanes) + vector(SHIFT, lanes)).astype(
                    jnp.bfloat16
                )

        @pl.when(item == 0)
        def _weights():
            for copy in constants[1:]:
                copy.wait()

        @pl.when(item + 1 < items)
        def _next():
            @pl.when(item >= 1)
            def _source_free():
                keep(kept - 1, 0, 1 - buffer).wait()

            load(item + 1, 1 - buffer)

        for part in (2, 3):
            keep(part, slot, buffer).start()
        for index, begin in enumerate(range(0, expand_ref.shape[1], WIDTH)):
            cols = slice(begin, begin + WIDTH)
            at = index % pre.shape[0]
            pre[at] = mix(normed[...], expand_ref[:, cols])
            for start in range(0, cells, PART):
                rows = slice(start, start + PART)
                act, slope = gelu_and_slope(pre[at, rows, :] + vector(EXPAND_BIAS, cols))
                hidden_s[buffer, rows, cols] = act.astype(jnp.bfloat16)
                slope_s[buffer, rows, cols] = slope.astype(jnp.bfloat16)
        for part in (4, 5):
            keep(part, slot, buffer).start()
        lanes = slice(0, channels)
        depth_rows = mix(hidden_s[buffer], reduce_ref[...])
        for at in range(side):
            rows = slice(at * side, (at + 1) * side)
            branch = vector(SCALE, lanes) * (depth_rows[rows] + vector(REDUCE_BIAS, lanes))
            line = (source_s[buffer, at].astype(jnp.float32) + branch).astype(jnp.bfloat16)
            normed[rows, :] = line
            out_s[buffer, at] = line
        for part in (0, 7):
            keep(part, slot, buffer).start()
        for index, begin in enumerate(range(0, head_ref.shape[1], WIDTH)):
            cols = slice(begin, begin + WIDTH)
            at = index % pre.shape[0]
            pre[at] = mix(normed[...], head_ref[:, cols])
            total = None
            for start in range(0, cells, PART):
                rows = slice(start, start + PART)
                act, slope = gelu_and_slope(pre[at, rows, :])
                head_slope_s[buffer, rows, cols] = slope.astype(jnp.bfloat16)
                folded = act[0:8]
                for piece in range(8, PART, 8):
                    folded = folded + act[piece : piece + 8]
                total = folded if total is None else total + folded
            mean = jnp.sum(total, axis=0, keepdims=True) * (1.0 / cells)
            embed_s[buffer, :, cols] = jnp.broadcast_to(mean, (8, WIDTH))
        for part in (1, 6):
            keep(part, slot, buffer).start()
        return carry

    lax.fori_loop(0, items, one_item, 0)
    for back in (1, 2):

        @pl.when(items >= back)
        def _drain():
            buffer = lax.rem(items - back, 2)
            for part in range(kept):
                keep(part, 0, buffer).wait()

    if last:
        filled = sum(table_ref[FILLED + proc] for proc in range(PROC))

        @pl.when(filled < PROC)
        def _zeros():
            for ref in held:
                ref[0] = jnp.zeros(ref.shape[1:], ref.dtype)

        for proc in range(PROC):

            @pl.when(table_ref[FILLED + proc] == 0)
            def _empty():
                for part in range(kept):
                    keep(part, proc, 0).start()
                wait_kept(0)
                keep(kept - 1, proc, 0).wait()


def pinned(array):
    return pltpu.with_memory_space_constraint(array, pltpu.HBM)


def forward_block(kind, last, table, tiles, taps, vectors, expand, reduce, head, before):
    side, channels = tiles[0].shape[-2:]
    cells, hid, embed = side * side, expand.shape[1], head.shape[1]
    bands = channels // LANES
    outs = (
        ((side, side, channels), jnp.bfloat16),
        ((8, embed), jnp.float32),
        ((cells, channels), jnp.float32),
        ((cells, LANES), jnp.float32),
        ((cells, hid), jnp.bfloat16),
        ((cells, hid), jnp.bfloat16),
        ((cells, embed), jnp.bfloat16),
        ((side, side, channels), jnp.bfloat16),
    )
    smem = pl.BlockSpec(memory_space=pltpu.SMEM)
    vmem = pl.BlockSpec(memory_space=pltpu.VMEM)
    if kind == 0:
        tiles = (pinned(tiles[0]),) + tuple(tiles[1:])
    first = 1 + len(tiles) + 5
    return pl.pallas_call(
        functools.partial(forward_kernel, kind, last, len(tiles), len(outs)),
        out_shape=tuple(pltpu.HBM((PROC,) + shape, dtype) for shape, dtype in outs),
        in_specs=[smem]
        + [HBM] * len(tiles)
        + [IN_HBM, vmem, IN_HBM, IN_HBM, IN_HBM]
        + [IN_HBM] * len(before),
        out_specs=(IN_HBM,) * len(outs),
        scratch_shapes=[pltpu.VMEM((2,) + shape, dtype) for shape, dtype in outs]
        + [
            pltpu.VMEM(taps.shape, jnp.float32),
            pltpu.VMEM(expand.shape, jnp.bfloat16),
            pltpu.VMEM(reduce.shape, jnp.bfloat16),
            pltpu.VMEM(head.shape, jnp.bfloat16),
            pltpu.VMEM((bands, side, side + ROW_UNIT, LANES), jnp.float32),
            pltpu.VMEM((bands, cells, LANES), jnp.float32),
            pltpu.VMEM((cells, channels), jnp.bfloat16),
            pltpu.VMEM((3, cells, WIDTH), jnp.float32),
            pltpu.SemaphoreType.DMA((4,)),
            pltpu.SemaphoreType.DMA((2,)),
            pltpu.SemaphoreType.DMA((len(outs), 2)),
        ],
        input_output_aliases={first + index: index for index in range(len(before))},
        compiler_params=pltpu.CompilerParams(vmem_limit_bytes=24 * MIB),
        cost_estimate=cost(1.0),
        name="forward_block_" + str(kind),
    )(table, *tiles, pinned(taps), vectors, pinned(expand), pinned(reduce), pinned(head), *before)


def cost(micros):
    return pl.CostEstimate(flops=int(micros * 1e9), bytes_accessed=1024, transcendentals=0)


def rows_kernel(slides, table_ref, embed_ref, small_ref, *refs):
    buffer_refs, (out_ref, smalls_ref, rows_ref, extra_ref, sems) = refs[: slides - 1], refs[slides - 1 :]
    copies = [
        pltpu.make_async_copy(ref.at[ref.shape[0] - 1], extra_ref.at[index], sems.at[index])
        for index, ref in enumerate(buffer_refs)
    ]
    for copy in copies:
        copy.start()
    my_slide, my_member = lax.axis_index(DP), lax.axis_index(GROUP)
    channels = extra_ref.shape[2]
    half = E // 2
    channel = lax.broadcasted_iota(jnp.int32, (1, E), 1)
    inner = jnp.where(channel < half, channel, channel - half)
    odd = lax.rem(inner, 2)
    frequency = jnp.exp((inner - odd).astype(jnp.float32) * (-math.log(10000.0) / half))
    phase = odd.astype(jnp.float32) * (0.5 * math.pi)
    lane = lax.broadcasted_iota(jnp.int32, (1, LANES), 1)
    smalls_ref[0] = small_ref[...]
    lines = SMALL // channels
    for index, copy in enumerate(copies):
        copy.wait()
        extra = extra_ref[index].astype(jnp.float32)
        for line in range(lines):
            total = extra[line : line + 1]
            for piece in range(1, PIECES):
                total = total + extra[piece * lines + line : piece * lines + line + 1]
            smalls_ref[1 + index, :, line * channels : (line + 1) * channels] = total
    for proc in range(PROC):
        filled = table_ref[FILLED + proc]
        slide = table_ref[SLIDE + proc]
        slot = table_ref[PLACE + proc]
        held = smalls_ref[0]
        for other in range(1, slides):
            held = jnp.where((slide ^ my_slide) == other, smalls_ref[other], held)
        spots = [
            jnp.sum(jnp.where(lane == slot, held[:, at : at + LANES], 0.0), axis=1, keepdims=True)
            for at in (ROWS_AT, COLS_AT)
        ]
        spot = jnp.where(channel < half, spots[0], spots[1])
        embed = embed_ref[proc, 0:1, :].astype(jnp.bfloat16).astype(jnp.float32)
        row = jnp.where(filled != 0, embed + jnp.sin(spot * frequency + phase), 0.0)
        target = jnp.where(lane == 0, slide, jnp.where(lane == 1, slot, my_member))
        target = jnp.where(filled != 0, target, jnp.where(lane == 2, -1, 0))
        target = jnp.where(lane < 3, target, 0)
        for copied in range(proc, ROW_UNIT, PROC):
            rows_ref[copied : copied + 1, 0:E] = row
            rows_ref[copied : copied + 1, E:] = target.astype(jnp.float32)
    sent = rows_ref[...].astype(jnp.bfloat16)
    for start in range(0, out_ref.shape[0], ROW_UNIT):
        out_ref[start : start + ROW_UNIT, :] = sent


def tile_rows(table, embeds, small, buffers, devices):
    smem = pl.BlockSpec(memory_space=pltpu.SMEM)
    vmem = pl.BlockSpec(memory_space=pltpu.VMEM)
    slides = 1 + len(buffers)
    return pl.pallas_call(
        functools.partial(rows_kernel, slides),
        out_shape=(
            jax.ShapeDtypeStruct((devices * PROC, E + LANES), jnp.bfloat16),
            jax.ShapeDtypeStruct((slides, 1, SMALL), jnp.float32),
        ),
        in_specs=[smem, vmem, vmem] + [HBM] * len(buffers),
        out_specs=(vmem, vmem),
        scratch_shapes=[
            pltpu.VMEM((ROW_UNIT, E + LANES), jnp.float32),
            pltpu.VMEM((len(buffers),) + buffers[0].shape[1:], jnp.bfloat16),
            pltpu.SemaphoreType.DMA((len(buffers),)),
        ],
        cost_estimate=cost(1.0),
        name="tile_rows",
    )(table, embeds, small, *buffers)


def slide_kernel(
    length,
    members,
    slides,
    table_ref,
    came_ref,
    taps_hbm,
    matrix_hbm,
    vectors_ref,
    smalls_ref,
    feature_ref,
    grad_ref,
    rows,
    back,
    mixed,
    pre,
    grad_agg,
    taps_ref,
    matrix_ref,
    sems,
):
    loads = [
        pltpu.make_async_copy(taps_hbm, taps_ref, sems.at[0]),
        pltpu.make_async_copy(matrix_hbm, matrix_ref, sems.at[1]),
    ]
    for load in loads:
        load.start()
    my_slide = lax.axis_index(DP)
    border = ROW_UNIT
    edge = jnp.zeros((border, rows.shape[2]), jnp.float32)
    reach = KERNEL_TAPS // 2
    blocks = [slice(start, start + WIDTH) for start in range(0, E, WIDTH)]
    lane = lax.broadcasted_iota(jnp.int32, (8, LANES), 1)
    scales = jnp.where(lane == 0, length, jnp.where(lane == 1, members, jnp.where(lane == 2, 1, 0)))
    target = mix_cols(scales.astype(jnp.float32).astype(jnp.bfloat16), came_ref[:, E:])[0:1, :]
    step = lax.broadcasted_iota(jnp.int32, (length, 1), 0).astype(jnp.float32)

    def dilate(ref, slide, direction, cols):
        total = ref[slide, border : border + length, cols]
        for tap in range(KERNEL_TAPS):
            start = border + direction * (tap - reach) * TILE_DILATION
            total = total + taps_ref[tap : tap + 1, cols] * ref[slide, start : start + length, cols]
        return total

    for other in range(slides):
        slide = my_slide ^ other
        small = smalls_ref[other]
        count = small[:, COUNT_AT : COUNT_AT + 1]
        here = step < count
        share = jnp.where(here, 1.0 / count, 0.0)
        first = lax.convert_element_type(slide * length, jnp.float32)
        pick = ((target - first) == step).astype(jnp.float32).astype(jnp.bfloat16)
        for ref in (rows, back):
            ref[slide, 0:border, :] = edge
            ref[slide, border + length :, :] = edge
        if other == 0:
            loads[0].wait()
        for cols in blocks:
            rows[slide, border : border + length, cols] = jnp.where(
                here, mix(pick, came_ref[:, cols]), 0.0
            )
            mixed[:, cols] = dilate(rows, slide, 1, cols).astype(jnp.bfloat16)
        if other == 0:
            loads[1].wait()
        for cols in blocks:
            pre[:, cols] = mix(mixed[...], matrix_ref[:, cols])
            total = None
            for start in range(0, length, PART):
                part = slice(start, start + PART)
                act, slope = gelu_and_slope(
                    pre[part, cols] + vectors_ref[SLIDE_BIAS : SLIDE_BIAS + 1, cols]
                )
                grad_agg[part, cols] = (small[:, cols] * share[part] * slope).astype(jnp.bfloat16)
                if other == 0:
                    piece = jnp.sum(act * share[part], axis=0, keepdims=True)
                    total = piece if total is None else total + piece
            if other == 0:
                feature_ref[:, cols] = total
        for cols in blocks:
            back[slide, border : border + length, cols] = mix_cols(
                grad_agg[...], matrix_ref[cols, :]
            )
            total = jnp.where(here, dilate(back, slide, -1, cols), 0.0)
            rows[slide, border : border + length, cols] = total.astype(jnp.bfloat16).astype(
                jnp.float32
            )
    my_member = lax.axis_index(GROUP)
    for proc in range(PROC):
        at = border + table_ref[PLACE + proc] * members + my_member
        row = rows[table_ref[SLIDE + proc], pl.ds(at, 1), :]
        grad_ref[proc] = jnp.where(table_ref[FILLED + proc] != 0, row, 0.0)


def slide_grads(length, members, table, came, taps, matrix, vectors, smalls):
    slides = smalls.shape[0]
    smem = pl.BlockSpec(memory_space=pltpu.SMEM)
    vmem = pl.BlockSpec(memory_space=pltpu.VMEM)
    padded = (slides, length + 2 * ROW_UNIT, E)
    return pl.pallas_call(
        functools.partial(slide_kernel, length, members, slides),
        out_shape=(
            jax.ShapeDtypeStruct((1, E), jnp.float32),
            jax.ShapeDtypeStruct((PROC, 1, E), jnp.float32),
        ),
        in_specs=[smem, vmem, IN_HBM, IN_HBM, vmem, vmem],
        out_specs=(vmem, vmem),
        scratch_shapes=[
            pltpu.VMEM(padded, jnp.float32),
            pltpu.VMEM(padded, jnp.float32),
            pltpu.VMEM((length, E), jnp.bfloat16),
            pltpu.VMEM((length, E), jnp.float32),
            pltpu.VMEM((length, E), jnp.bfloat16),
            pltpu.VMEM(taps.shape, jnp.float32),
            pltpu.VMEM(matrix.shape, jnp.bfloat16),
            pltpu.SemaphoreType.DMA((2,)),
        ],
        compiler_params=pltpu.CompilerParams(vmem_limit_bytes=24 * MIB),
        cost_estimate=cost(6.0),
        name="slide_grads",
    )(table, came, pinned(taps), pinned(matrix), vectors, smalls)


class Plan:
    def __init__(self, slides, members, channels, hid):
        self.devices = slides * members
        self.ys, self.g1, self.g2 = slides // 2, 4, members // 4
        assert self.ys == self.g2
        self.channels = channels
        self.pieces = hid // channels
        self.expand_rows = channels // self.devices
        self.reduce_rows = hid // self.devices
        self.block_rows = -(-self.reduce_rows // ROW_UNIT) * ROW_UNIT
        self.share = KS * KS * channels // self.devices

    def spots(self):
        my_core, my_y = lax.axis_index("core"), lax.axis_index("y")
        my_z, my_x = lax.axis_index("g1"), lax.axis_index("g2")
        for device in range(self.devices):
            slide, member = divmod(device, self.g1 * self.g2)
            (y, core), (z, x) = divmod(slide, 2), divmod(member, self.g2)
            yield (
                my_core ^ core,
                lax.rem(y - my_y + self.ys, self.ys),
                lax.rem(x - my_x + self.g2, self.g2),
                lax.rem(z - my_z + self.g1, self.g1),
            )


def send_out(staged, sems, refs):
    copies = [
        pltpu.make_async_copy(staged.at[index], ref, sems.at[index]) for index, ref in enumerate(refs)
    ]
    for copy in copies:
        copy.start()
    for copy in copies:
        copy.wait()


def padded_block(block, rows):
    extra = rows - block.shape[0]
    if extra:
        block = jnp.concatenate([block, jnp.zeros((extra, block.shape[1]), block.dtype)], axis=0)
    return block.astype(jnp.bfloat16)


def weights_kernel(
    plan,
    grad_ref,
    hidden_ref,
    head_slope_ref,
    slope_ref,
    unit_ref,
    vectors_ref,
    head_ref,
    reduce_ref,
    grad_pre_hbm,
    keep_ref,
    send_ref,
    grad_pre,
    turned,
    normed,
    grad_head,
    eye_ref,
    staged,
    sems,
    pre_sems,
):
    cells, channels = unit_ref.shape[1:]
    hid = reduce_ref.shape[0]
    every = slice(0, channels)

    def vector(index, lanes):
        return vectors_ref[index : index + 1, lanes]

    spot = lax.broadcasted_iota(jnp.int32, eye_ref.shape, 0)
    same = spot == lax.broadcasted_iota(jnp.int32, eye_ref.shape, 1)
    eye_ref[...] = same.astype(jnp.float32).astype(jnp.bfloat16)

    def one_slot(slot, carry):
        rows_all = pl.ds(pl.multiple_of(slot * cells, cells), cells)
        row = grad_ref[slot] * (1.0 / cells)
        for start in range(0, cells, PART):
            rows = slice(start, start + PART)
            grad_head[rows, :] = (row * head_slope_ref[slot, rows, :].astype(jnp.float32)).astype(
                jnp.bfloat16
            )
            normed[rows, :] = (
                unit_ref[slot, rows, :] * vector(GAIN, every) + vector(SHIFT, every)
            ).astype(jnp.bfloat16)
        grad_mlp = (vector(SCALE, every) * mix_cols(grad_head[...], head_ref[...])).astype(
            jnp.bfloat16
        )
        turned[0, :, rows_all] = mix_cols(eye_ref[...], grad_mlp).astype(jnp.bfloat16)
        turned[1, :, rows_all] = mix_cols(eye_ref[...], normed[...]).astype(jnp.bfloat16)
        for begin in range(0, hid, WIDTH):
            cols = slice(begin, begin + WIDTH)
            grad_hidden = mix_cols(grad_mlp, reduce_ref[cols, :])
            grad_pre[rows_all, cols] = (
                grad_hidden * slope_ref[slot, :, cols].astype(jnp.float32)
            ).astype(jnp.bfloat16)
        return carry

    lax.fori_loop(0, PROC, one_slot, 0)
    writes = [
        pltpu.make_async_copy(
            grad_pre.at[pl.ds(slot * cells, cells)], grad_pre_hbm.at[slot], pre_sems.at[slot]
        )
        for slot in range(PROC)
    ]
    for write in writes:
        write.start()
    spots = list(plan.spots())
    per_block = channels // plan.reduce_rows
    tall = plan.block_rows
    for index in range(plan.pieces):
        cols = slice(index * channels, (index + 1) * channels)
        total = mix(turned[0], hidden_ref[:, cols]).astype(jnp.bfloat16)
        back = mix_cols(eye_ref[...], total)
        for part in range(per_block):
            block = back[part * plan.reduce_rows : (part + 1) * plan.reduce_rows]
            core, y, x, z = spots[index * per_block + part]
            staged[core, 0, x, y, z] = padded_block(block, tall)
    totals = []
    for quarter in range(plan.pieces):
        cols = slice(quarter * channels, (quarter + 1) * channels)
        totals.append(mix(turned[1], grad_pre[:, cols]))
    size = plan.expand_rows
    for device in range(plan.devices):
        rows = slice(device * size, (device + 1) * size)
        block = jnp.concatenate([total[rows] for total in totals], axis=0)
        core, y, x, z = spots[device]
        staged[core, 1, y, x, z] = padded_block(block, tall)
    send_out(staged, sems, (keep_ref, send_ref))
    for write in writes:
        write.wait()


def taps_kernel(
    plan,
    first,
    last,
    table_ref,
    source_ref,
    grad_pre_ref,
    unit_ref,
    inv_ref,
    before_ref,
    vectors_ref,
    expand_ref,
    out_ref,
    padded,
    tap_sums,
    tap_rows,
    grad_norm,
    depth_back,
):
    step = pl.program_id(0)
    filled = table_ref[FILLED + first + step]
    side, channels = source_ref.shape[1], source_ref.shape[3]
    bands = channels // LANES
    low = ROW_UNIT // 2
    reach = KS // 2

    @pl.when(step == 0)
    def _start():
        if first:
            tap_sums[...] = before_ref[...]
        else:
            tap_sums[...] = jnp.zeros(tap_sums.shape, jnp.float32)

    @pl.when(filled != 0)
    def _work():
        cells = side * side
        gain = vectors_ref[GAIN : GAIN + 1, 0:channels]
        grad_norm[...] = mix_cols(grad_pre_ref[0], expand_ref[...])
        for start in range(0, cells, PART):
            rows = slice(start, start + PART)
            scaled = grad_norm[rows, :] * gain
            unit = unit_ref[0, rows, :]
            mean = jnp.sum(scaled, axis=1, keepdims=True) * (1.0 / channels)
            mean_unit = jnp.sum(scaled * unit, axis=1, keepdims=True) * (1.0 / channels)
            inv = inv_ref[0, rows, 0:1]
            for band in range(bands):
                lanes = slice(band * LANES, (band + 1) * LANES)
                depth_back[band, rows, :] = inv * (
                    scaled[:, lanes] - mean - unit[:, lanes] * mean_unit
                )
        edge = jnp.zeros((side, low, LANES), jnp.float32)
        for band in range(bands):
            lanes = slice(band * LANES, (band + 1) * LANES)
            padded[band, :, 0:low, :] = edge
            padded[band, :, low + side :, :] = edge
            for at in range(side):
                padded[band, at, low : low + side, :] = source_ref[0, at, :, lanes].astype(
                    jnp.float32
                )

        def taps_of(band, carry):
            for col in range(KS):
                start = low - reach + col
                sums = [None] * KS
                grads = {}
                for at in range(side):
                    line = padded[band, at, start : start + side, :]
                    for row in range(KS):
                        place = at - row + reach
                        if 0 <= place < side:
                            if place not in grads:
                                grads[place] = depth_back[
                                    band, place * side : (place + 1) * side, :
                                ]
                            term = line * grads[place]
                            sums[row] = term if sums[row] is None else sums[row] + term
                for row in range(KS):
                    total = sums[row]
                    folded = total[0:8, :]
                    for piece in range(8, side, 8):
                        folded = folded + total[piece : piece + 8, :]
                    tap_sums[band, row * KS + col] = tap_sums[band, row * KS + col] + folded
            return carry

        lax.fori_loop(0, bands, taps_of, 0)

    @pl.when(step == pl.num_programs(0) - 1)
    def _finish():
        if not last:
            out_ref[...] = tap_sums[...]
            return
        for band in range(bands):
            lanes = slice(band * LANES, (band + 1) * LANES)
            tap_rows[0 : KS * KS, lanes] = jnp.sum(tap_sums[band], axis=1)
            tap_rows[KS * KS :, lanes] = jnp.zeros((tap_rows.shape[0] - KS * KS, LANES), jnp.float32)
        my_z = lax.axis_index("g1")
        for part in range(2 * plan.ys * plan.g2):
            cross, core = divmod(part, 2)
            y, x = divmod(cross, plan.g2)
            for z in range(plan.g1):
                away = lax.rem(z - my_z + plan.g1, plan.g1)
                device = ((y * 2 + core) * plan.g1 + z) * plan.g2 + x
                start = device * plan.share // channels
                out_ref[part, away] = tap_rows[start : start + TAP_ROWS, :]


def per_slot(array):
    shape = array.shape[1:]
    return pl.BlockSpec((1,) + shape, lambda i, table: (i,) + (0,) * len(shape))


def weight_grads(plan, embed_grad, saved, vectors, head, reduce):
    unit, hidden, slope, head_slope = saved
    cells, channels = unit.shape[1:]
    hid = reduce.shape[0]
    vmem = pl.BlockSpec(memory_space=pltpu.VMEM)
    blocks = jax.ShapeDtypeStruct(
        (2, plan.ys, plan.g2, plan.g1, plan.block_rows, channels), jnp.bfloat16
    )
    return pl.pallas_call(
        functools.partial(weights_kernel, plan),
        out_shape=(pltpu.HBM((PROC, cells, hid), jnp.bfloat16), blocks, blocks),
        in_specs=[vmem] * 8,
        out_specs=(IN_HBM, HBM, HBM),
        scratch_shapes=[
            pltpu.VMEM((PROC * cells, hid), jnp.bfloat16),
            pltpu.VMEM((2, channels, PROC * cells), jnp.bfloat16),
            pltpu.VMEM((cells, channels), jnp.bfloat16),
            pltpu.VMEM((cells, head.shape[1]), jnp.bfloat16),
            pltpu.VMEM((channels, channels), jnp.bfloat16),
            pltpu.VMEM((2,) + blocks.shape, jnp.bfloat16),
            pltpu.SemaphoreType.DMA((2,)),
            pltpu.SemaphoreType.DMA((PROC,)),
        ],
        compiler_params=pltpu.CompilerParams(vmem_limit_bytes=36 * MIB),
        cost_estimate=cost(12.0),
        name="weight_grads",
    )(embed_grad, hidden.reshape(PROC * cells, hid), head_slope, slope, unit, vectors, head, reduce)


def tap_grads(plan, first, last, table, streams, before, vectors, expand):
    side, channels = streams[0].shape[1], streams[0].shape[3]
    bands = channels // LANES
    sums = (bands, KS * KS, 8, LANES)
    out = (2 * plan.ys * plan.g2, plan.g1, TAP_ROWS, channels) if last else sums

    def items(array):
        shape = array.shape[1:]
        return pl.BlockSpec((1,) + shape, lambda i, table: (first + i,) + (0,) * len(shape))

    return pl.pallas_call(
        functools.partial(taps_kernel, plan, first, last),
        out_shape=jax.ShapeDtypeStruct(out, jnp.float32),
        grid_spec=pltpu.PrefetchScalarGridSpec(
            num_scalar_prefetch=1,
            grid=(PROC // 2,),
            in_specs=[items(stream) for stream in streams]
            + [whole(before.shape), whole(vectors.shape), whole(expand.shape)],
            out_specs=pl.BlockSpec(out, lambda i, table: (0,) * len(out)),
            scratch_shapes=[
                pltpu.VMEM((bands, side, side + ROW_UNIT, LANES), jnp.float32),
                pltpu.VMEM(sums, jnp.float32),
                pltpu.VMEM((KS * KS + 7, channels), jnp.float32),
                pltpu.VMEM((side * side, channels), jnp.float32),
                pltpu.VMEM((bands, side * side, LANES), jnp.float32),
            ],
        ),
        compiler_params=pltpu.CompilerParams(vmem_limit_bytes=16 * MIB),
        cost_estimate=cost(4.0),
        name="tap_grads_" + str(first),
    )(table, *streams, before, vectors, expand)


def shifted(values, names, sizes, shift):
    count = math.prod(sizes)
    pairs = []
    for index in range(count):
        spot = []
        rest = index
        for size in reversed(sizes):
            spot.append(rest % size)
            rest //= size
        spot = spot[::-1]
        target = 0
        for at, step, size in zip(spot, shift, sizes):
            target = target * size + (at + step) % size
        pairs.append((index, target))
    return lax.ppermute(values, names, pairs)


def shifts(sizes):
    steps = [()]
    for size in sizes:
        steps = [step + (more,) for step in steps for more in range(size)]
    return steps


def exchange(values, names):
    return lax.all_to_all(values, names, split_axis=0, concat_axis=0, tiled=True)


def add_all(parts, kind=jnp.bfloat16):
    total = parts[0].astype(jnp.float32)
    for part in parts[1:]:
        total = total + part.astype(jnp.float32)
    return total.astype(kind)


def other_core(values):
    return shifted(values, ("core",), (2,), (1,))


def sum_axis(kept, sent, name, size, kind=jnp.bfloat16):
    return [kept] + [shifted(part, (name,), (size,), (step + 1,)) for step, part in enumerate(sent)]


def on_device(
    tile_maps,
    positions,
    counts,
    routing,
    depth_kernel,
    depth_bias,
    norm_gain,
    norm_shift,
    expand_weight,
    expand_bias,
    reduce_weight,
    reduce_bias,
    layer_scale,
    head_weight,
    slide_taps,
    slide_weight,
    slide_bias,
    cotangent,
):
    slides = lax.axis_size(DP)
    members = lax.axis_size(GROUP)
    my_device = lax.axis_index(ALL)
    slots, channels = tile_maps.shape[0], tile_maps.shape[3]
    devices, length, places = slides * members, slots * members, slots // slides
    plan = Plan(slides, members, channels, expand_weight.shape[1])

    raw = (
        norm_gain,
        norm_shift,
        layer_scale,
        reduce_bias,
        depth_bias,
        expand_bias,
        slide_bias,
    )
    packed, (table, small, vectors) = pack_tiles(
        counts, routing, tile_maps, positions, cotangent, raw, slides, places
    )

    def from_other(buffer, other):
        return lax.ppermute(buffer, DP, [(index, index ^ other) for index in range(slides)])

    from_core = from_other(packed[0], 1)
    arrived = []
    for rank in range(places):
        buffers = packed[1 + rank * (slides - 2) : 1 + (rank + 1) * (slides - 2)]
        if rank:
            buffers, from_core = lax.optimization_barrier((buffers, from_core))
        arrived.append([from_other(buffer, other + 2) for other, buffer in enumerate(buffers)])

    consts = (depth_kernel, vectors, expand_weight, reduce_weight, head_weight)
    saved = forward_block(0, False, table, (tile_maps, from_core), *consts, ())
    for rank in range(places):
        saved = forward_block(1 + rank, rank + 1 == places, table, arrived[rank], *consts, saved)
    tile_out, tile_embed, unit, inv, hidden, slope, head_slope, source = saved
    came, smalls = tile_rows(table, tile_embed, small, [from_core] + arrived[0], devices)
    came = exchange(came, ALL)

    feature, embed_grad = slide_grads(
        length, members, table, came, slide_taps, slide_weight, vectors, smalls
    )
    grad_pre, kept, sent = weight_grads(
        plan,
        embed_grad,
        (unit, hidden, slope, head_slope),
        vectors,
        head_weight,
        reduce_weight,
    )
    streams = (source, pinned(grad_pre), unit, inv)

    names = ("g2", "y")
    size = plan.ys
    came = other_core(sent)
    none = jnp.zeros((channels // LANES, KS * KS, 8, LANES), jnp.float32)
    tap_sums = tap_grads(plan, 0, False, table, streams, none, vectors, expand_weight)
    came, tap_sums = lax.optimization_barrier((came, tap_sums))
    out = [
        [add_all([kept[kind, step], came[kind, step]]) for step in range(1, size)]
        for kind in range(2)
    ]
    stay = [add_all([kept[kind, 0], came[kind, 0]]) for kind in range(2)]
    out, tap_sums = lax.optimization_barrier((out, tap_sums))
    parts = [sum_axis(stay[kind], out[kind], names[kind], size) for kind in range(2)]
    taps = tap_grads(plan, PROC // 2, True, table, streams, tap_sums, vectors, expand_weight)
    out = [
        [add_all([part[step] for part in parts[kind]]) for step in range(1, size)]
        for kind in range(2)
    ]
    stay = [add_all([part[0] for part in parts[kind]]) for kind in range(2)]
    out, taps = lax.optimization_barrier((out, taps))
    parts = [sum_axis(stay[kind], out[kind], names[1 - kind], size) for kind in range(2)]
    taps = exchange(taps[:, :, :DEPTH_ROWS].astype(jnp.bfloat16), ("y", "g2", "core"))
    taps = jnp.sum(taps.astype(jnp.float32), axis=0).astype(jnp.bfloat16)
    both = jnp.concatenate([add_all(parts[0]), add_all(parts[1]), taps], axis=1)
    total = add_all(
        sum_axis(both[0], [both[step] for step in range(1, plan.g1)], "g1", plan.g1), jnp.float32
    )
    reduce_share = total[: plan.reduce_rows]
    expand_share = total[plan.block_rows : plan.block_rows + plan.pieces * plan.expand_rows]
    expand_share = expand_share.reshape(plan.pieces, plan.expand_rows, channels).transpose(1, 0, 2)
    depth_share = lax.dynamic_slice(
        total[2 * plan.block_rows :].reshape(-1),
        (my_device * plan.share % channels,),
        (plan.share,),
    )
    return (tile_out, feature, expand_share.reshape(-1), reduce_share.reshape(-1), depth_share)


def solution(mesh):
    slides, members = mesh.shape["dp"], mesh.shape["group"]
    fine = Mesh(mesh.devices.reshape(slides // 2, 2, 4, members // 4), ALL)
    return jax.shard_map(
        on_device,
        mesh=fine,
        in_specs=(
            P(ALL, None, None, None),
            P(None, ALL),
            P(DP),
            P(None, GROUP, None),
        )
        + (P(),) * 13
        + (P(DP, None),),
        out_specs=(
            P(ALL, None, None, None),
            P(DP, None),
            P(ALL),
            P(ALL),
            P(ALL),
        ),
        check_vma=False,
    )
```

```python
import functools
import math

import jax
import jax.numpy as jnp
from jax import lax
from jax.experimental import pallas as pl
from jax.experimental.pallas import tpu as pltpu
from jax.sharding import Mesh, PartitionSpec as P

E = 768
KS = 7
KERNEL_TAPS = 7
TILE_DILATION = 3
PROC = 4
DP = ("y", "core")
GROUP = ("g1", "g2")
ALL = DP + GROUP

EPSILON = 1e-06
HALF_ROOT = 0.7071067811865476
INV_ROOT_TAU = 0.3989422804014327
BELL_SCALE = -0.7213475204444817
LANES = 128
ROW_UNIT = 16
DEPTH_ROWS = 4
TAP_ROWS = 8
MIB = 1024 * 1024
PART = 32
WIDTH = 256
GAIN, SHIFT, SCALE, REDUCE_BIAS, DEPTH_BIAS, EXPAND_BIAS, SLIDE_BIAS = range(7)
VECTORS = 7
ERFC_P = 0.3275911
ERFC_A = (0.254829592, -0.284496736, 1.421413741, -1.453152027, 1.061405429)

HBM = pl.BlockSpec(memory_space=pl.ANY)
IN_HBM = pl.BlockSpec(memory_space=pltpu.HBM)
ROWS_AT, COLS_AT, COUNT_AT, SMALL = E, E + LANES, E + 2 * LANES, E + 3 * LANES
PIECES = 3


def whole(shape):
    return pl.BlockSpec(shape, lambda *_: (0,) * len(shape), pipeline_mode=pl.Buffered(1))


def gelu_and_slope(values):
    size = jnp.abs(values)
    divisor = 1.0 + (ERFC_P * HALF_ROOT) * size
    t = pl.reciprocal(divisor, approx=True)
    bell = jnp.exp2(values * (values * BELL_SCALE))
    poly = 0.5 * ERFC_A[4]
    for coefficient in ERFC_A[3::-1]:
        poly = poly * t + 0.5 * coefficient
    tail = poly * t * bell
    phi = jnp.where(values >= 0.0, 1.0 - tail, tail)
    return values * phi, phi + values * (INV_ROOT_TAU * bell)


def mix_cols(left_side, right_side):
    return lax.dot_general(
        left_side, right_side, (((1,), (1,)), ((), ())), preferred_element_type=jnp.float32
    )


def mix(left_side, right_side):
    return jnp.dot(left_side, right_side, preferred_element_type=jnp.float32)


FILLED, SLIDE, PLACE, CLASSES = 0, PROC, 2 * PROC, 3 * PROC
CLASS_SIZE = 1 + 3 * PROC


def class_field(kind, field, item=0):
    return CLASSES + kind * CLASS_SIZE + (1 + field * PROC + item if field >= 0 else 0)


SLOT, FROM, OWN = range(3)


def pack_kernel(slides, slots, places, counts_ref, route_ref, tiles_ref, pos_ref, cot_ref, *refs):
    inputs = (pos_ref, cot_ref) + refs[:VECTORS]
    refs = refs[VECTORS:]
    held_refs, refs = refs[-len(inputs) - 1 : -1], refs[: -len(inputs) - 1] + refs[-1:]
    send_refs, refs = refs[:-7], refs[-7:]
    table_ref, small_ref, vectors_ref, count_ref, slot_ref, sems, input_sems = refs
    loads = [
        pltpu.make_async_copy(ref, held, input_sems.at[index])
        for index, (ref, held) in enumerate(zip(inputs, held_refs))
    ]
    for load in loads:
        load.start()
    pos_ref, cot_ref = held_refs[:2]
    vector_refs = held_refs[2:]
    my_slide = lax.axis_index(DP)

    targets = [(0, rank, rank) for rank in range(places)]
    for rank in range(places):
        for other in range(2, slides):
            targets.append((1 + rank * (slides - 2) + other - 2, 0, other * places + rank))
    targets[:places] = [(0, rank, places + rank) for rank in range(places)]

    def copy_of(index, slot):
        buffer, row, _ = targets[index]
        side = tiles_ref.shape[1]
        lines = send_refs[buffer].at[pl.ds(row * side, side)]
        return pltpu.make_async_copy(tiles_ref.at[slot], lines, sems.at[index])

    for index in range(slides):
        count_ref[index] = 0
    for index in range(slides * places):
        slot_ref[index] = -1

    def place_slot(slot, carry):
        entry = route_ref[my_slide, 0, slot]

        @pl.when(entry >= 0)
        def _send():
            other = lax.div(entry, PROC) ^ my_slide
            rank = count_ref[other]
            count_ref[other] = rank + 1
            slot_ref[other * places + rank] = slot

        return carry

    lax.fori_loop(0, slots, place_slot, 0)
    for index, (_, _, key) in enumerate(targets):
        slot = slot_ref[key]

        @pl.when(slot >= 0)
        def _start():
            copy_of(index, slot).start()

    for load in loads:
        load.wait()
    small_ref[:, 0:E] = cot_ref[...]
    for row, start in enumerate((ROWS_AT, COLS_AT)):
        small_ref[:, start : start + LANES] = jnp.zeros((1, LANES), jnp.float32)
        small_ref[:, start : start + slots] = pos_ref[row : row + 1, :].astype(jnp.float32)
    small_ref[:, COUNT_AT:SMALL] = jnp.full((1, LANES), counts_ref[0], jnp.int32).astype(jnp.float32)
    channels = tiles_ref.shape[3]
    extra = []
    rest = small_ref[...]
    for piece in range(PIECES):
        part = rest.astype(jnp.bfloat16).astype(jnp.float32)
        rest = rest - part
        extra += [part[:, at : at + channels] for at in range(0, SMALL, channels)]
    extra.append(jnp.zeros((ROW_UNIT - len(extra), channels), jnp.float32))
    extra = jnp.concatenate(extra, axis=0).astype(jnp.bfloat16)
    for ref in send_refs[: slides - 1]:
        ref[ref.shape[0] - 1] = extra
    vectors_ref[...] = jnp.zeros(vectors_ref.shape, jnp.float32)
    for index, ref in enumerate(vector_refs):
        size = ref.shape[0]
        vectors_ref[index : index + 1, 0:size] = ref[...].reshape(1, size)

    kinds = 1 + places
    for field in range(CLASSES + kinds * CLASS_SIZE):
        table_ref[field] = 0
    for kind in range(kinds):
        for item in range(PROC):
            table_ref[class_field(kind, SLOT, item)] = PROC
    for other in range(slides):
        source = my_slide ^ other
        count_ref[0] = 0

        def take(slot, carry):
            entry = route_ref[source, 0, slot]
            proc = entry - my_slide * PROC

            @pl.when((proc >= 0) & (proc < PROC))
            def _take():
                rank = count_ref[0]
                count_ref[0] = rank + 1
                table_ref[FILLED + proc] = 1
                table_ref[SLIDE + proc] = source
                table_ref[PLACE + proc] = slot
                kind = 0 if other < 2 else 1 + rank
                base = CLASSES + kind * CLASS_SIZE
                item = table_ref[base]
                table_ref[base] = item + 1
                table_ref[base + 1 + SLOT * PROC + item] = proc
                if other == 0:
                    table_ref[base + 1 + FROM * PROC + item] = 0
                    table_ref[base + 1 + OWN * PROC + item] = slot
                else:
                    table_ref[base + 1 + FROM * PROC + item] = 1 + rank if other == 1 else other - 2

            return carry

        lax.fori_loop(0, slots, take, 0)
        if other == 0:
            own = table_ref[class_field(0, -1)]
            for item in range(1, PROC):

                @pl.when(item >= own)
                def _hold():
                    table_ref[class_field(0, OWN, item)] = table_ref[class_field(0, OWN, item - 1)]

    for kind in range(kinds):
        items = table_ref[class_field(kind, -1)]
        for item in range(1, PROC):

            @pl.when(item >= items)
            def _hold_slot():
                table_ref[class_field(kind, SLOT, item)] = table_ref[class_field(kind, SLOT, item - 1)]

    for index, (_, _, key) in enumerate(targets):

        @pl.when(slot_ref[key] >= 0)
        def _wait():
            copy_of(index, 0).wait()


def pack_tiles(counts, routing, tile_maps, positions, cotangent, vectors, slides, places):
    slots = tile_maps.shape[0]
    smem = pl.BlockSpec(memory_space=pltpu.SMEM)
    vmem = pl.BlockSpec(memory_space=pltpu.VMEM)
    buffers = 1 + places * (slides - 2)
    side = tile_maps.shape[1]
    shapes = [places * side + 1] + [side + 1] * (slides - 2) + [side] * (buffers - slides + 1)
    widest = max(vector.shape[0] for vector in vectors)
    inputs = (positions, cotangent) + vectors
    fixed = [pinned(x) for x in (tile_maps,) + inputs]
    outs = pl.pallas_call(
        functools.partial(pack_kernel, slides, slots, places),
        out_shape=tuple(
            jax.ShapeDtypeStruct((size,) + tile_maps.shape[2:], tile_maps.dtype) for size in shapes
        )
        + (
            jax.ShapeDtypeStruct((CLASSES + (1 + places) * CLASS_SIZE,), jnp.int32),
            jax.ShapeDtypeStruct((1, SMALL), jnp.float32),
            jax.ShapeDtypeStruct((8, widest), jnp.float32),
        ),
        in_specs=[smem, smem] + [IN_HBM] * len(fixed),
        out_specs=(vmem,) * buffers + (smem, vmem, vmem),
        scratch_shapes=[
            pltpu.SMEM((slides,), jnp.int32),
            pltpu.SMEM((slides * places,), jnp.int32),
            pltpu.SemaphoreType.DMA((slides * places,)),
        ]
        + [pltpu.VMEM(x.shape, x.dtype) for x in inputs]
        + [pltpu.SemaphoreType.DMA((len(inputs),))],
        compiler_params=pltpu.CompilerParams(vmem_limit_bytes=8 * MIB),
        name="pack_tiles",
    )(counts, routing, *fixed)
    return outs[:-3], outs[-3:]


def forward_kernel(kind, last, inputs, kept, table_ref, *refs):
    tile_refs, refs = refs[:inputs], refs[inputs:]
    taps_hbm, vectors_ref, expand_hbm, reduce_hbm, head_hbm = refs[:5]
    refs = refs[5 + (0 if kind == 0 else kept) :]
    out_hbms, refs = refs[:kept], refs[kept:]
    held, refs = refs[:kept], refs[kept:]
    taps_ref, expand_ref, reduce_ref, head_ref, padded, depth_out, normed, pre, load_sems = refs[:9]
    tile_sems, out_sems = refs[9:]
    out_s, embed_s, unit_s, inv_s, hidden_s, slope_s, head_slope_s, source_s = held
    items = table_ref[class_field(kind, -1)]
    side, channels = out_s.shape[1], out_s.shape[3]
    cells = side * side
    bands = channels // LANES
    low = ROW_UNIT // 2
    reach = KS // 2
    constants = [
        pltpu.make_async_copy(source, target, load_sems.at[index])
        for index, (source, target) in enumerate(
            (
                (taps_hbm, taps_ref),
                (expand_hbm, expand_ref),
                (reduce_hbm, reduce_ref),
                (head_hbm, head_ref),
            )
        )
    ]

    def tile_copy(ref, row, buffer):
        lines = ref.at[row] if len(ref.shape) == 4 else ref.at[pl.ds(row * side, side)]
        return pltpu.make_async_copy(lines, source_s.at[buffer], tile_sems.at[buffer])

    def load(item, buffer):
        origin = table_ref[class_field(kind, FROM) + item]
        place = 0
        for index, ref in enumerate(tile_refs):
            own = kind == 0 and index == 0
            for row in range(1 if own else ref.shape[0] // side):

                @pl.when(origin == place)
                def _load():
                    at = table_ref[class_field(kind, OWN) + item] if own else row
                    tile_copy(ref, at, buffer).start()

                place += 1

    def keep(part, slot, buffer):
        return pltpu.make_async_copy(
            held[part].at[buffer], out_hbms[part].at[slot], out_sems.at[part, buffer]
        )

    def wait_kept(buffer):
        for part in range(kept - 1):
            keep(part, 0, buffer).wait()

    def vector(index, lanes):
        return vectors_ref[index : index + 1, lanes]

    @pl.when(items > 0)
    def _first():
        load(0, 0)
        for copy in constants:
            copy.start()
        edge = jnp.zeros((side, low, LANES), jnp.float32)
        for band in range(bands):
            padded[band, :, 0:low, :] = edge
            padded[band, :, low + side :, :] = edge

    def one_item(item, carry):
        buffer = lax.rem(item, 2)
        slot = table_ref[class_field(kind, SLOT) + item]

        @pl.when(item >= 2)
        def _free():
            wait_kept(buffer)

        tile_copy(tile_refs[0], 0, buffer).wait()

        @pl.when(item == 0)
        def _taps():
            constants[0].wait()

        for band in range(bands):
            for at in range(side):
                padded[band, at, low : low + side, :] = source_s[
                    buffer, at, :, band * LANES : (band + 1) * LANES
                ].astype(jnp.float32)

        def convolve(band, carry):
            lanes = pl.ds(pl.multiple_of(band * LANES, LANES), LANES)
            bias = jnp.broadcast_to(vectors_ref[DEPTH_BIAS : DEPTH_BIAS + 1, lanes], (side, LANES))
            totals = [bias for _ in range(side)]
            for col in range(KS):
                start = low - reach + col
                weights = [
                    jnp.broadcast_to(
                        taps_ref[row * KS + col : row * KS + col + 1, lanes], (side, LANES)
                    ).astype(jnp.bfloat16)
                    for row in range(KS)
                ]
                sums = [None] * side
                for at in range(side):
                    line = padded[band, at, start : start + side, :].astype(jnp.bfloat16)
                    for row in range(KS):
                        place = at - row + reach
                        if 0 <= place < side:
                            term = weights[row] * line
                            sums[place] = term if sums[place] is None else sums[place] + term
                for place in range(side):
                    totals[place] = totals[place] + sums[place].astype(jnp.float32)
            for place in range(side):
                depth_out[band, place * side : (place + 1) * side, :] = totals[place]
            return carry

        lax.fori_loop(0, bands, convolve, 0)
        for start in range(0, cells, PART):
            rows = slice(start, start + PART)
            pieces = [depth_out[band, rows, :] for band in range(bands)]
            mean = jnp.sum(sum(pieces), axis=1, keepdims=True) * (1.0 / channels)
            pieces = [piece - mean for piece in pieces]
            var = jnp.sum(sum(p * p for p in pieces), axis=1, keepdims=True) * (1.0 / channels)
            inv = lax.rsqrt(var + EPSILON)
            inv_s[buffer, rows, :] = jnp.broadcast_to(inv, (PART, LANES))
            for band in range(bands):
                lanes = slice(band * LANES, (band + 1) * LANES)
                unit = pieces[band] * inv
                unit_s[buffer, rows, lanes] = unit
                normed[rows, lanes] = (unit * vector(GAIN, lanes) + vector(SHIFT, lanes)).astype(
                    jnp.bfloat16
                )

        @pl.when(item == 0)
        def _weights():
            for copy in constants[1:]:
                copy.wait()

        @pl.when(item + 1 < items)
        def _next():
            @pl.when(item >= 1)
            def _source_free():
                keep(kept - 1, 0, 1 - buffer).wait()

            load(item + 1, 1 - buffer)

        for part in (2, 3):
            keep(part, slot, buffer).start()
        for index, begin in enumerate(range(0, expand_ref.shape[1], WIDTH)):
            cols = slice(begin, begin + WIDTH)
            at = index % pre.shape[0]
            pre[at] = mix(normed[...], expand_ref[:, cols])
            for start in range(0, cells, PART):
                rows = slice(start, start + PART)
                act, slope = gelu_and_slope(pre[at, rows, :] + vector(EXPAND_BIAS, cols))
                hidden_s[buffer, rows, cols] = act.astype(jnp.bfloat16)
                slope_s[buffer, rows, cols] = slope.astype(jnp.bfloat16)
        for part in (4, 5):
            keep(part, slot, buffer).start()
        lanes = slice(0, channels)
        depth_rows = mix(hidden_s[buffer], reduce_ref[...])
        for at in range(side):
            rows = slice(at * side, (at + 1) * side)
            branch = vector(SCALE, lanes) * (depth_rows[rows] + vector(REDUCE_BIAS, lanes))
            line = (source_s[buffer, at].astype(jnp.float32) + branch).astype(jnp.bfloat16)
            normed[rows, :] = line
            out_s[buffer, at] = line
        for part in (0, 7):
            keep(part, slot, buffer).start()
        for index, begin in enumerate(range(0, head_ref.shape[1], WIDTH)):
            cols = slice(begin, begin + WIDTH)
            at = index % pre.shape[0]
            pre[at] = mix(normed[...], head_ref[:, cols])
            total = None
            for start in range(0, cells, PART):
                rows = slice(start, start + PART)
                act, slope = gelu_and_slope(pre[at, rows, :])
                head_slope_s[buffer, rows, cols] = slope.astype(jnp.bfloat16)
                folded = act[0:8]
                for piece in range(8, PART, 8):
                    folded = folded + act[piece : piece + 8]
                total = folded if total is None else total + folded
            mean = jnp.sum(total, axis=0, keepdims=True) * (1.0 / cells)
            embed_s[buffer, :, cols] = jnp.broadcast_to(mean, (8, WIDTH))
        for part in (1, 6):
            keep(part, slot, buffer).start()
        return carry

    lax.fori_loop(0, items, one_item, 0)
    for back in (1, 2):

        @pl.when(items >= back)
        def _drain():
            buffer = lax.rem(items - back, 2)
            for part in range(kept):
                keep(part, 0, buffer).wait()

    if last:
        filled = sum(table_ref[FILLED + proc] for proc in range(PROC))

        @pl.when(filled < PROC)
        def _zeros():
            for ref in held:
                ref[0] = jnp.zeros(ref.shape[1:], ref.dtype)

        for proc in range(PROC):

            @pl.when(table_ref[FILLED + proc] == 0)
            def _empty():
                for part in range(kept):
                    keep(part, proc, 0).start()
                wait_kept(0)
                keep(kept - 1, proc, 0).wait()


def pinned(array):
    return pltpu.with_memory_space_constraint(array, pltpu.HBM)


def forward_block(kind, last, table, tiles, taps, vectors, expand, reduce, head, before):
    side, channels = tiles[0].shape[-2:]
    cells, hid, embed = side * side, expand.shape[1], head.shape[1]
    bands = channels // LANES
    outs = (
        ((side, side, channels), jnp.bfloat16),
        ((8, embed), jnp.float32),
        ((cells, channels), jnp.float32),
        ((cells, LANES), jnp.float32),
        ((cells, hid), jnp.bfloat16),
        ((cells, hid), jnp.bfloat16),
        ((cells, embed), jnp.bfloat16),
        ((side, side, channels), jnp.bfloat16),
    )
    smem = pl.BlockSpec(memory_space=pltpu.SMEM)
    vmem = pl.BlockSpec(memory_space=pltpu.VMEM)
    if kind == 0:
        tiles = (pinned(tiles[0]),) + tuple(tiles[1:])
    first = 1 + len(tiles) + 5
    return pl.pallas_call(
        functools.partial(forward_kernel, kind, last, len(tiles), len(outs)),
        out_shape=tuple(pltpu.HBM((PROC,) + shape, dtype) for shape, dtype in outs),
        in_specs=[smem]
        + [HBM] * len(tiles)
        + [IN_HBM, vmem, IN_HBM, IN_HBM, IN_HBM]
        + [IN_HBM] * len(before),
        out_specs=(IN_HBM,) * len(outs),
        scratch_shapes=[pltpu.VMEM((2,) + shape, dtype) for shape, dtype in outs]
        + [
            pltpu.VMEM(taps.shape, jnp.float32),
            pltpu.VMEM(expand.shape, jnp.bfloat16),
            pltpu.VMEM(reduce.shape, jnp.bfloat16),
            pltpu.VMEM(head.shape, jnp.bfloat16),
            pltpu.VMEM((bands, side, side + ROW_UNIT, LANES), jnp.float32),
            pltpu.VMEM((bands, cells, LANES), jnp.float32),
            pltpu.VMEM((cells, channels), jnp.bfloat16),
            pltpu.VMEM((3, cells, WIDTH), jnp.float32),
            pltpu.SemaphoreType.DMA((4,)),
            pltpu.SemaphoreType.DMA((2,)),
            pltpu.SemaphoreType.DMA((len(outs), 2)),
        ],
        input_output_aliases={first + index: index for index in range(len(before))},
        compiler_params=pltpu.CompilerParams(vmem_limit_bytes=24 * MIB),
        cost_estimate=cost(1.0),
        name="forward_block_" + str(kind),
    )(table, *tiles, pinned(taps), vectors, pinned(expand), pinned(reduce), pinned(head), *before)


def cost(micros):
    return pl.CostEstimate(flops=int(micros * 1e9), bytes_accessed=1024, transcendentals=0)


def rows_kernel(slides, table_ref, embed_ref, small_ref, *refs):
    buffer_refs, (out_ref, smalls_ref, rows_ref, extra_ref, sems) = refs[: slides - 1], refs[slides - 1 :]
    copies = [
        pltpu.make_async_copy(ref.at[ref.shape[0] - 1], extra_ref.at[index], sems.at[index])
        for index, ref in enumerate(buffer_refs)
    ]
    for copy in copies:
        copy.start()
    my_slide, my_member = lax.axis_index(DP), lax.axis_index(GROUP)
    channels = extra_ref.shape[2]
    half = E // 2
    channel = lax.broadcasted_iota(jnp.int32, (1, E), 1)
    inner = jnp.where(channel < half, channel, channel - half)
    odd = lax.rem(inner, 2)
    frequency = jnp.exp((inner - odd).astype(jnp.float32) * (-math.log(10000.0) / half))
    phase = odd.astype(jnp.float32) * (0.5 * math.pi)
    lane = lax.broadcasted_iota(jnp.int32, (1, LANES), 1)
    smalls_ref[0] = small_ref[...]
    lines = SMALL // channels
    for index, copy in enumerate(copies):
        copy.wait()
        extra = extra_ref[index].astype(jnp.float32)
        for line in range(lines):
            total = extra[line : line + 1]
            for piece in range(1, PIECES):
                total = total + extra[piece * lines + line : piece * lines + line + 1]
            smalls_ref[1 + index, :, line * channels : (line + 1) * channels] = total
    for proc in range(PROC):
        filled = table_ref[FILLED + proc]
        slide = table_ref[SLIDE + proc]
        slot = table_ref[PLACE + proc]
        held = smalls_ref[0]
        for other in range(1, slides):
            held = jnp.where((slide ^ my_slide) == other, smalls_ref[other], held)
        spots = [
            jnp.sum(jnp.where(lane == slot, held[:, at : at + LANES], 0.0), axis=1, keepdims=True)
            for at in (ROWS_AT, COLS_AT)
        ]
        angle = jnp.where(channel < half, spots[0], spots[1]) * frequency + phase
        target = jnp.where(lane == 0, slide, jnp.where(lane == 1, slot, my_member))
        target = jnp.where(filled != 0, target, jnp.where(lane == 2, -1, 0))
        target = jnp.where(lane < 3, target, 0)
        rows_ref[proc : proc + 1, 0:E] = angle
        rows_ref[2 * PROC + proc : 2 * PROC + proc + 1, 0:E] = embed_ref[proc, 0:1, :]
        for copied in range(proc, ROW_UNIT, PROC):
            rows_ref[copied : copied + 1, E:] = target.astype(jnp.float32)
    code = jnp.sin(rows_ref[0 : 2 * PROC, 0:E])
    embed = rows_ref[2 * PROC : 4 * PROC, 0:E].astype(jnp.bfloat16).astype(jnp.float32)
    row_id = lax.broadcasted_iota(jnp.int32, (2 * PROC, E), 0)
    there = row_id < 0
    for proc in range(PROC):
        there = there | ((row_id == proc) & (table_ref[FILLED + proc] != 0))
    total = jnp.where(there, embed + code, 0.0)
    rows_ref[0 : 2 * PROC, 0:E] = total
    for copied in range(PROC, ROW_UNIT):
        rows_ref[copied : copied + 1, 0:E] = rows_ref[copied - PROC : copied - PROC + 1, 0:E]
    sent = rows_ref[...].astype(jnp.bfloat16)
    for start in range(0, out_ref.shape[0], ROW_UNIT):
        out_ref[start : start + ROW_UNIT, :] = sent


def tile_rows(table, embeds, small, buffers, devices):
    smem = pl.BlockSpec(memory_space=pltpu.SMEM)
    vmem = pl.BlockSpec(memory_space=pltpu.VMEM)
    slides = 1 + len(buffers)
    return pl.pallas_call(
        functools.partial(rows_kernel, slides),
        out_shape=(
            jax.ShapeDtypeStruct((devices * PROC, E + LANES), jnp.bfloat16),
            jax.ShapeDtypeStruct((slides, 1, SMALL), jnp.float32),
        ),
        in_specs=[smem, vmem, vmem] + [HBM] * len(buffers),
        out_specs=(vmem, vmem),
        scratch_shapes=[
            pltpu.VMEM((4 * PROC, E + LANES), jnp.float32),
            pltpu.VMEM((len(buffers),) + buffers[0].shape[1:], jnp.bfloat16),
            pltpu.SemaphoreType.DMA((len(buffers),)),
        ],
        cost_estimate=cost(1.0),
        name="tile_rows",
    )(table, embeds, small, *buffers)


def slide_kernel(
    length,
    members,
    slides,
    table_ref,
    came_ref,
    taps_hbm,
    matrix_hbm,
    vectors_ref,
    smalls_ref,
    feature_ref,
    grad_ref,
    rows,
    back,
    mixed,
    pre,
    grad_agg,
    taps_ref,
    matrix_ref,
    sems,
):
    loads = [
        pltpu.make_async_copy(taps_hbm, taps_ref, sems.at[0]),
        pltpu.make_async_copy(matrix_hbm, matrix_ref, sems.at[1]),
    ]
    for load in loads:
        load.start()
    my_slide = lax.axis_index(DP)
    border = ROW_UNIT
    edge = jnp.zeros((border, rows.shape[2]), jnp.float32)
    reach = KERNEL_TAPS // 2
    blocks = [slice(start, start + WIDTH) for start in range(0, E, WIDTH)]
    lane = lax.broadcasted_iota(jnp.int32, (8, LANES), 1)
    scales = jnp.where(lane == 0, length, jnp.where(lane == 1, members, jnp.where(lane == 2, 1, 0)))
    target = mix_cols(scales.astype(jnp.float32).astype(jnp.bfloat16), came_ref[:, E:])[0:1, :]
    step = lax.broadcasted_iota(jnp.int32, (length, 1), 0).astype(jnp.float32)

    def dilate(ref, slide, direction, cols):
        total = ref[slide, border : border + length, cols]
        for tap in range(KERNEL_TAPS):
            start = border + direction * (tap - reach) * TILE_DILATION
            total = total + taps_ref[tap : tap + 1, cols] * ref[slide, start : start + length, cols]
        return total

    for other in range(slides):
        slide = my_slide ^ other
        small = smalls_ref[other]
        count = small[:, COUNT_AT : COUNT_AT + 1]
        here = step < count
        first = lax.convert_element_type(slide * length, jnp.float32)
        pick = ((target - first) == step).astype(jnp.float32).astype(jnp.bfloat16)
        for ref in (rows, back):
            ref[slide, 0:border, :] = edge
            ref[slide, border + length :, :] = edge
        if other == 0:
            loads[0].wait()
        for cols in blocks:
            rows[slide, border : border + length, cols] = jnp.where(
                here, mix(pick, came_ref[:, cols]), 0.0
            )
            mixed[other, :, cols] = dilate(rows, slide, 1, cols).astype(jnp.bfloat16)
    loads[1].wait()
    for other in range(slides):
        slide = my_slide ^ other
        small = smalls_ref[other]
        here = step < small[:, COUNT_AT : COUNT_AT + 1]
        share = jnp.where(here, 1.0 / small[:, COUNT_AT : COUNT_AT + 1], 0.0)
        for cols in blocks:
            pre[:, cols] = mix(mixed[other], matrix_ref[:, cols])
            total = None
            for start in range(0, length, PART):
                part = slice(start, start + PART)
                act, slope = gelu_and_slope(
                    pre[part, cols] + vectors_ref[SLIDE_BIAS : SLIDE_BIAS + 1, cols]
                )
                grad_agg[part, cols] = (small[:, cols] * share[part] * slope).astype(jnp.bfloat16)
                if other == 0:
                    piece = jnp.sum(act * share[part], axis=0, keepdims=True)
                    total = piece if total is None else total + piece
            if other == 0:
                feature_ref[:, cols] = total
        for cols in blocks:
            back[slide, border : border + length, cols] = mix_cols(
                grad_agg[...], matrix_ref[cols, :]
            )
            total = jnp.where(here, dilate(back, slide, -1, cols), 0.0)
            rows[slide, border : border + length, cols] = total.astype(jnp.bfloat16).astype(
                jnp.float32
            )
    my_member = lax.axis_index(GROUP)
    for proc in range(PROC):
        at = border + table_ref[PLACE + proc] * members + my_member
        row = rows[table_ref[SLIDE + proc], pl.ds(at, 1), :]
        grad_ref[proc] = jnp.where(table_ref[FILLED + proc] != 0, row, 0.0)


def slide_grads(length, members, table, came, taps, matrix, vectors, smalls):
    slides = smalls.shape[0]
    smem = pl.BlockSpec(memory_space=pltpu.SMEM)
    vmem = pl.BlockSpec(memory_space=pltpu.VMEM)
    padded = (slides, length + 2 * ROW_UNIT, E)
    return pl.pallas_call(
        functools.partial(slide_kernel, length, members, slides),
        out_shape=(
            jax.ShapeDtypeStruct((1, E), jnp.float32),
            jax.ShapeDtypeStruct((PROC, 1, E), jnp.float32),
        ),
        in_specs=[smem, vmem, IN_HBM, IN_HBM, vmem, vmem],
        out_specs=(vmem, vmem),
        scratch_shapes=[
            pltpu.VMEM(padded, jnp.float32),
            pltpu.VMEM(padded, jnp.float32),
            pltpu.VMEM((slides, length, E), jnp.bfloat16),
            pltpu.VMEM((length, E), jnp.float32),
            pltpu.VMEM((length, E), jnp.bfloat16),
            pltpu.VMEM(taps.shape, jnp.float32),
            pltpu.VMEM(matrix.shape, jnp.bfloat16),
            pltpu.SemaphoreType.DMA((2,)),
        ],
        compiler_params=pltpu.CompilerParams(vmem_limit_bytes=24 * MIB),
        cost_estimate=cost(6.0),
        name="slide_grads",
    )(table, came, pinned(taps), pinned(matrix), vectors, smalls)


class Plan:
    def __init__(self, slides, members, channels, hid):
        self.devices = slides * members
        self.ys, self.g1, self.g2 = slides // 2, 4, members // 4
        assert self.ys == self.g2
        self.channels = channels
        self.pieces = hid // channels
        self.expand_rows = channels // self.devices
        self.reduce_rows = hid // self.devices
        self.block_rows = -(-self.reduce_rows // ROW_UNIT) * ROW_UNIT
        self.share = KS * KS * channels // self.devices

    def spots(self):
        my_core, my_y = lax.axis_index("core"), lax.axis_index("y")
        my_z, my_x = lax.axis_index("g1"), lax.axis_index("g2")
        for device in range(self.devices):
            slide, member = divmod(device, self.g1 * self.g2)
            (y, core), (z, x) = divmod(slide, 2), divmod(member, self.g2)
            yield (
                my_core ^ core,
                lax.rem(y - my_y + self.ys, self.ys),
                lax.rem(x - my_x + self.g2, self.g2),
                lax.rem(z - my_z + self.g1, self.g1),
            )


def send_out(staged, sems, refs):
    copies = [
        pltpu.make_async_copy(staged.at[index], ref, sems.at[index]) for index, ref in enumerate(refs)
    ]
    for copy in copies:
        copy.start()
    for copy in copies:
        copy.wait()


def padded_block(block, rows):
    extra = rows - block.shape[0]
    if extra:
        block = jnp.concatenate([block, jnp.zeros((extra, block.shape[1]), block.dtype)], axis=0)
    return block.astype(jnp.bfloat16)


def weights_kernel(
    plan,
    grad_ref,
    hidden_ref,
    head_slope_ref,
    slope_ref,
    unit_ref,
    vectors_ref,
    head_ref,
    reduce_ref,
    grad_pre_hbm,
    keep_ref,
    send_ref,
    grad_pre,
    turned,
    normed,
    grad_head,
    eye_ref,
    staged,
    sems,
    pre_sems,
):
    cells, channels = unit_ref.shape[1:]
    hid = reduce_ref.shape[0]
    every = slice(0, channels)

    def vector(index, lanes):
        return vectors_ref[index : index + 1, lanes]

    spot = lax.broadcasted_iota(jnp.int32, eye_ref.shape, 0)
    same = spot == lax.broadcasted_iota(jnp.int32, eye_ref.shape, 1)
    eye_ref[...] = same.astype(jnp.float32).astype(jnp.bfloat16)

    def one_slot(slot, carry):
        rows_all = pl.ds(pl.multiple_of(slot * cells, cells), cells)
        row = grad_ref[slot] * (1.0 / cells)
        for start in range(0, cells, PART):
            rows = slice(start, start + PART)
            grad_head[rows, :] = (row * head_slope_ref[slot, rows, :].astype(jnp.float32)).astype(
                jnp.bfloat16
            )
            normed[rows, :] = (
                unit_ref[slot, rows, :] * vector(GAIN, every) + vector(SHIFT, every)
            ).astype(jnp.bfloat16)
        grad_mlp = (vector(SCALE, every) * mix_cols(grad_head[...], head_ref[...])).astype(
            jnp.bfloat16
        )
        turned[0, :, rows_all] = mix_cols(eye_ref[...], grad_mlp).astype(jnp.bfloat16)
        turned[1, :, rows_all] = mix_cols(eye_ref[...], normed[...]).astype(jnp.bfloat16)
        for begin in range(0, hid, WIDTH):
            cols = slice(begin, begin + WIDTH)
            grad_hidden = mix_cols(grad_mlp, reduce_ref[cols, :])
            grad_pre[rows_all, cols] = (
                grad_hidden * slope_ref[slot, :, cols].astype(jnp.float32)
            ).astype(jnp.bfloat16)
        return carry

    lax.fori_loop(0, PROC, one_slot, 0)
    writes = [
        pltpu.make_async_copy(
            grad_pre.at[pl.ds(slot * cells, cells)], grad_pre_hbm.at[slot], pre_sems.at[slot]
        )
        for slot in range(PROC)
    ]
    for write in writes:
        write.start()
    spots = list(plan.spots())
    per_block = channels // plan.reduce_rows
    tall = plan.block_rows
    for index in range(plan.pieces):
        cols = slice(index * channels, (index + 1) * channels)
        total = mix(turned[0], hidden_ref[:, cols]).astype(jnp.bfloat16)
        back = mix_cols(eye_ref[...], total)
        for part in range(per_block):
            block = back[part * plan.reduce_rows : (part + 1) * plan.reduce_rows]
            core, y, x, z = spots[index * per_block + part]
            staged[core, 0, x, y, z] = padded_block(block, tall)
    totals = []
    for quarter in range(plan.pieces):
        cols = slice(quarter * channels, (quarter + 1) * channels)
        totals.append(mix(turned[1], grad_pre[:, cols]))
    size = plan.expand_rows
    for device in range(plan.devices):
        rows = slice(device * size, (device + 1) * size)
        block = jnp.concatenate([total[rows] for total in totals], axis=0)
        core, y, x, z = spots[device]
        staged[core, 1, y, x, z] = padded_block(block, tall)
    send_out(staged, sems, (keep_ref, send_ref))
    for write in writes:
        write.wait()


def taps_kernel(
    plan,
    first,
    last,
    table_ref,
    source_ref,
    grad_pre_ref,
    unit_ref,
    inv_ref,
    before_ref,
    vectors_ref,
    expand_ref,
    out_ref,
    padded,
    tap_sums,
    tap_rows,
    grad_norm,
    depth_back,
):
    step = pl.program_id(0)
    filled = table_ref[FILLED + first + step]
    side, channels = source_ref.shape[1], source_ref.shape[3]
    bands = channels // LANES
    low = ROW_UNIT // 2
    reach = KS // 2

    @pl.when(step == 0)
    def _start():
        if first:
            tap_sums[...] = before_ref[...]
        else:
            tap_sums[...] = jnp.zeros(tap_sums.shape, jnp.float32)

    @pl.when(filled != 0)
    def _work():
        cells = side * side
        gain = vectors_ref[GAIN : GAIN + 1, 0:channels]
        grad_norm[...] = mix_cols(grad_pre_ref[0], expand_ref[...])
        for start in range(0, cells, PART):
            rows = slice(start, start + PART)
            scaled = grad_norm[rows, :] * gain
            unit = unit_ref[0, rows, :]
            mean = jnp.sum(scaled, axis=1, keepdims=True) * (1.0 / channels)
            mean_unit = jnp.sum(scaled * unit, axis=1, keepdims=True) * (1.0 / channels)
            inv = inv_ref[0, rows, 0:1]
            for band in range(bands):
                lanes = slice(band * LANES, (band + 1) * LANES)
                depth_back[band, rows, :] = (
                    inv * (scaled[:, lanes] - mean - unit[:, lanes] * mean_unit)
                ).astype(jnp.bfloat16)
        edge = jnp.zeros((side, low, LANES), jnp.float32)
        for band in range(bands):
            lanes = slice(band * LANES, (band + 1) * LANES)
            padded[band, :, 0:low, :] = edge
            padded[band, :, low + side :, :] = edge
            for at in range(side):
                padded[band, at, low : low + side, :] = source_ref[0, at, :, lanes].astype(
                    jnp.float32
                )

        def taps_of(band, carry):
            for col in range(KS):
                start = low - reach + col
                folded = [None] * KS
                grads = {}
                for half in range(2):
                    sums = [None] * KS
                    for at in range(half * side // 2, (half + 1) * side // 2):
                        line = padded[band, at, start : start + side, :].astype(jnp.bfloat16)
                        for row in range(KS):
                            place = at - row + reach
                            if 0 <= place < side:
                                if place not in grads:
                                    grads[place] = depth_back[
                                        band, place * side : (place + 1) * side, :
                                    ]
                                term = line * grads[place]
                                sums[row] = term if sums[row] is None else sums[row] + term
                    for row in range(KS):
                        total = sums[row].astype(jnp.float32)
                        for piece in range(0, side, 8):
                            block = total[piece : piece + 8, :]
                            folded[row] = block if folded[row] is None else folded[row] + block
                for row in range(KS):
                    tap_sums[band, row * KS + col] = tap_sums[band, row * KS + col] + folded[row]
            return carry

        lax.fori_loop(0, bands, taps_of, 0)

    @pl.when(step == pl.num_programs(0) - 1)
    def _finish():
        if not last:
            out_ref[...] = tap_sums[...]
            return
        for band in range(bands):
            lanes = slice(band * LANES, (band + 1) * LANES)
            tap_rows[0 : KS * KS, lanes] = jnp.sum(tap_sums[band], axis=1)
            tap_rows[KS * KS :, lanes] = jnp.zeros((tap_rows.shape[0] - KS * KS, LANES), jnp.float32)
        for device in range(plan.devices):
            start = device * plan.share // channels
            out_ref[device] = tap_rows[start : start + TAP_ROWS, :]


def per_slot(array):
    shape = array.shape[1:]
    return pl.BlockSpec((1,) + shape, lambda i, table: (i,) + (0,) * len(shape))


def weight_grads(plan, embed_grad, saved, vectors, head, reduce):
    unit, hidden, slope, head_slope = saved
    cells, channels = unit.shape[1:]
    hid = reduce.shape[0]
    vmem = pl.BlockSpec(memory_space=pltpu.VMEM)
    blocks = jax.ShapeDtypeStruct(
        (2, plan.ys, plan.g2, plan.g1, plan.block_rows, channels), jnp.bfloat16
    )
    return pl.pallas_call(
        functools.partial(weights_kernel, plan),
        out_shape=(pltpu.HBM((PROC, cells, hid), jnp.bfloat16), blocks, blocks),
        in_specs=[vmem] * 8,
        out_specs=(IN_HBM, HBM, HBM),
        scratch_shapes=[
            pltpu.VMEM((PROC * cells, hid), jnp.bfloat16),
            pltpu.VMEM((2, channels, PROC * cells), jnp.bfloat16),
            pltpu.VMEM((cells, channels), jnp.bfloat16),
            pltpu.VMEM((cells, head.shape[1]), jnp.bfloat16),
            pltpu.VMEM((channels, channels), jnp.bfloat16),
            pltpu.VMEM((2,) + blocks.shape, jnp.bfloat16),
            pltpu.SemaphoreType.DMA((2,)),
            pltpu.SemaphoreType.DMA((PROC,)),
        ],
        compiler_params=pltpu.CompilerParams(vmem_limit_bytes=36 * MIB),
        cost_estimate=cost(12.0),
        name="weight_grads",
    )(embed_grad, hidden.reshape(PROC * cells, hid), head_slope, slope, unit, vectors, head, reduce)


def tap_grads(plan, first, last, table, streams, before, vectors, expand):
    side, channels = streams[0].shape[1], streams[0].shape[3]
    bands = channels // LANES
    sums = (bands, KS * KS, 8, LANES)
    out = (plan.devices, TAP_ROWS, channels) if last else sums

    def items(array):
        shape = array.shape[1:]
        return pl.BlockSpec((1,) + shape, lambda i, table: (first + i,) + (0,) * len(shape))

    return pl.pallas_call(
        functools.partial(taps_kernel, plan, first, last),
        out_shape=jax.ShapeDtypeStruct(out, jnp.float32),
        grid_spec=pltpu.PrefetchScalarGridSpec(
            num_scalar_prefetch=1,
            grid=(PROC // 2,),
            in_specs=[items(stream) for stream in streams]
            + [whole(before.shape), whole(vectors.shape), whole(expand.shape)],
            out_specs=pl.BlockSpec(out, lambda i, table: (0,) * len(out)),
            scratch_shapes=[
                pltpu.VMEM((bands, side, side + ROW_UNIT, LANES), jnp.float32),
                pltpu.VMEM(sums, jnp.float32),
                pltpu.VMEM((KS * KS + 7, channels), jnp.float32),
                pltpu.VMEM((side * side, channels), jnp.float32),
                pltpu.VMEM((bands, side * side, LANES), jnp.bfloat16),
            ],
        ),
        compiler_params=pltpu.CompilerParams(vmem_limit_bytes=16 * MIB),
        cost_estimate=cost(4.0),
        name="tap_grads_" + str(first),
    )(table, *streams, before, vectors, expand)


def shifted(values, names, sizes, shift):
    count = math.prod(sizes)
    pairs = []
    for index in range(count):
        spot = []
        rest = index
        for size in reversed(sizes):
            spot.append(rest % size)
            rest //= size
        spot = spot[::-1]
        target = 0
        for at, step, size in zip(spot, shift, sizes):
            target = target * size + (at + step) % size
        pairs.append((index, target))
    return lax.ppermute(values, names, pairs)


def shifts(sizes):
    steps = [()]
    for size in sizes:
        steps = [step + (more,) for step in steps for more in range(size)]
    return steps


def exchange(values, names):
    return lax.all_to_all(values, names, split_axis=0, concat_axis=0, tiled=True)


def add_all(parts, kind=jnp.bfloat16):
    total = parts[0].astype(jnp.float32)
    for part in parts[1:]:
        total = total + part.astype(jnp.float32)
    return total.astype(kind)


def other_core(values):
    return shifted(values, ("core",), (2,), (1,))


def sum_axis(kept, sent, name, size, kind=jnp.bfloat16):
    return [kept] + [shifted(part, (name,), (size,), (step + 1,)) for step, part in enumerate(sent)]


def on_device(
    tile_maps,
    positions,
    counts,
    routing,
    depth_kernel,
    depth_bias,
    norm_gain,
    norm_shift,
    expand_weight,
    expand_bias,
    reduce_weight,
    reduce_bias,
    layer_scale,
    head_weight,
    slide_taps,
    slide_weight,
    slide_bias,
    cotangent,
):
    slides = lax.axis_size(DP)
    members = lax.axis_size(GROUP)
    my_device = lax.axis_index(ALL)
    slots, channels = tile_maps.shape[0], tile_maps.shape[3]
    devices, length, places = slides * members, slots * members, slots // slides
    plan = Plan(slides, members, channels, expand_weight.shape[1])

    raw = (
        norm_gain,
        norm_shift,
        layer_scale,
        reduce_bias,
        depth_bias,
        expand_bias,
        slide_bias,
    )
    packed, (table, small, vectors) = pack_tiles(
        counts, routing, tile_maps, positions, cotangent, raw, slides, places
    )

    def from_other(buffer, other):
        return lax.ppermute(buffer, DP, [(index, index ^ other) for index in range(slides)])

    from_core = from_other(packed[0], 1)
    arrived = []
    for rank in range(places):
        buffers = packed[1 + rank * (slides - 2) : 1 + (rank + 1) * (slides - 2)]
        if rank:
            buffers, from_core = lax.optimization_barrier((buffers, from_core))
        arrived.append([from_other(buffer, other + 2) for other, buffer in enumerate(buffers)])

    consts = (depth_kernel, vectors, expand_weight, reduce_weight, head_weight)
    saved = forward_block(0, False, table, (tile_maps, from_core), *consts, ())
    for rank in range(places):
        saved = forward_block(1 + rank, rank + 1 == places, table, arrived[rank], *consts, saved)
    tile_out, tile_embed, unit, inv, hidden, slope, head_slope, source = saved
    came, smalls = tile_rows(table, tile_embed, small, [from_core] + arrived[0], devices)
    came = exchange(came, ALL)

    feature, embed_grad = slide_grads(
        length, members, table, came, slide_taps, slide_weight, vectors, smalls
    )
    grad_pre, kept, sent = weight_grads(
        plan,
        embed_grad,
        (unit, hidden, slope, head_slope),
        vectors,
        head_weight,
        reduce_weight,
    )
    streams = (source, pinned(grad_pre), unit, inv)

    names = ("g2", "y")
    size = plan.ys
    came = other_core(sent)
    none = jnp.zeros((channels // LANES, KS * KS, 8, LANES), jnp.float32)
    tap_sums = tap_grads(plan, 0, False, table, streams, none, vectors, expand_weight)
    came, tap_sums = lax.optimization_barrier((came, tap_sums))
    out = [
        [add_all([kept[kind, step], came[kind, step]]) for step in range(1, size)]
        for kind in range(2)
    ]
    stay = [add_all([kept[kind, 0], came[kind, 0]]) for kind in range(2)]
    out, tap_sums = lax.optimization_barrier((out, tap_sums))
    parts = [sum_axis(stay[kind], out[kind], names[kind], size) for kind in range(2)]
    taps = tap_grads(plan, PROC // 2, True, table, streams, tap_sums, vectors, expand_weight)
    out = [
        [add_all([part[step] for part in parts[kind]]) for step in range(1, size)]
        for kind in range(2)
    ]
    stay = [add_all([part[0] for part in parts[kind]]) for kind in range(2)]
    taps = taps[:, :DEPTH_ROWS].astype(jnp.bfloat16)
    out, taps = lax.optimization_barrier((out, taps))
    parts = [sum_axis(stay[kind], out[kind], names[1 - kind], size) for kind in range(2)]
    taps = exchange(taps, ALL)
    both = jnp.concatenate([add_all(parts[0]), add_all(parts[1])], axis=1)
    total = add_all(
        sum_axis(both[0], [both[step] for step in range(1, plan.g1)], "g1", plan.g1), jnp.float32
    )
    reduce_share = total[: plan.reduce_rows]
    expand_share = total[plan.block_rows : plan.block_rows + plan.pieces * plan.expand_rows]
    expand_share = expand_share.reshape(plan.pieces, plan.expand_rows, channels).transpose(1, 0, 2)
    depth_share = lax.dynamic_slice(
        jnp.sum(taps.astype(jnp.float32), axis=0).reshape(-1),
        (my_device * plan.share % channels,),
        (plan.share,),
    )
    return (tile_out, feature, expand_share.reshape(-1), reduce_share.reshape(-1), depth_share)


def solution(mesh):
    slides, members = mesh.shape["dp"], mesh.shape["group"]
    fine = Mesh(mesh.devices.reshape(slides // 2, 2, 4, members // 4), ALL)
    return jax.shard_map(
        on_device,
        mesh=fine,
        in_specs=(
            P(ALL, None, None, None),
            P(None, ALL),
            P(DP),
            P(None, GROUP, None),
        )
        + (P(),) * 13
        + (P(DP, None),),
        out_specs=(
            P(ALL, None, None, None),
            P(DP, None),
            P(ALL),
            P(ALL),
            P(ALL),
        ),
        check_vma=False,
    )
```

```python
import functools
import math

import jax
import jax.numpy as jnp
from jax import lax
from jax.experimental import pallas as pl
from jax.experimental.pallas import tpu as pltpu
from jax.sharding import Mesh, PartitionSpec as P

E = 768
KS = 7
KERNEL_TAPS = 7
TILE_DILATION = 3
PROC = 4
DP = ("y", "core")
GROUP = ("g1", "g2")
ALL = DP + GROUP

EPSILON = 1e-06
HALF_ROOT = 0.7071067811865476
INV_ROOT_TAU = 0.3989422804014327
BELL_SCALE = -0.7213475204444817
LANES = 128
ROW_UNIT = 16
DEPTH_ROWS = 4
TAP_ROWS = 8
MIB = 1024 * 1024
PART = 32
WIDTH = 256
GAIN, SHIFT, SCALE, REDUCE_BIAS, DEPTH_BIAS, EXPAND_BIAS, SLIDE_BIAS = range(7)
VECTORS = 7
ERFC_P = 0.3275911
ERFC_A = (0.254829592, -0.284496736, 1.421413741, -1.453152027, 1.061405429)

HBM = pl.BlockSpec(memory_space=pl.ANY)
IN_HBM = pl.BlockSpec(memory_space=pltpu.HBM)
ROWS_AT, COLS_AT, COUNT_AT, SMALL = E, E + LANES, E + 2 * LANES, E + 3 * LANES
PIECES = 3
HALF = 512


def whole(shape):
    return pl.BlockSpec(shape, lambda *_: (0,) * len(shape), pipeline_mode=pl.Buffered(1))


def gelu_and_slope(values):
    size = jnp.abs(values)
    divisor = 1.0 + (ERFC_P * HALF_ROOT) * size
    t = pl.reciprocal(divisor, approx=True)
    bell = jnp.exp2(values * (values * BELL_SCALE))
    poly = 0.5 * ERFC_A[4]
    for coefficient in ERFC_A[3::-1]:
        poly = poly * t + 0.5 * coefficient
    tail = poly * t * bell
    phi = jnp.where(values >= 0.0, 1.0 - tail, tail)
    return values * phi, phi + values * (INV_ROOT_TAU * bell)


def mix_cols(left_side, right_side):
    return lax.dot_general(
        left_side, right_side, (((1,), (1,)), ((), ())), preferred_element_type=jnp.float32
    )


def mix(left_side, right_side):
    return jnp.dot(left_side, right_side, preferred_element_type=jnp.float32)


FILLED, SLIDE, PLACE, CLASSES = 0, PROC, 2 * PROC, 3 * PROC
CLASS_SIZE = 1 + 3 * PROC


def class_field(kind, field, item=0):
    return CLASSES + kind * CLASS_SIZE + (1 + field * PROC + item if field >= 0 else 0)


SLOT, FROM, OWN = range(3)


def pack_kernel(slides, slots, places, counts_ref, route_ref, tiles_ref, pos_ref, cot_ref, *refs):
    inputs = (pos_ref, cot_ref) + refs[:VECTORS]
    refs = refs[VECTORS:]
    held_refs, refs = refs[-len(inputs) - 1 : -1], refs[: -len(inputs) - 1] + refs[-1:]
    send_refs, refs = refs[:-7], refs[-7:]
    table_ref, small_ref, vectors_ref, count_ref, slot_ref, sems, input_sems = refs
    loads = [
        pltpu.make_async_copy(ref, held, input_sems.at[index])
        for index, (ref, held) in enumerate(zip(inputs, held_refs))
    ]
    for load in loads:
        load.start()
    pos_ref, cot_ref = held_refs[:2]
    vector_refs = held_refs[2:]
    my_slide = lax.axis_index(DP)

    targets = [(0, rank, rank) for rank in range(places)]
    for rank in range(places):
        for other in range(2, slides):
            targets.append((1 + rank * (slides - 2) + other - 2, 0, other * places + rank))
    targets[:places] = [(0, rank, places + rank) for rank in range(places)]

    def copy_of(index, slot):
        buffer, row, _ = targets[index]
        side = tiles_ref.shape[1]
        lines = send_refs[buffer].at[pl.ds(row * side, side)]
        return pltpu.make_async_copy(tiles_ref.at[slot], lines, sems.at[index])

    for index in range(slides):
        count_ref[index] = 0
    for index in range(slides * places):
        slot_ref[index] = -1

    def place_slot(slot, carry):
        entry = route_ref[my_slide, 0, slot]

        @pl.when(entry >= 0)
        def _send():
            other = lax.div(entry, PROC) ^ my_slide
            rank = count_ref[other]
            count_ref[other] = rank + 1
            slot_ref[other * places + rank] = slot

        return carry

    lax.fori_loop(0, slots, place_slot, 0)
    for index, (_, _, key) in enumerate(targets):
        slot = slot_ref[key]

        @pl.when(slot >= 0)
        def _start():
            copy_of(index, slot).start()

    for load in loads:
        load.wait()
    small_ref[:, 0:E] = cot_ref[...]
    for row, start in enumerate((ROWS_AT, COLS_AT)):
        small_ref[:, start : start + LANES] = jnp.zeros((1, LANES), jnp.float32)
        small_ref[:, start : start + slots] = pos_ref[row : row + 1, :].astype(jnp.float32)
    small_ref[:, COUNT_AT:SMALL] = jnp.full((1, LANES), counts_ref[0], jnp.int32).astype(jnp.float32)
    channels = tiles_ref.shape[3]
    extra = []
    rest = small_ref[...]
    for piece in range(PIECES):
        part = rest.astype(jnp.bfloat16).astype(jnp.float32)
        rest = rest - part
        extra += [part[:, at : at + channels] for at in range(0, SMALL, channels)]
    extra.append(jnp.zeros((ROW_UNIT - len(extra), channels), jnp.float32))
    extra = jnp.concatenate(extra, axis=0).astype(jnp.bfloat16)
    for ref in send_refs[: slides - 1]:
        ref[ref.shape[0] - 1] = extra
    vectors_ref[...] = jnp.zeros(vectors_ref.shape, jnp.float32)
    for index, ref in enumerate(vector_refs):
        size = ref.shape[0]
        vectors_ref[index : index + 1, 0:size] = ref[...].reshape(1, size)

    kinds = 1 + places
    for field in range(CLASSES + kinds * CLASS_SIZE):
        table_ref[field] = 0
    for kind in range(kinds):
        for item in range(PROC):
            table_ref[class_field(kind, SLOT, item)] = PROC
    for other in range(slides):
        source = my_slide ^ other
        count_ref[0] = 0

        def take(slot, carry):
            entry = route_ref[source, 0, slot]
            proc = entry - my_slide * PROC

            @pl.when((proc >= 0) & (proc < PROC))
            def _take():
                rank = count_ref[0]
                count_ref[0] = rank + 1
                table_ref[FILLED + proc] = 1
                table_ref[SLIDE + proc] = source
                table_ref[PLACE + proc] = slot
                kind = 0 if other < 2 else 1 + rank
                base = CLASSES + kind * CLASS_SIZE
                item = table_ref[base]
                table_ref[base] = item + 1
                table_ref[base + 1 + SLOT * PROC + item] = proc
                if other == 0:
                    table_ref[base + 1 + FROM * PROC + item] = 0
                    table_ref[base + 1 + OWN * PROC + item] = slot
                else:
                    table_ref[base + 1 + FROM * PROC + item] = 1 + rank if other == 1 else other - 2

            return carry

        lax.fori_loop(0, slots, take, 0)
        if other == 0:
            own = table_ref[class_field(0, -1)]
            for item in range(1, PROC):

                @pl.when(item >= own)
                def _hold():
                    table_ref[class_field(0, OWN, item)] = table_ref[class_field(0, OWN, item - 1)]

    for kind in range(kinds):
        items = table_ref[class_field(kind, -1)]
        for item in range(1, PROC):

            @pl.when(item >= items)
            def _hold_slot():
                table_ref[class_field(kind, SLOT, item)] = table_ref[class_field(kind, SLOT, item - 1)]

    for index, (_, _, key) in enumerate(targets):

        @pl.when(slot_ref[key] >= 0)
        def _wait():
            copy_of(index, 0).wait()


def pack_tiles(counts, routing, tile_maps, positions, cotangent, vectors, slides, places):
    slots = tile_maps.shape[0]
    smem = pl.BlockSpec(memory_space=pltpu.SMEM)
    vmem = pl.BlockSpec(memory_space=pltpu.VMEM)
    buffers = 1 + places * (slides - 2)
    side = tile_maps.shape[1]
    shapes = [places * side + 1] + [side + 1] * (slides - 2) + [side] * (buffers - slides + 1)
    widest = max(vector.shape[0] for vector in vectors)
    inputs = (positions, cotangent) + vectors
    fixed = [pinned(x) for x in (tile_maps,) + inputs]
    outs = pl.pallas_call(
        functools.partial(pack_kernel, slides, slots, places),
        out_shape=tuple(
            jax.ShapeDtypeStruct((size,) + tile_maps.shape[2:], tile_maps.dtype) for size in shapes
        )
        + (
            jax.ShapeDtypeStruct((CLASSES + (1 + places) * CLASS_SIZE,), jnp.int32),
            jax.ShapeDtypeStruct((1, SMALL), jnp.float32),
            jax.ShapeDtypeStruct((8, widest), jnp.float32),
        ),
        in_specs=[smem, smem] + [IN_HBM] * len(fixed),
        out_specs=(vmem,) * buffers + (smem, vmem, vmem),
        scratch_shapes=[
            pltpu.SMEM((slides,), jnp.int32),
            pltpu.SMEM((slides * places,), jnp.int32),
            pltpu.SemaphoreType.DMA((slides * places,)),
        ]
        + [pltpu.VMEM(x.shape, x.dtype) for x in inputs]
        + [pltpu.SemaphoreType.DMA((len(inputs),))],
        compiler_params=pltpu.CompilerParams(vmem_limit_bytes=8 * MIB),
        name="pack_tiles",
    )(counts, routing, *fixed)
    return outs[:-3], outs[-3:]


def forward_kernel(kind, last, inputs, kept, table_ref, *refs):
    tile_refs, refs = refs[:inputs], refs[inputs:]
    taps_hbm, vectors_ref, expand_hbm, reduce_hbm, head_hbm = refs[:5]
    refs = refs[5 + (0 if kind == 0 else kept) :]
    out_hbms, refs = refs[:kept], refs[kept:]
    held, refs = refs[:kept], refs[kept:]
    taps_ref, expand_ref, reduce_ref, head_ref, padded, depth_out, normed, pre, load_sems = refs[:9]
    tile_sems, out_sems = refs[9:]
    out_s, embed_s, unit_s, inv_s, hidden_s, slope_s, head_slope_s, source_s = held
    items = table_ref[class_field(kind, -1)]
    side, channels = out_s.shape[1], out_s.shape[3]
    cells = side * side
    bands = channels // LANES
    low = ROW_UNIT // 2
    reach = KS // 2
    constants = [
        pltpu.make_async_copy(source, target, load_sems.at[index])
        for index, (source, target) in enumerate(
            (
                (taps_hbm, taps_ref),
                (expand_hbm, expand_ref),
                (reduce_hbm, reduce_ref),
                (head_hbm, head_ref),
            )
        )
    ]

    def tile_copy(ref, row, buffer):
        lines = ref.at[row] if len(ref.shape) == 4 else ref.at[pl.ds(row * side, side)]
        return pltpu.make_async_copy(lines, source_s.at[buffer], tile_sems.at[buffer])

    def load(item, buffer):
        origin = table_ref[class_field(kind, FROM) + item]
        place = 0
        for index, ref in enumerate(tile_refs):
            own = kind == 0 and index == 0
            for row in range(1 if own else ref.shape[0] // side):

                @pl.when(origin == place)
                def _load():
                    at = table_ref[class_field(kind, OWN) + item] if own else row
                    tile_copy(ref, at, buffer).start()

                place += 1

    def keep(part, slot, buffer):
        return pltpu.make_async_copy(
            held[part].at[buffer], out_hbms[part].at[slot], out_sems.at[part, buffer]
        )

    def wait_kept(buffer):
        for part in range(kept - 1):
            keep(part, 0, buffer).wait()

    def vector(index, lanes):
        return vectors_ref[index : index + 1, lanes]

    @pl.when(items > 0)
    def _first():
        load(0, 0)
        for copy in constants:
            copy.start()
        edge = jnp.zeros((side, low, LANES), jnp.float32)
        for band in range(bands):
            padded[band, :, 0:low, :] = edge
            padded[band, :, low + side :, :] = edge

    def one_item(item, carry):
        buffer = lax.rem(item, 2)
        slot = table_ref[class_field(kind, SLOT) + item]

        @pl.when(item >= 2)
        def _free():
            wait_kept(buffer)

        tile_copy(tile_refs[0], 0, buffer).wait()

        @pl.when(item == 0)
        def _taps():
            constants[0].wait()

        for band in range(bands):
            for at in range(side):
                padded[band, at, low : low + side, :] = source_s[
                    buffer, at, :, band * LANES : (band + 1) * LANES
                ].astype(jnp.float32)

        def convolve(band, carry):
            lanes = pl.ds(pl.multiple_of(band * LANES, LANES), LANES)
            bias = jnp.broadcast_to(vectors_ref[DEPTH_BIAS : DEPTH_BIAS + 1, lanes], (side, LANES))
            totals = [bias for _ in range(side)]
            for col in range(KS):
                start = low - reach + col
                weights = [
                    jnp.broadcast_to(
                        taps_ref[row * KS + col : row * KS + col + 1, lanes], (side, LANES)
                    ).astype(jnp.bfloat16)
                    for row in range(KS)
                ]
                sums = [None] * side
                for at in range(side):
                    line = padded[band, at, start : start + side, :].astype(jnp.bfloat16)
                    for row in range(KS):
                        place = at - row + reach
                        if 0 <= place < side:
                            term = weights[row] * line
                            sums[place] = term if sums[place] is None else sums[place] + term
                for place in range(side):
                    totals[place] = totals[place] + sums[place].astype(jnp.float32)
            for place in range(side):
                depth_out[band, place * side : (place + 1) * side, :] = totals[place]
            return carry

        lax.fori_loop(0, bands, convolve, 0)
        for start in range(0, cells, PART):
            rows = slice(start, start + PART)
            pieces = [depth_out[band, rows, :] for band in range(bands)]
            mean = jnp.sum(sum(pieces), axis=1, keepdims=True) * (1.0 / channels)
            pieces = [piece - mean for piece in pieces]
            var = jnp.sum(sum(p * p for p in pieces), axis=1, keepdims=True) * (1.0 / channels)
            inv = lax.rsqrt(var + EPSILON)
            inv_s[buffer, rows, :] = jnp.broadcast_to(inv, (PART, LANES))
            for band in range(bands):
                lanes = slice(band * LANES, (band + 1) * LANES)
                unit = pieces[band] * inv
                unit_s[buffer, rows, lanes] = unit
                normed[rows, lanes] = (unit * vector(GAIN, lanes) + vector(SHIFT, lanes)).astype(
                    jnp.bfloat16
                )

        @pl.when(item == 0)
        def _weights():
            for copy in constants[1:]:
                copy.wait()

        @pl.when(item + 1 < items)
        def _next():
            @pl.when(item >= 1)
            def _source_free():
                keep(kept - 1, 0, 1 - buffer).wait()

            load(item + 1, 1 - buffer)

        for part in (2, 3):
            keep(part, slot, buffer).start()
        for index, begin in enumerate(range(0, expand_ref.shape[1], WIDTH)):
            cols = slice(begin, begin + WIDTH)
            at = index % pre.shape[0]
            pre[at] = mix(normed[...], expand_ref[:, cols])
            for start in range(0, cells, PART):
                rows = slice(start, start + PART)
                act, slope = gelu_and_slope(pre[at, rows, :] + vector(EXPAND_BIAS, cols))
                hidden_s[buffer, rows, cols] = act.astype(jnp.bfloat16)
                slope_s[buffer, rows, cols] = slope.astype(jnp.bfloat16)
        for part in (4, 5):
            keep(part, slot, buffer).start()
        lanes = slice(0, channels)
        depth_rows = mix(hidden_s[buffer], reduce_ref[...])
        for at in range(side):
            rows = slice(at * side, (at + 1) * side)
            branch = vector(SCALE, lanes) * (depth_rows[rows] + vector(REDUCE_BIAS, lanes))
            line = (source_s[buffer, at].astype(jnp.float32) + branch).astype(jnp.bfloat16)
            normed[rows, :] = line
            out_s[buffer, at] = line
        for part in (0, 7):
            keep(part, slot, buffer).start()
        for index, begin in enumerate(range(0, head_ref.shape[1], WIDTH)):
            cols = slice(begin, begin + WIDTH)
            at = index % pre.shape[0]
            pre[at] = mix(normed[...], head_ref[:, cols])
            total = None
            for start in range(0, cells, PART):
                rows = slice(start, start + PART)
                act, slope = gelu_and_slope(pre[at, rows, :])
                head_slope_s[buffer, rows, cols] = slope.astype(jnp.bfloat16)
                folded = act[0:8]
                for piece in range(8, PART, 8):
                    folded = folded + act[piece : piece + 8]
                total = folded if total is None else total + folded
            mean = jnp.sum(total, axis=0, keepdims=True) * (1.0 / cells)
            embed_s[buffer, :, cols] = jnp.broadcast_to(mean, (8, WIDTH))
        for part in (1, 6):
            keep(part, slot, buffer).start()
        return carry

    lax.fori_loop(0, items, one_item, 0)
    for back in (1, 2):

        @pl.when(items >= back)
        def _drain():
            buffer = lax.rem(items - back, 2)
            for part in range(kept):
                keep(part, 0, buffer).wait()

    if last:
        filled = sum(table_ref[FILLED + proc] for proc in range(PROC))

        @pl.when(filled < PROC)
        def _zeros():
            for ref in held:
                ref[0] = jnp.zeros(ref.shape[1:], ref.dtype)

        for proc in range(PROC):

            @pl.when(table_ref[FILLED + proc] == 0)
            def _empty():
                for part in range(kept):
                    keep(part, proc, 0).start()
                wait_kept(0)
                keep(kept - 1, proc, 0).wait()


def pinned(array):
    return pltpu.with_memory_space_constraint(array, pltpu.HBM)


def forward_block(kind, last, table, tiles, taps, vectors, expand, reduce, head, before):
    side, channels = tiles[0].shape[-2:]
    cells, hid, embed = side * side, expand.shape[1], head.shape[1]
    bands = channels // LANES
    outs = (
        ((side, side, channels), jnp.bfloat16),
        ((8, embed), jnp.float32),
        ((cells, channels), jnp.float32),
        ((cells, LANES), jnp.float32),
        ((cells, hid), jnp.bfloat16),
        ((cells, hid), jnp.bfloat16),
        ((cells, embed), jnp.bfloat16),
        ((side, side, channels), jnp.bfloat16),
    )
    smem = pl.BlockSpec(memory_space=pltpu.SMEM)
    vmem = pl.BlockSpec(memory_space=pltpu.VMEM)
    if kind == 0:
        tiles = (pinned(tiles[0]),) + tuple(tiles[1:])
    first = 1 + len(tiles) + 5
    return pl.pallas_call(
        functools.partial(forward_kernel, kind, last, len(tiles), len(outs)),
        out_shape=tuple(pltpu.HBM((PROC,) + shape, dtype) for shape, dtype in outs),
        in_specs=[smem]
        + [HBM] * len(tiles)
        + [IN_HBM, vmem, IN_HBM, IN_HBM, IN_HBM]
        + [IN_HBM] * len(before),
        out_specs=(IN_HBM,) * len(outs),
        scratch_shapes=[pltpu.VMEM((2,) + shape, dtype) for shape, dtype in outs]
        + [
            pltpu.VMEM(taps.shape, jnp.float32),
            pltpu.VMEM(expand.shape, jnp.bfloat16),
            pltpu.VMEM(reduce.shape, jnp.bfloat16),
            pltpu.VMEM(head.shape, jnp.bfloat16),
            pltpu.VMEM((bands, side, side + ROW_UNIT, LANES), jnp.float32),
            pltpu.VMEM((bands, cells, LANES), jnp.float32),
            pltpu.VMEM((cells, channels), jnp.bfloat16),
            pltpu.VMEM((3, cells, WIDTH), jnp.float32),
            pltpu.SemaphoreType.DMA((4,)),
            pltpu.SemaphoreType.DMA((2,)),
            pltpu.SemaphoreType.DMA((len(outs), 2)),
        ],
        input_output_aliases={first + index: index for index in range(len(before))},
        compiler_params=pltpu.CompilerParams(vmem_limit_bytes=24 * MIB),
        cost_estimate=cost(1.0),
        name="forward_block_" + str(kind),
    )(table, *tiles, pinned(taps), vectors, pinned(expand), pinned(reduce), pinned(head), *before)


def cost(micros):
    return pl.CostEstimate(flops=int(micros * 1e9), bytes_accessed=1024, transcendentals=0)


def rows_kernel(slides, table_ref, embed_ref, small_ref, *refs):
    buffer_refs, (out_ref, smalls_ref, rows_ref, lines_ref, extra_ref, sems) = (
        refs[: slides - 1],
        refs[slides - 1 :],
    )
    copies = [
        pltpu.make_async_copy(ref.at[ref.shape[0] - 1], extra_ref.at[index], sems.at[index])
        for index, ref in enumerate(buffer_refs)
    ]
    for copy in copies:
        copy.start()
    my_slide, my_member = lax.axis_index(DP), lax.axis_index(GROUP)
    channels = extra_ref.shape[2]
    half = E // 2
    channel = lax.broadcasted_iota(jnp.int32, (1, E), 1)
    inner = jnp.where(channel < half, channel, channel - half)
    odd = lax.rem(inner, 2)
    frequency = jnp.exp((inner - odd).astype(jnp.float32) * (-math.log(10000.0) / half))
    phase = odd.astype(jnp.float32) * (0.5 * math.pi)
    lane = lax.broadcasted_iota(jnp.int32, (1, LANES), 1)
    smalls_ref[0] = small_ref[...]
    lines = SMALL // channels
    for index, copy in enumerate(copies):
        copy.wait()
        extra = extra_ref[index].astype(jnp.float32)
        for line in range(lines):
            total = extra[line : line + 1]
            for piece in range(1, PIECES):
                total = total + extra[piece * lines + line : piece * lines + line + 1]
            smalls_ref[1 + index, :, line * channels : (line + 1) * channels] = total
    for proc in range(PROC):
        filled = table_ref[FILLED + proc]
        slide = table_ref[SLIDE + proc]
        slot = table_ref[PLACE + proc]
        held = smalls_ref[0]
        for other in range(1, slides):
            held = jnp.where((slide ^ my_slide) == other, smalls_ref[other], held)
        spots = [
            jnp.sum(jnp.where(lane == slot, held[:, at : at + LANES], 0.0), axis=1, keepdims=True)
            for at in (ROWS_AT, COLS_AT)
        ]
        angle = jnp.where(channel < half, spots[0], spots[1]) * frequency + phase
        target = jnp.where(lane == 0, slide, jnp.where(lane == 1, slot, my_member))
        target = jnp.where(filled != 0, target, jnp.where(lane == 2, -1, 0))
        target = jnp.where(lane < 3, target, 0)
        rows_ref[proc : proc + 1, 0:E] = angle
        rows_ref[2 * PROC + proc : 2 * PROC + proc + 1, 0:E] = embed_ref[proc, 0:1, :]
        rows_ref[proc : proc + 1, E:] = target.astype(jnp.float32)
    code = jnp.sin(rows_ref[0 : 2 * PROC, 0:E])
    embed = rows_ref[2 * PROC : 4 * PROC, 0:E].astype(jnp.bfloat16).astype(jnp.float32)
    row_id = lax.broadcasted_iota(jnp.int32, (2 * PROC, E), 0)
    there = row_id < 0
    for proc in range(PROC):
        there = there | ((row_id == proc) & (table_ref[FILLED + proc] != 0))
    total = jnp.where(there, embed + code, 0.0)
    rows_ref[0 : 2 * PROC, 0:E] = total
    lines_ref[...] = jnp.zeros(lines_ref.shape, jnp.float32)
    for copied in range(0, ROW_UNIT, 2 * PROC):
        lines_ref[copied : copied + PROC, :] = rows_ref[0:PROC, 0:HALF]
        lines_ref[copied + PROC : copied + 2 * PROC, 0 : E + LANES - HALF] = rows_ref[0:PROC, HALF:]
    sent = lines_ref[...].astype(jnp.bfloat16)
    for start in range(0, out_ref.shape[0], ROW_UNIT):
        out_ref[start : start + ROW_UNIT, :] = sent


def tile_rows(table, embeds, small, buffers, devices):
    smem = pl.BlockSpec(memory_space=pltpu.SMEM)
    vmem = pl.BlockSpec(memory_space=pltpu.VMEM)
    slides = 1 + len(buffers)
    return pl.pallas_call(
        functools.partial(rows_kernel, slides),
        out_shape=(
            jax.ShapeDtypeStruct((devices * 2 * PROC, HALF), jnp.bfloat16),
            jax.ShapeDtypeStruct((slides, 1, SMALL), jnp.float32),
        ),
        in_specs=[smem, vmem, vmem] + [HBM] * len(buffers),
        out_specs=(vmem, vmem),
        scratch_shapes=[
            pltpu.VMEM((4 * PROC, E + LANES), jnp.float32),
            pltpu.VMEM((ROW_UNIT, HALF), jnp.float32),
            pltpu.VMEM((len(buffers),) + buffers[0].shape[1:], jnp.bfloat16),
            pltpu.SemaphoreType.DMA((len(buffers),)),
        ],
        cost_estimate=cost(1.0),
        name="tile_rows",
    )(table, embeds, small, *buffers)


def slide_kernel(
    length,
    members,
    slides,
    table_ref,
    came_ref,
    taps_hbm,
    matrix_hbm,
    vectors_ref,
    smalls_ref,
    feature_ref,
    grad_ref,
    rows,
    back,
    mixed,
    pre,
    grad_agg,
    taps_ref,
    matrix_ref,
    sems,
):
    loads = [
        pltpu.make_async_copy(taps_hbm, taps_ref, sems.at[0]),
        pltpu.make_async_copy(matrix_hbm, matrix_ref, sems.at[1]),
    ]
    for load in loads:
        load.start()
    my_slide = lax.axis_index(DP)
    border = ROW_UNIT
    edge = jnp.zeros((border, rows.shape[2]), jnp.float32)
    reach = KERNEL_TAPS // 2
    blocks = [slice(start, start + WIDTH) for start in range(0, E, WIDTH)]
    lane = lax.broadcasted_iota(jnp.int32, (8, LANES), 1)
    scales = jnp.where(lane == 0, length, jnp.where(lane == 1, members, jnp.where(lane == 2, 1, 0)))
    tail = came_ref[:, E - HALF : E - HALF + LANES]
    target = mix_cols(scales.astype(jnp.float32).astype(jnp.bfloat16), tail)[0:1, :]
    lines = came_ref.shape[0]
    second = lax.rem(lax.broadcasted_iota(jnp.int32, (1, lines), 1), 2 * PROC) >= PROC
    target = jnp.where(second, target, -1.0)
    step = lax.broadcasted_iota(jnp.int32, (length, 1), 0).astype(jnp.float32)

    def dilate(ref, slide, direction, cols):
        total = ref[slide, border : border + length, cols]
        for tap in range(KERNEL_TAPS):
            start = border + direction * (tap - reach) * TILE_DILATION
            total = total + taps_ref[tap : tap + 1, cols] * ref[slide, start : start + length, cols]
        return total

    def seen(other):
        count = smalls_ref[other][:, COUNT_AT : COUNT_AT + 1]
        here = step < count
        return here, jnp.where(here, 1.0 / count, 0.0)

    for other in range(slides):
        slide = my_slide ^ other
        here, _ = seen(other)
        first = lax.convert_element_type(slide * length, jnp.float32)
        late = ((target - first) == step).astype(jnp.float32)
        early = pltpu.roll(late, lines - PROC, axis=1).astype(jnp.bfloat16)
        late = late.astype(jnp.bfloat16)
        for ref in (rows, back):
            ref[slide, 0:border, :] = edge
            ref[slide, border + length :, :] = edge
        if other == 0:
            loads[0].wait()
        for cols in blocks:
            pick, at = (early, cols.start) if cols.start < HALF else (late, cols.start - HALF)
            rows[slide, border : border + length, cols] = jnp.where(
                here, mix(pick, came_ref[:, at : at + WIDTH]), 0.0
            )
            mixed[other * length : (other + 1) * length, cols] = dilate(
                rows, slide, 1, cols
            ).astype(jnp.bfloat16)
    loads[1].wait()
    for cols in blocks:
        pre[:, cols] = mix(mixed[...], matrix_ref[:, cols])
        for other in range(slides):
            small = smalls_ref[other]
            _, share = seen(other)
            total = None
            for start in range(0, length, PART):
                part = slice(other * length + start, other * length + start + PART)
                weight = share[start : start + PART]
                act, slope = gelu_and_slope(
                    pre[part, cols] + vectors_ref[SLIDE_BIAS : SLIDE_BIAS + 1, cols]
                )
                grad_agg[part, cols] = (small[:, cols] * weight * slope).astype(jnp.bfloat16)
                if other == 0:
                    piece = jnp.sum(act * weight, axis=0, keepdims=True)
                    total = piece if total is None else total + piece
            if other == 0:
                feature_ref[:, cols] = total
    for cols in blocks:
        pre[:, cols] = mix_cols(grad_agg[...], matrix_ref[cols, :])
        for other in range(slides):
            slide = my_slide ^ other
            here, _ = seen(other)
            back[slide, border : border + length, cols] = pre[
                other * length : (other + 1) * length, cols
            ]
            total = jnp.where(here, dilate(back, slide, -1, cols), 0.0)
            rows[slide, border : border + length, cols] = total.astype(jnp.bfloat16).astype(
                jnp.float32
            )
    my_member = lax.axis_index(GROUP)
    for proc in range(PROC):
        at = border + table_ref[PLACE + proc] * members + my_member
        row = rows[table_ref[SLIDE + proc], pl.ds(at, 1), :]
        grad_ref[proc] = jnp.where(table_ref[FILLED + proc] != 0, row, 0.0)


def slide_grads(length, members, table, came, taps, matrix, vectors, smalls):
    slides = smalls.shape[0]
    smem = pl.BlockSpec(memory_space=pltpu.SMEM)
    vmem = pl.BlockSpec(memory_space=pltpu.VMEM)
    padded = (slides, length + 2 * ROW_UNIT, E)
    return pl.pallas_call(
        functools.partial(slide_kernel, length, members, slides),
        out_shape=(
            jax.ShapeDtypeStruct((1, E), jnp.float32),
            jax.ShapeDtypeStruct((PROC, 1, E), jnp.float32),
        ),
        in_specs=[smem, vmem, IN_HBM, IN_HBM, vmem, vmem],
        out_specs=(vmem, vmem),
        scratch_shapes=[
            pltpu.VMEM(padded, jnp.float32),
            pltpu.VMEM(padded, jnp.float32),
            pltpu.VMEM((slides * length, E), jnp.bfloat16),
            pltpu.VMEM((slides * length, E), jnp.float32),
            pltpu.VMEM((slides * length, E), jnp.bfloat16),
            pltpu.VMEM(taps.shape, jnp.float32),
            pltpu.VMEM(matrix.shape, jnp.bfloat16),
            pltpu.SemaphoreType.DMA((2,)),
        ],
        compiler_params=pltpu.CompilerParams(vmem_limit_bytes=24 * MIB),
        cost_estimate=cost(6.0),
        name="slide_grads",
    )(table, came, pinned(taps), pinned(matrix), vectors, smalls)


class Plan:
    def __init__(self, slides, members, channels, hid):
        self.devices = slides * members
        self.ys, self.g1, self.g2 = slides // 2, 4, members // 4
        assert self.ys == self.g2
        self.channels = channels
        self.pieces = hid // channels
        self.expand_rows = channels // self.devices
        self.reduce_rows = hid // self.devices
        self.block_rows = -(-self.reduce_rows // ROW_UNIT) * ROW_UNIT
        self.share = KS * KS * channels // self.devices

    def spots(self):
        my_core, my_y = lax.axis_index("core"), lax.axis_index("y")
        my_z, my_x = lax.axis_index("g1"), lax.axis_index("g2")
        for device in range(self.devices):
            slide, member = divmod(device, self.g1 * self.g2)
            (y, core), (z, x) = divmod(slide, 2), divmod(member, self.g2)
            yield (
                my_core ^ core,
                lax.rem(y - my_y + self.ys, self.ys),
                lax.rem(x - my_x + self.g2, self.g2),
                lax.rem(z - my_z + self.g1, self.g1),
            )


def send_out(staged, sems, refs):
    copies = [
        pltpu.make_async_copy(staged.at[index], ref, sems.at[index]) for index, ref in enumerate(refs)
    ]
    for copy in copies:
        copy.start()
    for copy in copies:
        copy.wait()


def padded_block(block, rows):
    extra = rows - block.shape[0]
    if extra:
        block = jnp.concatenate([block, jnp.zeros((extra, block.shape[1]), block.dtype)], axis=0)
    return block.astype(jnp.bfloat16)


def turn_kernel(unit_ref, vectors_ref, out_ref, normed, eye_ref):
    cells, channels = unit_ref.shape[1:]
    eye_ref[...] = unit_matrix(channels)
    for start in range(0, cells, PART):
        rows = slice(start, start + PART)
        gain = vectors_ref[GAIN : GAIN + 1, 0:channels]
        shift = vectors_ref[SHIFT : SHIFT + 1, 0:channels]
        normed[rows, :] = (unit_ref[0, rows, :] * gain + shift).astype(jnp.bfloat16)
    out_ref[...] = mix_cols(eye_ref[...], normed[...]).astype(jnp.bfloat16)


def unit_matrix(size):
    spot = lax.broadcasted_iota(jnp.int32, (size, size), 0)
    same = spot == lax.broadcasted_iota(jnp.int32, (size, size), 1)
    return same.astype(jnp.float32).astype(jnp.bfloat16)


def turned_normed(unit, vectors):
    cells, channels = unit.shape[1:]
    return pl.pallas_call(
        turn_kernel,
        out_shape=jax.ShapeDtypeStruct((channels, PROC * cells), jnp.bfloat16),
        grid=(PROC,),
        in_specs=[pl.BlockSpec((1, cells, channels), lambda i: (i, 0, 0)), whole(vectors.shape)],
        out_specs=pl.BlockSpec((channels, cells), lambda i: (0, i)),
        scratch_shapes=[
            pltpu.VMEM((cells, channels), jnp.bfloat16),
            pltpu.VMEM((channels, channels), jnp.bfloat16),
        ],
        compiler_params=pltpu.CompilerParams(vmem_limit_bytes=8 * MIB),
        cost_estimate=cost(3.0),
        name="turned_normed",
    )(unit, vectors)


def weights_kernel(
    plan,
    grad_ref,
    hidden_ref,
    head_slope_ref,
    slope_ref,
    normed_ref,
    vectors_ref,
    head_ref,
    reduce_ref,
    grad_pre_hbm,
    keep_ref,
    send_ref,
    grad_pre,
    turned,
    grad_head,
    eye_ref,
    staged,
    sems,
    pre_sems,
):
    cells, channels = slope_ref.shape[1], normed_ref.shape[0]
    hid = reduce_ref.shape[0]
    every = slice(0, channels)

    def vector(index, lanes):
        return vectors_ref[index : index + 1, lanes]

    eye_ref[...] = unit_matrix(channels)

    def one_slot(slot, carry):
        rows_all = pl.ds(pl.multiple_of(slot * cells, cells), cells)
        row = grad_ref[slot] * (1.0 / cells)
        for start in range(0, cells, PART):
            rows = slice(start, start + PART)
            grad_head[rows, :] = (row * head_slope_ref[slot, rows, :].astype(jnp.float32)).astype(
                jnp.bfloat16
            )
        grad_mlp = (vector(SCALE, every) * mix_cols(grad_head[...], head_ref[...])).astype(
            jnp.bfloat16
        )
        turned[:, rows_all] = mix_cols(eye_ref[...], grad_mlp).astype(jnp.bfloat16)
        for begin in range(0, hid, WIDTH):
            cols = slice(begin, begin + WIDTH)
            grad_hidden = mix_cols(grad_mlp, reduce_ref[cols, :])
            grad_pre[rows_all, cols] = (
                grad_hidden * slope_ref[slot, :, cols].astype(jnp.float32)
            ).astype(jnp.bfloat16)
        return carry

    lax.fori_loop(0, PROC, one_slot, 0)
    writes = [
        pltpu.make_async_copy(
            grad_pre.at[pl.ds(slot * cells, cells)], grad_pre_hbm.at[slot], pre_sems.at[slot]
        )
        for slot in range(PROC)
    ]
    for write in writes:
        write.start()
    spots = list(plan.spots())
    per_block = channels // plan.reduce_rows
    tall = plan.block_rows
    for index in range(plan.pieces):
        cols = slice(index * channels, (index + 1) * channels)
        total = mix(turned[...], hidden_ref[:, cols]).astype(jnp.bfloat16)
        back = mix_cols(eye_ref[...], total)
        for part in range(per_block):
            block = back[part * plan.reduce_rows : (part + 1) * plan.reduce_rows]
            core, y, x, z = spots[index * per_block + part]
            staged[core, 0, x, y, z] = padded_block(block, tall)
    totals = []
    for quarter in range(plan.pieces):
        cols = slice(quarter * channels, (quarter + 1) * channels)
        totals.append(mix(normed_ref[...], grad_pre[:, cols]))
    size = plan.expand_rows
    for device in range(plan.devices):
        rows = slice(device * size, (device + 1) * size)
        block = jnp.concatenate([total[rows] for total in totals], axis=0)
        core, y, x, z = spots[device]
        staged[core, 1, y, x, z] = padded_block(block, tall)
    send_out(staged, sems, (keep_ref, send_ref))
    for write in writes:
        write.wait()


def taps_kernel(
    plan,
    first,
    last,
    table_ref,
    source_ref,
    grad_pre_ref,
    unit_ref,
    inv_ref,
    before_ref,
    vectors_ref,
    expand_ref,
    out_ref,
    padded,
    tap_sums,
    tap_rows,
    grad_norm,
    depth_back,
):
    step = pl.program_id(0)
    filled = table_ref[FILLED + first + step]
    side, channels = source_ref.shape[1], source_ref.shape[3]
    bands = channels // LANES
    low = ROW_UNIT // 2
    reach = KS // 2

    @pl.when(step == 0)
    def _start():
        if first:
            tap_sums[...] = before_ref[...]
        else:
            tap_sums[...] = jnp.zeros(tap_sums.shape, jnp.float32)

    @pl.when(filled != 0)
    def _work():
        cells = side * side
        gain = vectors_ref[GAIN : GAIN + 1, 0:channels]
        grad_norm[...] = mix_cols(grad_pre_ref[0], expand_ref[...])
        for start in range(0, cells, PART):
            rows = slice(start, start + PART)
            scaled = grad_norm[rows, :] * gain
            unit = unit_ref[0, rows, :]
            mean = jnp.sum(scaled, axis=1, keepdims=True) * (1.0 / channels)
            mean_unit = jnp.sum(scaled * unit, axis=1, keepdims=True) * (1.0 / channels)
            inv = inv_ref[0, rows, 0:1]
            for band in range(bands):
                lanes = slice(band * LANES, (band + 1) * LANES)
                depth_back[band, rows, :] = (
                    inv * (scaled[:, lanes] - mean - unit[:, lanes] * mean_unit)
                ).astype(jnp.bfloat16)
        edge = jnp.zeros((side, low, LANES), jnp.float32)
        for band in range(bands):
            lanes = slice(band * LANES, (band + 1) * LANES)
            padded[band, :, 0:low, :] = edge
            padded[band, :, low + side :, :] = edge
            for at in range(side):
                padded[band, at, low : low + side, :] = source_ref[0, at, :, lanes].astype(
                    jnp.float32
                )

        def taps_of(band, carry):
            for col in range(KS):
                start = low - reach + col
                folded = [None] * KS
                grads = {}
                for half in range(2):
                    sums = [None] * KS
                    for at in range(half * side // 2, (half + 1) * side // 2):
                        line = padded[band, at, start : start + side, :].astype(jnp.bfloat16)
                        for row in range(KS):
                            place = at - row + reach
                            if 0 <= place < side:
                                if place not in grads:
                                    grads[place] = depth_back[
                                        band, place * side : (place + 1) * side, :
                                    ]
                                term = line * grads[place]
                                sums[row] = term if sums[row] is None else sums[row] + term
                    for row in range(KS):
                        total = sums[row].astype(jnp.float32)
                        for piece in range(0, side, 8):
                            block = total[piece : piece + 8, :]
                            folded[row] = block if folded[row] is None else folded[row] + block
                for row in range(KS):
                    tap_sums[band, row * KS + col] = tap_sums[band, row * KS + col] + folded[row]
            return carry

        lax.fori_loop(0, bands, taps_of, 0)

    @pl.when(step == pl.num_programs(0) - 1)
    def _finish():
        if not last:
            out_ref[...] = tap_sums[...]
            return
        for band in range(bands):
            lanes = slice(band * LANES, (band + 1) * LANES)
            tap_rows[0 : KS * KS, lanes] = jnp.sum(tap_sums[band], axis=1)
            tap_rows[KS * KS :, lanes] = jnp.zeros((tap_rows.shape[0] - KS * KS, LANES), jnp.float32)
        for device in range(plan.devices):
            start = device * plan.share // channels
            out_ref[device] = tap_rows[start : start + TAP_ROWS, :]


def per_slot(array):
    shape = array.shape[1:]
    return pl.BlockSpec((1,) + shape, lambda i, table: (i,) + (0,) * len(shape))


def weight_grads(plan, embed_grad, saved, vectors, head, reduce):
    normed, hidden, slope, head_slope = saved
    cells, channels = slope.shape[1], normed.shape[0]
    hid = reduce.shape[0]
    vmem = pl.BlockSpec(memory_space=pltpu.VMEM)
    blocks = jax.ShapeDtypeStruct(
        (2, plan.ys, plan.g2, plan.g1, plan.block_rows, channels), jnp.bfloat16
    )
    return pl.pallas_call(
        functools.partial(weights_kernel, plan),
        out_shape=(pltpu.HBM((PROC, cells, hid), jnp.bfloat16), blocks, blocks),
        in_specs=[vmem] * 8,
        out_specs=(IN_HBM, HBM, HBM),
        scratch_shapes=[
            pltpu.VMEM((PROC * cells, hid), jnp.bfloat16),
            pltpu.VMEM((channels, PROC * cells), jnp.bfloat16),
            pltpu.VMEM((cells, head.shape[1]), jnp.bfloat16),
            pltpu.VMEM((channels, channels), jnp.bfloat16),
            pltpu.VMEM((2,) + blocks.shape, jnp.bfloat16),
            pltpu.SemaphoreType.DMA((2,)),
            pltpu.SemaphoreType.DMA((PROC,)),
        ],
        compiler_params=pltpu.CompilerParams(vmem_limit_bytes=36 * MIB),
        cost_estimate=cost(12.0),
        name="weight_grads",
    )(embed_grad, hidden.reshape(PROC * cells, hid), head_slope, slope, normed, vectors, head, reduce)


def tap_grads(plan, first, last, table, streams, before, vectors, expand):
    side, channels = streams[0].shape[1], streams[0].shape[3]
    bands = channels // LANES
    sums = (bands, KS * KS, 8, LANES)
    out = (plan.devices, TAP_ROWS, channels) if last else sums

    def items(array):
        shape = array.shape[1:]
        return pl.BlockSpec((1,) + shape, lambda i, table: (first + i,) + (0,) * len(shape))

    return pl.pallas_call(
        functools.partial(taps_kernel, plan, first, last),
        out_shape=jax.ShapeDtypeStruct(out, jnp.float32),
        grid_spec=pltpu.PrefetchScalarGridSpec(
            num_scalar_prefetch=1,
            grid=(PROC // 2,),
            in_specs=[items(stream) for stream in streams]
            + [whole(before.shape), whole(vectors.shape), whole(expand.shape)],
            out_specs=pl.BlockSpec(out, lambda i, table: (0,) * len(out)),
            scratch_shapes=[
                pltpu.VMEM((bands, side, side + ROW_UNIT, LANES), jnp.float32),
                pltpu.VMEM(sums, jnp.float32),
                pltpu.VMEM((KS * KS + 7, channels), jnp.float32),
                pltpu.VMEM((side * side, channels), jnp.float32),
                pltpu.VMEM((bands, side * side, LANES), jnp.bfloat16),
            ],
        ),
        compiler_params=pltpu.CompilerParams(vmem_limit_bytes=16 * MIB),
        cost_estimate=cost(4.0),
        name="tap_grads_" + str(first),
    )(table, *streams, before, vectors, expand)


def shifted(values, names, sizes, shift):
    count = math.prod(sizes)
    pairs = []
    for index in range(count):
        spot = []
        rest = index
        for size in reversed(sizes):
            spot.append(rest % size)
            rest //= size
        spot = spot[::-1]
        target = 0
        for at, step, size in zip(spot, shift, sizes):
            target = target * size + (at + step) % size
        pairs.append((index, target))
    return lax.ppermute(values, names, pairs)


def shifts(sizes):
    steps = [()]
    for size in sizes:
        steps = [step + (more,) for step in steps for more in range(size)]
    return steps


def exchange(values, names):
    return lax.all_to_all(values, names, split_axis=0, concat_axis=0, tiled=True)


def add_all(parts, kind=jnp.bfloat16):
    total = parts[0].astype(jnp.float32)
    for part in parts[1:]:
        total = total + part.astype(jnp.float32)
    return total.astype(kind)


def other_core(values):
    return shifted(values, ("core",), (2,), (1,))


def sum_axis(kept, sent, name, size, kind=jnp.bfloat16):
    return [kept] + [shifted(part, (name,), (size,), (step + 1,)) for step, part in enumerate(sent)]


def on_device(
    tile_maps,
    positions,
    counts,
    routing,
    depth_kernel,
    depth_bias,
    norm_gain,
    norm_shift,
    expand_weight,
    expand_bias,
    reduce_weight,
    reduce_bias,
    layer_scale,
    head_weight,
    slide_taps,
    slide_weight,
    slide_bias,
    cotangent,
):
    slides = lax.axis_size(DP)
    members = lax.axis_size(GROUP)
    my_device = lax.axis_index(ALL)
    slots, channels = tile_maps.shape[0], tile_maps.shape[3]
    devices, length, places = slides * members, slots * members, slots // slides
    plan = Plan(slides, members, channels, expand_weight.shape[1])

    raw = (
        norm_gain,
        norm_shift,
        layer_scale,
        reduce_bias,
        depth_bias,
        expand_bias,
        slide_bias,
    )
    packed, (table, small, vectors) = pack_tiles(
        counts, routing, tile_maps, positions, cotangent, raw, slides, places
    )

    def from_other(buffer, other):
        return lax.ppermute(buffer, DP, [(index, index ^ other) for index in range(slides)])

    from_core = from_other(packed[0], 1)
    arrived = []
    for rank in range(places):
        buffers = packed[1 + rank * (slides - 2) : 1 + (rank + 1) * (slides - 2)]
        if rank:
            buffers, from_core = lax.optimization_barrier((buffers, from_core))
        arrived.append([from_other(buffer, other + 2) for other, buffer in enumerate(buffers)])

    consts = (depth_kernel, vectors, expand_weight, reduce_weight, head_weight)
    saved = forward_block(0, False, table, (tile_maps, from_core), *consts, ())
    for rank in range(places):
        saved = forward_block(1 + rank, rank + 1 == places, table, arrived[rank], *consts, saved)
    tile_out, tile_embed, unit, inv, hidden, slope, head_slope, source = saved
    came, smalls = tile_rows(table, tile_embed, small, [from_core] + arrived[0], devices)
    came = exchange(came, ALL)
    normed = turned_normed(unit, vectors)
    came, normed = lax.optimization_barrier((came, normed))

    feature, embed_grad = slide_grads(
        length, members, table, came, slide_taps, slide_weight, vectors, smalls
    )
    grad_pre, kept, sent = weight_grads(
        plan,
        embed_grad,
        (normed, hidden, slope, head_slope),
        vectors,
        head_weight,
        reduce_weight,
    )
    streams = (source, pinned(grad_pre), unit, inv)

    names = ("g2", "y")
    size = plan.ys
    came = other_core(sent)
    none = jnp.zeros((channels // LANES, KS * KS, 8, LANES), jnp.float32)
    tap_sums = tap_grads(plan, 0, False, table, streams, none, vectors, expand_weight)
    came, tap_sums = lax.optimization_barrier((came, tap_sums))
    out = [
        [add_all([kept[kind, step], came[kind, step]]) for step in range(1, size)]
        for kind in range(2)
    ]
    stay = [add_all([kept[kind, 0], came[kind, 0]]) for kind in range(2)]
    out, tap_sums = lax.optimization_barrier((out, tap_sums))
    parts = [sum_axis(stay[kind], out[kind], names[kind], size) for kind in range(2)]
    taps = tap_grads(plan, PROC // 2, True, table, streams, tap_sums, vectors, expand_weight)
    out = [
        [add_all([part[step] for part in parts[kind]]) for step in range(1, size)]
        for kind in range(2)
    ]
    stay = [add_all([part[0] for part in parts[kind]]) for kind in range(2)]
    taps = taps[:, :DEPTH_ROWS].astype(jnp.bfloat16)
    out, taps = lax.optimization_barrier((out, taps))
    parts = [sum_axis(stay[kind], out[kind], names[1 - kind], size) for kind in range(2)]
    taps = exchange(taps, ALL)
    both = jnp.concatenate([add_all(parts[0]), add_all(parts[1])], axis=1)
    total = add_all(
        sum_axis(both[0], [both[step] for step in range(1, plan.g1)], "g1", plan.g1), jnp.float32
    )
    reduce_share = total[: plan.reduce_rows]
    expand_share = total[plan.block_rows : plan.block_rows + plan.pieces * plan.expand_rows]
    expand_share = expand_share.reshape(plan.pieces, plan.expand_rows, channels).transpose(1, 0, 2)
    depth_share = lax.dynamic_slice(
        jnp.sum(taps.astype(jnp.float32), axis=0).reshape(-1),
        (my_device * plan.share % channels,),
        (plan.share,),
    )
    return (tile_out, feature, expand_share.reshape(-1), reduce_share.reshape(-1), depth_share)


def solution(mesh):
    slides, members = mesh.shape["dp"], mesh.shape["group"]
    fine = Mesh(mesh.devices.reshape(slides // 2, 2, 4, members // 4), ALL)
    return jax.shard_map(
        on_device,
        mesh=fine,
        in_specs=(
            P(ALL, None, None, None),
            P(None, ALL),
            P(DP),
            P(None, GROUP, None),
        )
        + (P(),) * 13
        + (P(DP, None),),
        out_specs=(
            P(ALL, None, None, None),
            P(DP, None),
            P(ALL),
            P(ALL),
            P(ALL),
        ),
        check_vma=False,
    )
```

```python
import functools
import math

import jax
import jax.numpy as jnp
from jax import lax
from jax.experimental import pallas as pl
from jax.experimental.pallas import tpu as pltpu
from jax.sharding import Mesh, PartitionSpec as P

E = 768
KS = 7
KERNEL_TAPS = 7
TILE_DILATION = 3
PROC = 4
DP = ("y", "core")
GROUP = ("g1", "g2")
ALL = DP + GROUP

EPSILON = 1e-06
HALF_ROOT = 0.7071067811865476
INV_ROOT_TAU = 0.3989422804014327
BELL_SCALE = -0.7213475204444817
LANES = 128
ROW_UNIT = 16
DEPTH_ROWS = 4
TAP_ROWS = 8
MIB = 1024 * 1024
PART = 32
WIDTH = 256
GAIN, SHIFT, SCALE, REDUCE_BIAS, DEPTH_BIAS, EXPAND_BIAS, SLIDE_BIAS = range(7)
VECTORS = 7
ERFC_P = 0.3275911
ERFC_A = (0.254829592, -0.284496736, 1.421413741, -1.453152027, 1.061405429)

HBM = pl.BlockSpec(memory_space=pl.ANY)
IN_HBM = pl.BlockSpec(memory_space=pltpu.HBM)
ROWS_AT, COLS_AT, COUNT_AT, SMALL = E, E + LANES, E + 2 * LANES, E + 3 * LANES
PIECES = 3
HALF = 512


def whole(shape):
    return pl.BlockSpec(shape, lambda *_: (0,) * len(shape), pipeline_mode=pl.Buffered(1))


def gelu_and_slope(values):
    size = jnp.abs(values)
    divisor = 1.0 + (ERFC_P * HALF_ROOT) * size
    t = pl.reciprocal(divisor, approx=True)
    bell = jnp.exp2(values * (values * BELL_SCALE))
    poly = 0.5 * ERFC_A[4]
    for coefficient in ERFC_A[3::-1]:
        poly = poly * t + 0.5 * coefficient
    tail = poly * t * bell
    phi = jnp.where(values >= 0.0, 1.0 - tail, tail)
    return values * phi, phi + values * (INV_ROOT_TAU * bell)


def mix_cols(left_side, right_side):
    return lax.dot_general(
        left_side, right_side, (((1,), (1,)), ((), ())), preferred_element_type=jnp.float32
    )


def mix(left_side, right_side):
    return jnp.dot(left_side, right_side, preferred_element_type=jnp.float32)


FILLED, SLIDE, PLACE, CLASSES = 0, PROC, 2 * PROC, 3 * PROC
CLASS_SIZE = 1 + 3 * PROC


def class_field(kind, field, item=0):
    return CLASSES + kind * CLASS_SIZE + (1 + field * PROC + item if field >= 0 else 0)


SLOT, FROM, OWN = range(3)


def pack_kernel(slides, slots, places, counts_ref, route_ref, tiles_ref, pos_ref, cot_ref, *refs):
    inputs = (pos_ref, cot_ref) + refs[:VECTORS]
    refs = refs[VECTORS:]
    held_refs, refs = refs[-len(inputs) - 1 : -1], refs[: -len(inputs) - 1] + refs[-1:]
    send_refs, refs = refs[:-7], refs[-7:]
    table_ref, small_ref, vectors_ref, count_ref, slot_ref, sems, input_sems = refs
    loads = [
        pltpu.make_async_copy(ref, held, input_sems.at[index])
        for index, (ref, held) in enumerate(zip(inputs, held_refs))
    ]
    for load in loads:
        load.start()
    pos_ref, cot_ref = held_refs[:2]
    vector_refs = held_refs[2:]
    my_slide = lax.axis_index(DP)

    targets = [(0, rank, rank) for rank in range(places)]
    for rank in range(places):
        for other in range(2, slides):
            targets.append((1 + rank * (slides - 2) + other - 2, 0, other * places + rank))
    targets[:places] = [(0, rank, places + rank) for rank in range(places)]

    def copy_of(index, slot):
        buffer, row, _ = targets[index]
        side = tiles_ref.shape[1]
        lines = send_refs[buffer].at[pl.ds(row * side, side)]
        return pltpu.make_async_copy(tiles_ref.at[slot], lines, sems.at[index])

    for index in range(slides):
        count_ref[index] = 0
    for index in range(slides * places):
        slot_ref[index] = -1

    def place_slot(slot, carry):
        entry = route_ref[my_slide, 0, slot]

        @pl.when(entry >= 0)
        def _send():
            other = lax.div(entry, PROC) ^ my_slide
            rank = count_ref[other]
            count_ref[other] = rank + 1
            slot_ref[other * places + rank] = slot

        return carry

    lax.fori_loop(0, slots, place_slot, 0)
    for index, (_, _, key) in enumerate(targets):
        slot = slot_ref[key]

        @pl.when(slot >= 0)
        def _start():
            copy_of(index, slot).start()

    for load in loads:
        load.wait()
    small_ref[:, 0:E] = cot_ref[...]
    for row, start in enumerate((ROWS_AT, COLS_AT)):
        small_ref[:, start : start + LANES] = jnp.zeros((1, LANES), jnp.float32)
        small_ref[:, start : start + slots] = pos_ref[row : row + 1, :].astype(jnp.float32)
    small_ref[:, COUNT_AT:SMALL] = jnp.full((1, LANES), counts_ref[0], jnp.int32).astype(jnp.float32)
    channels = tiles_ref.shape[3]
    extra = []
    rest = small_ref[...]
    for piece in range(PIECES):
        part = rest.astype(jnp.bfloat16).astype(jnp.float32)
        rest = rest - part
        extra += [part[:, at : at + channels] for at in range(0, SMALL, channels)]
    extra.append(jnp.zeros((ROW_UNIT - len(extra), channels), jnp.float32))
    extra = jnp.concatenate(extra, axis=0).astype(jnp.bfloat16)
    for ref in send_refs[: slides - 1]:
        ref[ref.shape[0] - 1] = extra
    vectors_ref[...] = jnp.zeros(vectors_ref.shape, jnp.float32)
    for index, ref in enumerate(vector_refs):
        size = ref.shape[0]
        vectors_ref[index : index + 1, 0:size] = ref[...].reshape(1, size)

    kinds = 1 + places
    for field in range(CLASSES + kinds * CLASS_SIZE):
        table_ref[field] = 0
    for kind in range(kinds):
        for item in range(PROC):
            table_ref[class_field(kind, SLOT, item)] = PROC
    for other in range(slides):
        source = my_slide ^ other
        count_ref[0] = 0

        def take(slot, carry):
            entry = route_ref[source, 0, slot]
            proc = entry - my_slide * PROC

            @pl.when((proc >= 0) & (proc < PROC))
            def _take():
                rank = count_ref[0]
                count_ref[0] = rank + 1
                table_ref[FILLED + proc] = 1
                table_ref[SLIDE + proc] = source
                table_ref[PLACE + proc] = slot
                kind = 0 if other < 2 else 1 + rank
                base = CLASSES + kind * CLASS_SIZE
                item = table_ref[base]
                table_ref[base] = item + 1
                table_ref[base + 1 + SLOT * PROC + item] = proc
                if other == 0:
                    table_ref[base + 1 + FROM * PROC + item] = 0
                    table_ref[base + 1 + OWN * PROC + item] = slot
                else:
                    table_ref[base + 1 + FROM * PROC + item] = 1 + rank if other == 1 else other - 2

            return carry

        lax.fori_loop(0, slots, take, 0)
        if other == 0:
            own = table_ref[class_field(0, -1)]
            for item in range(1, PROC):

                @pl.when(item >= own)
                def _hold():
                    table_ref[class_field(0, OWN, item)] = table_ref[class_field(0, OWN, item - 1)]

    for kind in range(kinds):
        items = table_ref[class_field(kind, -1)]
        for item in range(1, PROC):

            @pl.when(item >= items)
            def _hold_slot():
                table_ref[class_field(kind, SLOT, item)] = table_ref[class_field(kind, SLOT, item - 1)]

    for index, (_, _, key) in enumerate(targets):

        @pl.when(slot_ref[key] >= 0)
        def _wait():
            copy_of(index, 0).wait()


def pack_tiles(counts, routing, tile_maps, positions, cotangent, vectors, slides, places):
    slots = tile_maps.shape[0]
    smem = pl.BlockSpec(memory_space=pltpu.SMEM)
    vmem = pl.BlockSpec(memory_space=pltpu.VMEM)
    buffers = 1 + places * (slides - 2)
    side = tile_maps.shape[1]
    shapes = [places * side + 1] + [side + 1] * (slides - 2) + [side] * (buffers - slides + 1)
    widest = max(vector.shape[0] for vector in vectors)
    inputs = (positions, cotangent) + vectors
    fixed = [pinned(x) for x in (tile_maps,) + inputs]
    outs = pl.pallas_call(
        functools.partial(pack_kernel, slides, slots, places),
        out_shape=tuple(
            jax.ShapeDtypeStruct((size,) + tile_maps.shape[2:], tile_maps.dtype) for size in shapes
        )
        + (
            jax.ShapeDtypeStruct((CLASSES + (1 + places) * CLASS_SIZE,), jnp.int32),
            jax.ShapeDtypeStruct((1, SMALL), jnp.float32),
            jax.ShapeDtypeStruct((8, widest), jnp.float32),
        ),
        in_specs=[smem, smem] + [IN_HBM] * len(fixed),
        out_specs=(vmem,) * buffers + (smem, vmem, vmem),
        scratch_shapes=[
            pltpu.SMEM((slides,), jnp.int32),
            pltpu.SMEM((slides * places,), jnp.int32),
            pltpu.SemaphoreType.DMA((slides * places,)),
        ]
        + [pltpu.VMEM(x.shape, x.dtype) for x in inputs]
        + [pltpu.SemaphoreType.DMA((len(inputs),))],
        compiler_params=pltpu.CompilerParams(vmem_limit_bytes=8 * MIB),
        name="pack_tiles",
    )(counts, routing, *fixed)
    return outs[:-3], outs[-3:]


def forward_kernel(kind, last, inputs, kept, table_ref, *refs):
    tile_refs, refs = refs[:inputs], refs[inputs:]
    taps_hbm, vectors_ref, expand_hbm, reduce_hbm, head_hbm = refs[:5]
    refs = refs[5 + (0 if kind == 0 else kept) :]
    out_hbms, refs = refs[:kept], refs[kept:]
    held, refs = refs[:kept], refs[kept:]
    taps_ref, expand_ref, reduce_ref, head_ref, padded, depth_out, normed, pre, load_sems = refs[:9]
    tile_sems, out_sems = refs[9:]
    out_s, embed_s, unit_s, inv_s, hidden_s, slope_s, head_slope_s, source_s = held
    items = table_ref[class_field(kind, -1)]
    side, channels = out_s.shape[1], out_s.shape[3]
    cells = side * side
    bands = channels // LANES
    low = ROW_UNIT // 2
    reach = KS // 2
    constants = [
        pltpu.make_async_copy(source, target, load_sems.at[index])
        for index, (source, target) in enumerate(
            (
                (taps_hbm, taps_ref),
                (expand_hbm, expand_ref),
                (reduce_hbm, reduce_ref),
                (head_hbm, head_ref),
            )
        )
    ]

    def tile_copy(ref, row, buffer):
        lines = ref.at[row] if len(ref.shape) == 4 else ref.at[pl.ds(row * side, side)]
        return pltpu.make_async_copy(lines, source_s.at[buffer], tile_sems.at[buffer])

    def load(item, buffer):
        origin = table_ref[class_field(kind, FROM) + item]
        place = 0
        for index, ref in enumerate(tile_refs):
            own = kind == 0 and index == 0
            for row in range(1 if own else ref.shape[0] // side):

                @pl.when(origin == place)
                def _load():
                    at = table_ref[class_field(kind, OWN) + item] if own else row
                    tile_copy(ref, at, buffer).start()

                place += 1

    def keep(part, slot, buffer):
        return pltpu.make_async_copy(
            held[part].at[buffer], out_hbms[part].at[slot], out_sems.at[part, buffer]
        )

    def wait_kept(buffer):
        for part in range(kept - 1):
            keep(part, 0, buffer).wait()

    def vector(index, lanes):
        return vectors_ref[index : index + 1, lanes]

    @pl.when(items > 0)
    def _first():
        load(0, 0)
        for copy in constants:
            copy.start()
        edge = jnp.zeros((side, low, LANES), jnp.float32)
        for band in range(bands):
            padded[band, :, 0:low, :] = edge
            padded[band, :, low + side :, :] = edge

    def one_item(item, carry):
        buffer = lax.rem(item, 2)
        slot = table_ref[class_field(kind, SLOT) + item]

        @pl.when(item >= 2)
        def _free():
            wait_kept(buffer)

        tile_copy(tile_refs[0], 0, buffer).wait()

        @pl.when(item == 0)
        def _taps():
            constants[0].wait()

        for band in range(bands):
            for at in range(side):
                padded[band, at, low : low + side, :] = source_s[
                    buffer, at, :, band * LANES : (band + 1) * LANES
                ].astype(jnp.float32)

        def convolve(band, carry):
            lanes = pl.ds(pl.multiple_of(band * LANES, LANES), LANES)
            bias = jnp.broadcast_to(vectors_ref[DEPTH_BIAS : DEPTH_BIAS + 1, lanes], (side, LANES))
            totals = [bias for _ in range(side)]
            for col in range(KS):
                start = low - reach + col
                weights = [
                    jnp.broadcast_to(
                        taps_ref[row * KS + col : row * KS + col + 1, lanes], (side, LANES)
                    ).astype(jnp.bfloat16)
                    for row in range(KS)
                ]
                sums = [None] * side
                for at in range(side):
                    line = padded[band, at, start : start + side, :].astype(jnp.bfloat16)
                    for row in range(KS):
                        place = at - row + reach
                        if 0 <= place < side:
                            term = weights[row] * line
                            sums[place] = term if sums[place] is None else sums[place] + term
                for place in range(side):
                    totals[place] = totals[place] + sums[place].astype(jnp.float32)
            for place in range(side):
                depth_out[band, place * side : (place + 1) * side, :] = totals[place]
            return carry

        lax.fori_loop(0, bands, convolve, 0)
        for start in range(0, cells, PART):
            rows = slice(start, start + PART)
            pieces = [depth_out[band, rows, :] for band in range(bands)]
            mean = jnp.sum(sum(pieces), axis=1, keepdims=True) * (1.0 / channels)
            pieces = [piece - mean for piece in pieces]
            var = jnp.sum(sum(p * p for p in pieces), axis=1, keepdims=True) * (1.0 / channels)
            inv = lax.rsqrt(var + EPSILON)
            inv_s[buffer, rows, :] = jnp.broadcast_to(inv, (PART, LANES))
            for band in range(bands):
                lanes = slice(band * LANES, (band + 1) * LANES)
                unit = pieces[band] * inv
                unit_s[buffer, rows, lanes] = unit
                normed[rows, lanes] = (unit * vector(GAIN, lanes) + vector(SHIFT, lanes)).astype(
                    jnp.bfloat16
                )

        @pl.when(item == 0)
        def _weights():
            for copy in constants[1:]:
                copy.wait()

        @pl.when(item + 1 < items)
        def _next():
            @pl.when(item >= 1)
            def _source_free():
                keep(kept - 1, 0, 1 - buffer).wait()

            load(item + 1, 1 - buffer)

        for part in (2, 3):
            keep(part, slot, buffer).start()
        for index, begin in enumerate(range(0, expand_ref.shape[1], WIDTH)):
            cols = slice(begin, begin + WIDTH)
            at = index % pre.shape[0]
            pre[at] = mix(normed[...], expand_ref[:, cols])
            for start in range(0, cells, PART):
                rows = slice(start, start + PART)
                act, slope = gelu_and_slope(pre[at, rows, :] + vector(EXPAND_BIAS, cols))
                hidden_s[buffer, rows, cols] = act.astype(jnp.bfloat16)
                slope_s[buffer, rows, cols] = slope.astype(jnp.bfloat16)
        for part in (4, 5):
            keep(part, slot, buffer).start()
        lanes = slice(0, channels)
        depth_rows = mix(hidden_s[buffer], reduce_ref[...])
        for at in range(side):
            rows = slice(at * side, (at + 1) * side)
            branch = vector(SCALE, lanes) * (depth_rows[rows] + vector(REDUCE_BIAS, lanes))
            line = (source_s[buffer, at].astype(jnp.float32) + branch).astype(jnp.bfloat16)
            normed[rows, :] = line
            out_s[buffer, at] = line
        for part in (0, 7):
            keep(part, slot, buffer).start()
        for index, begin in enumerate(range(0, head_ref.shape[1], WIDTH)):
            cols = slice(begin, begin + WIDTH)
            at = index % pre.shape[0]
            pre[at] = mix(normed[...], head_ref[:, cols])
            total = None
            for start in range(0, cells, PART):
                rows = slice(start, start + PART)
                act, slope = gelu_and_slope(pre[at, rows, :])
                head_slope_s[buffer, rows, cols] = slope.astype(jnp.bfloat16)
                folded = act[0:8]
                for piece in range(8, PART, 8):
                    folded = folded + act[piece : piece + 8]
                total = folded if total is None else total + folded
            mean = jnp.sum(total, axis=0, keepdims=True) * (1.0 / cells)
            embed_s[buffer, :, cols] = jnp.broadcast_to(mean, (8, WIDTH))
        for part in (1, 6):
            keep(part, slot, buffer).start()
        return carry

    lax.fori_loop(0, items, one_item, 0)
    for back in (1, 2):

        @pl.when(items >= back)
        def _drain():
            buffer = lax.rem(items - back, 2)
            for part in range(kept):
                keep(part, 0, buffer).wait()

    if last:
        filled = sum(table_ref[FILLED + proc] for proc in range(PROC))

        @pl.when(filled < PROC)
        def _zeros():
            for ref in held:
                ref[0] = jnp.zeros(ref.shape[1:], ref.dtype)

        for proc in range(PROC):

            @pl.when(table_ref[FILLED + proc] == 0)
            def _empty():
                for part in range(kept):
                    keep(part, proc, 0).start()
                wait_kept(0)
                keep(kept - 1, proc, 0).wait()


def pinned(array):
    return pltpu.with_memory_space_constraint(array, pltpu.HBM)


def forward_block(kind, last, table, tiles, taps, vectors, expand, reduce, head, before):
    side, channels = tiles[0].shape[-2:]
    cells, hid, embed = side * side, expand.shape[1], head.shape[1]
    bands = channels // LANES
    outs = (
        ((side, side, channels), jnp.bfloat16),
        ((8, embed), jnp.float32),
        ((cells, channels), jnp.float32),
        ((cells, LANES), jnp.float32),
        ((cells, hid), jnp.bfloat16),
        ((cells, hid), jnp.bfloat16),
        ((cells, embed), jnp.bfloat16),
        ((side, side, channels), jnp.bfloat16),
    )
    smem = pl.BlockSpec(memory_space=pltpu.SMEM)
    vmem = pl.BlockSpec(memory_space=pltpu.VMEM)
    if kind == 0:
        tiles = (pinned(tiles[0]),) + tuple(tiles[1:])
    first = 1 + len(tiles) + 5
    return pl.pallas_call(
        functools.partial(forward_kernel, kind, last, len(tiles), len(outs)),
        out_shape=tuple(pltpu.HBM((PROC,) + shape, dtype) for shape, dtype in outs),
        in_specs=[smem]
        + [HBM] * len(tiles)
        + [IN_HBM, vmem, IN_HBM, IN_HBM, IN_HBM]
        + [IN_HBM] * len(before),
        out_specs=(IN_HBM,) * len(outs),
        scratch_shapes=[pltpu.VMEM((2,) + shape, dtype) for shape, dtype in outs]
        + [
            pltpu.VMEM(taps.shape, jnp.float32),
            pltpu.VMEM(expand.shape, jnp.bfloat16),
            pltpu.VMEM(reduce.shape, jnp.bfloat16),
            pltpu.VMEM(head.shape, jnp.bfloat16),
            pltpu.VMEM((bands, side, side + ROW_UNIT, LANES), jnp.float32),
            pltpu.VMEM((bands, cells, LANES), jnp.float32),
            pltpu.VMEM((cells, channels), jnp.bfloat16),
            pltpu.VMEM((3, cells, WIDTH), jnp.float32),
            pltpu.SemaphoreType.DMA((4,)),
            pltpu.SemaphoreType.DMA((2,)),
            pltpu.SemaphoreType.DMA((len(outs), 2)),
        ],
        input_output_aliases={first + index: index for index in range(len(before))},
        compiler_params=pltpu.CompilerParams(vmem_limit_bytes=24 * MIB),
        cost_estimate=cost(1.0),
        name="forward_block_" + str(kind),
    )(table, *tiles, pinned(taps), vectors, pinned(expand), pinned(reduce), pinned(head), *before)


def cost(micros):
    return pl.CostEstimate(flops=int(micros * 1e9), bytes_accessed=1024, transcendentals=0)


def rows_kernel(slides, table_ref, embed_ref, small_ref, *refs):
    buffer_refs, (out_ref, smalls_ref, rows_ref, lines_ref, extra_ref, sems) = (
        refs[: slides - 1],
        refs[slides - 1 :],
    )
    copies = [
        pltpu.make_async_copy(ref.at[ref.shape[0] - 1], extra_ref.at[index], sems.at[index])
        for index, ref in enumerate(buffer_refs)
    ]
    for copy in copies:
        copy.start()
    my_slide, my_member = lax.axis_index(DP), lax.axis_index(GROUP)
    channels = extra_ref.shape[2]
    half = E // 2
    channel = lax.broadcasted_iota(jnp.int32, (1, E), 1)
    inner = jnp.where(channel < half, channel, channel - half)
    odd = lax.rem(inner, 2)
    frequency = jnp.exp((inner - odd).astype(jnp.float32) * (-math.log(10000.0) / half))
    phase = odd.astype(jnp.float32) * (0.5 * math.pi)
    lane = lax.broadcasted_iota(jnp.int32, (1, LANES), 1)
    smalls_ref[0] = small_ref[...]
    lines = SMALL // channels
    for index, copy in enumerate(copies):
        copy.wait()
        extra = extra_ref[index].astype(jnp.float32)
        for line in range(lines):
            total = extra[line : line + 1]
            for piece in range(1, PIECES):
                total = total + extra[piece * lines + line : piece * lines + line + 1]
            smalls_ref[1 + index, :, line * channels : (line + 1) * channels] = total
    for proc in range(PROC):
        filled = table_ref[FILLED + proc]
        slide = table_ref[SLIDE + proc]
        slot = table_ref[PLACE + proc]
        held = smalls_ref[0]
        for other in range(1, slides):
            held = jnp.where((slide ^ my_slide) == other, smalls_ref[other], held)
        spots = [
            jnp.sum(jnp.where(lane == slot, held[:, at : at + LANES], 0.0), axis=1, keepdims=True)
            for at in (ROWS_AT, COLS_AT)
        ]
        angle = jnp.where(channel < half, spots[0], spots[1]) * frequency + phase
        target = jnp.where(lane == 0, slide, jnp.where(lane == 1, slot, my_member))
        target = jnp.where(filled != 0, target, jnp.where(lane == 2, -1, 0))
        target = jnp.where(lane < 3, target, 0)
        rows_ref[proc : proc + 1, 0:E] = angle
        rows_ref[2 * PROC + proc : 2 * PROC + proc + 1, 0:E] = embed_ref[proc, 0:1, :]
        rows_ref[proc : proc + 1, E:] = target.astype(jnp.float32)
    code = jnp.sin(rows_ref[0 : 2 * PROC, 0:E])
    embed = rows_ref[2 * PROC : 4 * PROC, 0:E].astype(jnp.bfloat16).astype(jnp.float32)
    row_id = lax.broadcasted_iota(jnp.int32, (2 * PROC, E), 0)
    there = row_id < 0
    for proc in range(PROC):
        there = there | ((row_id == proc) & (table_ref[FILLED + proc] != 0))
    total = jnp.where(there, embed + code, 0.0)
    rows_ref[0 : 2 * PROC, 0:E] = total
    lines_ref[...] = jnp.zeros(lines_ref.shape, jnp.float32)
    for copied in range(0, ROW_UNIT, 2 * PROC):
        lines_ref[copied : copied + PROC, :] = rows_ref[0:PROC, 0:HALF]
        lines_ref[copied + PROC : copied + 2 * PROC, 0 : E + LANES - HALF] = rows_ref[0:PROC, HALF:]
    sent = lines_ref[...].astype(jnp.bfloat16)
    for start in range(0, out_ref.shape[0], ROW_UNIT):
        out_ref[start : start + ROW_UNIT, :] = sent


def tile_rows(table, embeds, small, buffers, devices):
    smem = pl.BlockSpec(memory_space=pltpu.SMEM)
    vmem = pl.BlockSpec(memory_space=pltpu.VMEM)
    slides = 1 + len(buffers)
    return pl.pallas_call(
        functools.partial(rows_kernel, slides),
        out_shape=(
            jax.ShapeDtypeStruct((devices * 2 * PROC, HALF), jnp.bfloat16),
            jax.ShapeDtypeStruct((slides, 1, SMALL), jnp.float32),
        ),
        in_specs=[smem, vmem, vmem] + [HBM] * len(buffers),
        out_specs=(vmem, vmem),
        scratch_shapes=[
            pltpu.VMEM((4 * PROC, E + LANES), jnp.float32),
            pltpu.VMEM((ROW_UNIT, HALF), jnp.float32),
            pltpu.VMEM((len(buffers),) + buffers[0].shape[1:], jnp.bfloat16),
            pltpu.SemaphoreType.DMA((len(buffers),)),
        ],
        cost_estimate=cost(1.0),
        name="tile_rows",
    )(table, embeds, small, *buffers)


def slide_kernel(
    length,
    members,
    slides,
    table_ref,
    came_ref,
    taps_hbm,
    matrix_hbm,
    vectors_ref,
    smalls_ref,
    feature_ref,
    grad_ref,
    picks,
    own_rows,
    tile_rows,
    mixed,
    grad_agg,
    taps_ref,
    matrix_ref,
    sems,
):
    loads = [
        pltpu.make_async_copy(taps_hbm, taps_ref, sems.at[0]),
        pltpu.make_async_copy(matrix_hbm, matrix_ref, sems.at[1]),
    ]
    for load in loads:
        load.start()
    my_slide, my_member = lax.axis_index(DP), lax.axis_index(GROUP)
    border = ROW_UNIT
    reach = KERNEL_TAPS // 2
    blocks = [slice(start, start + WIDTH) for start in range(0, E, WIDTH)]
    lane = lax.broadcasted_iota(jnp.int32, (8, LANES), 1)
    scales = jnp.where(lane == 0, length, jnp.where(lane == 1, members, jnp.where(lane == 2, 1, 0)))
    tail = came_ref[:, E - HALF : E - HALF + LANES]
    target = mix_cols(scales.astype(jnp.float32).astype(jnp.bfloat16), tail)[0:1, :]
    lines = came_ref.shape[0]
    second = lax.rem(lax.broadcasted_iota(jnp.int32, (1, lines), 1), 2 * PROC) >= PROC
    target = jnp.where(second, target, -1.0)
    step = lax.broadcasted_iota(jnp.int32, (length, 1), 0)

    want = (my_slide * length + step).astype(jnp.float32)
    picks[0:length, :] = (target == want).astype(jnp.float32)
    index = lax.broadcasted_iota(jnp.int32, (ROW_UNIT, 1), 0)
    short = lax.broadcasted_iota(jnp.int32, (8, 1), 0)
    helds, shares = [], []
    for proc in range(PROC):
        filled = table_ref[FILLED + proc]
        slide = table_ref[SLIDE + proc]
        place = table_ref[PLACE + proc] * members + my_member
        at = place + (index - 2 * reach) * TILE_DILATION
        inside = (at >= 0) & (at < length) & (index <= 4 * reach) & (filled != 0)
        want = jnp.where(inside, slide * length + at, -2).astype(jnp.float32)
        start = length + proc * ROW_UNIT
        picks[start : start + ROW_UNIT, :] = (target == want).astype(jnp.float32)
        held = smalls_ref[0]
        for other in range(1, slides):
            held = jnp.where((slide ^ my_slide) == other, smalls_ref[other], held)
        helds.append(held)
        count = held[:, COUNT_AT : COUNT_AT + 1]
        at = (place + (short - reach) * TILE_DILATION).astype(jnp.float32)
        shares.append(jnp.where((at >= 0.0) & (at < count), 1.0 / count, 0.0))
    late = picks[...]
    early = pltpu.roll(late, lines - PROC, axis=1).astype(jnp.bfloat16)
    late = late.astype(jnp.bfloat16)
    edge = jnp.zeros((border, E), jnp.float32)
    own_rows[0:border, :] = edge
    own_rows[border + length :, :] = edge
    loads[0].wait()

    def tap(number, cols):
        return taps_ref[number : number + 1, cols]

    for cols in blocks:
        pick, at = (early, cols.start) if cols.start < HALF else (late, cols.start - HALF)
        found = mix(pick, came_ref[:, at : at + WIDTH])
        own_rows[border : border + length, cols] = found[0:length]
        tile_rows[:, cols] = found[length:]
        total = found[0:length]
        for number in range(KERNEL_TAPS):
            start = border + (number - reach) * TILE_DILATION
            total = total + tap(number, cols) * own_rows[start : start + length, cols]
        mixed[0:length, cols] = total.astype(jnp.bfloat16)
        totals = []
        for proc in range(PROC):
            base = proc * ROW_UNIT
            total = tile_rows[base + reach : base + reach + 8, cols]
            for number in range(KERNEL_TAPS):
                total = total + tap(number, cols) * tile_rows[base + number : base + number + 8, cols]
            totals.append(total)
        mixed[length:, cols] = jnp.concatenate(totals, axis=0).astype(jnp.bfloat16)
    count = smalls_ref[0][:, COUNT_AT : COUNT_AT + 1]
    share = jnp.where(step.astype(jnp.float32) < count, 1.0 / count, 0.0)
    loads[1].wait()
    for cols in blocks:
        bias = vectors_ref[SLIDE_BIAS : SLIDE_BIAS + 1, cols]
        pre = mix(mixed[...], matrix_ref[:, cols]) + bias
        total = None
        for start in range(0, length, PART):
            act, _ = gelu_and_slope(pre[start : start + PART])
            piece = jnp.sum(act * share[start : start + PART], axis=0, keepdims=True)
            total = piece if total is None else total + piece
        feature_ref[:, cols] = total
        _, slope = gelu_and_slope(pre[length:])
        parts = [
            helds[proc][:, cols] * shares[proc] * slope[proc * 8 : (proc + 1) * 8]
            for proc in range(PROC)
        ]
        grad_agg[:, cols] = jnp.concatenate(parts, axis=0).astype(jnp.bfloat16)
    for cols in blocks:
        grads = mix_cols(grad_agg[...], matrix_ref[cols, :])
        for proc in range(PROC):
            block = grads[proc * 8 : (proc + 1) * 8]
            total = block[reach : reach + 1]
            for number in range(KERNEL_TAPS):
                at = 2 * reach - number
                total = total + tap(number, cols) * block[at : at + 1]
            total = jnp.where(table_ref[FILLED + proc] != 0, total, 0.0)
            grad_ref[proc, :, cols] = total.astype(jnp.bfloat16).astype(jnp.float32)


def slide_grads(length, members, table, came, taps, matrix, vectors, smalls):
    slides = smalls.shape[0]
    smem = pl.BlockSpec(memory_space=pltpu.SMEM)
    vmem = pl.BlockSpec(memory_space=pltpu.VMEM)
    return pl.pallas_call(
        functools.partial(slide_kernel, length, members, slides),
        out_shape=(
            jax.ShapeDtypeStruct((1, E), jnp.float32),
            jax.ShapeDtypeStruct((PROC, 1, E), jnp.float32),
        ),
        in_specs=[smem, vmem, IN_HBM, IN_HBM, vmem, vmem],
        out_specs=(vmem, vmem),
        scratch_shapes=[
            pltpu.VMEM((length + PROC * ROW_UNIT, came.shape[0]), jnp.float32),
            pltpu.VMEM((length + 2 * ROW_UNIT, E), jnp.float32),
            pltpu.VMEM((PROC * ROW_UNIT, E), jnp.float32),
            pltpu.VMEM((length + PROC * 8, E), jnp.bfloat16),
            pltpu.VMEM((PROC * 8, E), jnp.bfloat16),
            pltpu.VMEM(taps.shape, jnp.float32),
            pltpu.VMEM(matrix.shape, jnp.bfloat16),
            pltpu.SemaphoreType.DMA((2,)),
        ],
        compiler_params=pltpu.CompilerParams(vmem_limit_bytes=16 * MIB),
        cost_estimate=cost(3.0),
        name="slide_grads",
    )(table, came, pinned(taps), pinned(matrix), vectors, smalls)


class Plan:
    def __init__(self, slides, members, channels, hid):
        self.devices = slides * members
        self.ys, self.g1, self.g2 = slides // 2, 4, members // 4
        assert self.ys == self.g2
        self.channels = channels
        self.pieces = hid // channels
        self.expand_rows = channels // self.devices
        self.reduce_rows = hid // self.devices
        self.block_rows = -(-self.reduce_rows // ROW_UNIT) * ROW_UNIT
        self.share = KS * KS * channels // self.devices

    def spots(self):
        my_core, my_y = lax.axis_index("core"), lax.axis_index("y")
        my_z, my_x = lax.axis_index("g1"), lax.axis_index("g2")
        for device in range(self.devices):
            slide, member = divmod(device, self.g1 * self.g2)
            (y, core), (z, x) = divmod(slide, 2), divmod(member, self.g2)
            yield (
                my_core ^ core,
                lax.rem(y - my_y + self.ys, self.ys),
                lax.rem(x - my_x + self.g2, self.g2),
                lax.rem(z - my_z + self.g1, self.g1),
            )


def send_out(staged, sems, refs):
    copies = [
        pltpu.make_async_copy(staged.at[index], ref, sems.at[index]) for index, ref in enumerate(refs)
    ]
    for copy in copies:
        copy.start()
    for copy in copies:
        copy.wait()


def padded_block(block, rows):
    extra = rows - block.shape[0]
    if extra:
        block = jnp.concatenate([block, jnp.zeros((extra, block.shape[1]), block.dtype)], axis=0)
    return block.astype(jnp.bfloat16)


def turn_kernel(unit_ref, vectors_ref, out_ref, normed, eye_ref):
    cells, channels = unit_ref.shape[1:]
    eye_ref[...] = unit_matrix(channels)
    for start in range(0, cells, PART):
        rows = slice(start, start + PART)
        gain = vectors_ref[GAIN : GAIN + 1, 0:channels]
        shift = vectors_ref[SHIFT : SHIFT + 1, 0:channels]
        normed[rows, :] = (unit_ref[0, rows, :] * gain + shift).astype(jnp.bfloat16)
    out_ref[...] = mix_cols(eye_ref[...], normed[...]).astype(jnp.bfloat16)


def unit_matrix(size):
    spot = lax.broadcasted_iota(jnp.int32, (size, size), 0)
    same = spot == lax.broadcasted_iota(jnp.int32, (size, size), 1)
    return same.astype(jnp.float32).astype(jnp.bfloat16)


def turned_normed(unit, vectors):
    cells, channels = unit.shape[1:]
    return pl.pallas_call(
        turn_kernel,
        out_shape=jax.ShapeDtypeStruct((channels, PROC * cells), jnp.bfloat16),
        grid=(PROC,),
        in_specs=[pl.BlockSpec((1, cells, channels), lambda i: (i, 0, 0)), whole(vectors.shape)],
        out_specs=pl.BlockSpec((channels, cells), lambda i: (0, i)),
        scratch_shapes=[
            pltpu.VMEM((cells, channels), jnp.bfloat16),
            pltpu.VMEM((channels, channels), jnp.bfloat16),
        ],
        compiler_params=pltpu.CompilerParams(vmem_limit_bytes=8 * MIB),
        cost_estimate=cost(3.0),
        name="turned_normed",
    )(unit, vectors)


def weights_kernel(
    plan,
    grad_ref,
    hidden_ref,
    head_slope_ref,
    slope_ref,
    normed_ref,
    vectors_ref,
    head_ref,
    reduce_ref,
    grad_pre_hbm,
    keep_ref,
    send_ref,
    grad_pre,
    turned,
    grad_head,
    eye_ref,
    staged,
    sems,
    pre_sems,
):
    cells, channels = slope_ref.shape[1], normed_ref.shape[0]
    hid = reduce_ref.shape[0]
    every = slice(0, channels)

    def vector(index, lanes):
        return vectors_ref[index : index + 1, lanes]

    eye_ref[...] = unit_matrix(channels)

    def one_slot(slot, carry):
        rows_all = pl.ds(pl.multiple_of(slot * cells, cells), cells)
        row = grad_ref[slot] * (1.0 / cells)
        for start in range(0, cells, PART):
            rows = slice(start, start + PART)
            grad_head[rows, :] = (row * head_slope_ref[slot, rows, :].astype(jnp.float32)).astype(
                jnp.bfloat16
            )
        grad_mlp = (vector(SCALE, every) * mix_cols(grad_head[...], head_ref[...])).astype(
            jnp.bfloat16
        )
        turned[:, rows_all] = mix_cols(eye_ref[...], grad_mlp).astype(jnp.bfloat16)
        for begin in range(0, hid, WIDTH):
            cols = slice(begin, begin + WIDTH)
            grad_hidden = mix_cols(grad_mlp, reduce_ref[cols, :])
            grad_pre[rows_all, cols] = (
                grad_hidden * slope_ref[slot, :, cols].astype(jnp.float32)
            ).astype(jnp.bfloat16)
        return carry

    lax.fori_loop(0, PROC, one_slot, 0)
    writes = [
        pltpu.make_async_copy(
            grad_pre.at[pl.ds(slot * cells, cells)], grad_pre_hbm.at[slot], pre_sems.at[slot]
        )
        for slot in range(PROC)
    ]
    for write in writes:
        write.start()
    spots = list(plan.spots())
    per_block = channels // plan.reduce_rows
    tall = plan.block_rows
    for index in range(plan.pieces):
        cols = slice(index * channels, (index + 1) * channels)
        total = mix(turned[...], hidden_ref[:, cols]).astype(jnp.bfloat16)
        back = mix_cols(eye_ref[...], total)
        for part in range(per_block):
            block = back[part * plan.reduce_rows : (part + 1) * plan.reduce_rows]
            core, y, x, z = spots[index * per_block + part]
            staged[core, 0, x, y, z] = padded_block(block, tall)
    totals = []
    for quarter in range(plan.pieces):
        cols = slice(quarter * channels, (quarter + 1) * channels)
        totals.append(mix(normed_ref[...], grad_pre[:, cols]))
    size = plan.expand_rows
    for device in range(plan.devices):
        rows = slice(device * size, (device + 1) * size)
        block = jnp.concatenate([total[rows] for total in totals], axis=0)
        core, y, x, z = spots[device]
        staged[core, 1, y, x, z] = padded_block(block, tall)
    send_out(staged, sems, (keep_ref, send_ref))
    for write in writes:
        write.wait()


def taps_kernel(
    plan,
    first,
    last,
    table_ref,
    source_ref,
    grad_pre_ref,
    unit_ref,
    inv_ref,
    before_ref,
    vectors_ref,
    expand_ref,
    out_ref,
    padded,
    tap_sums,
    tap_rows,
    grad_norm,
    depth_back,
):
    step = pl.program_id(0)
    filled = table_ref[FILLED + first + step]
    side, channels = source_ref.shape[1], source_ref.shape[3]
    bands = channels // LANES
    low = ROW_UNIT // 2
    reach = KS // 2

    @pl.when(step == 0)
    def _start():
        if first:
            tap_sums[...] = before_ref[...]
        else:
            tap_sums[...] = jnp.zeros(tap_sums.shape, jnp.float32)

    @pl.when(filled != 0)
    def _work():
        cells = side * side
        gain = vectors_ref[GAIN : GAIN + 1, 0:channels]
        grad_norm[...] = mix_cols(grad_pre_ref[0], expand_ref[...])
        for start in range(0, cells, PART):
            rows = slice(start, start + PART)
            scaled = grad_norm[rows, :] * gain
            unit = unit_ref[0, rows, :]
            mean = jnp.sum(scaled, axis=1, keepdims=True) * (1.0 / channels)
            mean_unit = jnp.sum(scaled * unit, axis=1, keepdims=True) * (1.0 / channels)
            inv = inv_ref[0, rows, 0:1]
            for band in range(bands):
                lanes = slice(band * LANES, (band + 1) * LANES)
                depth_back[band, rows, :] = (
                    inv * (scaled[:, lanes] - mean - unit[:, lanes] * mean_unit)
                ).astype(jnp.bfloat16)
        edge = jnp.zeros((side, low, LANES), jnp.float32)
        for band in range(bands):
            lanes = slice(band * LANES, (band + 1) * LANES)
            padded[band, :, 0:low, :] = edge
            padded[band, :, low + side :, :] = edge
            for at in range(side):
                padded[band, at, low : low + side, :] = source_ref[0, at, :, lanes].astype(
                    jnp.float32
                )

        def taps_of(band, carry):
            for col in range(KS):
                start = low - reach + col
                folded = [None] * KS
                grads = {}
                for half in range(2):
                    sums = [None] * KS
                    for at in range(half * side // 2, (half + 1) * side // 2):
                        line = padded[band, at, start : start + side, :].astype(jnp.bfloat16)
                        for row in range(KS):
                            place = at - row + reach
                            if 0 <= place < side:
                                if place not in grads:
                                    grads[place] = depth_back[
                                        band, place * side : (place + 1) * side, :
                                    ]
                                term = line * grads[place]
                                sums[row] = term if sums[row] is None else sums[row] + term
                    for row in range(KS):
                        total = sums[row].astype(jnp.float32)
                        for piece in range(0, side, 8):
                            block = total[piece : piece + 8, :]
                            folded[row] = block if folded[row] is None else folded[row] + block
                for row in range(KS):
                    tap_sums[band, row * KS + col] = tap_sums[band, row * KS + col] + folded[row]
            return carry

        lax.fori_loop(0, bands, taps_of, 0)

    @pl.when(step == pl.num_programs(0) - 1)
    def _finish():
        if not last:
            out_ref[...] = tap_sums[...]
            return
        for band in range(bands):
            lanes = slice(band * LANES, (band + 1) * LANES)
            tap_rows[0 : KS * KS, lanes] = jnp.sum(tap_sums[band], axis=1)
            tap_rows[KS * KS :, lanes] = jnp.zeros((tap_rows.shape[0] - KS * KS, LANES), jnp.float32)
        for device in range(plan.devices):
            start = device * plan.share // channels
            out_ref[device] = tap_rows[start : start + TAP_ROWS, :]


def per_slot(array):
    shape = array.shape[1:]
    return pl.BlockSpec((1,) + shape, lambda i, table: (i,) + (0,) * len(shape))


def weight_grads(plan, embed_grad, saved, vectors, head, reduce):
    normed, hidden, slope, head_slope = saved
    cells, channels = slope.shape[1], normed.shape[0]
    hid = reduce.shape[0]
    vmem = pl.BlockSpec(memory_space=pltpu.VMEM)
    blocks = jax.ShapeDtypeStruct(
        (2, plan.ys, plan.g2, plan.g1, plan.block_rows, channels), jnp.bfloat16
    )
    return pl.pallas_call(
        functools.partial(weights_kernel, plan),
        out_shape=(pltpu.HBM((PROC, cells, hid), jnp.bfloat16), blocks, blocks),
        in_specs=[vmem] * 8,
        out_specs=(IN_HBM, HBM, HBM),
        scratch_shapes=[
            pltpu.VMEM((PROC * cells, hid), jnp.bfloat16),
            pltpu.VMEM((channels, PROC * cells), jnp.bfloat16),
            pltpu.VMEM((cells, head.shape[1]), jnp.bfloat16),
            pltpu.VMEM((channels, channels), jnp.bfloat16),
            pltpu.VMEM((2,) + blocks.shape, jnp.bfloat16),
            pltpu.SemaphoreType.DMA((2,)),
            pltpu.SemaphoreType.DMA((PROC,)),
        ],
        compiler_params=pltpu.CompilerParams(vmem_limit_bytes=36 * MIB),
        cost_estimate=cost(12.0),
        name="weight_grads",
    )(embed_grad, hidden.reshape(PROC * cells, hid), head_slope, slope, normed, vectors, head, reduce)


def tap_grads(plan, first, last, table, streams, before, vectors, expand):
    side, channels = streams[0].shape[1], streams[0].shape[3]
    bands = channels // LANES
    sums = (bands, KS * KS, 8, LANES)
    out = (plan.devices, TAP_ROWS, channels) if last else sums

    def items(array):
        shape = array.shape[1:]
        return pl.BlockSpec((1,) + shape, lambda i, table: (first + i,) + (0,) * len(shape))

    return pl.pallas_call(
        functools.partial(taps_kernel, plan, first, last),
        out_shape=jax.ShapeDtypeStruct(out, jnp.float32),
        grid_spec=pltpu.PrefetchScalarGridSpec(
            num_scalar_prefetch=1,
            grid=(PROC // 2,),
            in_specs=[items(stream) for stream in streams]
            + [whole(before.shape), whole(vectors.shape), whole(expand.shape)],
            out_specs=pl.BlockSpec(out, lambda i, table: (0,) * len(out)),
            scratch_shapes=[
                pltpu.VMEM((bands, side, side + ROW_UNIT, LANES), jnp.float32),
                pltpu.VMEM(sums, jnp.float32),
                pltpu.VMEM((KS * KS + 7, channels), jnp.float32),
                pltpu.VMEM((side * side, channels), jnp.float32),
                pltpu.VMEM((bands, side * side, LANES), jnp.bfloat16),
            ],
        ),
        compiler_params=pltpu.CompilerParams(vmem_limit_bytes=16 * MIB),
        cost_estimate=cost(4.0),
        name="tap_grads_" + str(first),
    )(table, *streams, before, vectors, expand)


def shifted(values, names, sizes, shift):
    count = math.prod(sizes)
    pairs = []
    for index in range(count):
        spot = []
        rest = index
        for size in reversed(sizes):
            spot.append(rest % size)
            rest //= size
        spot = spot[::-1]
        target = 0
        for at, step, size in zip(spot, shift, sizes):
            target = target * size + (at + step) % size
        pairs.append((index, target))
    return lax.ppermute(values, names, pairs)


def shifts(sizes):
    steps = [()]
    for size in sizes:
        steps = [step + (more,) for step in steps for more in range(size)]
    return steps


def exchange(values, names):
    return lax.all_to_all(values, names, split_axis=0, concat_axis=0, tiled=True)


def add_all(parts, kind=jnp.bfloat16):
    total = parts[0].astype(jnp.float32)
    for part in parts[1:]:
        total = total + part.astype(jnp.float32)
    return total.astype(kind)


def other_core(values):
    return shifted(values, ("core",), (2,), (1,))


def sum_axis(kept, sent, name, size, kind=jnp.bfloat16):
    return [kept] + [shifted(part, (name,), (size,), (step + 1,)) for step, part in enumerate(sent)]


def on_device(
    tile_maps,
    positions,
    counts,
    routing,
    depth_kernel,
    depth_bias,
    norm_gain,
    norm_shift,
    expand_weight,
    expand_bias,
    reduce_weight,
    reduce_bias,
    layer_scale,
    head_weight,
    slide_taps,
    slide_weight,
    slide_bias,
    cotangent,
):
    slides = lax.axis_size(DP)
    members = lax.axis_size(GROUP)
    my_device = lax.axis_index(ALL)
    slots, channels = tile_maps.shape[0], tile_maps.shape[3]
    devices, length, places = slides * members, slots * members, slots // slides
    plan = Plan(slides, members, channels, expand_weight.shape[1])

    raw = (
        norm_gain,
        norm_shift,
        layer_scale,
        reduce_bias,
        depth_bias,
        expand_bias,
        slide_bias,
    )
    packed, (table, small, vectors) = pack_tiles(
        counts, routing, tile_maps, positions, cotangent, raw, slides, places
    )

    def from_other(buffer, other):
        return lax.ppermute(buffer, DP, [(index, index ^ other) for index in range(slides)])

    from_core = from_other(packed[0], 1)
    arrived = []
    for rank in range(places):
        buffers = packed[1 + rank * (slides - 2) : 1 + (rank + 1) * (slides - 2)]
        if rank:
            buffers, from_core = lax.optimization_barrier((buffers, from_core))
        arrived.append([from_other(buffer, other + 2) for other, buffer in enumerate(buffers)])

    consts = (depth_kernel, vectors, expand_weight, reduce_weight, head_weight)
    saved = forward_block(0, False, table, (tile_maps, from_core), *consts, ())
    for rank in range(places):
        saved = forward_block(1 + rank, rank + 1 == places, table, arrived[rank], *consts, saved)
    tile_out, tile_embed, unit, inv, hidden, slope, head_slope, source = saved
    came, smalls = tile_rows(table, tile_embed, small, [from_core] + arrived[0], devices)
    came = exchange(came, ALL)
    normed = turned_normed(unit, vectors)
    came, normed = lax.optimization_barrier((came, normed))

    feature, embed_grad = slide_grads(
        length, members, table, came, slide_taps, slide_weight, vectors, smalls
    )
    grad_pre, kept, sent = weight_grads(
        plan,
        embed_grad,
        (normed, hidden, slope, head_slope),
        vectors,
        head_weight,
        reduce_weight,
    )
    streams = (source, pinned(grad_pre), unit, inv)

    names = ("g2", "y")
    size = plan.ys
    came = other_core(sent)
    none = jnp.zeros((channels // LANES, KS * KS, 8, LANES), jnp.float32)
    tap_sums = tap_grads(plan, 0, False, table, streams, none, vectors, expand_weight)
    came, tap_sums = lax.optimization_barrier((came, tap_sums))
    out = [
        [add_all([kept[kind, step], came[kind, step]]) for step in range(1, size)]
        for kind in range(2)
    ]
    stay = [add_all([kept[kind, 0], came[kind, 0]]) for kind in range(2)]
    out, tap_sums = lax.optimization_barrier((out, tap_sums))
    parts = [sum_axis(stay[kind], out[kind], names[kind], size) for kind in range(2)]
    taps = tap_grads(plan, PROC // 2, True, table, streams, tap_sums, vectors, expand_weight)
    out = [
        [add_all([part[step] for part in parts[kind]]) for step in range(1, size)]
        for kind in range(2)
    ]
    stay = [add_all([part[0] for part in parts[kind]]) for kind in range(2)]
    taps = taps[:, :DEPTH_ROWS].astype(jnp.bfloat16)
    out, taps = lax.optimization_barrier((out, taps))
    parts = [sum_axis(stay[kind], out[kind], names[1 - kind], size) for kind in range(2)]
    taps = exchange(taps, ALL)
    both = jnp.concatenate([add_all(parts[0]), add_all(parts[1])], axis=1)
    total = add_all(
        sum_axis(both[0], [both[step] for step in range(1, plan.g1)], "g1", plan.g1), jnp.float32
    )
    reduce_share = total[: plan.reduce_rows]
    expand_share = total[plan.block_rows : plan.block_rows + plan.pieces * plan.expand_rows]
    expand_share = expand_share.reshape(plan.pieces, plan.expand_rows, channels).transpose(1, 0, 2)
    depth_share = lax.dynamic_slice(
        jnp.sum(taps.astype(jnp.float32), axis=0).reshape(-1),
        (my_device * plan.share % channels,),
        (plan.share,),
    )
    return (tile_out, feature, expand_share.reshape(-1), reduce_share.reshape(-1), depth_share)


def solution(mesh):
    slides, members = mesh.shape["dp"], mesh.shape["group"]
    fine = Mesh(mesh.devices.reshape(slides // 2, 2, 4, members // 4), ALL)
    return jax.shard_map(
        on_device,
        mesh=fine,
        in_specs=(
            P(ALL, None, None, None),
            P(None, ALL),
            P(DP),
            P(None, GROUP, None),
        )
        + (P(),) * 13
        + (P(DP, None),),
        out_specs=(
            P(ALL, None, None, None),
            P(DP, None),
            P(ALL),
            P(ALL),
            P(ALL),
        ),
        check_vma=False,
    )
```

```python
import functools
import math

import jax
import jax.numpy as jnp
from jax import lax
from jax.experimental import pallas as pl
from jax.experimental.pallas import tpu as pltpu
from jax.sharding import Mesh, PartitionSpec as P

E = 768
KS = 7
KERNEL_TAPS = 7
TILE_DILATION = 3
PROC = 4
DP = ("y", "core")
GROUP = ("g1", "g2")
ALL = DP + GROUP

EPSILON = 1e-06
HALF_ROOT = 0.7071067811865476
INV_ROOT_TAU = 0.3989422804014327
BELL_SCALE = -0.7213475204444817
LANES = 128
ROW_UNIT = 16
DEPTH_ROWS = 4
TAP_ROWS = 8
MIB = 1024 * 1024
PART = 32
WIDTH = 256
GAIN, SHIFT, SCALE, REDUCE_BIAS, DEPTH_BIAS, EXPAND_BIAS, SLIDE_BIAS = range(7)
VECTORS = 7
ERFC_P = 0.3275911
ERFC_A = (0.254829592, -0.284496736, 1.421413741, -1.453152027, 1.061405429)

HBM = pl.BlockSpec(memory_space=pl.ANY)
IN_HBM = pl.BlockSpec(memory_space=pltpu.HBM)
ROWS_AT, COLS_AT, COUNT_AT, SMALL = E, E + LANES, E + 2 * LANES, E + 3 * LANES
PIECES = 3
HALF = 512


def whole(shape):
    return pl.BlockSpec(shape, lambda *_: (0,) * len(shape), pipeline_mode=pl.Buffered(1))


def gelu_and_slope(values):
    size = jnp.abs(values)
    divisor = 1.0 + (ERFC_P * HALF_ROOT) * size
    t = pl.reciprocal(divisor, approx=True)
    bell = jnp.exp2(values * (values * BELL_SCALE))
    poly = 0.5 * ERFC_A[4]
    for coefficient in ERFC_A[3::-1]:
        poly = poly * t + 0.5 * coefficient
    tail = poly * t * bell
    phi = jnp.where(values >= 0.0, 1.0 - tail, tail)
    return values * phi, phi + values * (INV_ROOT_TAU * bell)


def mix_cols(left_side, right_side):
    return lax.dot_general(
        left_side, right_side, (((1,), (1,)), ((), ())), preferred_element_type=jnp.float32
    )


def mix(left_side, right_side):
    return jnp.dot(left_side, right_side, preferred_element_type=jnp.float32)


FILLED, SLIDE, PLACE, CLASSES = 0, PROC, 2 * PROC, 3 * PROC
CLASS_SIZE = 1 + 3 * PROC


def class_field(kind, field, item=0):
    return CLASSES + kind * CLASS_SIZE + (1 + field * PROC + item if field >= 0 else 0)


SLOT, FROM, OWN = range(3)


def pack_kernel(slides, slots, places, counts_ref, route_ref, tiles_ref, pos_ref, cot_ref, *refs):
    inputs = (pos_ref, cot_ref) + refs[:VECTORS]
    refs = refs[VECTORS:]
    held_refs, refs = refs[-len(inputs) - 1 : -1], refs[: -len(inputs) - 1] + refs[-1:]
    send_refs, refs = refs[:-7], refs[-7:]
    table_ref, small_ref, vectors_ref, count_ref, slot_ref, sems, input_sems = refs
    loads = [
        pltpu.make_async_copy(ref, held, input_sems.at[index])
        for index, (ref, held) in enumerate(zip(inputs, held_refs))
    ]
    for load in loads:
        load.start()
    pos_ref, cot_ref = held_refs[:2]
    vector_refs = held_refs[2:]
    my_slide = lax.axis_index(DP)

    targets = [(0, rank, rank) for rank in range(places)]
    for rank in range(places):
        for other in range(2, slides):
            targets.append((1 + rank * (slides - 2) + other - 2, 0, other * places + rank))
    targets[:places] = [(0, rank, places + rank) for rank in range(places)]

    def copy_of(index, slot):
        buffer, row, _ = targets[index]
        side = tiles_ref.shape[1]
        lines = send_refs[buffer].at[pl.ds(row * side, side)]
        return pltpu.make_async_copy(tiles_ref.at[slot], lines, sems.at[index])

    for index in range(slides):
        count_ref[index] = 0
    for index in range(slides * places):
        slot_ref[index] = -1

    def place_slot(slot, carry):
        entry = route_ref[my_slide, 0, slot]

        @pl.when(entry >= 0)
        def _send():
            other = lax.div(entry, PROC) ^ my_slide
            rank = count_ref[other]
            count_ref[other] = rank + 1
            slot_ref[other * places + rank] = slot

        return carry

    lax.fori_loop(0, slots, place_slot, 0)
    for index, (_, _, key) in enumerate(targets):
        slot = slot_ref[key]

        @pl.when(slot >= 0)
        def _start():
            copy_of(index, slot).start()

    for load in loads:
        load.wait()
    small_ref[:, 0:E] = cot_ref[...]
    for row, start in enumerate((ROWS_AT, COLS_AT)):
        small_ref[:, start : start + LANES] = jnp.zeros((1, LANES), jnp.float32)
        small_ref[:, start : start + slots] = pos_ref[row : row + 1, :].astype(jnp.float32)
    small_ref[:, COUNT_AT:SMALL] = jnp.full((1, LANES), counts_ref[0], jnp.int32).astype(jnp.float32)
    channels = tiles_ref.shape[3]
    extra = []
    rest = small_ref[...]
    for piece in range(PIECES):
        part = rest.astype(jnp.bfloat16).astype(jnp.float32)
        rest = rest - part
        extra += [part[:, at : at + channels] for at in range(0, SMALL, channels)]
    extra.append(jnp.zeros((ROW_UNIT - len(extra), channels), jnp.float32))
    extra = jnp.concatenate(extra, axis=0).astype(jnp.bfloat16)
    for ref in send_refs[: slides - 1]:
        ref[ref.shape[0] - 1] = extra
    vectors_ref[...] = jnp.zeros(vectors_ref.shape, jnp.float32)
    for index, ref in enumerate(vector_refs):
        size = ref.shape[0]
        vectors_ref[index : index + 1, 0:size] = ref[...].reshape(1, size)

    kinds = 1 + places
    for field in range(CLASSES + kinds * CLASS_SIZE):
        table_ref[field] = 0
    for kind in range(kinds):
        for item in range(PROC):
            table_ref[class_field(kind, SLOT, item)] = PROC
    for other in range(slides):
        source = my_slide ^ other
        count_ref[0] = 0

        def take(slot, carry):
            entry = route_ref[source, 0, slot]
            proc = entry - my_slide * PROC

            @pl.when((proc >= 0) & (proc < PROC))
            def _take():
                rank = count_ref[0]
                count_ref[0] = rank + 1
                table_ref[FILLED + proc] = 1
                table_ref[SLIDE + proc] = source
                table_ref[PLACE + proc] = slot
                kind = 0 if other < 2 else 1 + rank
                base = CLASSES + kind * CLASS_SIZE
                item = table_ref[base]
                table_ref[base] = item + 1
                table_ref[base + 1 + SLOT * PROC + item] = proc
                if other == 0:
                    table_ref[base + 1 + FROM * PROC + item] = 0
                    table_ref[base + 1 + OWN * PROC + item] = slot
                else:
                    table_ref[base + 1 + FROM * PROC + item] = 1 + rank if other == 1 else other - 2

            return carry

        lax.fori_loop(0, slots, take, 0)
        if other == 0:
            own = table_ref[class_field(0, -1)]
            for item in range(1, PROC):

                @pl.when(item >= own)
                def _hold():
                    table_ref[class_field(0, OWN, item)] = table_ref[class_field(0, OWN, item - 1)]

    for kind in range(kinds):
        items = table_ref[class_field(kind, -1)]
        for item in range(1, PROC):

            @pl.when(item >= items)
            def _hold_slot():
                table_ref[class_field(kind, SLOT, item)] = table_ref[class_field(kind, SLOT, item - 1)]

    for index, (_, _, key) in enumerate(targets):

        @pl.when(slot_ref[key] >= 0)
        def _wait():
            copy_of(index, 0).wait()


def pack_tiles(counts, routing, tile_maps, positions, cotangent, vectors, slides, places):
    slots = tile_maps.shape[0]
    smem = pl.BlockSpec(memory_space=pltpu.SMEM)
    vmem = pl.BlockSpec(memory_space=pltpu.VMEM)
    buffers = 1 + places * (slides - 2)
    side = tile_maps.shape[1]
    shapes = [places * side + 1] + [side + 1] * (slides - 2) + [side] * (buffers - slides + 1)
    widest = max(vector.shape[0] for vector in vectors)
    inputs = (positions, cotangent) + vectors
    fixed = [pinned(x) for x in (tile_maps,) + inputs]
    outs = pl.pallas_call(
        functools.partial(pack_kernel, slides, slots, places),
        out_shape=tuple(
            jax.ShapeDtypeStruct((size,) + tile_maps.shape[2:], tile_maps.dtype) for size in shapes
        )
        + (
            jax.ShapeDtypeStruct((CLASSES + (1 + places) * CLASS_SIZE,), jnp.int32),
            jax.ShapeDtypeStruct((1, SMALL), jnp.float32),
            jax.ShapeDtypeStruct((8, widest), jnp.float32),
        ),
        in_specs=[smem, smem] + [IN_HBM] * len(fixed),
        out_specs=(vmem,) * buffers + (smem, vmem, vmem),
        scratch_shapes=[
            pltpu.SMEM((slides,), jnp.int32),
            pltpu.SMEM((slides * places,), jnp.int32),
            pltpu.SemaphoreType.DMA((slides * places,)),
        ]
        + [pltpu.VMEM(x.shape, x.dtype) for x in inputs]
        + [pltpu.SemaphoreType.DMA((len(inputs),))],
        compiler_params=pltpu.CompilerParams(vmem_limit_bytes=8 * MIB),
        name="pack_tiles",
    )(counts, routing, *fixed)
    return outs[:-3], outs[-3:]


def forward_kernel(kind, last, inputs, kept, table_ref, *refs):
    tile_refs, refs = refs[:inputs], refs[inputs:]
    taps_hbm, vectors_ref, expand_hbm, reduce_hbm, head_hbm = refs[:5]
    refs = refs[5 + (0 if kind == 0 else kept) :]
    out_hbms, refs = refs[:kept], refs[kept:]
    held, refs = refs[:kept], refs[kept:]
    taps_ref, expand_ref, reduce_ref, head_ref, padded, depth_out, normed, pre, load_sems = refs[:9]
    tile_sems, out_sems = refs[9:]
    out_s, embed_s, unit_s, inv_s, hidden_s, slope_s, head_slope_s, source_s = held
    items = table_ref[class_field(kind, -1)]
    side, channels = out_s.shape[1], out_s.shape[3]
    cells = side * side
    bands = channels // LANES
    low = ROW_UNIT // 2
    reach = KS // 2
    constants = [
        pltpu.make_async_copy(source, target, load_sems.at[index])
        for index, (source, target) in enumerate(
            (
                (taps_hbm, taps_ref),
                (expand_hbm, expand_ref),
                (reduce_hbm, reduce_ref),
                (head_hbm, head_ref),
            )
        )
    ]

    def tile_copy(ref, row, buffer):
        lines = ref.at[row] if len(ref.shape) == 4 else ref.at[pl.ds(row * side, side)]
        return pltpu.make_async_copy(lines, source_s.at[buffer], tile_sems.at[buffer])

    def load(item, buffer):
        origin = table_ref[class_field(kind, FROM) + item]
        place = 0
        for index, ref in enumerate(tile_refs):
            own = kind == 0 and index == 0
            for row in range(1 if own else ref.shape[0] // side):

                @pl.when(origin == place)
                def _load():
                    at = table_ref[class_field(kind, OWN) + item] if own else row
                    tile_copy(ref, at, buffer).start()

                place += 1

    def keep(part, slot, buffer):
        return pltpu.make_async_copy(
            held[part].at[buffer], out_hbms[part].at[slot], out_sems.at[part, buffer]
        )

    def wait_kept(buffer):
        for part in range(kept - 1):
            keep(part, 0, buffer).wait()

    def vector(index, lanes):
        return vectors_ref[index : index + 1, lanes]

    @pl.when(items > 0)
    def _first():
        load(0, 0)
        for copy in constants:
            copy.start()
        edge = jnp.zeros((side, low, LANES), jnp.float32)
        for band in range(bands):
            padded[band, :, 0:low, :] = edge
            padded[band, :, low + side :, :] = edge

    def one_item(item, carry):
        buffer = lax.rem(item, 2)
        slot = table_ref[class_field(kind, SLOT) + item]

        @pl.when(item >= 2)
        def _free():
            wait_kept(buffer)

        tile_copy(tile_refs[0], 0, buffer).wait()

        @pl.when(item == 0)
        def _taps():
            constants[0].wait()

        for band in range(bands):
            for at in range(side):
                padded[band, at, low : low + side, :] = source_s[
                    buffer, at, :, band * LANES : (band + 1) * LANES
                ].astype(jnp.float32)

        def convolve(band, carry):
            lanes = pl.ds(pl.multiple_of(band * LANES, LANES), LANES)
            bias = jnp.broadcast_to(vectors_ref[DEPTH_BIAS : DEPTH_BIAS + 1, lanes], (side, LANES))
            totals = [bias for _ in range(side)]
            for col in range(KS):
                start = low - reach + col
                weights = [
                    jnp.broadcast_to(
                        taps_ref[row * KS + col : row * KS + col + 1, lanes], (side, LANES)
                    ).astype(jnp.bfloat16)
                    for row in range(KS)
                ]
                sums = [None] * side
                for at in range(side):
                    line = padded[band, at, start : start + side, :].astype(jnp.bfloat16)
                    for row in range(KS):
                        place = at - row + reach
                        if 0 <= place < side:
                            term = weights[row] * line
                            sums[place] = term if sums[place] is None else sums[place] + term
                for place in range(side):
                    totals[place] = totals[place] + sums[place].astype(jnp.float32)
            for place in range(side):
                depth_out[band, place * side : (place + 1) * side, :] = totals[place]
            return carry

        lax.fori_loop(0, bands, convolve, 0)
        for start in range(0, cells, PART):
            rows = slice(start, start + PART)
            pieces = [depth_out[band, rows, :] for band in range(bands)]
            mean = jnp.sum(sum(pieces), axis=1, keepdims=True) * (1.0 / channels)
            pieces = [piece - mean for piece in pieces]
            var = jnp.sum(sum(p * p for p in pieces), axis=1, keepdims=True) * (1.0 / channels)
            inv = lax.rsqrt(var + EPSILON)
            inv_s[buffer, rows, :] = jnp.broadcast_to(inv, (PART, LANES))
            for band in range(bands):
                lanes = slice(band * LANES, (band + 1) * LANES)
                unit = pieces[band] * inv
                unit_s[buffer, rows, lanes] = unit
                normed[rows, lanes] = (unit * vector(GAIN, lanes) + vector(SHIFT, lanes)).astype(
                    jnp.bfloat16
                )

        @pl.when(item == 0)
        def _weights():
            for copy in constants[1:]:
                copy.wait()

        @pl.when(item + 1 < items)
        def _next():
            @pl.when(item >= 1)
            def _source_free():
                keep(kept - 1, 0, 1 - buffer).wait()

            load(item + 1, 1 - buffer)

        for part in (2, 3):
            keep(part, slot, buffer).start()
        for index, begin in enumerate(range(0, expand_ref.shape[1], WIDTH)):
            cols = slice(begin, begin + WIDTH)
            at = index % pre.shape[0]
            pre[at] = mix(normed[...], expand_ref[:, cols])
            for start in range(0, cells, PART):
                rows = slice(start, start + PART)
                act, slope = gelu_and_slope(pre[at, rows, :] + vector(EXPAND_BIAS, cols))
                hidden_s[buffer, rows, cols] = act.astype(jnp.bfloat16)
                slope_s[buffer, rows, cols] = slope.astype(jnp.bfloat16)
        for part in (4, 5):
            keep(part, slot, buffer).start()
        lanes = slice(0, channels)
        depth_rows = mix(hidden_s[buffer], reduce_ref[...])
        for at in range(side):
            rows = slice(at * side, (at + 1) * side)
            branch = vector(SCALE, lanes) * (depth_rows[rows] + vector(REDUCE_BIAS, lanes))
            line = (source_s[buffer, at].astype(jnp.float32) + branch).astype(jnp.bfloat16)
            normed[rows, :] = line
            out_s[buffer, at] = line
        for part in (0, 7):
            keep(part, slot, buffer).start()
        for index, begin in enumerate(range(0, head_ref.shape[1], WIDTH)):
            cols = slice(begin, begin + WIDTH)
            at = index % pre.shape[0]
            pre[at] = mix(normed[...], head_ref[:, cols])
            total = None
            for start in range(0, cells, PART):
                rows = slice(start, start + PART)
                act, slope = gelu_and_slope(pre[at, rows, :])
                head_slope_s[buffer, rows, cols] = slope.astype(jnp.bfloat16)
                folded = act[0:8]
                for piece in range(8, PART, 8):
                    folded = folded + act[piece : piece + 8]
                total = folded if total is None else total + folded
            mean = jnp.sum(total, axis=0, keepdims=True) * (1.0 / cells)
            embed_s[buffer, :, cols] = jnp.broadcast_to(mean, (8, WIDTH))
        for part in (1, 6):
            keep(part, slot, buffer).start()
        return carry

    lax.fori_loop(0, items, one_item, 0)
    for back in (1, 2):

        @pl.when(items >= back)
        def _drain():
            buffer = lax.rem(items - back, 2)
            for part in range(kept):
                keep(part, 0, buffer).wait()

    if last:
        filled = sum(table_ref[FILLED + proc] for proc in range(PROC))

        @pl.when(filled < PROC)
        def _zeros():
            for ref in held:
                ref[0] = jnp.zeros(ref.shape[1:], ref.dtype)

        for proc in range(PROC):

            @pl.when(table_ref[FILLED + proc] == 0)
            def _empty():
                for part in range(kept):
                    keep(part, proc, 0).start()
                wait_kept(0)
                keep(kept - 1, proc, 0).wait()


def pinned(array):
    return pltpu.with_memory_space_constraint(array, pltpu.HBM)


def forward_block(kind, last, table, tiles, taps, vectors, expand, reduce, head, before):
    side, channels = tiles[0].shape[-2:]
    cells, hid, embed = side * side, expand.shape[1], head.shape[1]
    bands = channels // LANES
    outs = (
        ((side, side, channels), jnp.bfloat16),
        ((8, embed), jnp.float32),
        ((cells, channels), jnp.float32),
        ((cells, LANES), jnp.float32),
        ((cells, hid), jnp.bfloat16),
        ((cells, hid), jnp.bfloat16),
        ((cells, embed), jnp.bfloat16),
        ((side, side, channels), jnp.bfloat16),
    )
    smem = pl.BlockSpec(memory_space=pltpu.SMEM)
    vmem = pl.BlockSpec(memory_space=pltpu.VMEM)
    if kind == 0:
        tiles = (pinned(tiles[0]),) + tuple(tiles[1:])
    first = 1 + len(tiles) + 5
    return pl.pallas_call(
        functools.partial(forward_kernel, kind, last, len(tiles), len(outs)),
        out_shape=tuple(pltpu.HBM((PROC,) + shape, dtype) for shape, dtype in outs),
        in_specs=[smem]
        + [HBM] * len(tiles)
        + [IN_HBM, vmem, IN_HBM, IN_HBM, IN_HBM]
        + [IN_HBM] * len(before),
        out_specs=(IN_HBM,) * len(outs),
        scratch_shapes=[pltpu.VMEM((2,) + shape, dtype) for shape, dtype in outs]
        + [
            pltpu.VMEM(taps.shape, jnp.float32),
            pltpu.VMEM(expand.shape, jnp.bfloat16),
            pltpu.VMEM(reduce.shape, jnp.bfloat16),
            pltpu.VMEM(head.shape, jnp.bfloat16),
            pltpu.VMEM((bands, side, side + ROW_UNIT, LANES), jnp.float32),
            pltpu.VMEM((bands, cells, LANES), jnp.float32),
            pltpu.VMEM((cells, channels), jnp.bfloat16),
            pltpu.VMEM((3, cells, WIDTH), jnp.float32),
            pltpu.SemaphoreType.DMA((4,)),
            pltpu.SemaphoreType.DMA((2,)),
            pltpu.SemaphoreType.DMA((len(outs), 2)),
        ],
        input_output_aliases={first + index: index for index in range(len(before))},
        compiler_params=pltpu.CompilerParams(vmem_limit_bytes=24 * MIB),
        cost_estimate=cost(1.0),
        name="forward_block_" + str(kind),
    )(table, *tiles, pinned(taps), vectors, pinned(expand), pinned(reduce), pinned(head), *before)


def cost(micros):
    return pl.CostEstimate(flops=int(micros * 1e9), bytes_accessed=1024, transcendentals=0)


def rows_kernel(slides, table_ref, embed_ref, small_ref, *refs):
    buffer_refs, (out_ref, smalls_ref, rows_ref, lines_ref, extra_ref, sems) = (
        refs[: slides - 1],
        refs[slides - 1 :],
    )
    copies = [
        pltpu.make_async_copy(ref.at[ref.shape[0] - 1], extra_ref.at[index], sems.at[index])
        for index, ref in enumerate(buffer_refs)
    ]
    for copy in copies:
        copy.start()
    my_slide, my_member = lax.axis_index(DP), lax.axis_index(GROUP)
    channels = extra_ref.shape[2]
    half = E // 2
    channel = lax.broadcasted_iota(jnp.int32, (1, E), 1)
    inner = jnp.where(channel < half, channel, channel - half)
    odd = lax.rem(inner, 2)
    frequency = jnp.exp((inner - odd).astype(jnp.float32) * (-math.log(10000.0) / half))
    phase = odd.astype(jnp.float32) * (0.5 * math.pi)
    lane = lax.broadcasted_iota(jnp.int32, (1, LANES), 1)
    smalls_ref[0] = small_ref[...]
    lines = SMALL // channels
    for index, copy in enumerate(copies):
        copy.wait()
        extra = extra_ref[index].astype(jnp.float32)
        for line in range(lines):
            total = extra[line : line + 1]
            for piece in range(1, PIECES):
                total = total + extra[piece * lines + line : piece * lines + line + 1]
            smalls_ref[1 + index, :, line * channels : (line + 1) * channels] = total
    for proc in range(PROC):
        filled = table_ref[FILLED + proc]
        slide = table_ref[SLIDE + proc]
        slot = table_ref[PLACE + proc]
        held = smalls_ref[0]
        for other in range(1, slides):
            held = jnp.where((slide ^ my_slide) == other, smalls_ref[other], held)
        spots = [
            jnp.sum(jnp.where(lane == slot, held[:, at : at + LANES], 0.0), axis=1, keepdims=True)
            for at in (ROWS_AT, COLS_AT)
        ]
        angle = jnp.where(channel < half, spots[0], spots[1]) * frequency + phase
        target = jnp.where(lane == 0, slide, jnp.where(lane == 1, slot, my_member))
        target = jnp.where(filled != 0, target, jnp.where(lane == 2, -1, 0))
        target = jnp.where(lane < 3, target, 0)
        rows_ref[proc : proc + 1, 0:E] = angle
        rows_ref[2 * PROC + proc : 2 * PROC + proc + 1, 0:E] = embed_ref[proc, 0:1, :]
        rows_ref[proc : proc + 1, E:] = target.astype(jnp.float32)
    code = jnp.sin(rows_ref[0 : 2 * PROC, 0:E])
    embed = rows_ref[2 * PROC : 4 * PROC, 0:E].astype(jnp.bfloat16).astype(jnp.float32)
    row_id = lax.broadcasted_iota(jnp.int32, (2 * PROC, E), 0)
    there = row_id < 0
    for proc in range(PROC):
        there = there | ((row_id == proc) & (table_ref[FILLED + proc] != 0))
    total = jnp.where(there, embed + code, 0.0)
    rows_ref[0 : 2 * PROC, 0:E] = total
    halves = jnp.concatenate(
        [
            rows_ref[0:PROC, 0:HALF],
            jnp.concatenate(
                [rows_ref[0:PROC, HALF:], jnp.zeros((PROC, 2 * HALF - E - LANES), jnp.float32)], axis=1
            ),
        ],
        axis=0,
    )
    core = lax.axis_index("core")
    for half in range(2):
        lines_ref[half * 2 * PROC : (half + 1) * 2 * PROC, :] = jnp.where(core == half, halves, 0.0)
    out_ref[...] = lines_ref[...].astype(jnp.bfloat16)


def tile_rows(table, embeds, small, buffers):
    smem = pl.BlockSpec(memory_space=pltpu.SMEM)
    vmem = pl.BlockSpec(memory_space=pltpu.VMEM)
    slides = 1 + len(buffers)
    return pl.pallas_call(
        functools.partial(rows_kernel, slides),
        out_shape=(
            jax.ShapeDtypeStruct((ROW_UNIT, HALF), jnp.bfloat16),
            jax.ShapeDtypeStruct((slides, 1, SMALL), jnp.float32),
        ),
        in_specs=[smem, vmem, vmem] + [HBM] * len(buffers),
        out_specs=(vmem, vmem),
        scratch_shapes=[
            pltpu.VMEM((4 * PROC, E + LANES), jnp.float32),
            pltpu.VMEM((ROW_UNIT, HALF), jnp.float32),
            pltpu.VMEM((len(buffers),) + buffers[0].shape[1:], jnp.bfloat16),
            pltpu.SemaphoreType.DMA((len(buffers),)),
        ],
        cost_estimate=cost(1.0),
        name="tile_rows",
    )(table, embeds, small, *buffers)


def slide_kernel(
    length,
    members,
    slides,
    pieces,
    table_ref,
    *refs,
):
    slide_parts(length, members, slides, table_ref, refs[:pieces], *refs[pieces:])


def slide_parts(
    length,
    members,
    slides,
    table_ref,
    piece_refs,
    taps_hbm,
    matrix_hbm,
    vectors_ref,
    smalls_ref,
    feature_ref,
    grad_ref,
    came_ref,
    picks,
    own_rows,
    tile_rows,
    mixed,
    grad_agg,
    taps_ref,
    matrix_ref,
    sems,
):
    loads = [
        pltpu.make_async_copy(taps_hbm, taps_ref, sems.at[0]),
        pltpu.make_async_copy(matrix_hbm, matrix_ref, sems.at[1]),
    ]
    for load in loads:
        load.start()
    for index, ref in enumerate(piece_refs):
        size = ref.shape[0]
        came_ref[index * size : (index + 1) * size, :] = ref[...]
    my_slide, my_member = lax.axis_index(DP), lax.axis_index(GROUP)
    border = ROW_UNIT
    reach = KERNEL_TAPS // 2
    blocks = [slice(start, start + WIDTH) for start in range(0, E, WIDTH)]
    lane = lax.broadcasted_iota(jnp.int32, (8, LANES), 1)
    scales = jnp.where(lane == 0, length, jnp.where(lane == 1, members, jnp.where(lane == 2, 1, 0)))
    tail = came_ref[:, E - HALF : E - HALF + LANES]
    target = mix_cols(scales.astype(jnp.float32).astype(jnp.bfloat16), tail)[0:1, :]
    lines = came_ref.shape[0]
    second = lax.rem(lax.broadcasted_iota(jnp.int32, (1, lines), 1), 2 * PROC) >= PROC
    target = jnp.where(second, target, -1.0)
    step = lax.broadcasted_iota(jnp.int32, (length, 1), 0)

    want = (my_slide * length + step).astype(jnp.float32)
    picks[0:length, :] = (target == want).astype(jnp.float32)
    index = lax.broadcasted_iota(jnp.int32, (ROW_UNIT, 1), 0)
    short = lax.broadcasted_iota(jnp.int32, (8, 1), 0)
    helds, shares = [], []
    for proc in range(PROC):
        filled = table_ref[FILLED + proc]
        slide = table_ref[SLIDE + proc]
        place = table_ref[PLACE + proc] * members + my_member
        at = place + (index - 2 * reach) * TILE_DILATION
        inside = (at >= 0) & (at < length) & (index <= 4 * reach) & (filled != 0)
        want = jnp.where(inside, slide * length + at, -2).astype(jnp.float32)
        start = length + proc * ROW_UNIT
        picks[start : start + ROW_UNIT, :] = (target == want).astype(jnp.float32)
        held = smalls_ref[0]
        for other in range(1, slides):
            held = jnp.where((slide ^ my_slide) == other, smalls_ref[other], held)
        helds.append(held)
        count = held[:, COUNT_AT : COUNT_AT + 1]
        at = (place + (short - reach) * TILE_DILATION).astype(jnp.float32)
        shares.append(jnp.where((at >= 0.0) & (at < count), 1.0 / count, 0.0))
    late = picks[...]
    early = pltpu.roll(late, lines - PROC, axis=1).astype(jnp.bfloat16)
    late = late.astype(jnp.bfloat16)
    edge = jnp.zeros((border, E), jnp.float32)
    own_rows[0:border, :] = edge
    own_rows[border + length :, :] = edge
    loads[0].wait()

    def tap(number, cols):
        return taps_ref[number : number + 1, cols]

    for cols in blocks:
        pick, at = (early, cols.start) if cols.start < HALF else (late, cols.start - HALF)
        found = mix(pick, came_ref[:, at : at + WIDTH])
        own_rows[border : border + length, cols] = found[0:length]
        tile_rows[:, cols] = found[length:]
        total = found[0:length]
        for number in range(KERNEL_TAPS):
            start = border + (number - reach) * TILE_DILATION
            total = total + tap(number, cols) * own_rows[start : start + length, cols]
        mixed[0:length, cols] = total.astype(jnp.bfloat16)
        totals = []
        for proc in range(PROC):
            base = proc * ROW_UNIT
            total = tile_rows[base + reach : base + reach + 8, cols]
            for number in range(KERNEL_TAPS):
                total = total + tap(number, cols) * tile_rows[base + number : base + number + 8, cols]
            totals.append(total)
        mixed[length:, cols] = jnp.concatenate(totals, axis=0).astype(jnp.bfloat16)
    count = smalls_ref[0][:, COUNT_AT : COUNT_AT + 1]
    share = jnp.where(step.astype(jnp.float32) < count, 1.0 / count, 0.0)
    loads[1].wait()
    for cols in blocks:
        bias = vectors_ref[SLIDE_BIAS : SLIDE_BIAS + 1, cols]
        pre = mix(mixed[...], matrix_ref[:, cols]) + bias
        total = None
        for start in range(0, length, PART):
            act, _ = gelu_and_slope(pre[start : start + PART])
            piece = jnp.sum(act * share[start : start + PART], axis=0, keepdims=True)
            total = piece if total is None else total + piece
        feature_ref[:, cols] = total
        _, slope = gelu_and_slope(pre[length:])
        parts = [
            helds[proc][:, cols] * shares[proc] * slope[proc * 8 : (proc + 1) * 8]
            for proc in range(PROC)
        ]
        grad_agg[:, cols] = jnp.concatenate(parts, axis=0).astype(jnp.bfloat16)
    for cols in blocks:
        grads = mix_cols(grad_agg[...], matrix_ref[cols, :])
        for proc in range(PROC):
            block = grads[proc * 8 : (proc + 1) * 8]
            total = block[reach : reach + 1]
            for number in range(KERNEL_TAPS):
                at = 2 * reach - number
                total = total + tap(number, cols) * block[at : at + 1]
            total = jnp.where(table_ref[FILLED + proc] != 0, total, 0.0)
            grad_ref[proc, :, cols] = total.astype(jnp.bfloat16).astype(jnp.float32)


def slide_grads(length, members, table, came, taps, matrix, vectors, smalls):
    slides = smalls.shape[0]
    lines = sum(piece.shape[0] for piece in came)
    smem = pl.BlockSpec(memory_space=pltpu.SMEM)
    vmem = pl.BlockSpec(memory_space=pltpu.VMEM)
    return pl.pallas_call(
        functools.partial(slide_kernel, length, members, slides, len(came)),
        out_shape=(
            jax.ShapeDtypeStruct((1, E), jnp.float32),
            jax.ShapeDtypeStruct((PROC, 1, E), jnp.float32),
        ),
        in_specs=[smem] + [vmem] * len(came) + [IN_HBM, IN_HBM, vmem, vmem],
        out_specs=(vmem, vmem),
        scratch_shapes=[
            pltpu.VMEM((lines, HALF), jnp.bfloat16),
            pltpu.VMEM((length + PROC * ROW_UNIT, lines), jnp.float32),
            pltpu.VMEM((length + 2 * ROW_UNIT, E), jnp.float32),
            pltpu.VMEM((PROC * ROW_UNIT, E), jnp.float32),
            pltpu.VMEM((length + PROC * 8, E), jnp.bfloat16),
            pltpu.VMEM((PROC * 8, E), jnp.bfloat16),
            pltpu.VMEM(taps.shape, jnp.float32),
            pltpu.VMEM(matrix.shape, jnp.bfloat16),
            pltpu.SemaphoreType.DMA((2,)),
        ],
        compiler_params=pltpu.CompilerParams(vmem_limit_bytes=16 * MIB),
        cost_estimate=cost(3.0),
        name="slide_grads",
    )(table, *came, pinned(taps), pinned(matrix), vectors, smalls)


class Plan:
    def __init__(self, slides, members, channels, hid):
        self.devices = slides * members
        self.ys, self.g1, self.g2 = slides // 2, 4, members // 4
        assert self.ys == self.g2
        self.channels = channels
        self.pieces = hid // channels
        self.expand_rows = channels // self.devices
        self.reduce_rows = hid // self.devices
        self.block_rows = -(-self.reduce_rows // ROW_UNIT) * ROW_UNIT
        self.share = KS * KS * channels // self.devices

    def spots(self):
        my_core, my_y = lax.axis_index("core"), lax.axis_index("y")
        my_z, my_x = lax.axis_index("g1"), lax.axis_index("g2")
        for device in range(self.devices):
            slide, member = divmod(device, self.g1 * self.g2)
            (y, core), (z, x) = divmod(slide, 2), divmod(member, self.g2)
            yield (
                my_core ^ core,
                lax.rem(y - my_y + self.ys, self.ys),
                lax.rem(x - my_x + self.g2, self.g2),
                lax.rem(z - my_z + self.g1, self.g1),
            )


def send_out(staged, sems, refs):
    copies = [
        pltpu.make_async_copy(staged.at[index], ref, sems.at[index]) for index, ref in enumerate(refs)
    ]
    for copy in copies:
        copy.start()
    for copy in copies:
        copy.wait()


def padded_block(block, rows):
    extra = rows - block.shape[0]
    if extra:
        block = jnp.concatenate([block, jnp.zeros((extra, block.shape[1]), block.dtype)], axis=0)
    return block.astype(jnp.bfloat16)


def turn_kernel(unit_ref, vectors_ref, out_ref, normed, eye_ref):
    cells, channels = unit_ref.shape[1:]
    eye_ref[...] = unit_matrix(channels)
    for start in range(0, cells, PART):
        rows = slice(start, start + PART)
        gain = vectors_ref[GAIN : GAIN + 1, 0:channels]
        shift = vectors_ref[SHIFT : SHIFT + 1, 0:channels]
        normed[rows, :] = (unit_ref[0, rows, :] * gain + shift).astype(jnp.bfloat16)
    out_ref[...] = mix_cols(eye_ref[...], normed[...]).astype(jnp.bfloat16)


def unit_matrix(size):
    spot = lax.broadcasted_iota(jnp.int32, (size, size), 0)
    same = spot == lax.broadcasted_iota(jnp.int32, (size, size), 1)
    return same.astype(jnp.float32).astype(jnp.bfloat16)


def turned_normed(unit, vectors):
    cells, channels = unit.shape[1:]
    return pl.pallas_call(
        turn_kernel,
        out_shape=jax.ShapeDtypeStruct((channels, PROC * cells), jnp.bfloat16),
        grid=(PROC,),
        in_specs=[pl.BlockSpec((1, cells, channels), lambda i: (i, 0, 0)), whole(vectors.shape)],
        out_specs=pl.BlockSpec((channels, cells), lambda i: (0, i)),
        scratch_shapes=[
            pltpu.VMEM((cells, channels), jnp.bfloat16),
            pltpu.VMEM((channels, channels), jnp.bfloat16),
        ],
        compiler_params=pltpu.CompilerParams(vmem_limit_bytes=8 * MIB),
        cost_estimate=cost(3.0),
        name="turned_normed",
    )(unit, vectors)


def weights_kernel(
    plan,
    grad_ref,
    hidden_ref,
    head_slope_ref,
    slope_ref,
    normed_ref,
    vectors_ref,
    head_ref,
    reduce_ref,
    grad_pre_hbm,
    keep_ref,
    send_ref,
    grad_pre,
    turned,
    grad_head,
    eye_ref,
    staged,
    sems,
    pre_sems,
):
    cells, channels = slope_ref.shape[1], normed_ref.shape[0]
    hid = reduce_ref.shape[0]
    every = slice(0, channels)

    def vector(index, lanes):
        return vectors_ref[index : index + 1, lanes]

    eye_ref[...] = unit_matrix(channels)

    def one_slot(slot, carry):
        rows_all = pl.ds(pl.multiple_of(slot * cells, cells), cells)
        row = grad_ref[slot] * (1.0 / cells)
        for start in range(0, cells, PART):
            rows = slice(start, start + PART)
            grad_head[rows, :] = (row * head_slope_ref[slot, rows, :].astype(jnp.float32)).astype(
                jnp.bfloat16
            )
        grad_mlp = (vector(SCALE, every) * mix_cols(grad_head[...], head_ref[...])).astype(
            jnp.bfloat16
        )
        turned[:, rows_all] = mix_cols(eye_ref[...], grad_mlp).astype(jnp.bfloat16)
        for begin in range(0, hid, WIDTH):
            cols = slice(begin, begin + WIDTH)
            grad_hidden = mix_cols(grad_mlp, reduce_ref[cols, :])
            grad_pre[rows_all, cols] = (
                grad_hidden * slope_ref[slot, :, cols].astype(jnp.float32)
            ).astype(jnp.bfloat16)
        return carry

    lax.fori_loop(0, PROC, one_slot, 0)
    writes = [
        pltpu.make_async_copy(
            grad_pre.at[pl.ds(slot * cells, cells)], grad_pre_hbm.at[slot], pre_sems.at[slot]
        )
        for slot in range(PROC)
    ]
    for write in writes:
        write.start()
    spots = list(plan.spots())
    per_block = channels // plan.reduce_rows
    tall = plan.block_rows
    for index in range(plan.pieces):
        cols = slice(index * channels, (index + 1) * channels)
        total = mix(turned[...], hidden_ref[:, cols]).astype(jnp.bfloat16)
        back = mix_cols(eye_ref[...], total)
        for part in range(per_block):
            block = back[part * plan.reduce_rows : (part + 1) * plan.reduce_rows]
            core, y, x, z = spots[index * per_block + part]
            staged[core, 0, x, y, z] = padded_block(block, tall)
    totals = []
    for quarter in range(plan.pieces):
        cols = slice(quarter * channels, (quarter + 1) * channels)
        totals.append(mix(normed_ref[...], grad_pre[:, cols]))
    size = plan.expand_rows
    for device in range(plan.devices):
        rows = slice(device * size, (device + 1) * size)
        block = jnp.concatenate([total[rows] for total in totals], axis=0)
        core, y, x, z = spots[device]
        staged[core, 1, y, x, z] = padded_block(block, tall)
    send_out(staged, sems, (keep_ref, send_ref))
    for write in writes:
        write.wait()


def taps_kernel(
    plan,
    first,
    last,
    table_ref,
    source_ref,
    grad_pre_ref,
    unit_ref,
    inv_ref,
    before_ref,
    vectors_ref,
    expand_ref,
    out_ref,
    padded,
    tap_sums,
    tap_rows,
    grad_norm,
    depth_back,
):
    step = pl.program_id(0)
    filled = table_ref[FILLED + first + step]
    side, channels = source_ref.shape[1], source_ref.shape[3]
    bands = channels // LANES
    low = ROW_UNIT // 2
    reach = KS // 2

    @pl.when(step == 0)
    def _start():
        if first:
            tap_sums[...] = before_ref[...]
        else:
            tap_sums[...] = jnp.zeros(tap_sums.shape, jnp.float32)

    @pl.when(filled != 0)
    def _work():
        cells = side * side
        gain = vectors_ref[GAIN : GAIN + 1, 0:channels]
        grad_norm[...] = mix_cols(grad_pre_ref[0], expand_ref[...])
        for start in range(0, cells, PART):
            rows = slice(start, start + PART)
            scaled = grad_norm[rows, :] * gain
            unit = unit_ref[0, rows, :]
            mean = jnp.sum(scaled, axis=1, keepdims=True) * (1.0 / channels)
            mean_unit = jnp.sum(scaled * unit, axis=1, keepdims=True) * (1.0 / channels)
            inv = inv_ref[0, rows, 0:1]
            for band in range(bands):
                lanes = slice(band * LANES, (band + 1) * LANES)
                depth_back[band, rows, :] = (
                    inv * (scaled[:, lanes] - mean - unit[:, lanes] * mean_unit)
                ).astype(jnp.bfloat16)
        edge = jnp.zeros((side, low, LANES), jnp.float32)
        for band in range(bands):
            lanes = slice(band * LANES, (band + 1) * LANES)
            padded[band, :, 0:low, :] = edge
            padded[band, :, low + side :, :] = edge
            for at in range(side):
                padded[band, at, low : low + side, :] = source_ref[0, at, :, lanes].astype(
                    jnp.float32
                )

        def taps_of(band, carry):
            for col in range(KS):
                start = low - reach + col
                folded = [None] * KS
                grads = {}
                for half in range(2):
                    sums = [None] * KS
                    for at in range(half * side // 2, (half + 1) * side // 2):
                        line = padded[band, at, start : start + side, :].astype(jnp.bfloat16)
                        for row in range(KS):
                            place = at - row + reach
                            if 0 <= place < side:
                                if place not in grads:
                                    grads[place] = depth_back[
                                        band, place * side : (place + 1) * side, :
                                    ]
                                term = line * grads[place]
                                sums[row] = term if sums[row] is None else sums[row] + term
                    for row in range(KS):
                        total = sums[row].astype(jnp.float32)
                        for piece in range(0, side, 8):
                            block = total[piece : piece + 8, :]
                            folded[row] = block if folded[row] is None else folded[row] + block
                for row in range(KS):
                    tap_sums[band, row * KS + col] = tap_sums[band, row * KS + col] + folded[row]
            return carry

        lax.fori_loop(0, bands, taps_of, 0)

    @pl.when(step == pl.num_programs(0) - 1)
    def _finish():
        if not last:
            out_ref[...] = tap_sums[...]
            return
        for band in range(bands):
            lanes = slice(band * LANES, (band + 1) * LANES)
            tap_rows[0 : KS * KS, lanes] = jnp.sum(tap_sums[band], axis=1)
            tap_rows[KS * KS :, lanes] = jnp.zeros((tap_rows.shape[0] - KS * KS, LANES), jnp.float32)
        for device in range(plan.devices):
            start = device * plan.share // channels
            out_ref[device] = tap_rows[start : start + TAP_ROWS, :]


def per_slot(array):
    shape = array.shape[1:]
    return pl.BlockSpec((1,) + shape, lambda i, table: (i,) + (0,) * len(shape))


def weight_grads(plan, embed_grad, saved, vectors, head, reduce):
    normed, hidden, slope, head_slope = saved
    cells, channels = slope.shape[1], normed.shape[0]
    hid = reduce.shape[0]
    vmem = pl.BlockSpec(memory_space=pltpu.VMEM)
    blocks = jax.ShapeDtypeStruct(
        (2, plan.ys, plan.g2, plan.g1, plan.block_rows, channels), jnp.bfloat16
    )
    return pl.pallas_call(
        functools.partial(weights_kernel, plan),
        out_shape=(pltpu.HBM((PROC, cells, hid), jnp.bfloat16), blocks, blocks),
        in_specs=[vmem] * 8,
        out_specs=(IN_HBM, HBM, HBM),
        scratch_shapes=[
            pltpu.VMEM((PROC * cells, hid), jnp.bfloat16),
            pltpu.VMEM((channels, PROC * cells), jnp.bfloat16),
            pltpu.VMEM((cells, head.shape[1]), jnp.bfloat16),
            pltpu.VMEM((channels, channels), jnp.bfloat16),
            pltpu.VMEM((2,) + blocks.shape, jnp.bfloat16),
            pltpu.SemaphoreType.DMA((2,)),
            pltpu.SemaphoreType.DMA((PROC,)),
        ],
        compiler_params=pltpu.CompilerParams(vmem_limit_bytes=36 * MIB),
        cost_estimate=cost(12.0),
        name="weight_grads",
    )(embed_grad, hidden.reshape(PROC * cells, hid), head_slope, slope, normed, vectors, head, reduce)


def tap_grads(plan, first, last, table, streams, before, vectors, expand):
    side, channels = streams[0].shape[1], streams[0].shape[3]
    bands = channels // LANES
    sums = (bands, KS * KS, 8, LANES)
    out = (plan.devices, TAP_ROWS, channels) if last else sums

    def items(array):
        shape = array.shape[1:]
        return pl.BlockSpec((1,) + shape, lambda i, table: (first + i,) + (0,) * len(shape))

    return pl.pallas_call(
        functools.partial(taps_kernel, plan, first, last),
        out_shape=jax.ShapeDtypeStruct(out, jnp.float32),
        grid_spec=pltpu.PrefetchScalarGridSpec(
            num_scalar_prefetch=1,
            grid=(PROC // 2,),
            in_specs=[items(stream) for stream in streams]
            + [whole(before.shape), whole(vectors.shape), whole(expand.shape)],
            out_specs=pl.BlockSpec(out, lambda i, table: (0,) * len(out)),
            scratch_shapes=[
                pltpu.VMEM((bands, side, side + ROW_UNIT, LANES), jnp.float32),
                pltpu.VMEM(sums, jnp.float32),
                pltpu.VMEM((KS * KS + 7, channels), jnp.float32),
                pltpu.VMEM((side * side, channels), jnp.float32),
                pltpu.VMEM((bands, side * side, LANES), jnp.bfloat16),
            ],
        ),
        compiler_params=pltpu.CompilerParams(vmem_limit_bytes=16 * MIB),
        cost_estimate=cost(4.0),
        name="tap_grads_" + str(first),
    )(table, *streams, before, vectors, expand)


def shifted(values, names, sizes, shift):
    count = math.prod(sizes)
    pairs = []
    for index in range(count):
        spot = []
        rest = index
        for size in reversed(sizes):
            spot.append(rest % size)
            rest //= size
        spot = spot[::-1]
        target = 0
        for at, step, size in zip(spot, shift, sizes):
            target = target * size + (at + step) % size
        pairs.append((index, target))
    return lax.ppermute(values, names, pairs)


def shifts(sizes):
    steps = [()]
    for size in sizes:
        steps = [step + (more,) for step in steps for more in range(size)]
    return steps


def exchange(values, names):
    return lax.all_to_all(values, names, split_axis=0, concat_axis=0, tiled=True)


def gather_all(plan, lines):
    pair = lines + other_core(lines)
    sizes = (plan.ys, plan.g2)
    column = [pair] + [
        shifted(pair, ("y", "g2"), sizes, (y, x)) for y in range(plan.ys) for x in range(plan.g2) if y + x
    ]
    column = jnp.concatenate(column, axis=0)
    return [column] + [shifted(column, ("g1",), (plan.g1,), (step,)) for step in range(1, plan.g1)]


def add_all(parts, kind=jnp.bfloat16):
    total = parts[0].astype(jnp.float32)
    for part in parts[1:]:
        total = total + part.astype(jnp.float32)
    return total.astype(kind)


def other_core(values):
    return shifted(values, ("core",), (2,), (1,))


def sum_axis(kept, sent, name, size, kind=jnp.bfloat16):
    return [kept] + [shifted(part, (name,), (size,), (step + 1,)) for step, part in enumerate(sent)]


def on_device(
    tile_maps,
    positions,
    counts,
    routing,
    depth_kernel,
    depth_bias,
    norm_gain,
    norm_shift,
    expand_weight,
    expand_bias,
    reduce_weight,
    reduce_bias,
    layer_scale,
    head_weight,
    slide_taps,
    slide_weight,
    slide_bias,
    cotangent,
):
    slides = lax.axis_size(DP)
    members = lax.axis_size(GROUP)
    my_device = lax.axis_index(ALL)
    slots, channels = tile_maps.shape[0], tile_maps.shape[3]
    devices, length, places = slides * members, slots * members, slots // slides
    plan = Plan(slides, members, channels, expand_weight.shape[1])

    raw = (
        norm_gain,
        norm_shift,
        layer_scale,
        reduce_bias,
        depth_bias,
        expand_bias,
        slide_bias,
    )
    packed, (table, small, vectors) = pack_tiles(
        counts, routing, tile_maps, positions, cotangent, raw, slides, places
    )

    def from_other(buffer, other):
        return lax.ppermute(buffer, DP, [(index, index ^ other) for index in range(slides)])

    from_core = from_other(packed[0], 1)
    arrived = []
    for rank in range(places):
        buffers = packed[1 + rank * (slides - 2) : 1 + (rank + 1) * (slides - 2)]
        if rank:
            buffers, from_core = lax.optimization_barrier((buffers, from_core))
        arrived.append([from_other(buffer, other + 2) for other, buffer in enumerate(buffers)])

    consts = (depth_kernel, vectors, expand_weight, reduce_weight, head_weight)
    saved = forward_block(0, False, table, (tile_maps, from_core), *consts, ())
    for rank in range(places):
        saved = forward_block(1 + rank, rank + 1 == places, table, arrived[rank], *consts, saved)
    tile_out, tile_embed, unit, inv, hidden, slope, head_slope, source = saved
    lines, smalls = tile_rows(table, tile_embed, small, [from_core] + arrived[0])
    came = gather_all(plan, lines)
    normed = turned_normed(unit, vectors)
    came, normed = lax.optimization_barrier((came, normed))

    feature, embed_grad = slide_grads(
        length, members, table, came, slide_taps, slide_weight, vectors, smalls
    )
    grad_pre, kept, sent = weight_grads(
        plan,
        embed_grad,
        (normed, hidden, slope, head_slope),
        vectors,
        head_weight,
        reduce_weight,
    )
    streams = (source, pinned(grad_pre), unit, inv)

    names = ("g2", "y")
    size = plan.ys
    came = other_core(sent)
    none = jnp.zeros((channels // LANES, KS * KS, 8, LANES), jnp.float32)
    tap_sums = tap_grads(plan, 0, False, table, streams, none, vectors, expand_weight)
    came, tap_sums = lax.optimization_barrier((came, tap_sums))
    out = [
        [add_all([kept[kind, step], came[kind, step]]) for step in range(1, size)]
        for kind in range(2)
    ]
    stay = [add_all([kept[kind, 0], came[kind, 0]]) for kind in range(2)]
    out, tap_sums = lax.optimization_barrier((out, tap_sums))
    parts = [sum_axis(stay[kind], out[kind], names[kind], size) for kind in range(2)]
    taps = tap_grads(plan, PROC // 2, True, table, streams, tap_sums, vectors, expand_weight)
    out = [
        [add_all([part[step] for part in parts[kind]]) for step in range(1, size)]
        for kind in range(2)
    ]
    stay = [add_all([part[0] for part in parts[kind]]) for kind in range(2)]
    taps = taps[:, :DEPTH_ROWS].astype(jnp.bfloat16)
    out, taps = lax.optimization_barrier((out, taps))
    parts = [sum_axis(stay[kind], out[kind], names[1 - kind], size) for kind in range(2)]
    taps = exchange(taps, ALL)
    both = jnp.concatenate([add_all(parts[0]), add_all(parts[1])], axis=1)
    total = add_all(
        sum_axis(both[0], [both[step] for step in range(1, plan.g1)], "g1", plan.g1), jnp.float32
    )
    reduce_share = total[: plan.reduce_rows]
    expand_share = total[plan.block_rows : plan.block_rows + plan.pieces * plan.expand_rows]
    expand_share = expand_share.reshape(plan.pieces, plan.expand_rows, channels).transpose(1, 0, 2)
    depth_share = lax.dynamic_slice(
        jnp.sum(taps.astype(jnp.float32), axis=0).reshape(-1),
        (my_device * plan.share % channels,),
        (plan.share,),
    )
    return (tile_out, feature, expand_share.reshape(-1), reduce_share.reshape(-1), depth_share)


def solution(mesh):
    slides, members = mesh.shape["dp"], mesh.shape["group"]
    fine = Mesh(mesh.devices.reshape(slides // 2, 2, 4, members // 4), ALL)
    return jax.shard_map(
        on_device,
        mesh=fine,
        in_specs=(
            P(ALL, None, None, None),
            P(None, ALL),
            P(DP),
            P(None, GROUP, None),
        )
        + (P(),) * 13
        + (P(DP, None),),
        out_specs=(
            P(ALL, None, None, None),
            P(DP, None),
            P(ALL),
            P(ALL),
            P(ALL),
        ),
        check_vma=False,
    )
```

```python
import functools
import math

import jax
import jax.numpy as jnp
from jax import lax
from jax.experimental import pallas as pl
from jax.experimental.pallas import tpu as pltpu
from jax.sharding import Mesh, PartitionSpec as P

E = 768
KS = 7
KERNEL_TAPS = 7
TILE_DILATION = 3
PROC = 4
DP = ("y", "core")
GROUP = ("g1", "g2")
ALL = DP + GROUP

EPSILON = 1e-06
HALF_ROOT = 0.7071067811865476
INV_ROOT_TAU = 0.3989422804014327
BELL_SCALE = -0.7213475204444817
LANES = 128
ROW_UNIT = 16
DEPTH_ROWS = 4
TAP_ROWS = 8
MIB = 1024 * 1024
PART = 32
WIDTH = 256
GAIN, SHIFT, SCALE, REDUCE_BIAS, DEPTH_BIAS, EXPAND_BIAS, SLIDE_BIAS = range(7)
VECTORS = 7
ERFC_P = 0.3275911
ERFC_A = (0.254829592, -0.284496736, 1.421413741, -1.453152027, 1.061405429)

HBM = pl.BlockSpec(memory_space=pl.ANY)
IN_HBM = pl.BlockSpec(memory_space=pltpu.HBM)
ROWS_AT, COLS_AT, COUNT_AT, SMALL = E, E + LANES, E + 2 * LANES, E + 3 * LANES
PIECES = 3
HALF = 512


def whole(shape):
    return pl.BlockSpec(shape, lambda *_: (0,) * len(shape), pipeline_mode=pl.Buffered(1))


def gelu_and_slope(values):
    size = jnp.abs(values)
    divisor = 1.0 + (ERFC_P * HALF_ROOT) * size
    t = pl.reciprocal(divisor, approx=True)
    bell = jnp.exp2(values * (values * BELL_SCALE))
    poly = 0.5 * ERFC_A[4]
    for coefficient in ERFC_A[3::-1]:
        poly = poly * t + 0.5 * coefficient
    tail = poly * t * bell
    phi = jnp.where(values >= 0.0, 1.0 - tail, tail)
    return values * phi, phi + values * (INV_ROOT_TAU * bell)


def mix_cols(left_side, right_side):
    return lax.dot_general(
        left_side, right_side, (((1,), (1,)), ((), ())), preferred_element_type=jnp.float32
    )


def mix(left_side, right_side):
    return jnp.dot(left_side, right_side, preferred_element_type=jnp.float32)


FILLED, SLIDE, PLACE, CLASSES = 0, PROC, 2 * PROC, 3 * PROC
CLASS_SIZE = 1 + 3 * PROC


def class_field(kind, field, item=0):
    return CLASSES + kind * CLASS_SIZE + (1 + field * PROC + item if field >= 0 else 0)


SLOT, FROM, OWN = range(3)


def pack_kernel(slides, slots, places, counts_ref, route_ref, tiles_ref, pos_ref, cot_ref, *refs):
    inputs = (pos_ref, cot_ref) + refs[:VECTORS]
    refs = refs[VECTORS:]
    held_refs, refs = refs[-len(inputs) - 1 : -1], refs[: -len(inputs) - 1] + refs[-1:]
    send_refs, refs = refs[:-7], refs[-7:]
    table_ref, small_ref, vectors_ref, count_ref, slot_ref, sems, input_sems = refs
    loads = [
        pltpu.make_async_copy(ref, held, input_sems.at[index])
        for index, (ref, held) in enumerate(zip(inputs, held_refs))
    ]
    for load in loads:
        load.start()
    pos_ref, cot_ref = held_refs[:2]
    vector_refs = held_refs[2:]
    my_slide = lax.axis_index(DP)

    targets = [(0, rank, rank) for rank in range(places)]
    for rank in range(places):
        for other in range(2, slides):
            targets.append((1 + rank * (slides - 2) + other - 2, 0, other * places + rank))
    targets[:places] = [(0, rank, places + rank) for rank in range(places)]

    def copy_of(index, slot):
        buffer, row, _ = targets[index]
        side = tiles_ref.shape[1]
        lines = send_refs[buffer].at[pl.ds(row * side, side)]
        return pltpu.make_async_copy(tiles_ref.at[slot], lines, sems.at[index])

    for index in range(slides):
        count_ref[index] = 0
    for index in range(slides * places):
        slot_ref[index] = -1

    def place_slot(slot, carry):
        entry = route_ref[my_slide, 0, slot]

        @pl.when(entry >= 0)
        def _send():
            other = lax.div(entry, PROC) ^ my_slide
            rank = count_ref[other]
            count_ref[other] = rank + 1
            slot_ref[other * places + rank] = slot

        return carry

    lax.fori_loop(0, slots, place_slot, 0)
    for index, (_, _, key) in enumerate(targets):
        slot = slot_ref[key]

        @pl.when(slot >= 0)
        def _start():
            copy_of(index, slot).start()

    for load in loads:
        load.wait()
    small_ref[:, 0:E] = cot_ref[...]
    for row, start in enumerate((ROWS_AT, COLS_AT)):
        small_ref[:, start : start + LANES] = jnp.zeros((1, LANES), jnp.float32)
        small_ref[:, start : start + slots] = pos_ref[row : row + 1, :].astype(jnp.float32)
    small_ref[:, COUNT_AT:SMALL] = jnp.full((1, LANES), counts_ref[0], jnp.int32).astype(jnp.float32)
    channels = tiles_ref.shape[3]
    extra = []
    rest = small_ref[...]
    for piece in range(PIECES):
        part = rest.astype(jnp.bfloat16).astype(jnp.float32)
        rest = rest - part
        extra += [part[:, at : at + channels] for at in range(0, SMALL, channels)]
    extra.append(jnp.zeros((ROW_UNIT - len(extra), channels), jnp.float32))
    extra = jnp.concatenate(extra, axis=0).astype(jnp.bfloat16)
    for ref in send_refs[: slides - 1]:
        ref[ref.shape[0] - 1] = extra
    vectors_ref[...] = jnp.zeros(vectors_ref.shape, jnp.float32)
    for index, ref in enumerate(vector_refs):
        size = ref.shape[0]
        vectors_ref[index : index + 1, 0:size] = ref[...].reshape(1, size)

    kinds = 1 + places
    for field in range(CLASSES + kinds * CLASS_SIZE):
        table_ref[field] = 0
    for kind in range(kinds):
        for item in range(PROC):
            table_ref[class_field(kind, SLOT, item)] = PROC
    for other in range(slides):
        source = my_slide ^ other
        count_ref[0] = 0

        def take(slot, carry):
            entry = route_ref[source, 0, slot]
            proc = entry - my_slide * PROC

            @pl.when((proc >= 0) & (proc < PROC))
            def _take():
                rank = count_ref[0]
                count_ref[0] = rank + 1
                table_ref[FILLED + proc] = 1
                table_ref[SLIDE + proc] = source
                table_ref[PLACE + proc] = slot
                kind = 0 if other < 2 else 1 + rank
                base = CLASSES + kind * CLASS_SIZE
                item = table_ref[base]
                table_ref[base] = item + 1
                table_ref[base + 1 + SLOT * PROC + item] = proc
                if other == 0:
                    table_ref[base + 1 + FROM * PROC + item] = 0
                    table_ref[base + 1 + OWN * PROC + item] = slot
                else:
                    table_ref[base + 1 + FROM * PROC + item] = 1 + rank if other == 1 else other - 2

            return carry

        lax.fori_loop(0, slots, take, 0)
        if other == 0:
            own = table_ref[class_field(0, -1)]
            for item in range(1, PROC):

                @pl.when(item >= own)
                def _hold():
                    table_ref[class_field(0, OWN, item)] = table_ref[class_field(0, OWN, item - 1)]

    for kind in range(kinds):
        items = table_ref[class_field(kind, -1)]
        for item in range(1, PROC):

            @pl.when(item >= items)
            def _hold_slot():
                table_ref[class_field(kind, SLOT, item)] = table_ref[class_field(kind, SLOT, item - 1)]

    for index, (_, _, key) in enumerate(targets):

        @pl.when(slot_ref[key] >= 0)
        def _wait():
            copy_of(index, 0).wait()


def pack_tiles(counts, routing, tile_maps, positions, cotangent, vectors, slides, places):
    slots = tile_maps.shape[0]
    smem = pl.BlockSpec(memory_space=pltpu.SMEM)
    vmem = pl.BlockSpec(memory_space=pltpu.VMEM)
    buffers = 1 + places * (slides - 2)
    side = tile_maps.shape[1]
    shapes = [places * side + 1] + [side + 1] * (slides - 2) + [side] * (buffers - slides + 1)
    widest = max(vector.shape[0] for vector in vectors)
    inputs = (positions, cotangent) + vectors
    fixed = [pinned(x) for x in (tile_maps,) + inputs]
    outs = pl.pallas_call(
        functools.partial(pack_kernel, slides, slots, places),
        out_shape=tuple(
            jax.ShapeDtypeStruct((size,) + tile_maps.shape[2:], tile_maps.dtype) for size in shapes
        )
        + (
            jax.ShapeDtypeStruct((CLASSES + (1 + places) * CLASS_SIZE,), jnp.int32),
            jax.ShapeDtypeStruct((1, SMALL), jnp.float32),
            jax.ShapeDtypeStruct((8, widest), jnp.float32),
        ),
        in_specs=[smem, smem] + [IN_HBM] * len(fixed),
        out_specs=(vmem,) * buffers + (smem, vmem, vmem),
        scratch_shapes=[
            pltpu.SMEM((slides,), jnp.int32),
            pltpu.SMEM((slides * places,), jnp.int32),
            pltpu.SemaphoreType.DMA((slides * places,)),
        ]
        + [pltpu.VMEM(x.shape, x.dtype) for x in inputs]
        + [pltpu.SemaphoreType.DMA((len(inputs),))],
        compiler_params=pltpu.CompilerParams(vmem_limit_bytes=8 * MIB),
        name="pack_tiles",
    )(counts, routing, *fixed)
    return outs[:-3], outs[-3:]


def forward_kernel(kind, last, inputs, kept, table_ref, *refs):
    tile_refs, refs = refs[:inputs], refs[inputs:]
    taps_hbm, vectors_ref, expand_hbm, reduce_hbm, head_hbm = refs[:5]
    refs = refs[5 + (0 if kind == 0 else kept) :]
    out_hbms, refs = refs[:kept], refs[kept:]
    held, refs = refs[:kept], refs[kept:]
    taps_ref, expand_ref, reduce_ref, head_ref, padded, depth_out, normed, pre, load_sems = refs[:9]
    tile_sems, out_sems = refs[9:]
    out_s, embed_s, unit_s, inv_s, hidden_s, slope_s, head_slope_s, source_s = held
    items = table_ref[class_field(kind, -1)]
    side, channels = out_s.shape[1], out_s.shape[3]
    cells = side * side
    bands = channels // LANES
    low = ROW_UNIT // 2
    reach = KS // 2
    constants = [
        pltpu.make_async_copy(source, target, load_sems.at[index])
        for index, (source, target) in enumerate(
            (
                (taps_hbm, taps_ref),
                (expand_hbm, expand_ref),
                (reduce_hbm, reduce_ref),
                (head_hbm, head_ref),
            )
        )
    ]

    def tile_copy(ref, row, buffer):
        lines = ref.at[row] if len(ref.shape) == 4 else ref.at[pl.ds(row * side, side)]
        return pltpu.make_async_copy(lines, source_s.at[buffer], tile_sems.at[buffer])

    def load(item, buffer):
        origin = table_ref[class_field(kind, FROM) + item]
        place = 0
        for index, ref in enumerate(tile_refs):
            own = kind == 0 and index == 0
            for row in range(1 if own else ref.shape[0] // side):

                @pl.when(origin == place)
                def _load():
                    at = table_ref[class_field(kind, OWN) + item] if own else row
                    tile_copy(ref, at, buffer).start()

                place += 1

    def keep(part, slot, buffer):
        return pltpu.make_async_copy(
            held[part].at[buffer], out_hbms[part].at[slot], out_sems.at[part, buffer]
        )

    def wait_kept(buffer):
        for part in range(kept - 1):
            keep(part, 0, buffer).wait()

    def vector(index, lanes):
        return vectors_ref[index : index + 1, lanes]

    @pl.when(items > 0)
    def _first():
        load(0, 0)
        for copy in constants:
            copy.start()
        edge = jnp.zeros((side, low, LANES), jnp.float32)
        for band in range(bands):
            padded[band, :, 0:low, :] = edge
            padded[band, :, low + side :, :] = edge

    def one_item(item, carry):
        buffer = lax.rem(item, 2)
        slot = table_ref[class_field(kind, SLOT) + item]

        @pl.when(item >= 2)
        def _free():
            wait_kept(buffer)

        tile_copy(tile_refs[0], 0, buffer).wait()

        @pl.when(item == 0)
        def _taps():
            constants[0].wait()

        for band in range(bands):
            for at in range(side):
                padded[band, at, low : low + side, :] = source_s[
                    buffer, at, :, band * LANES : (band + 1) * LANES
                ].astype(jnp.float32)

        def convolve(band, carry):
            lanes = slice(band * LANES, (band + 1) * LANES)
            bias = jnp.broadcast_to(vectors_ref[DEPTH_BIAS : DEPTH_BIAS + 1, lanes], (side, LANES))
            totals = [bias for _ in range(side)]
            for col in range(KS):
                start = low - reach + col
                weights = [
                    jnp.broadcast_to(
                        taps_ref[row * KS + col : row * KS + col + 1, lanes], (side, LANES)
                    ).astype(jnp.bfloat16)
                    for row in range(KS)
                ]
                sums = [None] * side
                for at in range(side):
                    line = padded[band, at, start : start + side, :].astype(jnp.bfloat16)
                    for row in range(KS):
                        place = at - row + reach
                        if 0 <= place < side:
                            term = weights[row] * line
                            sums[place] = term if sums[place] is None else sums[place] + term
                for place in range(side):
                    totals[place] = totals[place] + sums[place].astype(jnp.float32)
            for place in range(side):
                depth_out[band, place * side : (place + 1) * side, :] = totals[place]
            return carry

        for band in range(bands):
            convolve(band, 0)
        for start in range(0, cells, PART):
            rows = slice(start, start + PART)
            pieces = [depth_out[band, rows, :] for band in range(bands)]
            mean = jnp.sum(sum(pieces), axis=1, keepdims=True) * (1.0 / channels)
            pieces = [piece - mean for piece in pieces]
            var = jnp.sum(sum(p * p for p in pieces), axis=1, keepdims=True) * (1.0 / channels)
            inv = lax.rsqrt(var + EPSILON)
            inv_s[buffer, rows, :] = jnp.broadcast_to(inv, (PART, LANES))
            for band in range(bands):
                lanes = slice(band * LANES, (band + 1) * LANES)
                unit = pieces[band] * inv
                unit_s[buffer, rows, lanes] = unit
                normed[rows, lanes] = (unit * vector(GAIN, lanes) + vector(SHIFT, lanes)).astype(
                    jnp.bfloat16
                )

        @pl.when(item == 0)
        def _weights():
            for copy in constants[1:]:
                copy.wait()

        @pl.when(item + 1 < items)
        def _next():
            @pl.when(item >= 1)
            def _source_free():
                keep(kept - 1, 0, 1 - buffer).wait()

            load(item + 1, 1 - buffer)

        for part in (2, 3):
            keep(part, slot, buffer).start()
        for index, begin in enumerate(range(0, expand_ref.shape[1], WIDTH)):
            cols = slice(begin, begin + WIDTH)
            at = index % pre.shape[0]
            pre[at] = mix(normed[...], expand_ref[:, cols])
            for start in range(0, cells, PART):
                rows = slice(start, start + PART)
                act, slope = gelu_and_slope(pre[at, rows, :] + vector(EXPAND_BIAS, cols))
                hidden_s[buffer, rows, cols] = act.astype(jnp.bfloat16)
                slope_s[buffer, rows, cols] = slope.astype(jnp.bfloat16)
        for part in (4, 5):
            keep(part, slot, buffer).start()
        lanes = slice(0, channels)
        depth_rows = mix(hidden_s[buffer], reduce_ref[...])
        for at in range(side):
            rows = slice(at * side, (at + 1) * side)
            branch = vector(SCALE, lanes) * (depth_rows[rows] + vector(REDUCE_BIAS, lanes))
            line = (source_s[buffer, at].astype(jnp.float32) + branch).astype(jnp.bfloat16)
            normed[rows, :] = line
            out_s[buffer, at] = line
        for part in (0, 7):
            keep(part, slot, buffer).start()
        for index, begin in enumerate(range(0, head_ref.shape[1], WIDTH)):
            cols = slice(begin, begin + WIDTH)
            at = index % pre.shape[0]
            pre[at] = mix(normed[...], head_ref[:, cols])
            total = None
            for start in range(0, cells, PART):
                rows = slice(start, start + PART)
                act, slope = gelu_and_slope(pre[at, rows, :])
                head_slope_s[buffer, rows, cols] = slope.astype(jnp.bfloat16)
                folded = act[0:8]
                for piece in range(8, PART, 8):
                    folded = folded + act[piece : piece + 8]
                total = folded if total is None else total + folded
            mean = jnp.sum(total, axis=0, keepdims=True) * (1.0 / cells)
            embed_s[buffer, :, cols] = jnp.broadcast_to(mean, (8, WIDTH))
        for part in (1, 6):
            keep(part, slot, buffer).start()
        return carry

    lax.fori_loop(0, items, one_item, 0)
    for back in (1, 2):

        @pl.when(items >= back)
        def _drain():
            buffer = lax.rem(items - back, 2)
            for part in range(kept):
                keep(part, 0, buffer).wait()

    if last:
        filled = sum(table_ref[FILLED + proc] for proc in range(PROC))

        @pl.when(filled < PROC)
        def _zeros():
            for ref in held:
                ref[0] = jnp.zeros(ref.shape[1:], ref.dtype)

        for proc in range(PROC):

            @pl.when(table_ref[FILLED + proc] == 0)
            def _empty():
                for part in range(kept):
                    keep(part, proc, 0).start()
                wait_kept(0)
                keep(kept - 1, proc, 0).wait()


def pinned(array):
    return pltpu.with_memory_space_constraint(array, pltpu.HBM)


def forward_block(kind, last, table, tiles, taps, vectors, expand, reduce, head, before):
    side, channels = tiles[0].shape[-2:]
    cells, hid, embed = side * side, expand.shape[1], head.shape[1]
    bands = channels // LANES
    outs = (
        ((side, side, channels), jnp.bfloat16),
        ((8, embed), jnp.float32),
        ((cells, channels), jnp.float32),
        ((cells, LANES), jnp.float32),
        ((cells, hid), jnp.bfloat16),
        ((cells, hid), jnp.bfloat16),
        ((cells, embed), jnp.bfloat16),
        ((side, side, channels), jnp.bfloat16),
    )
    smem = pl.BlockSpec(memory_space=pltpu.SMEM)
    vmem = pl.BlockSpec(memory_space=pltpu.VMEM)
    if kind == 0:
        tiles = (pinned(tiles[0]),) + tuple(tiles[1:])
    first = 1 + len(tiles) + 5
    return pl.pallas_call(
        functools.partial(forward_kernel, kind, last, len(tiles), len(outs)),
        out_shape=tuple(pltpu.HBM((PROC,) + shape, dtype) for shape, dtype in outs),
        in_specs=[smem]
        + [HBM] * len(tiles)
        + [IN_HBM, vmem, IN_HBM, IN_HBM, IN_HBM]
        + [IN_HBM] * len(before),
        out_specs=(IN_HBM,) * len(outs),
        scratch_shapes=[pltpu.VMEM((2,) + shape, dtype) for shape, dtype in outs]
        + [
            pltpu.VMEM(taps.shape, jnp.float32),
            pltpu.VMEM(expand.shape, jnp.bfloat16),
            pltpu.VMEM(reduce.shape, jnp.bfloat16),
            pltpu.VMEM(head.shape, jnp.bfloat16),
            pltpu.VMEM((bands, side, side + ROW_UNIT, LANES), jnp.float32),
            pltpu.VMEM((bands, cells, LANES), jnp.float32),
            pltpu.VMEM((cells, channels), jnp.bfloat16),
            pltpu.VMEM((3, cells, WIDTH), jnp.float32),
            pltpu.SemaphoreType.DMA((4,)),
            pltpu.SemaphoreType.DMA((2,)),
            pltpu.SemaphoreType.DMA((len(outs), 2)),
        ],
        input_output_aliases={first + index: index for index in range(len(before))},
        compiler_params=pltpu.CompilerParams(vmem_limit_bytes=24 * MIB),
        cost_estimate=cost(1.0),
        name="forward_block_" + str(kind),
    )(table, *tiles, pinned(taps), vectors, pinned(expand), pinned(reduce), pinned(head), *before)


def cost(micros):
    return pl.CostEstimate(flops=int(micros * 1e9), bytes_accessed=1024, transcendentals=0)


def rows_kernel(slides, table_ref, embed_ref, small_ref, *refs):
    buffer_refs, (out_ref, smalls_ref, rows_ref, lines_ref, extra_ref, sems) = (
        refs[: slides - 1],
        refs[slides - 1 :],
    )
    copies = [
        pltpu.make_async_copy(ref.at[ref.shape[0] - 1], extra_ref.at[index], sems.at[index])
        for index, ref in enumerate(buffer_refs)
    ]
    for copy in copies:
        copy.start()
    my_slide, my_member = lax.axis_index(DP), lax.axis_index(GROUP)
    channels = extra_ref.shape[2]
    half = E // 2
    channel = lax.broadcasted_iota(jnp.int32, (1, E), 1)
    inner = jnp.where(channel < half, channel, channel - half)
    odd = lax.rem(inner, 2)
    frequency = jnp.exp((inner - odd).astype(jnp.float32) * (-math.log(10000.0) / half))
    phase = odd.astype(jnp.float32) * (0.5 * math.pi)
    lane = lax.broadcasted_iota(jnp.int32, (1, LANES), 1)
    smalls_ref[0] = small_ref[...]
    lines = SMALL // channels
    for index, copy in enumerate(copies):
        copy.wait()
        extra = extra_ref[index].astype(jnp.float32)
        for line in range(lines):
            total = extra[line : line + 1]
            for piece in range(1, PIECES):
                total = total + extra[piece * lines + line : piece * lines + line + 1]
            smalls_ref[1 + index, :, line * channels : (line + 1) * channels] = total
    for proc in range(PROC):
        filled = table_ref[FILLED + proc]
        slide = table_ref[SLIDE + proc]
        slot = table_ref[PLACE + proc]
        held = smalls_ref[0]
        for other in range(1, slides):
            held = jnp.where((slide ^ my_slide) == other, smalls_ref[other], held)
        spots = [
            jnp.sum(jnp.where(lane == slot, held[:, at : at + LANES], 0.0), axis=1, keepdims=True)
            for at in (ROWS_AT, COLS_AT)
        ]
        angle = jnp.where(channel < half, spots[0], spots[1]) * frequency + phase
        target = jnp.where(lane == 0, slide, jnp.where(lane == 1, slot, my_member))
        target = jnp.where(filled != 0, target, jnp.where(lane == 2, -1, 0))
        target = jnp.where(lane < 3, target, 0)
        rows_ref[proc : proc + 1, 0:E] = angle
        rows_ref[2 * PROC + proc : 2 * PROC + proc + 1, 0:E] = embed_ref[proc, 0:1, :]
        rows_ref[proc : proc + 1, E:] = target.astype(jnp.float32)
    code = jnp.sin(rows_ref[0 : 2 * PROC, 0:E])
    embed = rows_ref[2 * PROC : 4 * PROC, 0:E].astype(jnp.bfloat16).astype(jnp.float32)
    row_id = lax.broadcasted_iota(jnp.int32, (2 * PROC, E), 0)
    there = row_id < 0
    for proc in range(PROC):
        there = there | ((row_id == proc) & (table_ref[FILLED + proc] != 0))
    total = jnp.where(there, embed + code, 0.0)
    rows_ref[0 : 2 * PROC, 0:E] = total
    lines_ref[...] = jnp.zeros(lines_ref.shape, jnp.float32)
    for copied in range(0, ROW_UNIT, 2 * PROC):
        lines_ref[copied : copied + PROC, :] = rows_ref[0:PROC, 0:HALF]
        lines_ref[copied + PROC : copied + 2 * PROC, 0 : E + LANES - HALF] = rows_ref[0:PROC, HALF:]
    sent = lines_ref[...].astype(jnp.bfloat16)
    for start in range(0, out_ref.shape[0], ROW_UNIT):
        out_ref[start : start + ROW_UNIT, :] = sent


def tile_rows(table, embeds, small, buffers, devices):
    smem = pl.BlockSpec(memory_space=pltpu.SMEM)
    vmem = pl.BlockSpec(memory_space=pltpu.VMEM)
    slides = 1 + len(buffers)
    return pl.pallas_call(
        functools.partial(rows_kernel, slides),
        out_shape=(
            jax.ShapeDtypeStruct((devices * 2 * PROC, HALF), jnp.bfloat16),
            jax.ShapeDtypeStruct((slides, 1, SMALL), jnp.float32),
        ),
        in_specs=[smem, vmem, vmem] + [HBM] * len(buffers),
        out_specs=(vmem, vmem),
        scratch_shapes=[
            pltpu.VMEM((4 * PROC, E + LANES), jnp.float32),
            pltpu.VMEM((ROW_UNIT, HALF), jnp.float32),
            pltpu.VMEM((len(buffers),) + buffers[0].shape[1:], jnp.bfloat16),
            pltpu.SemaphoreType.DMA((len(buffers),)),
        ],
        cost_estimate=cost(1.0),
        name="tile_rows",
    )(table, embeds, small, *buffers)


def slide_kernel(
    length,
    members,
    slides,
    table_ref,
    came_ref,
    taps_hbm,
    matrix_hbm,
    vectors_ref,
    smalls_ref,
    feature_ref,
    grad_ref,
    picks,
    own_rows,
    tile_rows,
    mixed,
    grad_agg,
    taps_ref,
    matrix_ref,
    sems,
):
    loads = [
        pltpu.make_async_copy(taps_hbm, taps_ref, sems.at[0]),
        pltpu.make_async_copy(matrix_hbm, matrix_ref, sems.at[1]),
    ]
    for load in loads:
        load.start()
    my_slide, my_member = lax.axis_index(DP), lax.axis_index(GROUP)
    border = ROW_UNIT
    reach = KERNEL_TAPS // 2
    blocks = [slice(start, start + WIDTH) for start in range(0, E, WIDTH)]
    lane = lax.broadcasted_iota(jnp.int32, (8, LANES), 1)
    scales = jnp.where(lane == 0, length, jnp.where(lane == 1, members, jnp.where(lane == 2, 1, 0)))
    tail = came_ref[:, E - HALF : E - HALF + LANES]
    target = mix_cols(scales.astype(jnp.float32).astype(jnp.bfloat16), tail)[0:1, :]
    lines = came_ref.shape[0]
    second = lax.rem(lax.broadcasted_iota(jnp.int32, (1, lines), 1), 2 * PROC) >= PROC
    target = jnp.where(second, target, -1.0)
    step = lax.broadcasted_iota(jnp.int32, (length, 1), 0)

    want = (my_slide * length + step).astype(jnp.float32)
    picks[0:length, :] = (target == want).astype(jnp.float32)
    index = lax.broadcasted_iota(jnp.int32, (ROW_UNIT, 1), 0)
    short = lax.broadcasted_iota(jnp.int32, (8, 1), 0)
    helds, shares = [], []
    for proc in range(PROC):
        filled = table_ref[FILLED + proc]
        slide = table_ref[SLIDE + proc]
        place = table_ref[PLACE + proc] * members + my_member
        at = place + (index - 2 * reach) * TILE_DILATION
        inside = (at >= 0) & (at < length) & (index <= 4 * reach) & (filled != 0)
        want = jnp.where(inside, slide * length + at, -2).astype(jnp.float32)
        start = length + proc * ROW_UNIT
        picks[start : start + ROW_UNIT, :] = (target == want).astype(jnp.float32)
        held = smalls_ref[0]
        for other in range(1, slides):
            held = jnp.where((slide ^ my_slide) == other, smalls_ref[other], held)
        helds.append(held)
        count = held[:, COUNT_AT : COUNT_AT + 1]
        at = (place + (short - reach) * TILE_DILATION).astype(jnp.float32)
        shares.append(jnp.where((at >= 0.0) & (at < count), 1.0 / count, 0.0))
    late = picks[...]
    early = pltpu.roll(late, lines - PROC, axis=1).astype(jnp.bfloat16)
    late = late.astype(jnp.bfloat16)
    edge = jnp.zeros((border, E), jnp.float32)
    own_rows[0:border, :] = edge
    own_rows[border + length :, :] = edge
    loads[0].wait()

    def tap(number, cols):
        return taps_ref[number : number + 1, cols]

    for cols in blocks:
        pick, at = (early, cols.start) if cols.start < HALF else (late, cols.start - HALF)
        found = mix(pick, came_ref[:, at : at + WIDTH])
        own_rows[border : border + length, cols] = found[0:length]
        tile_rows[:, cols] = found[length:]
        total = found[0:length]
        for number in range(KERNEL_TAPS):
            start = border + (number - reach) * TILE_DILATION
            total = total + tap(number, cols) * own_rows[start : start + length, cols]
        mixed[0:length, cols] = total.astype(jnp.bfloat16)
        totals = []
        for proc in range(PROC):
            base = proc * ROW_UNIT
            total = tile_rows[base + reach : base + reach + 8, cols]
            for number in range(KERNEL_TAPS):
                total = total + tap(number, cols) * tile_rows[base + number : base + number + 8, cols]
            totals.append(total)
        mixed[length:, cols] = jnp.concatenate(totals, axis=0).astype(jnp.bfloat16)
    count = smalls_ref[0][:, COUNT_AT : COUNT_AT + 1]
    share = jnp.where(step.astype(jnp.float32) < count, 1.0 / count, 0.0)
    loads[1].wait()
    for cols in blocks:
        bias = vectors_ref[SLIDE_BIAS : SLIDE_BIAS + 1, cols]
        pre = mix(mixed[...], matrix_ref[:, cols]) + bias
        total = None
        for start in range(0, length, PART):
            act, _ = gelu_and_slope(pre[start : start + PART])
            piece = jnp.sum(act * share[start : start + PART], axis=0, keepdims=True)
            total = piece if total is None else total + piece
        feature_ref[:, cols] = total
        _, slope = gelu_and_slope(pre[length:])
        parts = [
            helds[proc][:, cols] * shares[proc] * slope[proc * 8 : (proc + 1) * 8]
            for proc in range(PROC)
        ]
        grad_agg[:, cols] = jnp.concatenate(parts, axis=0).astype(jnp.bfloat16)
    for cols in blocks:
        grads = mix_cols(grad_agg[...], matrix_ref[cols, :])
        for proc in range(PROC):
            block = grads[proc * 8 : (proc + 1) * 8]
            total = block[reach : reach + 1]
            for number in range(KERNEL_TAPS):
                at = 2 * reach - number
                total = total + tap(number, cols) * block[at : at + 1]
            total = jnp.where(table_ref[FILLED + proc] != 0, total, 0.0)
            grad_ref[proc, :, cols] = total.astype(jnp.bfloat16).astype(jnp.float32)


def slide_grads(length, members, table, came, taps, matrix, vectors, smalls):
    slides = smalls.shape[0]
    smem = pl.BlockSpec(memory_space=pltpu.SMEM)
    vmem = pl.BlockSpec(memory_space=pltpu.VMEM)
    return pl.pallas_call(
        functools.partial(slide_kernel, length, members, slides),
        out_shape=(
            jax.ShapeDtypeStruct((1, E), jnp.float32),
            jax.ShapeDtypeStruct((PROC, 1, E), jnp.float32),
        ),
        in_specs=[smem, vmem, IN_HBM, IN_HBM, vmem, vmem],
        out_specs=(vmem, vmem),
        scratch_shapes=[
            pltpu.VMEM((length + PROC * ROW_UNIT, came.shape[0]), jnp.float32),
            pltpu.VMEM((length + 2 * ROW_UNIT, E), jnp.float32),
            pltpu.VMEM((PROC * ROW_UNIT, E), jnp.float32),
            pltpu.VMEM((length + PROC * 8, E), jnp.bfloat16),
            pltpu.VMEM((PROC * 8, E), jnp.bfloat16),
            pltpu.VMEM(taps.shape, jnp.float32),
            pltpu.VMEM(matrix.shape, jnp.bfloat16),
            pltpu.SemaphoreType.DMA((2,)),
        ],
        compiler_params=pltpu.CompilerParams(vmem_limit_bytes=16 * MIB),
        cost_estimate=cost(3.0),
        name="slide_grads",
    )(table, came, pinned(taps), pinned(matrix), vectors, smalls)


class Plan:
    def __init__(self, slides, members, channels, hid):
        self.devices = slides * members
        self.ys, self.g1, self.g2 = slides // 2, 4, members // 4
        assert self.ys == self.g2
        self.channels = channels
        self.pieces = hid // channels
        self.expand_rows = channels // self.devices
        self.reduce_rows = hid // self.devices
        self.block_rows = -(-self.reduce_rows // ROW_UNIT) * ROW_UNIT
        self.share = KS * KS * channels // self.devices

    def spots(self):
        my_core, my_y = lax.axis_index("core"), lax.axis_index("y")
        my_z, my_x = lax.axis_index("g1"), lax.axis_index("g2")
        for device in range(self.devices):
            slide, member = divmod(device, self.g1 * self.g2)
            (y, core), (z, x) = divmod(slide, 2), divmod(member, self.g2)
            yield (
                my_core ^ core,
                lax.rem(y - my_y + self.ys, self.ys),
                lax.rem(x - my_x + self.g2, self.g2),
                lax.rem(z - my_z + self.g1, self.g1),
            )


def send_out(staged, sems, refs):
    copies = [
        pltpu.make_async_copy(staged.at[index], ref, sems.at[index]) for index, ref in enumerate(refs)
    ]
    for copy in copies:
        copy.start()
    for copy in copies:
        copy.wait()


def padded_block(block, rows):
    extra = rows - block.shape[0]
    if extra:
        block = jnp.concatenate([block, jnp.zeros((extra, block.shape[1]), block.dtype)], axis=0)
    return block.astype(jnp.bfloat16)


def turn_kernel(unit_ref, vectors_ref, out_ref, normed, eye_ref):
    cells, channels = unit_ref.shape[1:]
    eye_ref[...] = unit_matrix(channels)
    for start in range(0, cells, PART):
        rows = slice(start, start + PART)
        gain = vectors_ref[GAIN : GAIN + 1, 0:channels]
        shift = vectors_ref[SHIFT : SHIFT + 1, 0:channels]
        normed[rows, :] = (unit_ref[0, rows, :] * gain + shift).astype(jnp.bfloat16)
    out_ref[...] = mix_cols(eye_ref[...], normed[...]).astype(jnp.bfloat16)


def unit_matrix(size):
    spot = lax.broadcasted_iota(jnp.int32, (size, size), 0)
    same = spot == lax.broadcasted_iota(jnp.int32, (size, size), 1)
    return same.astype(jnp.float32).astype(jnp.bfloat16)


def turned_normed(unit, vectors):
    cells, channels = unit.shape[1:]
    return pl.pallas_call(
        turn_kernel,
        out_shape=jax.ShapeDtypeStruct((channels, PROC * cells), jnp.bfloat16),
        grid=(PROC,),
        in_specs=[pl.BlockSpec((1, cells, channels), lambda i: (i, 0, 0)), whole(vectors.shape)],
        out_specs=pl.BlockSpec((channels, cells), lambda i: (0, i)),
        scratch_shapes=[
            pltpu.VMEM((cells, channels), jnp.bfloat16),
            pltpu.VMEM((channels, channels), jnp.bfloat16),
        ],
        compiler_params=pltpu.CompilerParams(vmem_limit_bytes=8 * MIB),
        cost_estimate=cost(3.0),
        name="turned_normed",
    )(unit, vectors)


def weights_kernel(
    plan,
    grad_ref,
    hidden_ref,
    head_slope_ref,
    slope_ref,
    normed_ref,
    vectors_ref,
    head_ref,
    reduce_ref,
    grad_pre_hbm,
    keep_ref,
    send_ref,
    grad_pre,
    turned,
    grad_head,
    eye_ref,
    staged,
    sems,
    pre_sems,
):
    cells, channels = slope_ref.shape[1], normed_ref.shape[0]
    hid = reduce_ref.shape[0]
    every = slice(0, channels)

    def vector(index, lanes):
        return vectors_ref[index : index + 1, lanes]

    eye_ref[...] = unit_matrix(channels)

    def one_slot(slot, carry):
        rows_all = pl.ds(pl.multiple_of(slot * cells, cells), cells)
        row = grad_ref[slot] * (1.0 / cells)
        for start in range(0, cells, PART):
            rows = slice(start, start + PART)
            grad_head[rows, :] = (row * head_slope_ref[slot, rows, :].astype(jnp.float32)).astype(
                jnp.bfloat16
            )
        grad_mlp = (vector(SCALE, every) * mix_cols(grad_head[...], head_ref[...])).astype(
            jnp.bfloat16
        )
        turned[:, rows_all] = mix_cols(eye_ref[...], grad_mlp).astype(jnp.bfloat16)
        for begin in range(0, hid, WIDTH):
            cols = slice(begin, begin + WIDTH)
            grad_hidden = mix_cols(grad_mlp, reduce_ref[cols, :])
            grad_pre[rows_all, cols] = (
                grad_hidden * slope_ref[slot, :, cols].astype(jnp.float32)
            ).astype(jnp.bfloat16)
        return carry

    lax.fori_loop(0, PROC, one_slot, 0)
    writes = [
        pltpu.make_async_copy(
            grad_pre.at[pl.ds(slot * cells, cells)], grad_pre_hbm.at[slot], pre_sems.at[slot]
        )
        for slot in range(PROC)
    ]
    for write in writes:
        write.start()
    spots = list(plan.spots())
    per_block = channels // plan.reduce_rows
    tall = plan.block_rows
    for index in range(plan.pieces):
        cols = slice(index * channels, (index + 1) * channels)
        total = mix(turned[...], hidden_ref[:, cols]).astype(jnp.bfloat16)
        back = mix_cols(eye_ref[...], total)
        for part in range(per_block):
            block = back[part * plan.reduce_rows : (part + 1) * plan.reduce_rows]
            core, y, x, z = spots[index * per_block + part]
            staged[core, 0, x, y, z] = padded_block(block, tall)
    totals = []
    for quarter in range(plan.pieces):
        cols = slice(quarter * channels, (quarter + 1) * channels)
        totals.append(mix(normed_ref[...], grad_pre[:, cols]))
    size = plan.expand_rows
    for device in range(plan.devices):
        rows = slice(device * size, (device + 1) * size)
        block = jnp.concatenate([total[rows] for total in totals], axis=0)
        core, y, x, z = spots[device]
        staged[core, 1, y, x, z] = padded_block(block, tall)
    send_out(staged, sems, (keep_ref, send_ref))
    for write in writes:
        write.wait()


def taps_kernel(
    plan,
    first,
    last,
    table_ref,
    source_ref,
    grad_pre_ref,
    unit_ref,
    inv_ref,
    before_ref,
    vectors_ref,
    expand_ref,
    out_ref,
    padded,
    tap_sums,
    tap_rows,
    grad_norm,
    depth_back,
):
    step = pl.program_id(0)
    filled = table_ref[FILLED + first + step]
    side, channels = source_ref.shape[1], source_ref.shape[3]
    bands = channels // LANES
    low = ROW_UNIT // 2
    reach = KS // 2

    @pl.when(step == 0)
    def _start():
        if first:
            tap_sums[...] = before_ref[...]
        else:
            tap_sums[...] = jnp.zeros(tap_sums.shape, jnp.float32)

    @pl.when(filled != 0)
    def _work():
        cells = side * side
        gain = vectors_ref[GAIN : GAIN + 1, 0:channels]
        grad_norm[...] = mix_cols(grad_pre_ref[0], expand_ref[...])
        for start in range(0, cells, PART):
            rows = slice(start, start + PART)
            scaled = grad_norm[rows, :] * gain
            unit = unit_ref[0, rows, :]
            mean = jnp.sum(scaled, axis=1, keepdims=True) * (1.0 / channels)
            mean_unit = jnp.sum(scaled * unit, axis=1, keepdims=True) * (1.0 / channels)
            inv = inv_ref[0, rows, 0:1]
            for band in range(bands):
                lanes = slice(band * LANES, (band + 1) * LANES)
                depth_back[band, rows, :] = (
                    inv * (scaled[:, lanes] - mean - unit[:, lanes] * mean_unit)
                ).astype(jnp.bfloat16)
        edge = jnp.zeros((side, low, LANES), jnp.float32)
        for band in range(bands):
            lanes = slice(band * LANES, (band + 1) * LANES)
            padded[band, :, 0:low, :] = edge
            padded[band, :, low + side :, :] = edge
            for at in range(side):
                padded[band, at, low : low + side, :] = source_ref[0, at, :, lanes].astype(
                    jnp.float32
                )

        def taps_of(band, carry):
            for col in range(KS):
                start = low - reach + col
                folded = [None] * KS
                grads = {}
                for half in range(2):
                    sums = [None] * KS
                    for at in range(half * side // 2, (half + 1) * side // 2):
                        line = padded[band, at, start : start + side, :].astype(jnp.bfloat16)
                        for row in range(KS):
                            place = at - row + reach
                            if 0 <= place < side:
                                if place not in grads:
                                    grads[place] = depth_back[
                                        band, place * side : (place + 1) * side, :
                                    ]
                                term = line * grads[place]
                                sums[row] = term if sums[row] is None else sums[row] + term
                    for row in range(KS):
                        total = sums[row].astype(jnp.float32)
                        for piece in range(0, side, 8):
                            block = total[piece : piece + 8, :]
                            folded[row] = block if folded[row] is None else folded[row] + block
                for row in range(KS):
                    tap_sums[band, row * KS + col] = tap_sums[band, row * KS + col] + folded[row]
            return carry

        for band in range(bands):
            taps_of(band, 0)

    @pl.when(step == pl.num_programs(0) - 1)
    def _finish():
        if not last:
            out_ref[...] = tap_sums[...]
            return
        for band in range(bands):
            lanes = slice(band * LANES, (band + 1) * LANES)
            tap_rows[0 : KS * KS, lanes] = jnp.sum(tap_sums[band], axis=1)
            tap_rows[KS * KS :, lanes] = jnp.zeros((tap_rows.shape[0] - KS * KS, LANES), jnp.float32)
        for device in range(plan.devices):
            start = device * plan.share // channels
            out_ref[device] = tap_rows[start : start + TAP_ROWS, :]


def per_slot(array):
    shape = array.shape[1:]
    return pl.BlockSpec((1,) + shape, lambda i, table: (i,) + (0,) * len(shape))


def weight_grads(plan, embed_grad, saved, vectors, head, reduce):
    normed, hidden, slope, head_slope = saved
    cells, channels = slope.shape[1], normed.shape[0]
    hid = reduce.shape[0]
    vmem = pl.BlockSpec(memory_space=pltpu.VMEM)
    blocks = jax.ShapeDtypeStruct(
        (2, plan.ys, plan.g2, plan.g1, plan.block_rows, channels), jnp.bfloat16
    )
    return pl.pallas_call(
        functools.partial(weights_kernel, plan),
        out_shape=(pltpu.HBM((PROC, cells, hid), jnp.bfloat16), blocks, blocks),
        in_specs=[vmem] * 8,
        out_specs=(IN_HBM, HBM, HBM),
        scratch_shapes=[
            pltpu.VMEM((PROC * cells, hid), jnp.bfloat16),
            pltpu.VMEM((channels, PROC * cells), jnp.bfloat16),
            pltpu.VMEM((cells, head.shape[1]), jnp.bfloat16),
            pltpu.VMEM((channels, channels), jnp.bfloat16),
            pltpu.VMEM((2,) + blocks.shape, jnp.bfloat16),
            pltpu.SemaphoreType.DMA((2,)),
            pltpu.SemaphoreType.DMA((PROC,)),
        ],
        compiler_params=pltpu.CompilerParams(vmem_limit_bytes=36 * MIB),
        cost_estimate=cost(12.0),
        name="weight_grads",
    )(embed_grad, hidden.reshape(PROC * cells, hid), head_slope, slope, normed, vectors, head, reduce)


def tap_grads(plan, first, last, table, streams, before, vectors, expand):
    side, channels = streams[0].shape[1], streams[0].shape[3]
    bands = channels // LANES
    sums = (bands, KS * KS, 8, LANES)
    out = (plan.devices, TAP_ROWS, channels) if last else sums

    def items(array):
        shape = array.shape[1:]
        return pl.BlockSpec((1,) + shape, lambda i, table: (first + i,) + (0,) * len(shape))

    return pl.pallas_call(
        functools.partial(taps_kernel, plan, first, last),
        out_shape=jax.ShapeDtypeStruct(out, jnp.float32),
        grid_spec=pltpu.PrefetchScalarGridSpec(
            num_scalar_prefetch=1,
            grid=(PROC // 2,),
            in_specs=[items(stream) for stream in streams]
            + [whole(before.shape), whole(vectors.shape), whole(expand.shape)],
            out_specs=pl.BlockSpec(out, lambda i, table: (0,) * len(out)),
            scratch_shapes=[
                pltpu.VMEM((bands, side, side + ROW_UNIT, LANES), jnp.float32),
                pltpu.VMEM(sums, jnp.float32),
                pltpu.VMEM((KS * KS + 7, channels), jnp.float32),
                pltpu.VMEM((side * side, channels), jnp.float32),
                pltpu.VMEM((bands, side * side, LANES), jnp.bfloat16),
            ],
        ),
        compiler_params=pltpu.CompilerParams(vmem_limit_bytes=16 * MIB),
        cost_estimate=cost(4.0),
        name="tap_grads_" + str(first),
    )(table, *streams, before, vectors, expand)


def shifted(values, names, sizes, shift):
    count = math.prod(sizes)
    pairs = []
    for index in range(count):
        spot = []
        rest = index
        for size in reversed(sizes):
            spot.append(rest % size)
            rest //= size
        spot = spot[::-1]
        target = 0
        for at, step, size in zip(spot, shift, sizes):
            target = target * size + (at + step) % size
        pairs.append((index, target))
    return lax.ppermute(values, names, pairs)


def shifts(sizes):
    steps = [()]
    for size in sizes:
        steps = [step + (more,) for step in steps for more in range(size)]
    return steps


def exchange(values, names):
    return lax.all_to_all(values, names, split_axis=0, concat_axis=0, tiled=True)


def add_all(parts, kind=jnp.bfloat16):
    total = parts[0].astype(jnp.float32)
    for part in parts[1:]:
        total = total + part.astype(jnp.float32)
    return total.astype(kind)


def other_core(values):
    return shifted(values, ("core",), (2,), (1,))


def sum_axis(kept, sent, name, size, kind=jnp.bfloat16):
    return [kept] + [shifted(part, (name,), (size,), (step + 1,)) for step, part in enumerate(sent)]


def on_device(
    tile_maps,
    positions,
    counts,
    routing,
    depth_kernel,
    depth_bias,
    norm_gain,
    norm_shift,
    expand_weight,
    expand_bias,
    reduce_weight,
    reduce_bias,
    layer_scale,
    head_weight,
    slide_taps,
    slide_weight,
    slide_bias,
    cotangent,
):
    slides = lax.axis_size(DP)
    members = lax.axis_size(GROUP)
    my_device = lax.axis_index(ALL)
    slots, channels = tile_maps.shape[0], tile_maps.shape[3]
    devices, length, places = slides * members, slots * members, slots // slides
    plan = Plan(slides, members, channels, expand_weight.shape[1])

    raw = (
        norm_gain,
        norm_shift,
        layer_scale,
        reduce_bias,
        depth_bias,
        expand_bias,
        slide_bias,
    )
    packed, (table, small, vectors) = pack_tiles(
        counts, routing, tile_maps, positions, cotangent, raw, slides, places
    )

    def from_other(buffer, other):
        return lax.ppermute(buffer, DP, [(index, index ^ other) for index in range(slides)])

    from_core = from_other(packed[0], 1)
    arrived = []
    for rank in range(places):
        buffers = packed[1 + rank * (slides - 2) : 1 + (rank + 1) * (slides - 2)]
        if rank:
            buffers, from_core = lax.optimization_barrier((buffers, from_core))
        arrived.append([from_other(buffer, other + 2) for other, buffer in enumerate(buffers)])

    consts = (depth_kernel, vectors, expand_weight, reduce_weight, head_weight)
    saved = forward_block(0, False, table, (tile_maps, from_core), *consts, ())
    for rank in range(places):
        saved = forward_block(1 + rank, rank + 1 == places, table, arrived[rank], *consts, saved)
    tile_out, tile_embed, unit, inv, hidden, slope, head_slope, source = saved
    came, smalls = tile_rows(table, tile_embed, small, [from_core] + arrived[0], devices)
    came = exchange(came, ALL)
    normed = turned_normed(unit, vectors)
    came, normed = lax.optimization_barrier((came, normed))

    feature, embed_grad = slide_grads(
        length, members, table, came, slide_taps, slide_weight, vectors, smalls
    )
    grad_pre, kept, sent = weight_grads(
        plan,
        embed_grad,
        (normed, hidden, slope, head_slope),
        vectors,
        head_weight,
        reduce_weight,
    )
    streams = (source, pinned(grad_pre), unit, inv)

    names = ("g2", "y")
    size = plan.ys
    came = other_core(sent)
    none = jnp.zeros((channels // LANES, KS * KS, 8, LANES), jnp.float32)
    tap_sums = tap_grads(plan, 0, False, table, streams, none, vectors, expand_weight)
    came, tap_sums = lax.optimization_barrier((came, tap_sums))
    out = [
        [add_all([kept[kind, step], came[kind, step]]) for step in range(1, size)]
        for kind in range(2)
    ]
    stay = [add_all([kept[kind, 0], came[kind, 0]]) for kind in range(2)]
    out, tap_sums = lax.optimization_barrier((out, tap_sums))
    parts = [sum_axis(stay[kind], out[kind], names[kind], size) for kind in range(2)]
    taps = tap_grads(plan, PROC // 2, True, table, streams, tap_sums, vectors, expand_weight)
    out = [
        [add_all([part[step] for part in parts[kind]]) for step in range(1, size)]
        for kind in range(2)
    ]
    stay = [add_all([part[0] for part in parts[kind]]) for kind in range(2)]
    taps = taps[:, :DEPTH_ROWS].astype(jnp.bfloat16)
    out, taps = lax.optimization_barrier((out, taps))
    parts = [sum_axis(stay[kind], out[kind], names[1 - kind], size) for kind in range(2)]
    taps = exchange(taps, ALL)
    both = jnp.concatenate([add_all(parts[0]), add_all(parts[1])], axis=1)
    total = add_all(
        sum_axis(both[0], [both[step] for step in range(1, plan.g1)], "g1", plan.g1), jnp.float32
    )
    reduce_share = total[: plan.reduce_rows]
    expand_share = total[plan.block_rows : plan.block_rows + plan.pieces * plan.expand_rows]
    expand_share = expand_share.reshape(plan.pieces, plan.expand_rows, channels).transpose(1, 0, 2)
    depth_share = lax.dynamic_slice(
        jnp.sum(taps.astype(jnp.float32), axis=0).reshape(-1),
        (my_device * plan.share % channels,),
        (plan.share,),
    )
    return (tile_out, feature, expand_share.reshape(-1), reduce_share.reshape(-1), depth_share)


def solution(mesh):
    slides, members = mesh.shape["dp"], mesh.shape["group"]
    fine = Mesh(mesh.devices.reshape(slides // 2, 2, 4, members // 4), ALL)
    return jax.shard_map(
        on_device,
        mesh=fine,
        in_specs=(
            P(ALL, None, None, None),
            P(None, ALL),
            P(DP),
            P(None, GROUP, None),
        )
        + (P(),) * 13
        + (P(DP, None),),
        out_specs=(
            P(ALL, None, None, None),
            P(DP, None),
            P(ALL),
            P(ALL),
            P(ALL),
        ),
        check_vma=False,
    )
```
